32 devices in a mesh: ctx: 8 (over y, x, core), fsdp: 4 (over z).
Axes of the slice: x: 2, y: 2, z: 4, core: 2. Of those that a mesh axis runs over, the one named last changes fastest.
Arguments:
- hidden_in: bfloat16 [4, 2048, 2048], P('fsdp', 'ctx'), may hold values from -6 to 6
- out_grad: bfloat16 [4, 2048, 2048], P('fsdp', 'ctx'), may hold values from -6 to 6
- seq_lengths: int32 [4, 3], P('fsdp'), may hold values from 1 to 1024, as said below
- block_perm: int32 [16], replicated, may hold values from 0 to 15, as said below
- first_gain: bfloat16 [2048], P('fsdp'), may hold values from 0.5 to 1.5
- query_weight: bfloat16 [2048, 2048], P(None, 'fsdp'), may hold values from -0.125 to 0.125
- key_matrix: bfloat16 [2048, 1024], P(None, 'fsdp'), may hold values from -0.125 to 0.125
- value_matrix: bfloat16 [2048, 1024], P(None, 'fsdp'), may hold values from -0.125 to 0.125
- output_weight: bfloat16 [2048, 2048], P(None, 'fsdp'), may hold values from -3 to 3
- second_gain: bfloat16 [2048], P('fsdp'), may hold values from 0.5 to 1.5
- gate_weight: bfloat16 [2048, 8192], P(None, 'fsdp'), may hold values from -0.125 to 0.125
- up_weight: bfloat16 [2048, 8192], P(None, 'fsdp'), may hold values from -0.125 to 0.125
- down_weight: bfloat16 [8192, 2048], P(None, 'fsdp'), may hold values from -0.0625 to 0.0625
- clip_limit: float32 [16], replicated, may hold values from 2 to 12
Outputs:
- layer_output: bfloat16 [4, 2048, 2048], P('fsdp', 'ctx')
- input_grad: bfloat16 [4, 2048, 2048], P('fsdp', 'ctx')
- first_gain_grad: float32 [2048], P(('ctx', 'fsdp'))
- query_grad: float32 [2048, 2048], P('ctx', 'fsdp')
- key_grad: float32 [2048, 1024], P('ctx', 'fsdp')
- value_grad: float32 [2048, 1024], P('ctx', 'fsdp')
- output_grad: float32 [2048, 2048], P('ctx', 'fsdp')
- second_gain_grad: float32 [2048], P(('ctx', 'fsdp'))
- gate_grad: float32 [2048, 8192], P('ctx', 'fsdp')
- up_grad: float32 [2048, 8192], P('ctx', 'fsdp')
- down_grad: float32 [8192, 2048], P('ctx', 'fsdp')
- head_max: float32 [16], replicated
- query_clipped: bfloat16 [2048, 2048], P(None, 'fsdp')
- key_clipped: bfloat16 [2048, 1024], P(None, 'fsdp')
The draws below stay inside these ranges and needn't reach their ends.
Inputs may be any that keep to these rules, and one draw needn't show every extreme that they name: `seq_lengths`: in each row the first length is 1024, and the later ones come in consecutive pairs that sum to 1024; each row sums to 2048. `block_perm`: A permutation; slots d * 2 to d * 2 + 1 lie on ctx index d. Block b lies in slot number b // 8 of its device; the blocks of one round b // 8 go to distinct devices, even rounds in one order of the devices and odd rounds in the reverse of that order.
All inputs are finite; a program needn't handle non-finite values.
Results may differ from the reference program's by a relative error of at most 0.02.
Values may be sent and summed in bfloat16 or wider, within the bound.
A program may use at most 576 MiB of HBM per device.

```python
import math
import jax
import jax.numpy as jnp
from jax import lax

MODEL_DIM = 2048
QUERY_HEADS = 16
KEY_VALUE_HEADS = 8
HEAD_SIZE = 128
FF = 8192
BLK = 128
BPD = 2
CYCLE = 8
GROUP_TOK = 2048
MAXLEN = 1024
NBLK = 16
GROUPS = 4


def draw_seq_lengths(key, part):
    key = jax.random.fold_in(key, 11)
    cut_points = jax.random.randint(key, (GROUPS, BPD - 1), 1, MAXLEN, dtype=jnp.int32)
    paired = jnp.stack([cut_points, MAXLEN - cut_points], 2).reshape(GROUPS, 2 * (BPD - 1))
    leading = jnp.full((GROUPS, 1), MAXLEN, jnp.int32)
    return jnp.concatenate([leading, paired], 1)


def draw_block_perm(key, part):
    key = jax.random.fold_in(key, 23)
    ordering = jax.random.permutation(key, CYCLE).astype(jnp.int32)
    blocks = jnp.arange(NBLK, dtype=jnp.int32)
    rounds = blocks // CYCLE
    places = blocks % CYCLE
    forward_device = ordering[places]
    backward_device = ordering[CYCLE - 1 - places]
    device = jnp.where(rounds % 2 == 0, forward_device, backward_device)
    return (device * BPD + rounds).astype(jnp.int32)


def steps_of(own_key, extent, pieces, smallest, high):
    gain = 1.0
    for dim, shards_of in pieces:
        draws = jax.random.uniform(jax.random.fold_in(jax.random.fold_in(own_key, 6), dim), (shards_of,), jnp.float32, smallest / len(pieces), high / len(pieces))
        gain = gain * jnp.repeat(jnp.exp(draws), extent[dim] // shards_of).reshape((-1,) + (1,) * (len(extent) - 1 - dim))
    return gain


def centred(rng, dims, scale, most, pieces=(), held_as=jnp.bfloat16):
    gain = steps_of(rng, dims, pieces, -0.22, 0.18) if pieces else 1.0
    drawn = jax.random.normal(rng, dims, jnp.float32) * scale * gain
    return jnp.minimum(jnp.maximum(drawn, -most), most).astype(held_as)


def setup_inputs(seed: int = 0) -> dict:
    splits = jax.random.split(jax.random.key(seed), 15)
    return {
        "hidden_in": centred(splits[0], (GROUPS, GROUP_TOK, MODEL_DIM), 1.0, 6.0, ((0, 4), (1, 8))),
        "out_grad": centred(splits[1], (GROUPS, GROUP_TOK, MODEL_DIM), 1.0, 6.0, ((0, 4), (1, 8))),
        "seq_lengths": draw_seq_lengths(jax.random.fold_in(splits[14], 71), 0),
        "block_perm": draw_block_perm(jax.random.fold_in(splits[14], 71), 0),
        "first_gain": jnp.clip(1.0 + 0.1 * jax.random.normal(splits[4], (MODEL_DIM,), jnp.float32), 0.5, 1.5).astype(jnp.bfloat16),
        "query_weight": centred(splits[5], (MODEL_DIM, QUERY_HEADS * HEAD_SIZE), MODEL_DIM ** -0.5, 0.125, ((1, 4),)),
        "key_matrix": centred(splits[6], (MODEL_DIM, KEY_VALUE_HEADS * HEAD_SIZE), MODEL_DIM ** -0.5, 0.125, ((1, 4),)),
        "value_matrix": centred(splits[7], (MODEL_DIM, KEY_VALUE_HEADS * HEAD_SIZE), MODEL_DIM ** -0.5, 0.125, ((1, 4),)),
        "output_weight": centred(splits[8], (QUERY_HEADS * HEAD_SIZE, MODEL_DIM), 4 ** -0.5, 3.0, ((1, 4),)),
        "second_gain": jnp.clip(1.0 + 0.1 * jax.random.normal(splits[9], (MODEL_DIM,), jnp.float32), 0.5, 1.5).astype(jnp.bfloat16),
        "gate_weight": centred(splits[10], (MODEL_DIM, FF), MODEL_DIM ** -0.5, 0.125, ((1, 4),)),
        "up_weight": centred(splits[11], (MODEL_DIM, FF), MODEL_DIM ** -0.5, 0.125, ((1, 4),)),
        "down_weight": centred(splits[12], (FF, MODEL_DIM), FF ** -0.5, 0.0625, ((1, 4),)),
        "clip_limit": jnp.clip(jnp.exp(jax.random.uniform(splits[13], (QUERY_HEADS,), jnp.float32, math.log(2.0), math.log(12.0))), 2.0, 12.0),
    }


epsilon = 1e-06
rope_base = 1000000.0
hidden_fill_value = -1e+30
top_value = lax.Precision.HIGHEST

@jax.custom_vjp
def lower_bound(v):
    return lax.optimization_barrier(v.astype(jnp.bfloat16)).astype(jnp.float32)

@jax.custom_vjp
def lower_backward(v):
    return v

def low_keep(v):
    return (lower_bound(v), None)

def low_pass(kept, grad):
    return (grad,)

def back_keep(v):
    return (v, None)

def back_low(kept, grad):
    return (lower_bound(grad),)
lower_bound.defvjp(low_keep, low_pass)
lower_backward.defvjp(back_keep, back_low)

def token_layout(length_row, block_slots, block_size):
    count_blocks = block_slots.shape[0]
    owner_block = jnp.zeros((count_blocks,), jnp.int32).at[block_slots].set(jnp.arange(count_blocks, dtype=jnp.int32))
    row_index = jnp.arange(count_blocks * block_size, dtype=jnp.int32)
    plain_order = jnp.repeat(owner_block, block_size) * block_size + row_index % block_size
    seq_ends = jnp.cumsum(length_row).astype(jnp.int32)
    seq_starts = seq_ends - length_row
    document_list = lax.optimization_barrier(jnp.sum((plain_order[:, None] >= seq_ends[None, :]).astype(jnp.int32), 1))
    matches = document_list[:, None] == jnp.arange(length_row.shape[0], dtype=jnp.int32)[None, :]
    begins = lax.optimization_barrier(jnp.sum(jnp.where(matches, seq_starts[None, :], 0), 1))
    return (plain_order, document_list, plain_order - begins)

def rope_tables(positions, head_dim):
    half_dim = head_dim // 2
    exponent = jnp.arange(half_dim, dtype=jnp.float32) * (2.0 / head_dim)
    inverse = rope_base ** (-exponent)
    angles = positions.astype(jnp.float32)[:, None] * inverse[None, :]
    return (jnp.cos(angles), jnp.sin(angles))

def apply_rotation(value_tensor, cosine_table, sine_values):
    half_dim = value_tensor.shape[-1] // 2
    first_half = value_tensor[..., :half_dim]
    second_half = value_tensor[..., half_dim:]
    cos_rows = cosine_table[:, None, :]
    sin_rows = sine_values[:, None, :]
    return jnp.concatenate([first_half * cos_rows - second_half * sin_rows, second_half * cos_rows + first_half * sin_rows], -1)

def rms_scale(value_tensor):
    return lax.rsqrt(lax.optimization_barrier(jnp.mean(value_tensor * value_tensor, -1, keepdims=True)) + epsilon)

def matrix_product(left_side, right_side):
    return jnp.dot(left_side, right_side, precision=top_value, preferred_element_type=jnp.float32)

def layer(tokens, plain_order, document_list, positions, first_gain, query_weight, key_matrix, value_matrix, output_weight, second_gain, gate_weight, up_weight, down_weight):
    rows_in_group = tokens.shape[0]
    repeat_count = QUERY_HEADS // KEY_VALUE_HEADS
    scale_of_score = 1.0 / math.sqrt(HEAD_SIZE)
    normalized = lower_bound(tokens * rms_scale(tokens) * first_gain)
    query_matrix = lower_backward(matrix_product(normalized, query_weight))
    rows_of_key = lower_backward(matrix_product(normalized, key_matrix))
    value_tensor = lower_bound(lower_backward(matrix_product(normalized, value_matrix))).reshape(rows_in_group, KEY_VALUE_HEADS, HEAD_SIZE)
    cosine_table, sine_values = rope_tables(positions, HEAD_SIZE)
    query_matrix = lower_bound(apply_rotation(query_matrix.reshape(rows_in_group, QUERY_HEADS, HEAD_SIZE), cosine_table, sine_values)).reshape(rows_in_group, KEY_VALUE_HEADS, repeat_count, HEAD_SIZE)
    rows_of_key = lower_bound(apply_rotation(rows_of_key.reshape(rows_in_group, KEY_VALUE_HEADS, HEAD_SIZE), cosine_table, sine_values))
    rows_in_block = min(512, rows_in_group)
    count_blocks = rows_in_group // rows_in_block

    def attend_rows(inputs):
        block_of_query, query_natural, query_docs = inputs
        score_matrix = jnp.einsum('pzjw,vzw->zjpv', block_of_query, rows_of_key, precision=top_value) * scale_of_score
        score_matrix = lower_backward(score_matrix)
        allowed = (query_docs[:, None] == document_list[None, :]) & (plain_order[None, :] <= query_natural[:, None])
        masked = jnp.where(allowed, score_matrix, hidden_fill_value)
        row_best = lax.optimization_barrier(jnp.max(masked, -1))
        summed = lax.optimization_barrier(jnp.sum(jnp.where(allowed, jnp.exp(masked - row_best[..., None]), 0.0), -1))
        log_total = row_best + jnp.log(summed)
        softmax_probs = lower_bound(jnp.where(allowed, jnp.exp(masked - log_total[..., None]), 0.0))
        merged_heads = jnp.einsum('eiqm,mel->qeil', softmax_probs, value_tensor, precision=top_value)
        return (merged_heads, lax.optimization_barrier(jnp.max(row_best, -1)))
    merged_heads, block_peak = lax.map(jax.checkpoint(attend_rows), (query_matrix.reshape(count_blocks, rows_in_block, KEY_VALUE_HEADS, repeat_count, HEAD_SIZE), plain_order.reshape(count_blocks, rows_in_block), document_list.reshape(count_blocks, rows_in_block)))
    attended = lower_bound(lower_backward(merged_heads.reshape(rows_in_group, QUERY_HEADS * HEAD_SIZE)))
    residual = tokens + lower_backward(matrix_product(attended, output_weight))
    normed_two = lower_bound(residual * rms_scale(residual) * second_gain)
    gate_act = lower_backward(matrix_product(normed_two, gate_weight))
    up_proj = lower_backward(matrix_product(normed_two, up_weight))
    hidden = lower_bound(jax.nn.silu(gate_act) * up_proj)
    result = residual + lower_backward(matrix_product(hidden, down_weight))
    return (result, lax.optimization_barrier(jnp.max(block_peak, 0)).reshape(QUERY_HEADS))

def reference(hidden_in, out_grad, seq_lengths, block_perm, first_gain, query_weight, key_matrix, value_matrix, output_weight, second_gain, gate_weight, up_weight, down_weight, clip_limit):

    def layout_row(length_row):
        return token_layout(length_row, block_perm, BLK)
    plain_order, document_list, positions = lax.map(layout_row, seq_lengths)
    weights = tuple((weight.astype(jnp.float32) for weight in (first_gain, query_weight, key_matrix, value_matrix, output_weight, second_gain, gate_weight, up_weight, down_weight)))

    def forward(tokens, *params):

        def one_group(inputs):
            group_tokens, group_natural, group_docs, group_positions = inputs
            return layer(group_tokens, group_natural, group_docs, group_positions, *params)
        return lax.map(one_group, (tokens, plain_order, document_list, positions))
    outputs, pullback, maxima = jax.vjp(forward, hidden_in.astype(jnp.float32), *weights, has_aux=True)
    gradients = pullback(out_grad.astype(jnp.float32))
    head_max = lax.optimization_barrier(jnp.max(maxima, 0))
    multiplier = jnp.sqrt(clip_limit / jnp.maximum(head_max, clip_limit))
    key_value_ratio = lax.optimization_barrier(jnp.min(multiplier.reshape(KEY_VALUE_HEADS, QUERY_HEADS // KEY_VALUE_HEADS), 1))
    query_clipped = (query_weight.astype(jnp.float32) * jnp.repeat(multiplier, HEAD_SIZE)[None, :]).astype(jnp.bfloat16)
    key_clipped = (key_matrix.astype(jnp.float32) * jnp.repeat(key_value_ratio, HEAD_SIZE)[None, :]).astype(jnp.bfloat16)
    return (outputs.astype(jnp.bfloat16), gradients[0].astype(jnp.bfloat16), gradients[1], gradients[2], gradients[3], gradients[4], gradients[5], gradients[6], gradients[7], gradients[8], gradients[9], head_max, query_clipped, key_clipped)
```

```python
import functools
import math

import jax
import jax.numpy as jnp
from jax import lax
from jax.experimental import pallas as pl
from jax.experimental.pallas import tpu as pltpu
from jax.sharding import PartitionSpec as P

QUERY_HEADS = 16
KEY_VALUE_HEADS = 8
HEAD_SIZE = 128
REPEAT = QUERY_HEADS // KEY_VALUE_HEADS
UNIT = (REPEAT + 2) * HEAD_SIZE

epsilon = 1e-06
rope_base = 1000000.0
hidden_fill_value = -1e30
bf16 = jnp.bfloat16
f32 = jnp.float32
SCALE = 1.0 / math.sqrt(HEAD_SIZE)


def swap(value, axis, mask):
    size = lax.axis_size(axis)
    return lax.ppermute(value, axis, [(i, i ^ mask) for i in range(size)])


def bits_down(size):
    mask = size // 2
    while mask:
        yield mask
        mask //= 2


def by_place(items, me):
    mask = 1
    while mask < len(items):
        odd = (me & mask) != 0
        items = [jnp.where(odd, items[j ^ mask], items[j]) for j in range(len(items))]
        mask *= 2
    return items


def add_rounded(left, right):
    return (left.astype(f32) + right.astype(f32)).astype(bf16)


def gather_ctx(block):
    size = lax.axis_size("ctx")
    if size != 8:
        whole = block[None]
        mask = 1
        while mask < size:
            whole = jnp.concatenate([whole, swap(whole, "ctx", mask)], 0)
            mask *= 2
        return [whole]
    half = block.shape[0] // 2
    over_x = swap(block, "ctx", 2)
    over_y = swap(block, "ctx", 4)
    other = swap(block, "ctx", 1)
    low = swap(over_x[:half], "ctx", 4)
    high = swap(over_y[half:], "ctx", 2)
    far = jnp.concatenate([low, high], 0)
    slots = [
        block,
        other,
        over_x,
        swap(over_x, "ctx", 1),
        over_y,
        swap(over_y, "ctx", 1),
        far,
        swap(far, "ctx", 1),
    ]
    return [slot[None] for slot in slots]


def sum_planes(even):
    s0, s2, s4, s6 = even
    half = s0.shape[0] // 2
    from_x = swap(s6[:half], "ctx", 2)
    from_y = swap(s6[half:], "ctx", 4)
    low2 = swap(s2[:half], "ctx", 2)
    high4 = swap(s4[half:], "ctx", 4)
    low4 = swap(add_rounded(s4[:half], from_x), "ctx", 4)
    high2 = swap(add_rounded(s2[half:], from_y), "ctx", 2)
    low = s0[:half].astype(f32) + low2.astype(f32) + low4.astype(f32)
    high = s0[half:].astype(f32) + high2.astype(f32) + high4.astype(f32)
    return jnp.concatenate([low, high], 0)


def sum_halving(slots, axis):
    for mask in bits_down(slots.shape[0]):
        keep = slots[:mask].astype(f32)
        slots = (keep + swap(slots[mask:], axis, mask).astype(f32)).astype(slots.dtype)
    return slots[0].astype(f32)


def sum_fsdp(pieces):
    total = pieces[0].astype(f32)
    for d in range(1, len(pieces)):
        total = total + swap(pieces[d].astype(bf16), "fsdp", d).astype(f32)
    return total


def params(flops, bytes_accessed):
    return dict(
        compiler_params=pltpu.CompilerParams(vmem_limit_bytes=48 * 2**20),
        cost_estimate=pl.CostEstimate(
            flops=flops, bytes_accessed=bytes_accessed, transcendentals=0
        ),
    )


def rotate(value, cosine, sine):
    return value * cosine + pltpu.roll(value, HEAD_SIZE // 2, 1) * sine


def slot_matmul_body(n_slots, parts, depth, rope, me_ref, x_ref, *refs):
    slot_refs = refs[:n_slots]
    out_ref = refs[-1]
    total = None
    for j in range(n_slots):
        for q in range(parts):
            owner = me_ref[0] ^ (j * parts + q)
            cols = pl.ds(pl.multiple_of(owner * depth, depth), depth)
            term = jnp.dot(x_ref[:, cols], slot_refs[j][q], preferred_element_type=f32)
            total = term if total is None else total + term
    if rope:
        cosine, sine = refs[n_slots][...], refs[n_slots + 1][...]
        parts_out = [
            rotate(total[:, i * HEAD_SIZE : (i + 1) * HEAD_SIZE], cosine, sine)
            for i in range(REPEAT + 1)
        ]
        total = jnp.concatenate(parts_out + [total[:, (REPEAT + 1) * HEAD_SIZE :]], 1)
    out_ref[...] = total.astype(out_ref.dtype)


def in_order(slots, me):
    whole = jnp.concatenate(slots, 0)
    whole = whole[me ^ jnp.arange(whole.shape[0], dtype=jnp.int32)]
    return whole.reshape(-1, whole.shape[2])


def slot_matmul(x, slots, me, tile, out_dtype, tables=None):
    rows = x.shape[0]
    parts, depth, width = slots[0].shape
    if depth % 128:
        total = product(x, in_order(slots, me))
        if tables is None:
            return total.astype(out_dtype)
        total = total.reshape(rows, width // UNIT, REPEAT + 2, HEAD_SIZE)
        cosine, sine = (t[:, None, None] for t in tables)
        turned = total[:, :, : REPEAT + 1]
        turned = turned * cosine + jnp.roll(turned, HEAD_SIZE // 2, -1) * sine
        total = jnp.concatenate([turned, total[:, :, REPEAT + 1 :]], 2)
        return total.reshape(rows, width).astype(out_dtype)
    extra = [] if tables is None else list(tables)
    body = functools.partial(
        slot_matmul_body, len(slots), parts, depth, tables is not None
    )
    return pl.pallas_call(
        body,
        out_shape=jax.ShapeDtypeStruct((rows, width), out_dtype),
        grid_spec=pltpu.PrefetchScalarGridSpec(
            num_scalar_prefetch=1,
            grid=(width // tile,),
            in_specs=[pl.BlockSpec(x.shape, lambda i, me: (0, 0))]
            + [pl.BlockSpec((parts, depth, tile), lambda i, me: (0, 0, i))] * len(slots)
            + [pl.BlockSpec(e.shape, lambda i, me: (0, 0)) for e in extra],
            out_specs=pl.BlockSpec((rows, tile), lambda i, me: (0, i)),
        ),
        **params(2 * rows * x.shape[1] * width, 2 * x.shape[1] * width),
    )(me, x, *slots, *extra)


def slot_matmul_t_body(n_slots, parts, depth, me_ref, x_ref, *refs):
    slot_refs = refs[:n_slots]
    out_ref, total_ref = refs[n_slots], refs[n_slots + 1]
    step = pl.program_id(0)

    @pl.when(step == 0)
    def _():
        total_ref[...] = jnp.zeros_like(total_ref)

    x = x_ref[...]
    for j in range(n_slots):
        for q in range(parts):
            owner = me_ref[0] ^ (j * parts + q)
            cols = pl.ds(pl.multiple_of(owner * depth, depth), depth)
            total_ref[:, cols] += lax.dot_general(
                x, slot_refs[j][q], (((1,), (1,)), ((), ())), preferred_element_type=f32
            )

    @pl.when(step == pl.num_programs(0) - 1)
    def _():
        out_ref[...] = total_ref[...].astype(out_ref.dtype)


def slot_matmul_t(x, slots, me, tile, out_dtype):
    rows, width = x.shape
    parts, depth, _ = slots[0].shape
    height = parts * depth * len(slots)
    if depth % 128:
        return product_t(x, in_order(slots, me)).astype(out_dtype)
    return pl.pallas_call(
        functools.partial(slot_matmul_t_body, len(slots), parts, depth),
        out_shape=jax.ShapeDtypeStruct((rows, height), out_dtype),
        grid_spec=pltpu.PrefetchScalarGridSpec(
            num_scalar_prefetch=1,
            grid=(width // tile,),
            in_specs=[pl.BlockSpec((rows, tile), lambda i, me: (0, i))]
            + [pl.BlockSpec((parts, depth, tile), lambda i, me: (0, 0, i))]
            * len(slots),
            out_specs=pl.BlockSpec((rows, height), lambda i, me: (0, 0)),
            scratch_shapes=[pltpu.VMEM((rows, height), f32)],
        ),
        **params(2 * rows * height * width, 2 * height * width),
    )(me, x, *slots)


def keys_of(slot_refs):
    def column(i):
        parts = [
            r[:, :, i * HEAD_SIZE : (i + 1) * HEAD_SIZE].reshape(-1, HEAD_SIZE)
            for r in slot_refs
        ]
        return parts[0] if len(parts) == 1 else jnp.concatenate(parts, 0)

    return column(0), column(1)


def scores_of(qkv_ref, keys, natural_ref, start_ref, key_natural_ref):
    blk = qkv_ref.shape[0]
    query = jnp.concatenate(
        [qkv_ref[:, i * HEAD_SIZE : (i + 1) * HEAD_SIZE] for i in range(REPEAT)], 0
    )
    scores = (
        lax.dot_general(
            query, keys, (((1,), (1,)), ((), ())), preferred_element_type=f32
        )
        * SCALE
    )
    key_natural = key_natural_ref[0]
    allowed = (key_natural >= start_ref[...]) & (key_natural <= natural_ref[...])
    allowed = jnp.concatenate([allowed] * REPEAT, 0)
    scores = jnp.where(allowed, scores, hidden_fill_value)
    best = jnp.max(scores, 1, keepdims=True)
    exps = jnp.exp(scores - best)
    return query, exps / jnp.sum(exps, 1, keepdims=True), best, blk


def attend_body(n_slots, natural_ref, start_ref, key_natural_ref, qkv_ref, *refs):
    slot_refs, (out_ref, best_ref) = refs[:n_slots], refs[n_slots:]
    keys, values = keys_of(slot_refs)
    _, probs, best, blk = scores_of(qkv_ref, keys, natural_ref, start_ref, key_natural_ref)
    heads = jnp.dot(probs.astype(bf16), values, preferred_element_type=f32)
    out_ref[...] = jnp.concatenate(
        [heads[i * blk : (i + 1) * blk] for i in range(REPEAT)], 1
    ).astype(bf16)
    tops = [
        jnp.broadcast_to(jnp.max(best[i * blk : (i + 1) * blk], 0, keepdims=True), (1, 128))
        for i in range(REPEAT)
    ]
    best_ref[0, 0] = jnp.concatenate(tops + [jnp.zeros((8 - REPEAT, 128), f32)], 0)


def attend_back_body(
    n_slots, natural_ref, start_ref, key_natural_ref, cosine_ref, sine_ref, qkv_ref, grad_ref, *refs
):
    slot_refs, (dq_ref, *dkv_refs) = refs[:n_slots], refs[n_slots:]
    keys, values = keys_of(slot_refs)
    query, probs, _, blk = scores_of(qkv_ref, keys, natural_ref, start_ref, key_natural_ref)
    grad = jnp.concatenate(
        [grad_ref[:, i * HEAD_SIZE : (i + 1) * HEAD_SIZE] for i in range(REPEAT)], 0
    )
    low = probs.astype(bf16)
    grad_probs = lax.dot_general(
        grad, values, (((1,), (1,)), ((), ())), preferred_element_type=f32
    )
    delta = jnp.sum(low.astype(f32) * grad_probs, 1, keepdims=True)
    score_grad = (probs * (grad_probs - delta)).astype(bf16)
    query_grad = jnp.dot(score_grad, keys, preferred_element_type=f32) * SCALE
    cosine, sine = cosine_ref[...], sine_ref[...]
    dq_ref[...] = jnp.concatenate(
        [
            rotate(query_grad[i * blk : (i + 1) * blk], cosine, -sine)
            for i in range(REPEAT)
        ],
        1,
    ).astype(bf16)
    over_rows = (((0,), (0,)), ((), ()))
    key_grad = (
        lax.dot_general(score_grad, query, over_rows, preferred_element_type=f32) * SCALE
    ).astype(bf16)
    value_grad = lax.dot_general(low, grad, over_rows, preferred_element_type=f32).astype(
        bf16
    )
    both = jnp.concatenate([key_grad, value_grad], 1)
    rows = both.shape[0] // n_slots
    for j, ref in enumerate(dkv_refs):
        ref[...] = both[j * rows : (j + 1) * rows].reshape(ref.shape)


def attention_specs(slots, blk, keys):
    parts = slots[0].shape[0]
    column = pl.BlockSpec((blk, 1), lambda r, h: (r, 0))
    slot = pl.BlockSpec((parts, blk, 2 * HEAD_SIZE), lambda r, h: (0, r, h))
    return (
        [column, column, pl.BlockSpec((1, 1, keys), lambda r, h: (r, 0, 0))],
        pl.BlockSpec((blk, UNIT), lambda r, h: (r, h)),
        pl.BlockSpec((blk, REPEAT * HEAD_SIZE), lambda r, h: (r, h)),
        slot,
    )


def attend(natural, start, key_natural, qkv, slots):
    rows = qkv.shape[0]
    rounds, _, keys = key_natural.shape
    blk = rows // rounds
    meta, unit, pair, slot = attention_specs(slots, blk, keys)
    return pl.pallas_call(
        functools.partial(attend_body, len(slots)),
        grid=(rounds, KEY_VALUE_HEADS),
        in_specs=meta + [unit] + [slot] * len(slots),
        out_specs=[pair, pl.BlockSpec((1, 1, 8, 128), lambda r, h: (r, h, 0, 0))],
        out_shape=[
            jax.ShapeDtypeStruct((rows, QUERY_HEADS * HEAD_SIZE), bf16),
            jax.ShapeDtypeStruct((rounds, KEY_VALUE_HEADS, 8, 128), f32),
        ],
        **params(4 * rows * keys * QUERY_HEADS * HEAD_SIZE, 12 * 2**20),
    )(natural, start, key_natural, qkv, *slots)


def attend_back(natural, start, key_natural, cosine, sine, qkv, grad, slots):
    rows = qkv.shape[0]
    rounds, _, keys = key_natural.shape
    blk = rows // rounds
    meta, unit, pair, slot = attention_specs(slots, blk, keys)
    table = pl.BlockSpec((blk, HEAD_SIZE), lambda r, h: (r, 0))
    return pl.pallas_call(
        functools.partial(attend_back_body, len(slots)),
        grid=(rounds, KEY_VALUE_HEADS),
        in_specs=meta + [table, table, unit, pair] + [slot] * len(slots),
        out_specs=[pair] + [slot] * len(slots),
        out_shape=[jax.ShapeDtypeStruct((rows, QUERY_HEADS * HEAD_SIZE), bf16)]
        + [jax.ShapeDtypeStruct(s.shape, bf16) for s in slots],
        **params(10 * rows * keys * QUERY_HEADS * HEAD_SIZE, 20 * 2**20),
    )(natural, start, key_natural, cosine, sine, qkv, grad, *slots)


def token_layout(length_row, block_slots, block_size):
    count_blocks = block_slots.shape[0]
    owner_block = jnp.argmax(
        block_slots[None, :] == jnp.arange(count_blocks, dtype=jnp.int32)[:, None], 1
    ).astype(jnp.int32)
    row_index = jnp.arange(count_blocks * block_size, dtype=jnp.int32)
    plain_order = jnp.repeat(owner_block, block_size) * block_size + row_index % block_size
    seq_ends = jnp.cumsum(length_row)
    seq_starts = seq_ends - length_row
    document_list = jnp.sum((plain_order[:, None] >= seq_ends[None, :]).astype(jnp.int32), 1)
    matches = document_list[:, None] == jnp.arange(length_row.shape[0], dtype=jnp.int32)[None, :]
    begins = jnp.sum(jnp.where(matches, seq_starts[None, :], 0), 1)
    return plain_order, begins


def rms_scale(value):
    return lax.rsqrt(jnp.mean(value * value, -1, keepdims=True) + epsilon)


def norm_back(grad_unit, unit_rows, scale_rows):
    return scale_rows * (grad_unit - unit_rows * jnp.mean(grad_unit * unit_rows, -1, keepdims=True))


def product(left, right):
    return jnp.dot(left, right, preferred_element_type=f32)


def product_t(left, right):
    return lax.dot_general(left, right, (((1,), (1,)), ((), ())), preferred_element_type=f32)


def over_rows(left, right):
    return lax.dot_general(left, right, (((0,), (0,)), ((), ())), preferred_element_type=f32)


def column_blocks(value, count, places):
    width = value.shape[1] // count
    return jnp.concatenate(
        [lax.dynamic_slice_in_dim(value, place * width, width, 1) for place in places], 1
    )


def gather_rows(piece, fsdp_place, ctx_count):
    count = lax.axis_size("fsdp")
    parts = [piece] + [swap(piece, "fsdp", d) for d in range(1, count)]
    return jnp.concatenate(by_place(parts, fsdp_place), 1)


def weight_grad_sum(left, right, me, count):
    depth = left.shape[1] // count
    if count == 8:
        sent = over_rows(column_blocks(left, 8, [me ^ j for j in (1, 3, 5, 7)]), right)
        kept = over_rows(column_blocks(left, 8, [me ^ j for j in (0, 2, 4, 6)]), right)
        both = add_rounded(kept.astype(bf16), swap(sent.astype(bf16), "ctx", 1))
        return sum_planes([both[i * depth : (i + 1) * depth] for i in range(4)])
    full = over_rows(column_blocks(left, count, [me ^ j for j in range(count)]), right)
    return sum_halving(full.astype(bf16).reshape(count, depth, right.shape[1]), "ctx")


def down_grad_sum(hidden, grad, me, count, fsdp_count):
    bands = count // fsdp_count
    band, column = me // fsdp_count, me % fsdp_count
    depth = hidden.shape[1] // bands
    width = grad.shape[1] // fsdp_count
    left = column_blocks(hidden, bands, [band ^ j for j in range(bands)])
    if count == 8:
        sent = over_rows(left, column_blocks(grad, 4, [column ^ 1, column ^ 3])).astype(bf16)
        kept = over_rows(left, column_blocks(grad, 4, [column, column ^ 2])).astype(bf16)
        both = add_rounded(kept, swap(sent, "ctx", 1))
        return sum_planes(
            [
                both[r * depth : (r + 1) * depth, s * width : (s + 1) * width]
                for r in range(2)
                for s in range(2)
            ]
        )
    right = column_blocks(grad, fsdp_count, [column ^ j for j in range(fsdp_count)])
    full = over_rows(left, right).astype(bf16).reshape(bands, depth, fsdp_count, width)
    return sum_halving(full.transpose(0, 2, 1, 3).reshape(count, depth, width), "ctx")


def clipped(weight, multiplier):
    columns = weight.shape[1]
    head_index = (
        lax.axis_index("fsdp") * columns + jnp.arange(columns, dtype=jnp.int32)
    ) // HEAD_SIZE
    matches = head_index[:, None] == jnp.arange(multiplier.shape[0], dtype=jnp.int32)[None, :]
    column_factor = jnp.sum(jnp.where(matches, multiplier[None, :], 0.0), 1)
    return (weight.astype(f32) * column_factor[None, :]).astype(bf16)


def gain_sum(term, me, place, count, fsdp_count):
    table = term.reshape(count, fsdp_count, -1)
    table = jnp.stack(by_place([table[i] for i in range(count)], me))
    mine = sum_halving(table, "ctx")
    mine = jnp.stack(by_place([mine[i] for i in range(fsdp_count)], place))
    return sum_halving(mine, "fsdp")


def on_device(
    hidden_in,
    out_grad,
    seq_lengths,
    block_perm,
    first_gain,
    query_weight,
    key_matrix,
    value_matrix,
    output_weight,
    second_gain,
    gate_weight,
    up_weight,
    down_weight,
    clip_limit,
):
    rows, model = hidden_in.shape[1], hidden_in.shape[2]
    count, fsdp_count = lax.axis_size("ctx"), lax.axis_size("fsdp")
    me, place = lax.axis_index("ctx"), lax.axis_index("fsdp")
    me_ref = me.astype(jnp.int32).reshape(1)
    depth = model // count
    blocks = block_perm.shape[0]
    rounds = blocks // count
    blk = rows // rounds
    shard_heads = KEY_VALUE_HEADS // fsdp_count

    def own_rows(weight):
        return lax.dynamic_slice_in_dim(weight, me * depth, depth, 0)

    unit_rows = jnp.concatenate(
        [
            own_rows(query_weight).reshape(depth, shard_heads, REPEAT, HEAD_SIZE),
            own_rows(key_matrix).reshape(depth, shard_heads, 1, HEAD_SIZE),
            own_rows(value_matrix).reshape(depth, shard_heads, 1, HEAD_SIZE),
        ],
        2,
    ).reshape(depth, shard_heads * UNIT)
    unit_rows = gather_rows(unit_rows, place, count)
    unit_slots = gather_ctx(unit_rows)
    gains = jnp.stack([first_gain, second_gain])
    gains = jnp.concatenate(
        by_place([gains] + [swap(gains, "fsdp", d) for d in range(1, fsdp_count)], place), 1
    ).astype(f32)
    first_full, second_full = gains[0], gains[1]
    output_rows = gather_rows(own_rows(output_weight), place, count)
    output_slots = gather_ctx(output_rows)

    hidden_width = gate_weight.shape[1]
    down_depth = hidden_width // count

    def down_piece(d):
        first = (place ^ d) * hidden_width + me * down_depth
        return lax.dynamic_slice_in_dim(down_weight, first, down_depth, 0)

    down_rows = [down_piece(0)] + [
        swap(down_piece(d), "fsdp", d) for d in range(1, fsdp_count)
    ]
    down_slots = gather_ctx(jnp.concatenate(by_place(down_rows, place), 1))

    plain_order, begins = token_layout(seq_lengths[0], block_perm, blk)
    first_row = me * rows
    natural = lax.dynamic_slice_in_dim(plain_order, first_row, rows)
    begin = lax.dynamic_slice_in_dim(begins, first_row, rows)
    half_dim = HEAD_SIZE // 2
    exponent = jnp.arange(half_dim, dtype=f32) * (2.0 / HEAD_SIZE)
    inverse = rope_base ** (-exponent)
    angles = (natural - begin).astype(f32)[:, None] * inverse[None, :]
    cosine = jnp.concatenate([jnp.cos(angles)] * 2, 1)
    sine = jnp.concatenate([-jnp.sin(angles), jnp.sin(angles)], 1)
    slot_order = plain_order.reshape(count, rounds, blk)
    slot_order = jnp.stack(by_place([slot_order[i] for i in range(count)], me), 1)
    key_natural = slot_order.reshape(rounds, 1, count * blk)
    natural_column, begin_column = natural[:, None], begin[:, None]

    tokens = hidden_in.reshape(rows, model).astype(f32)
    scale_one = rms_scale(tokens)
    unit_one = tokens * scale_one
    normalized = (unit_one * first_full).astype(bf16)
    qkv = slot_matmul(normalized, unit_slots, me_ref, UNIT, bf16, (cosine, sine))
    kv_local = qkv.reshape(rows, KEY_VALUE_HEADS, UNIT)[:, :, REPEAT * HEAD_SIZE :].reshape(
        rows, KEY_VALUE_HEADS * 2 * HEAD_SIZE
    )
    kv_slots = gather_ctx(kv_local)
    attended, best = attend(natural_column, begin_column, key_natural, qkv, kv_slots)
    head_max = jnp.max(best[:, :, :REPEAT, 0], 0).reshape(QUERY_HEADS)
    for mask in bits_down(count):
        head_max = jnp.maximum(head_max, swap(head_max, "ctx", mask))
    for mask in bits_down(fsdp_count):
        head_max = jnp.maximum(head_max, swap(head_max, "fsdp", mask))
    residual = tokens + slot_matmul(attended, output_slots, me_ref, 512, f32)
    scale_two = rms_scale(residual)
    unit_two = residual * scale_two
    normed_two = (unit_two * second_full).astype(bf16)

    grad_out = out_grad.reshape(rows, model)
    others = range(1, fsdp_count)
    grads = [grad_out] + [swap(grad_out, "fsdp", d) for d in others]
    normed = [normed_two] + [swap(normed_two, "fsdp", d) for d in others]
    hidden_parts, gate_parts, up_parts, sums, backs = [], [], [], [], []
    for d in range(fsdp_count):
        grad_hidden = slot_matmul_t(grads[d], down_slots, me_ref, 512, f32)
        gate_act = product(normed[d], gate_weight)
        up_proj = product(normed[d], up_weight)
        sigmoid = jax.nn.sigmoid(gate_act)
        hidden = (gate_act * sigmoid * up_proj).astype(bf16)
        grad_gate = (
            grad_hidden * up_proj * sigmoid * (1.0 + gate_act * (1.0 - sigmoid))
        ).astype(bf16)
        grad_up = (grad_hidden * gate_act * sigmoid).astype(bf16)
        hidden_parts.append(hidden)
        gate_parts.append(grad_gate)
        up_parts.append(grad_up)
        backs.append(product_t(grad_gate, gate_weight) + product_t(grad_up, up_weight))
        sums.append(slot_matmul(hidden, down_slots, me_ref, 512, f32 if d == 0 else bf16))
    grad_normed_two = sum_fsdp(backs)
    result = (residual + sum_fsdp(sums)).astype(bf16)

    second_term = jnp.sum(grad_normed_two * unit_two, 0)
    grad_residual = grad_out.astype(f32) + norm_back(
        grad_normed_two * second_full, unit_two, scale_two
    )
    grad_branch = grad_residual.astype(bf16)
    head_grad = slot_matmul_t(grad_branch, output_slots, me_ref, 512, bf16)
    query_grad, *dkv_slots = attend_back(
        natural_column, begin_column, key_natural, cosine, sine, qkv, head_grad, kv_slots
    )
    if count == 8:
        even = [
            add_rounded(dkv_slots[j][0], swap(dkv_slots[j + 1][0], "ctx", 1))
            for j in (0, 2, 4, 6)
        ]
        dkv = sum_planes(even)
    else:
        dkv = sum_halving(dkv_slots[0], "ctx")
    dkv = dkv.reshape(rows, KEY_VALUE_HEADS, 2, HEAD_SIZE)
    grad_key = dkv[:, :, 0]
    first, second = grad_key[..., :half_dim], grad_key[..., half_dim:]
    cos, sin = cosine[:, None, :half_dim], sine[:, None, half_dim:]
    grad_key = jnp.concatenate([first * cos + second * sin, second * cos - first * sin], -1)
    dqkv = jnp.concatenate(
        [
            query_grad.reshape(rows, KEY_VALUE_HEADS, REPEAT, HEAD_SIZE),
            grad_key[:, :, None].astype(bf16),
            dkv[:, :, 1:].astype(bf16),
        ],
        2,
    ).reshape(rows, KEY_VALUE_HEADS * UNIT)
    grad_normed_one = slot_matmul_t(dqkv, unit_slots, me_ref, 512, f32)
    first_term = jnp.sum(grad_normed_one * unit_one, 0)
    grad_input = grad_residual + norm_back(grad_normed_one * first_full, unit_one, scale_one)

    hidden_all = jnp.concatenate(hidden_parts, 0)
    normed_all = jnp.concatenate(normed, 0)
    grads_all = jnp.concatenate(grads, 0)
    down_sum = down_grad_sum(hidden_all, grads_all, me, count, fsdp_count).astype(bf16)
    bands = count // fsdp_count
    places = [
        (c * fsdp_count + f, (bands * f + c // fsdp_count) * fsdp_count + c % fsdp_count)
        for c in range(count)
        for f in range(fsdp_count)
    ]
    down_grad = lax.ppermute(down_sum, ("ctx", "fsdp"), places).astype(f32)
    gate_grad = weight_grad_sum(normed_all, jnp.concatenate(gate_parts, 0), me, count)
    up_grad = weight_grad_sum(normed_all, jnp.concatenate(up_parts, 0), me, count)

    def over_fsdp(summed):
        width = summed.shape[1] // fsdp_count
        return sum_fsdp(
            [
                lax.dynamic_slice_in_dim(summed, (place ^ d) * width, width, 1)
                for d in range(fsdp_count)
            ]
        )

    output_grad = over_fsdp(weight_grad_sum(attended, grad_branch, me, count))
    unit_grad = over_fsdp(weight_grad_sum(normalized, dqkv, me, count))
    unit_grad = unit_grad.reshape(depth, shard_heads, REPEAT + 2, HEAD_SIZE)
    query_out = unit_grad[:, :, :REPEAT].reshape(depth, -1)
    key_out = unit_grad[:, :, REPEAT].reshape(depth, -1)
    value_out = unit_grad[:, :, REPEAT + 1].reshape(depth, -1)

    first_out = gain_sum(first_term, me, place, count, fsdp_count)
    second_out = gain_sum(second_term, me, place, count, fsdp_count)
    multiplier = jnp.sqrt(clip_limit / jnp.maximum(head_max, clip_limit))
    key_ratio = jnp.min(multiplier.reshape(KEY_VALUE_HEADS, REPEAT), 1)
    return (
        result.reshape(1, rows, model),
        grad_input.astype(bf16).reshape(1, rows, model),
        first_out,
        query_out,
        key_out,
        value_out,
        output_grad,
        second_out,
        gate_grad,
        up_grad,
        down_grad,
        head_max,
        clipped(query_weight, multiplier),
        clipped(key_matrix, key_ratio),
    )


def solution(mesh):
    shard, whole = P(None, "fsdp"), P()
    token, block = P("fsdp", "ctx", None), P("ctx", "fsdp")
    gain = P(("ctx", "fsdp"))
    return jax.shard_map(
        on_device,
        mesh=mesh,
        in_specs=(token, token, P("fsdp", None), whole, P("fsdp"))
        + (shard,) * 4
        + (P("fsdp"),)
        + (shard,) * 3
        + (whole,),
        out_specs=(token, token, gain)
        + (block,) * 4
        + (gain,)
        + (block,) * 3
        + (whole, shard, shard),
        check_vma=False,
    )
```

```python
import functools
import math

import jax
import jax.numpy as jnp
from jax import lax
from jax.experimental import pallas as pl
from jax.experimental.pallas import tpu as pltpu
from jax.sharding import PartitionSpec as P

QUERY_HEADS = 16
KEY_VALUE_HEADS = 8
HEAD_SIZE = 128
REPEAT = QUERY_HEADS // KEY_VALUE_HEADS
UNIT = (REPEAT + 2) * HEAD_SIZE

epsilon = 1e-06
rope_base = 1000000.0
hidden_fill_value = -1e30
bf16 = jnp.bfloat16
f32 = jnp.float32
SCALE = 1.0 / math.sqrt(HEAD_SIZE)


def swap(value, axis, mask):
    size = lax.axis_size(axis)
    return lax.ppermute(value, axis, [(i, i ^ mask) for i in range(size)])


def bits_down(size):
    mask = size // 2
    while mask:
        yield mask
        mask //= 2


def by_place(items, me):
    mask = 1
    while mask < len(items):
        odd = (me & mask) != 0
        items = [jnp.where(odd, items[j ^ mask], items[j]) for j in range(len(items))]
        mask *= 2
    return items


def gather_ctx(block):
    size = lax.axis_size("ctx")
    whole = block[None]
    mask = 1
    while mask < size:
        whole = jnp.concatenate([whole, swap(whole, "ctx", mask)], 0)
        mask *= 2
    return [whole]


def sum_halving(slots, axis):
    for mask in bits_down(slots.shape[0]):
        keep = slots[:mask].astype(f32)
        slots = (keep + swap(slots[mask:], axis, mask).astype(f32)).astype(slots.dtype)
    return slots[0].astype(f32)


def sum_fsdp(pieces):
    total = pieces[0].astype(f32)
    for d in range(1, len(pieces)):
        total = total + swap(pieces[d].astype(bf16), "fsdp", d).astype(f32)
    return total


def params(flops, bytes_accessed):
    return dict(
        compiler_params=pltpu.CompilerParams(vmem_limit_bytes=48 * 2**20),
        cost_estimate=pl.CostEstimate(
            flops=flops, bytes_accessed=bytes_accessed, transcendentals=0
        ),
    )


def rotate(value, cosine, sine):
    return value * cosine + pltpu.roll(value, HEAD_SIZE // 2, 1) * sine


def slot_matmul_body(n_slots, parts, depth, rope, me_ref, x_ref, *refs):
    slot_refs = refs[:n_slots]
    out_ref = refs[-1]
    total = None
    for j in range(n_slots):
        for q in range(parts):
            owner = me_ref[0] ^ (j * parts + q)
            cols = pl.ds(pl.multiple_of(owner * depth, depth), depth)
            term = jnp.dot(x_ref[:, cols], slot_refs[j][q], preferred_element_type=f32)
            total = term if total is None else total + term
    if rope:
        cosine, sine = refs[n_slots][...], refs[n_slots + 1][...]
        parts_out = [
            rotate(total[:, i * HEAD_SIZE : (i + 1) * HEAD_SIZE], cosine, sine)
            for i in range(REPEAT + 1)
        ]
        total = jnp.concatenate(parts_out + [total[:, (REPEAT + 1) * HEAD_SIZE :]], 1)
    out_ref[...] = total.astype(out_ref.dtype)


def in_order(slots, me):
    whole = jnp.concatenate(slots, 0)
    whole = whole[me ^ jnp.arange(whole.shape[0], dtype=jnp.int32)]
    return whole.reshape(-1, whole.shape[2])


def in_order(slots, me):
    whole = jnp.concatenate(slots, 0)
    whole = whole[me ^ jnp.arange(whole.shape[0], dtype=jnp.int32)]
    return whole.reshape(-1, whole.shape[2])


def slot_matmul(x, slots, me, tile, out_dtype, tables=None):
    rows = x.shape[0]
    parts, depth, width = slots[0].shape
    if depth % 128:
        total = product(x, in_order(slots, me))
        if tables is None:
            return total.astype(out_dtype)
        total = total.reshape(rows, width // UNIT, REPEAT + 2, HEAD_SIZE)
        cosine, sine = (t[:, None, None] for t in tables)
        turned = total[:, :, : REPEAT + 1]
        turned = turned * cosine + jnp.roll(turned, HEAD_SIZE // 2, -1) * sine
        total = jnp.concatenate([turned, total[:, :, REPEAT + 1 :]], 2)
        return total.reshape(rows, width).astype(out_dtype)
    extra = [] if tables is None else list(tables)
    body = functools.partial(
        slot_matmul_body, len(slots), parts, depth, tables is not None
    )
    return pl.pallas_call(
        body,
        out_shape=jax.ShapeDtypeStruct((rows, width), out_dtype),
        grid_spec=pltpu.PrefetchScalarGridSpec(
            num_scalar_prefetch=1,
            grid=(width // tile,),
            in_specs=[pl.BlockSpec(x.shape, lambda i, me: (0, 0))]
            + [pl.BlockSpec((parts, depth, tile), lambda i, me: (0, 0, i))] * len(slots)
            + [pl.BlockSpec(e.shape, lambda i, me: (0, 0)) for e in extra],
            out_specs=pl.BlockSpec((rows, tile), lambda i, me: (0, i)),
        ),
        **params(2 * rows * x.shape[1] * width, 2 * x.shape[1] * width),
    )(me, x, *slots, *extra)


def slot_matmul_t_body(n_slots, parts, depth, me_ref, x_ref, *refs):
    slot_refs = refs[:n_slots]
    out_ref, total_ref = refs[n_slots], refs[n_slots + 1]
    step = pl.program_id(0)

    @pl.when(step == 0)
    def _():
        total_ref[...] = jnp.zeros_like(total_ref)

    x = x_ref[...]
    for j in range(n_slots):
        for q in range(parts):
            owner = me_ref[0] ^ (j * parts + q)
            cols = pl.ds(pl.multiple_of(owner * depth, depth), depth)
            total_ref[:, cols] += lax.dot_general(
                x, slot_refs[j][q], (((1,), (1,)), ((), ())), preferred_element_type=f32
            )

    @pl.when(step == pl.num_programs(0) - 1)
    def _():
        out_ref[...] = total_ref[...].astype(out_ref.dtype)


def slot_matmul_t(x, slots, me, tile, out_dtype):
    rows, width = x.shape
    parts, depth, _ = slots[0].shape
    height = parts * depth * len(slots)
    if depth % 128:
        return product_t(x, in_order(slots, me)).astype(out_dtype)
    return pl.pallas_call(
        functools.partial(slot_matmul_t_body, len(slots), parts, depth),
        out_shape=jax.ShapeDtypeStruct((rows, height), out_dtype),
        grid_spec=pltpu.PrefetchScalarGridSpec(
            num_scalar_prefetch=1,
            grid=(width // tile,),
            in_specs=[pl.BlockSpec((rows, tile), lambda i, me: (0, i))]
            + [pl.BlockSpec((parts, depth, tile), lambda i, me: (0, 0, i))]
            * len(slots),
            out_specs=pl.BlockSpec((rows, height), lambda i, me: (0, 0)),
            scratch_shapes=[pltpu.VMEM((rows, height), f32)],
        ),
        **params(2 * rows * height * width, 2 * height * width),
    )(me, x, *slots)


def keys_of(slot_refs):
    def column(i):
        parts = [
            r[:, :, i * HEAD_SIZE : (i + 1) * HEAD_SIZE].reshape(-1, HEAD_SIZE)
            for r in slot_refs
        ]
        return parts[0] if len(parts) == 1 else jnp.concatenate(parts, 0)

    return column(0), column(1)


def scores_of(qkv_ref, keys, natural_ref, start_ref, key_natural_ref):
    blk = qkv_ref.shape[0]
    query = jnp.concatenate(
        [qkv_ref[:, i * HEAD_SIZE : (i + 1) * HEAD_SIZE] for i in range(REPEAT)], 0
    )
    scores = (
        lax.dot_general(
            query, keys, (((1,), (1,)), ((), ())), preferred_element_type=f32
        )
        * SCALE
    )
    key_natural = key_natural_ref[0]
    allowed = (key_natural >= start_ref[...]) & (key_natural <= natural_ref[...])
    allowed = jnp.concatenate([allowed] * REPEAT, 0)
    scores = jnp.where(allowed, scores, hidden_fill_value)
    best = jnp.max(scores, 1, keepdims=True)
    exps = jnp.exp(scores - best)
    return query, exps / jnp.sum(exps, 1, keepdims=True), best, blk


def attend_body(n_slots, place_ref, natural_ref, start_ref, key_natural_ref, qkv_ref, *refs):
    slot_refs, (out_ref, best_ref) = refs[:n_slots], refs[n_slots:]
    keys, values = keys_of(slot_refs)
    _, probs, best, blk = scores_of(qkv_ref, keys, natural_ref, start_ref, key_natural_ref)
    heads = jnp.dot(probs.astype(bf16), values, preferred_element_type=f32)
    out_ref[...] = jnp.concatenate(
        [heads[i * blk : (i + 1) * blk] for i in range(REPEAT)], 1
    ).astype(bf16)
    tops = [
        jnp.broadcast_to(jnp.max(best[i * blk : (i + 1) * blk], 0, keepdims=True), (1, 128))
        for i in range(REPEAT)
    ]
    best_ref[0, 0] = jnp.concatenate(tops + [jnp.zeros((8 - REPEAT, 128), f32)], 0)


def attend_back_body(
    n_slots, place_ref, natural_ref, start_ref, key_natural_ref, cosine_ref, sine_ref, qkv_ref, grad_ref, *refs
):
    slot_refs, (dq_ref, *dkv_refs) = refs[:n_slots], refs[n_slots:]
    keys, values = keys_of(slot_refs)
    query, probs, _, blk = scores_of(qkv_ref, keys, natural_ref, start_ref, key_natural_ref)
    grad = jnp.concatenate(
        [grad_ref[:, i * HEAD_SIZE : (i + 1) * HEAD_SIZE] for i in range(REPEAT)], 0
    )
    low = probs.astype(bf16)
    grad_probs = lax.dot_general(
        grad, values, (((1,), (1,)), ((), ())), preferred_element_type=f32
    )
    delta = jnp.sum(low.astype(f32) * grad_probs, 1, keepdims=True)
    score_grad = (probs * (grad_probs - delta)).astype(bf16)
    query_grad = jnp.dot(score_grad, keys, preferred_element_type=f32) * SCALE
    cosine, sine = cosine_ref[...], sine_ref[...]
    dq_ref[...] = jnp.concatenate(
        [
            rotate(query_grad[i * blk : (i + 1) * blk], cosine, -sine)
            for i in range(REPEAT)
        ],
        1,
    ).astype(bf16)
    over_rows = (((0,), (0,)), ((), ()))
    key_grad = (
        lax.dot_general(score_grad, query, over_rows, preferred_element_type=f32) * SCALE
    ).astype(bf16)
    value_grad = lax.dot_general(low, grad, over_rows, preferred_element_type=f32).astype(
        bf16
    )
    both = jnp.concatenate([key_grad, value_grad], 1)
    first = 0
    for ref in dkv_refs:
        rows = ref.shape[0] * ref.shape[1]
        ref[...] = both[first : first + rows].reshape(ref.shape)
        first += rows


def attention_specs(slots, blk, keys, shard_heads):
    def own_place(r, h, place):
        return (r, (place[0] ^ (h // shard_heads)) * shard_heads + h % shard_heads)

    column = pl.BlockSpec((blk, 1), lambda r, h, p: (r, 0))
    return (
        [column, column, pl.BlockSpec((1, 1, keys), lambda r, h, p: (r, 0, 0))],
        pl.BlockSpec((blk, UNIT), lambda r, h, p: (r, h)),
        pl.BlockSpec((blk, REPEAT * HEAD_SIZE), lambda r, h, p: (r, h)),
        pl.BlockSpec((blk, REPEAT * HEAD_SIZE), own_place),
        pl.BlockSpec((1, 1, 8, 128), lambda r, h, p: own_place(r, h, p) + (0, 0)),
        [
            pl.BlockSpec((s.shape[0], blk, 2 * HEAD_SIZE), lambda r, h, p: (0, r, h))
            for s in slots
        ],
    )


def attend(place, natural, start, key_natural, qkv, slots):
    rows, heads = qkv.shape[0], qkv.shape[1] // UNIT
    rounds, _, keys = key_natural.shape
    blk = rows // rounds
    meta, unit, _, placed, best, slot = attention_specs(
        slots, blk, keys, heads // lax.axis_size("fsdp")
    )
    return pl.pallas_call(
        functools.partial(attend_body, len(slots)),
        out_shape=[
            jax.ShapeDtypeStruct((rows, heads * REPEAT * HEAD_SIZE), bf16),
            jax.ShapeDtypeStruct((rounds, heads, 8, 128), f32),
        ],
        grid_spec=pltpu.PrefetchScalarGridSpec(
            num_scalar_prefetch=1,
            grid=(rounds, heads),
            in_specs=meta + [unit] + slot,
            out_specs=[placed, best],
        ),
        **params(4 * rows * keys * heads * REPEAT * HEAD_SIZE, 12 * 2**20),
    )(place, natural, start, key_natural, qkv, *slots)


def attend_back(place, natural, start, key_natural, cosine, sine, qkv, grad, slots):
    rows, heads = qkv.shape[0], qkv.shape[1] // UNIT
    rounds, _, keys = key_natural.shape
    blk = rows // rounds
    meta, unit, pair, placed, _, slot = attention_specs(
        slots, blk, keys, heads // lax.axis_size("fsdp")
    )
    table = pl.BlockSpec((blk, HEAD_SIZE), lambda r, h, p: (r, 0))
    return pl.pallas_call(
        functools.partial(attend_back_body, len(slots)),
        out_shape=[jax.ShapeDtypeStruct((rows, heads * REPEAT * HEAD_SIZE), bf16)]
        + [jax.ShapeDtypeStruct(s.shape, bf16) for s in slots],
        grid_spec=pltpu.PrefetchScalarGridSpec(
            num_scalar_prefetch=1,
            grid=(rounds, heads),
            in_specs=meta + [table, table, unit, placed] + slot,
            out_specs=[pair] + slot,
        ),
        **params(10 * rows * keys * heads * REPEAT * HEAD_SIZE, 20 * 2**20),
    )(place, natural, start, key_natural, cosine, sine, qkv, grad, *slots)


ANY = pl.BlockSpec(memory_space=pl.ANY)
VMEM = pl.BlockSpec(memory_space=pltpu.VMEM)
MESH = pl.DeviceIdType.MESH
OVER_ROWS = (((0,), (0,)), ((), ()))
OVER_COLUMNS = (((1,), (1,)), ((), ()))


def flip(place, mask):
    for bit in (1, 2, 4):
        if mask & bit:
            place = place + bit - 2 * bit * lax.rem(lax.div(place, bit), 2)
    return place


def device(ctx, fsdp):
    return {
        "ctx": flip(lax.axis_index("ctx"), ctx),
        "fsdp": flip(lax.axis_index("fsdp"), fsdp),
    }


def greet(ctx_masks, fsdp_masks):
    barrier = pltpu.get_barrier_semaphore()
    partners = [(m, 0) for m in ctx_masks] + [(0, m) for m in fsdp_masks]
    for ctx, fsdp in partners:
        pl.semaphore_signal(barrier, inc=1, device_id=device(ctx, fsdp), device_id_type=MESH)
    pl.semaphore_wait(barrier, len(partners))


class Transfers:
    def __init__(self, send, recv):
        self.send, self.recv, self.count, self.open = send, recv, 0, {}

    def start(self, src, dst, ctx=0, fsdp=0):
        number = self.count
        copy = pltpu.make_async_remote_copy(
            src_ref=src,
            dst_ref=dst,
            send_sem=self.send.at[number],
            recv_sem=self.recv.at[number],
            device_id=device(ctx, fsdp),
            device_id_type=MESH,
        )
        copy.start()
        copy_key = id(copy)
        self.open[copy_key] = copy
        self.count += 1
        return copy

    def release(self, copy):
        self.open.pop(id(copy)).wait_send()

    def finish(self):
        for copy in self.open.values():
            copy.wait_send()


def remote_call(body, outs, out_specs, in_specs, scratch, transfers, number, flops=0, moved=2**22):
    return pl.pallas_call(
        body,
        out_shape=outs,
        in_specs=in_specs,
        out_specs=out_specs,
        scratch_shapes=list(scratch)
        + [pltpu.SemaphoreType.DMA((transfers,)), pltpu.SemaphoreType.DMA((transfers,))],
        compiler_params=pltpu.CompilerParams(
            vmem_limit_bytes=60 * 2**20, collective_id=number, has_side_effects=True
        ),
        cost_estimate=pl.CostEstimate(flops=flops, bytes_accessed=moved, transcendentals=0),
    )


class PlaneGather:
    def __init__(self, transfers, slots):
        self.t, self.s = transfers, slots
        self.half = slots[0].shape[0] // 2

    def begin(self):
        s, t = self.s, self.t
        self.x = t.start(s[0], s[2], ctx=2)
        self.y = t.start(s[0], s[4], ctx=4)
        self.c = [t.start(s[0], s[1], ctx=1)]

    def middle(self):
        s, t, h = self.s, self.t, self.half
        self.x.wait_recv()
        self.low = t.start(s[2].at[:h], s[6].at[:h], ctx=4)
        self.c.append(t.start(s[2], s[3], ctx=1))
        self.y.wait_recv()
        self.high = t.start(s[4].at[h:], s[6].at[h:], ctx=2)
        self.c.append(t.start(s[4], s[5], ctx=1))

    def end(self):
        s, t = self.s, self.t
        self.low.wait_recv()
        self.high.wait_recv()
        self.c.append(t.start(s[6], s[7], ctx=1))

    def ready(self):
        for copy in self.c:
            copy.wait_recv()


def run_gathers(gathers):
    for k in range(len(gathers) + 2):
        if k < len(gathers):
            for over in gathers[k][0]:
                over.wait_recv()
            gathers[k][1].begin()
        if 0 <= k - 1 < len(gathers):
            gathers[k - 1][1].middle()
        if 0 <= k - 2 < len(gathers):
            gathers[k - 2][1].end()
    for _, gather in gathers:
        gather.ready()


def weight_gather_body(
    query_ref, key_ref, value_ref, output_ref, down_ref, unit_out, output_out, down_out, send, recv
):
    me, place = lax.axis_index("ctx"), lax.axis_index("fsdp")
    depth = unit_out.shape[2]
    own = pl.ds(pl.multiple_of(me * depth, depth), depth)
    greet((1, 2, 4), (1, 2, 3))
    t = Transfers(send, recv)
    gathers = []
    for d in (1, 2, 3):
        first, overs = 0, []
        for ref in (query_ref, key_ref, value_ref):
            width = ref.shape[1]
            overs.append(
                t.start(ref.at[own], unit_out.at[d - 1, 0, :, first : first + width], fsdp=d)
            )
            first += width
        gathers.append((overs, PlaneGather(t, [unit_out.at[d - 1, j] for j in range(8)])))
    for d in (1, 2, 3):
        over = t.start(output_ref.at[own], output_out.at[d - 1, 0], fsdp=d)
        gathers.append(([over], PlaneGather(t, [output_out.at[d - 1, j] for j in range(8)])))
    for d in (1, 2, 3):
        row = flip(place, d) * 8 * depth + me * depth
        over = t.start(
            down_ref.at[pl.ds(pl.multiple_of(row, depth), depth)], down_out.at[d - 1, 0], fsdp=d
        )
        gathers.append(([over], PlaneGather(t, [down_out.at[d - 1, j] for j in range(8)])))
    run_gathers(gathers)
    t.finish()


def weight_gather(query, key, value, output, down):
    depth = query.shape[0] // 8
    widths = (query.shape[1] + key.shape[1] + value.shape[1], output.shape[1], down.shape[1])
    outs = [jax.ShapeDtypeStruct((3, 8, depth, w), bf16) for w in widths]
    return remote_call(weight_gather_body, outs, [ANY] * 3, [ANY] * 5, [], 15 + 9 * 8, 0)(
        query, key, value, output, down
    )


class RowGather:
    def __init__(self, own, slots, send, recv):
        self.own, self.slots, self.send, self.recv = own, slots, send, recv
        place = lax.axis_index("fsdp")
        self.inner = (place == 1) | (place == 2)

    def copy(self, src, dst, number, fsdp):
        return pltpu.make_async_remote_copy(
            src_ref=src,
            dst_ref=self.slots[dst],
            send_sem=self.send.at[number],
            recv_sem=self.recv.at[dst - 1],
            device_id=device(0, fsdp),
            device_id_type=MESH,
        )

    def near(self):
        return self.copy(self.own, 1, 0, 1)

    def across(self):
        return self.copy(self.own, 3, 1, 3)

    def near_on(self):
        return self.copy(self.slots[1], 2, 2, 3)

    def across_on(self):
        return self.copy(self.slots[3], 2, 3, 1)

    def second_on(self):
        return self.copy(self.slots[2], 3, 4, 1)

    def begin(self):
        self.near().start()

        @pl.when(self.inner)
        def _():
            self.across().start()

    def first(self):
        self.near().wait_recv()

        @pl.when(self.inner)
        def _():
            self.near_on().start()
            self.across().wait_recv()
            self.across_on().start()

    def second(self):
        self.near_on().wait_recv()

        @pl.when(self.inner)
        def _():
            self.second_on().start()

    def third(self):
        @pl.when(jnp.logical_not(self.inner))
        def _():
            self.second_on().wait_recv()

    def finish(self):
        self.near().wait_send()

        @pl.when(self.inner)
        def _():
            self.across().wait_send()
            self.near_on().wait_send()
            self.across_on().wait_send()
            self.second_on().wait_send()


def kv_gather_body(kv_ref, dy_ref, kv_out, dy_out, row_send, row_recv, send, recv):
    greet((1, 2, 4), (1, 3))
    t = Transfers(send, recv)
    gather = PlaneGather(t, [kv_ref] + [kv_out.at[j] for j in range(7)])
    row = RowGather(dy_ref, [None] + [dy_out.at[d] for d in range(3)], row_send, row_recv)
    gather.begin()
    row.begin()
    gather.middle()
    row.first()
    gather.end()
    gather.ready()
    row.second()
    row.third()
    row.finish()
    t.finish()


def kv_gather(kv, dy):
    return remote_call(
        kv_gather_body,
        [jax.ShapeDtypeStruct((7,) + kv.shape, bf16), jax.ShapeDtypeStruct((3,) + dy.shape, bf16)],
        [ANY] * 2,
        [ANY] * 2,
        [pltpu.SemaphoreType.DMA((5,)), pltpu.SemaphoreType.DMA((3,))],
        8,
        1,
    )(kv, dy)


TILE = 256


def feed_forward_row_body(
    h_ref, dy_ref, dy_rest, gate_ref, up_ref, down_own, down_rest,
    hid_out, dg_out, du_out, h_out, y_out, y_rest, back_out,
    gates, ups, downs, hs, dys, y_acc, back_acc, back_send, back_land, y_send, stage,
    load_sem, down_sem, dy_sem, h_sem, stage_sem, y_sem, row_send, row_recv, send, recv,
):
    rows, model = h_ref.shape
    tiles = gates.shape[0]
    me, place = lax.axis_index("ctx"), lax.axis_index("fsdp")
    width = down_own.shape[1]
    loads = []
    for i in range(tiles):
        cols = pl.ds(i * TILE, TILE)
        loads.append(pltpu.make_async_copy(gate_ref.at[:, cols], gates.at[i], load_sem.at[0, i]))
        loads.append(pltpu.make_async_copy(up_ref.at[:, cols], ups.at[i], load_sem.at[1, i]))
    for j in range(tiles):
        block = flip(me, j)
        own_rows = pl.ds(pl.multiple_of(place * tiles * TILE + block * TILE, TILE), TILE)
        for d in range(4):
            cols = pl.ds(pl.multiple_of(flip(place, d) * width, width), width)
            src = down_own.at[own_rows] if d == 0 else down_rest.at[d - 1, j]
            loads.append(pltpu.make_async_copy(src, downs.at[block, :, cols], down_sem.at[j, d]))
    for d in range(4):
        src = dy_ref if d == 0 else dy_rest.at[d - 1]
        loads.append(pltpu.make_async_copy(src, dys.at[d], dy_sem.at[d]))
    for load in loads:
        load.start()
    greet((), (1, 2, 3))
    t = Transfers(send, recv)
    row = RowGather(h_ref, [None] + [hs.at[d] for d in range(3)], row_send, row_recv)
    row.begin()
    for load in loads:
        load.wait()

    def stage_copy(slot, k, part, i):
        out = (hid_out, dg_out, du_out)[k]
        cols = pl.ds(pl.multiple_of(i * TILE, TILE), TILE)
        return pltpu.make_async_copy(
            stage.at[slot, k], out.at[pl.ds(part * rows, rows), cols], stage_sem.at[slot, k]
        )

    def chunk(part, h):
        def step(i, carry):
            slot = lax.rem(i, 2)
            gate, up, down = gates[i], ups[i], downs[i]
            g = jnp.dot(h[...], gate, preferred_element_type=f32)
            u = jnp.dot(h[...], up, preferred_element_type=f32)
            grad = lax.dot_general(dys[part], down, OVER_COLUMNS, preferred_element_type=f32)
            sigmoid = jax.nn.sigmoid(g)
            silu = g * sigmoid
            hidden = (silu * u).astype(bf16)
            grad_gate = (grad * u * sigmoid * (1.0 + g * (1.0 - sigmoid))).astype(bf16)
            grad_up = (grad * silu).astype(bf16)

            @pl.when(i >= 2)
            def _():
                for k in range(3):
                    stage_copy(slot, k, part, i - 2).wait()

            stage[slot, 0] = hidden
            stage[slot, 1] = grad_gate
            stage[slot, 2] = grad_up
            for k in range(3):
                stage_copy(slot, k, part, i).start()
            y = jnp.dot(hidden, down, preferred_element_type=f32)
            back = lax.dot_general(grad_gate, gate, OVER_COLUMNS, preferred_element_type=f32)
            back += lax.dot_general(grad_up, up, OVER_COLUMNS, preferred_element_type=f32)

            @pl.when(i == 0)
            def _():
                y_acc[...] = y
                back_acc[...] = back

            @pl.when(i > 0)
            def _():
                y_acc[...] += y
                back_acc[...] += back

            return carry

        lax.fori_loop(0, tiles, step, 0)
        for i in (tiles - 2, tiles - 1):
            for k in range(3):
                stage_copy(i % 2, k, part, i).wait()

    def keep_h(part, h):
        return pltpu.make_async_copy(h, h_out.at[pl.ds(part * rows, rows)], h_sem.at[part])

    keep_h(0, h_ref).start()
    chunk(0, h_ref)
    y_out[...] = y_acc[...]
    back_out[...] = back_acc[...]
    row.first()
    backs, y_copy = [], None
    for part in (1, 2, 3):
        h = hs.at[part - 1]
        if part == 2:
            row.second()
        if part == 3:
            row.third()
        keep_h(part, h).start()
        chunk(part, h)
        back_send[part - 1] = back_acc[...].astype(bf16)
        backs.append(t.start(back_send.at[part - 1], back_land.at[part - 1], fsdp=part))
        if y_copy is not None:
            y_copy.wait()
        y_send[...] = y_acc[...].astype(bf16)
        y_copy = pltpu.make_async_copy(y_send, y_rest.at[part - 1], y_sem.at[part - 1])
        y_copy.start()
    y_copy.wait()
    for part in range(4):
        keep_h(part, h_ref if part == 0 else hs.at[part - 1]).wait()
    for d in range(3):
        backs[d].wait_recv()
        back_out[...] += back_land[d].astype(f32)
    row.finish()
    t.finish()


def feed_forward_row(h, dy, dy_rest, gate, up, down_own, down_rest):
    rows, model = h.shape
    units = gate.shape[1]
    tiles = units // TILE
    wide = jax.ShapeDtypeStruct((4 * rows, units), bf16)
    block = pltpu.VMEM((rows, model), f32)
    dma = pltpu.SemaphoreType.DMA
    return remote_call(
        feed_forward_row_body,
        [wide, wide, wide, jax.ShapeDtypeStruct((4 * rows, model), bf16)]
        + [jax.ShapeDtypeStruct((rows, model), f32), jax.ShapeDtypeStruct((3, rows, model), bf16)]
        + [jax.ShapeDtypeStruct((rows, model), f32)],
        [ANY] * 4 + [VMEM, ANY, VMEM],
        [VMEM] + [ANY] * 6,
        [
            pltpu.VMEM((tiles, model, TILE), bf16),
            pltpu.VMEM((tiles, model, TILE), bf16),
            pltpu.VMEM((tiles, TILE, model), bf16),
            pltpu.VMEM((3, rows, model), bf16),
            pltpu.VMEM((4, rows, model), bf16),
            block,
            block,
            pltpu.VMEM((3, rows, model), bf16),
            pltpu.VMEM((3, rows, model), bf16),
            pltpu.VMEM((rows, model), bf16),
            pltpu.VMEM((2, 3, rows, TILE), bf16),
            dma((2, tiles)),
            dma((tiles, 4)),
            dma((4,)),
            dma((4,)),
            dma((2, 3)),
            dma((3,)),
            dma((5,)),
            dma((3,)),
        ],
        3,
        2,
        flops=48 * rows * model * units,
    )(h, dy, dy_rest, gate, up, down_own, down_rest)


class PlaneSum:
    def __init__(self, transfers, cores, far, near, sums, total):
        self.t, self.cores, self.far, self.near = transfers, cores, far, near
        self.sums, self.total = sums, total
        self.half = cores.shape[1] // 2
        self.over = {}

    def send_odd(self, j, src):
        self.over[j - 1] = self.t.start(src, self.cores.at[(j - 1) // 2], ctx=1)
        return self.over[j - 1]

    def even(self, j, value):
        t, h = self.t, self.half
        self.over[j].wait_recv()
        value = value + self.cores[j // 2].astype(f32)
        if j == 0:
            self.total[...] = value
            return
        out = self.sums.at[(6, 2, 4).index(j)]
        out[...] = value.astype(bf16)
        if j == 6:
            self.x6 = t.start(out.at[:h], self.far.at[:h], ctx=2)
            self.y6 = t.start(out.at[h:], self.far.at[h:], ctx=4)
        elif j == 2:
            self.x2 = t.start(out.at[:h], self.near.at[0, :h], ctx=2)
        else:
            self.y4 = t.start(out.at[h:], self.near.at[1, h:], ctx=4)

    def pass_on(self):
        t, h = self.t, self.half
        two, four = self.sums.at[1], self.sums.at[2]
        self.y6.wait_recv()
        two[h:] = (two[h:].astype(f32) + self.far[h:].astype(f32)).astype(bf16)
        self.x2b = t.start(two.at[h:], self.near.at[0, h:], ctx=2)
        self.x6.wait_recv()
        four[:h] = (four[:h].astype(f32) + self.far[:h].astype(f32)).astype(bf16)
        self.y4b = t.start(four.at[:h], self.near.at[1, :h], ctx=4)

    def close(self):
        for copy in (self.x2, self.x2b, self.y4, self.y4b):
            copy.wait_recv()
        return self.total[...] + self.near[0].astype(f32) + self.near[1].astype(f32)


def plane_sum_scratch(count, rows, columns):
    return [
        pltpu.VMEM((count, 4, rows, columns), bf16),
        pltpu.VMEM((count, rows, columns), bf16),
        pltpu.VMEM((count, 2, rows, columns), bf16),
        pltpu.VMEM((count, 3, rows, columns), bf16),
        pltpu.VMEM((count, rows, columns), f32),
    ]


def grads_body(
    h_ref, dg_ref, du_ref, hid_ref, dy_ref, dy_rest, y_rest,
    gate_out, up_out, down_out, y_land,
    left, rights, odd, cores, far, near, sums, totals, left_sem, right_sem, dy_sem, out_sem,
    send, recv,
):
    me = lax.axis_index("ctx")
    rows = dy_ref.shape[0]
    depth = cores.shape[2]
    dys = [dy_ref] + [dy_rest.at[d] for d in range(3)]
    right_copies = [
        [pltpu.make_async_copy(dg_ref, rights.at[0], right_sem.at[0])],
        [pltpu.make_async_copy(du_ref, rights.at[1], right_sem.at[1])],
        [
            pltpu.make_async_copy(p, rights.at[0, i * rows : (i + 1) * rows], dy_sem.at[i])
            for i, p in enumerate(dys)
        ],
    ]
    left_copies = [
        pltpu.make_async_copy(h_ref, left, left_sem.at[0]),
        pltpu.make_async_copy(hid_ref, left, left_sem.at[1]),
    ]
    left_copies[0].start()
    right_copies[0][0].start()
    right_copies[1][0].start()
    greet((1, 2, 4), (1, 2, 3))
    t = Transfers(send, recv)
    y_copies = [t.start(y_rest.at[d - 1], y_land.at[d - 1], fsdp=d) for d in (1, 2, 3)]
    left_copies[0].wait()
    jobs, odd_copies, outs = [], {}, []

    def close(k):
        totals[k] = jobs[k].close()
        out = pltpu.make_async_copy(totals.at[k], (gate_out, up_out)[k], out_sem.at[k])
        out.start()
        outs.append(out)

    for k in range(3):
        job = PlaneSum(t, cores.at[k], far.at[k], near.at[k], sums.at[k], totals.at[k])
        jobs.append(job)
        if k == 2:
            for copy in [left_copies[1]] + right_copies[2]:
                copy.start()
            left_copies[1].wait()
        for copy in right_copies[k]:
            copy.wait()

        def partial(j):
            block = pl.ds(pl.multiple_of(flip(me, j) * depth, depth), depth)
            return lax.dot_general(
                left[:, block], rights[k % 2], OVER_ROWS, preferred_element_type=f32
            )

        for j in (7, 5, 3, 1):
            if j in odd_copies:
                t.release(odd_copies[j])
            odd[j // 2] = partial(j).astype(bf16)
            odd_copies[j] = job.send_odd(j, odd.at[j // 2])
        if k:
            jobs[k - 1].pass_on()
        for j in (6, 2, 4, 0):
            job.even(j, partial(j))
        if k:
            close(k - 1)
    jobs[2].pass_on()
    for copy in y_copies:
        copy.wait_recv()
    down_out[...] = jobs[2].close().astype(bf16)
    for copy in outs:
        copy.wait()
    t.finish()


def grads_row(h, dg, du, hid, dy, dy_rest, y_rest):
    rows, model = dy.shape
    depth = model // 8
    dma = pltpu.SemaphoreType.DMA
    summed = jax.ShapeDtypeStruct((depth, dg.shape[1]), f32)
    return remote_call(
        grads_body,
        [summed, summed, jax.ShapeDtypeStruct((depth, model), bf16), jax.ShapeDtypeStruct(y_rest.shape, bf16)],
        [ANY, ANY, VMEM, ANY],
        [ANY] * 7,
        [
            pltpu.VMEM(h.shape, bf16),
            pltpu.VMEM((2,) + h.shape, bf16),
            pltpu.VMEM((4, depth, model), bf16),
        ]
        + plane_sum_scratch(3, depth, model)
        + [dma((2,)), dma((2,)), dma((4,)), dma((2,))],
        3 + 3 * 10,
        3,
        flops=6 * h.shape[0] * model * model,
    )(h, dg, du, hid, dy, dy_rest, y_rest)


def kv_sum_body(
    first_ref, rest_ref, cosine_ref, sine_ref, out_ref,
    evens, cores, far, near, sums, totals, even_sem, send, recv,
):
    slots = [first_ref.at[0]] + [rest_ref.at[j] for j in range(7)]
    copies = {
        j: pltpu.make_async_copy(slots[j], evens.at[j // 2], even_sem.at[j // 2])
        for j in (6, 2, 4, 0)
    }
    for copy in copies.values():
        copy.start()
    greet((1, 2, 4), ())
    t = Transfers(send, recv)
    job = PlaneSum(t, cores.at[0], far.at[0], near.at[0], sums.at[0], totals.at[0])
    for j in (7, 3, 5, 1):
        job.send_odd(j, slots[j])
    for j in (6, 2, 4, 0):
        copies[j].wait()
        job.even(j, evens[j // 2].astype(f32))
    job.pass_on()
    total = job.close()
    cosine, sine = cosine_ref[...], -sine_ref[...]
    for h in range(total.shape[1] // (2 * HEAD_SIZE)):
        first = 2 * h * HEAD_SIZE
        middle = first + HEAD_SIZE
        out_ref[:, first:middle] = rotate(total[:, first:middle], cosine, sine).astype(bf16)
        out_ref[:, middle : middle + HEAD_SIZE] = total[:, middle : middle + HEAD_SIZE].astype(bf16)
    t.finish()


def kv_sum(first, rest, cosine, sine):
    _, rows, width = first.shape
    return remote_call(
        kv_sum_body,
        jax.ShapeDtypeStruct((rows, width), bf16),
        VMEM,
        [ANY, ANY, VMEM, VMEM],
        [pltpu.VMEM((4, rows, width), bf16)]
        + plane_sum_scratch(1, rows, width)
        + [pltpu.SemaphoreType.DMA((4,))],
        10,
        4,
    )(first, rest, cosine, sine)


def unit_grads_body(
    h_ref, dq_ref, dkv_ref, attended_ref, db_ref,
    query_out, key_out, value_out, output_out,
    odd, cores, far, near, sums, totals, row_send, row_land,
    send, recv,
):
    me, place = lax.axis_index("ctx"), lax.axis_index("fsdp")
    depth = cores.shape[2]
    width = row_land.shape[3]
    greet((1, 2, 4), (1, 2, 3))
    t = Transfers(send, recv)
    pairs = ((attended_ref, db_ref), (h_ref, dq_ref), (h_ref, dkv_ref))
    jobs, odd_copies, over = [], {}, [None] * 3

    def columns(k, d):
        if k == 0:
            return pl.ds(pl.multiple_of(flip(place, d) * width, width), width)
        return pl.ds(d * width, width)

    def close(k):
        totals[k] = jobs[k].close()
        over[k] = []
        for d in (1, 2, 3):
            row_send[k, d - 1] = totals[k, :, columns(k, d)].astype(bf16)
            over[k].append(t.start(row_send.at[k, d - 1], row_land.at[k, d - 1], fsdp=d))

    for k in range(3):
        left, right = pairs[k]
        job = PlaneSum(t, cores.at[k], far.at[k], near.at[k], sums.at[k], totals.at[k])
        jobs.append(job)

        def partial(j):
            block = pl.ds(pl.multiple_of(flip(me, j) * depth, depth), depth)
            return lax.dot_general(
                left[:, block], right[...], OVER_ROWS, preferred_element_type=f32
            )

        for j in (7, 5, 3, 1):
            if j in odd_copies:
                t.release(odd_copies[j])
            odd[j // 2] = partial(j).astype(bf16)
            odd_copies[j] = job.send_odd(j, odd.at[j // 2])
        if k:
            jobs[k - 1].pass_on()
        for j in (6, 2, 4, 0):
            job.even(j, partial(j))
        if k:
            close(k - 1)
    jobs[2].pass_on()
    close(2)
    for k in range(3):
        total = totals[k, :, columns(k, 0)]
        for d in range(3):
            over[k][d].wait_recv()
            total = total + row_land[k, d].astype(f32)
        if k == 0:
            output_out[...] = total
        elif k == 1:
            query_out[...] = total
        else:
            for h in range(total.shape[1] // (2 * HEAD_SIZE)):
                first = 2 * h * HEAD_SIZE
                here = slice(h * HEAD_SIZE, (h + 1) * HEAD_SIZE)
                key_out[:, here] = total[:, first : first + HEAD_SIZE]
                value_out[:, here] = total[:, first + HEAD_SIZE : first + 2 * HEAD_SIZE]
    t.finish()


def unit_grads(h, dq, dkv, attended, db):
    rows, model = h.shape
    depth, width = model // 8, model // 4
    wide = jax.ShapeDtypeStruct((depth, width), f32)
    half = jax.ShapeDtypeStruct((depth, width // 2), f32)
    return remote_call(
        unit_grads_body,
        [wide, half, half, wide],
        [VMEM] * 4,
        [VMEM] * 5,
        [pltpu.VMEM((4, depth, model), bf16)]
        + plane_sum_scratch(3, depth, model)
        + [pltpu.VMEM((3, 3, depth, width), bf16)] * 2,
        3 * (10 + 3),
        5,
        flops=6 * rows * model * model,
    )(h, dq, dkv, attended, db)


def unit_specs(depth, slots):
    def of_rest(width, first):
        return pl.BlockSpec(
            (1, slots, depth, width), lambda d, h, p: (jnp.maximum(d - 1, 0), 0, 0, first + h)
        )

    def of_own(width):
        return pl.BlockSpec(
            (slots * depth, width), lambda d, h, p: (0, jnp.where(d == 0, h, 1))
        )

    widths = ((2 * HEAD_SIZE, 0), (HEAD_SIZE, 4), (HEAD_SIZE, 6))
    return [of_own(w) for w, _ in widths] + [of_rest(w, first) for w, first in widths]


def unit_forward_body(
    place_ref, h_ref, cosine_ref, sine_ref, q_own, k_own, v_own, q_rest, k_rest, v_rest,
    unit_out, kv_out, total,
):
    d = pl.program_id(0)

    @pl.when(d == 0)
    def _():
        weight = jnp.concatenate([q_own[...], k_own[...], v_own[...]], 1)
        total[...] = jnp.dot(h_ref[...], weight, preferred_element_type=f32)

    @pl.when(d > 0)
    def _():
        slots, depth = q_rest.shape[1], q_rest.shape[2]
        value = None
        for j in range(slots):
            owner = place_ref[0] ^ j
            part = h_ref[:, pl.ds(pl.multiple_of(owner * depth, depth), depth)]
            weight = jnp.concatenate([q_rest[0, j], k_rest[0, j], v_rest[0, j]], 1)
            term = jnp.dot(part, weight, preferred_element_type=f32)
            value = term if value is None else value + term
        total[...] = value

    cosine, sine = cosine_ref[...], sine_ref[...]
    turned = [
        rotate(total[:, i * HEAD_SIZE : (i + 1) * HEAD_SIZE], cosine, sine).astype(bf16)
        for i in range(REPEAT + 1)
    ]
    value = total[:, (REPEAT + 1) * HEAD_SIZE :].astype(bf16)
    unit_out[...] = jnp.concatenate(turned + [value], 1)
    kv_out[...] = jnp.concatenate([turned[REPEAT], value], 1)


def unit_forward(places, h, cosine, sine, query, key, value, rest):
    rows = h.shape[0]
    heads = query.shape[1] // (REPEAT * HEAD_SIZE)
    _, slots, depth, _ = rest.shape
    whole = lambda a: pl.BlockSpec(a.shape, lambda d, h, p: (0, 0))
    return pl.pallas_call(
        unit_forward_body,
        out_shape=[
            jax.ShapeDtypeStruct((rows, 4 * heads * UNIT), bf16),
            jax.ShapeDtypeStruct((rows, 4 * heads * 2 * HEAD_SIZE), bf16),
        ],
        grid_spec=pltpu.PrefetchScalarGridSpec(
            num_scalar_prefetch=1,
            grid=(4, heads),
            in_specs=[whole(h), whole(cosine), whole(sine)] + unit_specs(depth, slots),
            out_specs=[
                pl.BlockSpec((rows, UNIT), lambda d, h, p: (0, d * heads + h)),
                pl.BlockSpec((rows, 2 * HEAD_SIZE), lambda d, h, p: (0, d * heads + h)),
            ],
            scratch_shapes=[pltpu.VMEM((rows, UNIT), f32)],
        ),
        **params(8 * rows * h.shape[1] * heads * UNIT, 8 * h.shape[1] * heads * UNIT),
    )(places, h, cosine, sine, query, key, value, rest, rest, rest)


def unit_back_body(
    place_ref, dq_ref, dkv_ref, q_own, k_own, v_own, q_rest, k_rest, v_rest, out_ref
):
    d, h = pl.program_id(0), pl.program_id(1)
    grad = jnp.concatenate([dq_ref[...], dkv_ref[...]], 1)

    @pl.when((d == 0) & (h == 0))
    def _():
        out_ref[...] = jnp.zeros_like(out_ref)

    @pl.when(d == 0)
    def _():
        weight = jnp.concatenate([q_own[...], k_own[...], v_own[...]], 1)
        out_ref[...] += lax.dot_general(grad, weight, OVER_COLUMNS, preferred_element_type=f32)

    @pl.when(d > 0)
    def _():
        slots, depth = q_rest.shape[1], q_rest.shape[2]
        for j in range(slots):
            owner = place_ref[0] ^ j
            cols = pl.ds(pl.multiple_of(owner * depth, depth), depth)
            weight = jnp.concatenate([q_rest[0, j], k_rest[0, j], v_rest[0, j]], 1)
            out_ref[:, cols] += lax.dot_general(
                grad, weight, OVER_COLUMNS, preferred_element_type=f32
            )


def unit_back(places, dq, dkv, query, key, value, rest):
    rows = dq.shape[0]
    heads = query.shape[1] // (REPEAT * HEAD_SIZE)
    _, slots, depth, _ = rest.shape
    model = slots * depth
    pair = pl.BlockSpec((rows, 2 * HEAD_SIZE), lambda d, h, p: (0, d * heads + h))
    return pl.pallas_call(
        unit_back_body,
        out_shape=jax.ShapeDtypeStruct((rows, model), f32),
        grid_spec=pltpu.PrefetchScalarGridSpec(
            num_scalar_prefetch=1,
            grid=(4, heads),
            in_specs=[pair, pair] + unit_specs(depth, slots),
            out_specs=pl.BlockSpec((rows, model), lambda d, h, p: (0, 0)),
        ),
        **params(8 * rows * model * heads * UNIT, 8 * model * heads * UNIT),
    )(places, dq, dkv, query, key, value, rest, rest, rest)


def output_specs(own, rest):
    _, slots, depth, width = rest.shape
    return [
        pl.BlockSpec(own.shape, lambda d, p: (0, 0)),
        pl.BlockSpec((1, slots, depth, width), lambda d, p: (jnp.maximum(d - 1, 0), 0, 0, 0)),
    ]


def output_forward_body(place_ref, attended_ref, x_ref, own_ref, rest_ref, out_ref):
    d = pl.program_id(0)
    x = x_ref[...].astype(f32)

    @pl.when(d == 0)
    def _():
        out_ref[...] = x + jnp.dot(attended_ref[...], own_ref[...], preferred_element_type=f32)

    @pl.when(d > 0)
    def _():
        slots, depth = rest_ref.shape[1], rest_ref.shape[2]
        value = x
        for j in range(slots):
            owner = place_ref[0] ^ j
            part = attended_ref[:, pl.ds(pl.multiple_of(owner * depth, depth), depth)]
            value = value + jnp.dot(part, rest_ref[0, j], preferred_element_type=f32)
        out_ref[...] = value


def output_forward(places, attended, x, own, rest):
    rows, model = x.shape
    width = own.shape[1]
    tile = pl.BlockSpec((rows, width), lambda d, p: (0, p[1] ^ d))
    return pl.pallas_call(
        output_forward_body,
        out_shape=jax.ShapeDtypeStruct((rows, model), f32),
        grid_spec=pltpu.PrefetchScalarGridSpec(
            num_scalar_prefetch=1,
            grid=(4,),
            in_specs=[pl.BlockSpec(attended.shape, lambda d, p: (0, 0)), tile]
            + output_specs(own, rest),
            out_specs=tile,
        ),
        **params(2 * rows * model * model, 2 * model * model),
    )(places, attended, x, own, rest)


def output_back_body(place_ref, db_ref, own_ref, rest_ref, out_ref, total):
    d = pl.program_id(0)
    db = db_ref[...]

    @pl.when(d == 0)
    def _():
        total[...] = lax.dot_general(db, own_ref[...], OVER_COLUMNS, preferred_element_type=f32)

    @pl.when(d > 0)
    def _():
        slots, depth = rest_ref.shape[1], rest_ref.shape[2]
        for j in range(slots):
            owner = place_ref[0] ^ j
            cols = pl.ds(pl.multiple_of(owner * depth, depth), depth)
            total[:, cols] += lax.dot_general(
                db, rest_ref[0, j], OVER_COLUMNS, preferred_element_type=f32
            )

    @pl.when(d == pl.num_programs(0) - 1)
    def _():
        out_ref[...] = total[...].astype(bf16)


def output_back(places, db, own, rest):
    rows, model = db.shape
    height, width = own.shape
    return pl.pallas_call(
        output_back_body,
        out_shape=jax.ShapeDtypeStruct((rows, height), bf16),
        grid_spec=pltpu.PrefetchScalarGridSpec(
            num_scalar_prefetch=1,
            grid=(4,),
            in_specs=[pl.BlockSpec((rows, width), lambda d, p: (0, p[1] ^ d))]
            + output_specs(own, rest),
            out_specs=pl.BlockSpec((rows, height), lambda d, p: (0, 0)),
            scratch_shapes=[pltpu.VMEM((rows, height), f32)],
        ),
        **params(2 * rows * model * height, 2 * model * height),
    )(places, db, own, rest)


def token_layout(length_row, block_slots, block_size):
    count_blocks = block_slots.shape[0]
    owner_block = jnp.argmax(
        block_slots[None, :] == jnp.arange(count_blocks, dtype=jnp.int32)[:, None], 1
    ).astype(jnp.int32)
    row_index = jnp.arange(count_blocks * block_size, dtype=jnp.int32)
    plain_order = jnp.repeat(owner_block, block_size) * block_size + row_index % block_size
    seq_ends = jnp.cumsum(length_row)
    seq_starts = seq_ends - length_row
    document_list = jnp.sum((plain_order[:, None] >= seq_ends[None, :]).astype(jnp.int32), 1)
    matches = document_list[:, None] == jnp.arange(length_row.shape[0], dtype=jnp.int32)[None, :]
    begins = jnp.sum(jnp.where(matches, seq_starts[None, :], 0), 1)
    return plain_order, begins


def rms_scale(value):
    return lax.rsqrt(jnp.mean(value * value, -1, keepdims=True) + epsilon)


def norm_back(grad_unit, unit_rows, scale_rows):
    return scale_rows * (grad_unit - unit_rows * jnp.mean(grad_unit * unit_rows, -1, keepdims=True))


def product(left, right):
    return jnp.dot(left, right, preferred_element_type=f32)


def product_t(left, right):
    return lax.dot_general(left, right, (((1,), (1,)), ((), ())), preferred_element_type=f32)


def over_rows(left, right):
    return lax.dot_general(left, right, (((0,), (0,)), ((), ())), preferred_element_type=f32)


def column_blocks(value, count, places):
    width = value.shape[1] // count
    return jnp.concatenate(
        [lax.dynamic_slice_in_dim(value, place * width, width, 1) for place in places], 1
    )


def gather_rows(piece, fsdp_place, ctx_count):
    count = lax.axis_size("fsdp")
    parts = [piece] + [swap(piece, "fsdp", d) for d in range(1, count)]
    return jnp.concatenate(by_place(parts, fsdp_place), 1)


def weight_grad_sum(left, right, me, count):
    depth = left.shape[1] // count
    full = over_rows(column_blocks(left, count, [me ^ j for j in range(count)]), right)
    return sum_halving(full.astype(bf16).reshape(count, depth, right.shape[1]), "ctx")


def down_grad_sum(hidden, grad, me, count, fsdp_count):
    bands = count // fsdp_count
    band, column = me // fsdp_count, me % fsdp_count
    depth = hidden.shape[1] // bands
    width = grad.shape[1] // fsdp_count
    left = column_blocks(hidden, bands, [band ^ j for j in range(bands)])
    right = column_blocks(grad, fsdp_count, [column ^ j for j in range(fsdp_count)])
    full = over_rows(left, right).astype(bf16).reshape(bands, depth, fsdp_count, width)
    return sum_halving(full.transpose(0, 2, 1, 3).reshape(count, depth, width), "ctx")


def clipped(weight, multiplier):
    columns = weight.shape[1]
    head_index = (
        lax.axis_index("fsdp") * columns + jnp.arange(columns, dtype=jnp.int32)
    ) // HEAD_SIZE
    matches = head_index[:, None] == jnp.arange(multiplier.shape[0], dtype=jnp.int32)[None, :]
    column_factor = jnp.sum(jnp.where(matches, multiplier[None, :], 0.0), 1)
    return (weight.astype(f32) * column_factor[None, :]).astype(bf16)


def gain_sum(term, me, place, count, fsdp_count):
    table = term.reshape(count, fsdp_count, -1)
    table = jnp.stack(by_place([table[i] for i in range(count)], me))
    mine = sum_halving(table, "ctx")
    mine = jnp.stack(by_place([mine[i] for i in range(fsdp_count)], place))
    return sum_halving(mine, "fsdp")


def attention_layout(seq_lengths, block_perm, rows):
    count, me = lax.axis_size("ctx"), lax.axis_index("ctx")
    rounds = block_perm.shape[0] // count
    blk = rows // rounds
    plain_order, begins = token_layout(seq_lengths[0], block_perm, blk)
    natural = lax.dynamic_slice_in_dim(plain_order, me * rows, rows)
    begin = lax.dynamic_slice_in_dim(begins, me * rows, rows)
    half_dim = HEAD_SIZE // 2
    exponent = jnp.arange(half_dim, dtype=f32) * (2.0 / HEAD_SIZE)
    inverse = rope_base ** (-exponent)
    angles = (natural - begin).astype(f32)[:, None] * inverse[None, :]
    cosine = jnp.concatenate([jnp.cos(angles)] * 2, 1)
    sine = jnp.concatenate([-jnp.sin(angles), jnp.sin(angles)], 1)
    order = plain_order.reshape(count, rounds, blk)
    order = jnp.stack(by_place([order[i] for i in range(count)], me), 1)
    return natural[:, None], begin[:, None], order.reshape(rounds, 1, count * blk), cosine, sine


def on_device(
    hidden_in,
    out_grad,
    seq_lengths,
    block_perm,
    first_gain,
    query_weight,
    key_matrix,
    value_matrix,
    output_weight,
    second_gain,
    gate_weight,
    up_weight,
    down_weight,
    clip_limit,
):
    rows, model = hidden_in.shape[1], hidden_in.shape[2]
    count, fsdp_count = lax.axis_size("ctx"), lax.axis_size("fsdp")
    me, place = lax.axis_index("ctx"), lax.axis_index("fsdp")
    me_ref = me.astype(jnp.int32).reshape(1)
    depth = model // count
    zero = jnp.zeros((1,), jnp.int32)
    shard_heads = KEY_VALUE_HEADS // fsdp_count

    def own_rows(weight):
        return lax.dynamic_slice_in_dim(weight, me * depth, depth, 0)

    unit_rows = jnp.concatenate(
        [
            own_rows(query_weight).reshape(depth, shard_heads, REPEAT, HEAD_SIZE),
            own_rows(key_matrix).reshape(depth, shard_heads, 1, HEAD_SIZE),
            own_rows(value_matrix).reshape(depth, shard_heads, 1, HEAD_SIZE),
        ],
        2,
    ).reshape(depth, shard_heads * UNIT)
    unit_rows = gather_rows(unit_rows, place, count)
    unit_slots = gather_ctx(unit_rows)
    gains = jnp.stack([first_gain, second_gain])
    gains = jnp.concatenate(
        by_place([gains] + [swap(gains, "fsdp", d) for d in range(1, fsdp_count)], place), 1
    ).astype(f32)
    first_full, second_full = gains[0], gains[1]
    output_rows = gather_rows(own_rows(output_weight), place, count)
    output_slots = gather_ctx(output_rows)

    hidden_width = gate_weight.shape[1]
    down_depth = hidden_width // count

    def down_piece(d):
        first = (place ^ d) * hidden_width + me * down_depth
        return lax.dynamic_slice_in_dim(down_weight, first, down_depth, 0)

    down_rows = [down_piece(0)] + [
        swap(down_piece(d), "fsdp", d) for d in range(1, fsdp_count)
    ]
    down_slots = gather_ctx(jnp.concatenate(by_place(down_rows, place), 1))

    natural_column, begin_column, key_natural, cosine, sine = attention_layout(
        seq_lengths, block_perm, rows
    )
    half_dim = HEAD_SIZE // 2

    tokens = hidden_in.reshape(rows, model).astype(f32)
    scale_one = rms_scale(tokens)
    unit_one = tokens * scale_one
    normalized = (unit_one * first_full).astype(bf16)
    qkv = slot_matmul(normalized, unit_slots, me_ref, UNIT, bf16, (cosine, sine))
    kv_local = qkv.reshape(rows, KEY_VALUE_HEADS, UNIT)[:, :, REPEAT * HEAD_SIZE :].reshape(
        rows, KEY_VALUE_HEADS * 2 * HEAD_SIZE
    )
    kv_slots = gather_ctx(kv_local)
    attended, best = attend(zero, natural_column, begin_column, key_natural, qkv, kv_slots)
    head_max = jnp.max(best[:, :, :REPEAT, 0], 0).reshape(QUERY_HEADS)
    for mask in bits_down(count):
        head_max = jnp.maximum(head_max, swap(head_max, "ctx", mask))
    for mask in bits_down(fsdp_count):
        head_max = jnp.maximum(head_max, swap(head_max, "fsdp", mask))
    residual = tokens + slot_matmul(attended, output_slots, me_ref, 512, f32)
    scale_two = rms_scale(residual)
    unit_two = residual * scale_two
    normed_two = (unit_two * second_full).astype(bf16)

    grad_out = out_grad.reshape(rows, model)
    others = range(1, fsdp_count)
    grads = [grad_out] + [swap(grad_out, "fsdp", d) for d in others]
    normed = [normed_two] + [swap(normed_two, "fsdp", d) for d in others]
    hidden_parts, gate_parts, up_parts, sums, backs = [], [], [], [], []
    for d in range(fsdp_count):
        grad_hidden = slot_matmul_t(grads[d], down_slots, me_ref, 512, f32)
        gate_act = product(normed[d], gate_weight)
        up_proj = product(normed[d], up_weight)
        sigmoid = jax.nn.sigmoid(gate_act)
        hidden = (gate_act * sigmoid * up_proj).astype(bf16)
        grad_gate = (
            grad_hidden * up_proj * sigmoid * (1.0 + gate_act * (1.0 - sigmoid))
        ).astype(bf16)
        grad_up = (grad_hidden * gate_act * sigmoid).astype(bf16)
        hidden_parts.append(hidden)
        gate_parts.append(grad_gate)
        up_parts.append(grad_up)
        backs.append(product_t(grad_gate, gate_weight) + product_t(grad_up, up_weight))
        sums.append(slot_matmul(hidden, down_slots, me_ref, 512, f32 if d == 0 else bf16))
    grad_normed_two = sum_fsdp(backs)
    result = (residual + sum_fsdp(sums)).astype(bf16)

    second_term = jnp.sum(grad_normed_two * unit_two, 0)
    grad_residual = grad_out.astype(f32) + norm_back(
        grad_normed_two * second_full, unit_two, scale_two
    )
    grad_branch = grad_residual.astype(bf16)
    head_grad = slot_matmul_t(grad_branch, output_slots, me_ref, 512, bf16)
    query_grad, *dkv_slots = attend_back(
        zero, natural_column, begin_column, key_natural, cosine, sine, qkv, head_grad, kv_slots
    )
    dkv = sum_halving(dkv_slots[0], "ctx")
    dkv = dkv.reshape(rows, KEY_VALUE_HEADS, 2, HEAD_SIZE)
    grad_key = dkv[:, :, 0]
    first, second = grad_key[..., :half_dim], grad_key[..., half_dim:]
    cos, sin = cosine[:, None, :half_dim], sine[:, None, half_dim:]
    grad_key = jnp.concatenate([first * cos + second * sin, second * cos - first * sin], -1)
    dqkv = jnp.concatenate(
        [
            query_grad.reshape(rows, KEY_VALUE_HEADS, REPEAT, HEAD_SIZE),
            grad_key[:, :, None].astype(bf16),
            dkv[:, :, 1:].astype(bf16),
        ],
        2,
    ).reshape(rows, KEY_VALUE_HEADS * UNIT)
    grad_normed_one = slot_matmul_t(dqkv, unit_slots, me_ref, 512, f32)
    first_term = jnp.sum(grad_normed_one * unit_one, 0)
    grad_input = grad_residual + norm_back(grad_normed_one * first_full, unit_one, scale_one)

    hidden_all = jnp.concatenate(hidden_parts, 0)
    normed_all = jnp.concatenate(normed, 0)
    grads_all = jnp.concatenate(grads, 0)
    down_sum = down_grad_sum(hidden_all, grads_all, me, count, fsdp_count).astype(bf16)
    bands = count // fsdp_count
    places = [
        (c * fsdp_count + f, (bands * f + c // fsdp_count) * fsdp_count + c % fsdp_count)
        for c in range(count)
        for f in range(fsdp_count)
    ]
    down_grad = lax.ppermute(down_sum, ("ctx", "fsdp"), places).astype(f32)
    gate_grad = weight_grad_sum(normed_all, jnp.concatenate(gate_parts, 0), me, count)
    up_grad = weight_grad_sum(normed_all, jnp.concatenate(up_parts, 0), me, count)

    def over_fsdp(summed):
        width = summed.shape[1] // fsdp_count
        return sum_fsdp(
            [
                lax.dynamic_slice_in_dim(summed, (place ^ d) * width, width, 1)
                for d in range(fsdp_count)
            ]
        )

    output_grad = over_fsdp(weight_grad_sum(attended, grad_branch, me, count))
    unit_grad = over_fsdp(weight_grad_sum(normalized, dqkv, me, count))
    unit_grad = unit_grad.reshape(depth, shard_heads, REPEAT + 2, HEAD_SIZE)
    query_out = unit_grad[:, :, :REPEAT].reshape(depth, -1)
    key_out = unit_grad[:, :, REPEAT].reshape(depth, -1)
    value_out = unit_grad[:, :, REPEAT + 1].reshape(depth, -1)

    first_out = gain_sum(first_term, me, place, count, fsdp_count)
    second_out = gain_sum(second_term, me, place, count, fsdp_count)
    multiplier = jnp.sqrt(clip_limit / jnp.maximum(head_max, clip_limit))
    key_ratio = jnp.min(multiplier.reshape(KEY_VALUE_HEADS, REPEAT), 1)
    return (
        result.reshape(1, rows, model),
        grad_input.astype(bf16).reshape(1, rows, model),
        first_out,
        query_out,
        key_out,
        value_out,
        output_grad,
        second_out,
        gate_grad,
        up_grad,
        down_grad,
        head_max,
        clipped(query_weight, multiplier),
        clipped(key_matrix, key_ratio),
    )


def full_gains(first_gain, second_gain):
    count, place = lax.axis_size("fsdp"), lax.axis_index("fsdp")
    gains = jnp.stack([first_gain, second_gain])
    parts = [gains] + [swap(gains, "fsdp", d) for d in range(1, count)]
    gains = jnp.concatenate(by_place(parts, place), 1).astype(f32)
    return gains[0], gains[1]


def on_row_of_chips(
    hidden_in,
    out_grad,
    seq_lengths,
    block_perm,
    first_gain,
    query_weight,
    key_matrix,
    value_matrix,
    output_weight,
    second_gain,
    gate_weight,
    up_weight,
    down_weight,
    clip_limit,
):
    rows, model = hidden_in.shape[1], hidden_in.shape[2]
    me, place = lax.axis_index("ctx"), lax.axis_index("fsdp")
    places = jnp.stack([me, place]).astype(jnp.int32)
    place_one = places[1:]
    natural, begin, key_natural, cosine, sine = attention_layout(seq_lengths, block_perm, rows)
    first_full, second_full = full_gains(first_gain, second_gain)
    tokens_low = hidden_in.reshape(rows, model)
    grad_out = out_grad.reshape(rows, model)

    unit_rest, output_rest, down_rest = weight_gather(
        query_weight, key_matrix, value_matrix, output_weight, down_weight
    )
    tokens = tokens_low.astype(f32)
    scale_one = rms_scale(tokens)
    unit_one = tokens * scale_one
    normalized = (unit_one * first_full).astype(bf16)
    qkv, kv_local = unit_forward(
        places, normalized, cosine, sine, query_weight, key_matrix, value_matrix, unit_rest
    )
    kv_rest, dy_rest = kv_gather(kv_local, grad_out)
    kv_slots = [kv_local[None], kv_rest]
    attended, best = attend(place_one, natural, begin, key_natural, qkv, kv_slots)
    head_max = jnp.max(best[:, :, :REPEAT, 0], 0).reshape(QUERY_HEADS)
    for mask in (4, 2, 1):
        head_max = jnp.maximum(head_max, swap(head_max, "ctx", mask))
    for mask in (2, 1):
        head_max = jnp.maximum(head_max, swap(head_max, "fsdp", mask))
    residual = output_forward(places, attended, tokens_low, output_weight, output_rest)
    scale_two = rms_scale(residual)
    unit_two = residual * scale_two
    normed_two = (unit_two * second_full).astype(bf16)

    hid, dg, du, h_all, y_own, y_rest, grad_normed_two = feed_forward_row(
        normed_two, grad_out, dy_rest, gate_weight, up_weight, down_weight, down_rest
    )
    second_term = jnp.sum(grad_normed_two * unit_two, 0)
    grad_residual = grad_out.astype(f32) + norm_back(
        grad_normed_two * second_full, unit_two, scale_two
    )
    grad_branch = grad_residual.astype(bf16)
    gate_grad, up_grad, down_sum, y_land = grads_row(h_all, dg, du, hid, grad_out, dy_rest, y_rest)
    result = (residual + y_own + jnp.sum(y_land.astype(f32), 0)).astype(bf16)
    width = model // 4
    moved = []
    for k in range(4):
        pairs = [
            (c * 4 + f, (2 * f + c // 4) * 4 + (c % 4 ^ k)) for c in range(8) for f in range(4)
        ]
        piece = lax.dynamic_slice_in_dim(down_sum, ((me % 4) ^ k) * width, width, 1)
        moved.append(lax.ppermute(piece, ("ctx", "fsdp"), pairs))
    down_grad = jnp.concatenate(by_place(moved, place), 0).astype(f32)

    head_grad = output_back(places, grad_branch, output_weight, output_rest)
    query_grad, dkv_first, dkv_rest = attend_back(
        place_one, natural, begin, key_natural, cosine, sine, qkv, head_grad, kv_slots
    )
    dkv = kv_sum(dkv_first, dkv_rest, cosine, sine)
    grad_normed_one = unit_back(
        places, query_grad, dkv, query_weight, key_matrix, value_matrix, unit_rest
    )
    first_term = jnp.sum(grad_normed_one * unit_one, 0)
    grad_input = grad_residual + norm_back(grad_normed_one * first_full, unit_one, scale_one)
    query_out, key_out, value_out, output_out = unit_grads(
        normalized, query_grad, dkv, attended, grad_branch
    )
    first_out = gain_sum(first_term, me, place, 8, 4)
    second_out = gain_sum(second_term, me, place, 8, 4)
    multiplier = jnp.sqrt(clip_limit / jnp.maximum(head_max, clip_limit))
    key_ratio = jnp.min(multiplier.reshape(KEY_VALUE_HEADS, REPEAT), 1)
    return (
        result.reshape(1, rows, model),
        grad_input.astype(bf16).reshape(1, rows, model),
        first_out,
        query_out,
        key_out,
        value_out,
        output_out,
        second_out,
        gate_grad,
        up_grad,
        down_grad,
        head_max,
        clipped(query_weight, multiplier),
        clipped(key_matrix, key_ratio),
    )


def solution(mesh):
    shard, whole = P(None, "fsdp"), P()
    token, block = P("fsdp", "ctx", None), P("ctx", "fsdp")
    gain = P(("ctx", "fsdp"))
    chips = mesh.shape["ctx"] == 8 and mesh.shape["fsdp"] == 4
    return jax.shard_map(
        on_row_of_chips if chips else on_device,
        mesh=mesh,
        in_specs=(token, token, P("fsdp", None), whole, P("fsdp"))
        + (shard,) * 4
        + (P("fsdp"),)
        + (shard,) * 3
        + (whole,),
        out_specs=(token, token, gain)
        + (block,) * 4
        + (gain,)
        + (block,) * 3
        + (whole, shard, shard),
        check_vma=False,
    )
```

```python
import functools
import math

import jax
import jax.numpy as jnp
from jax import lax
from jax.experimental import pallas as pl
from jax.experimental.pallas import tpu as pltpu
from jax.sharding import PartitionSpec as P

QUERY_HEADS = 16
KEY_VALUE_HEADS = 8
HEAD_SIZE = 128
REPEAT = QUERY_HEADS // KEY_VALUE_HEADS
UNIT = (REPEAT + 2) * HEAD_SIZE

epsilon = 1e-06
rope_base = 1000000.0
hidden_fill_value = -1e30
bf16 = jnp.bfloat16
f32 = jnp.float32
SCALE = 1.0 / math.sqrt(HEAD_SIZE)


def swap(value, axis, mask):
    size = lax.axis_size(axis)
    return lax.ppermute(value, axis, [(i, i ^ mask) for i in range(size)])


def bits_down(size):
    mask = size // 2
    while mask:
        yield mask
        mask //= 2


def by_place(items, me):
    mask = 1
    while mask < len(items):
        odd = (me & mask) != 0
        items = [jnp.where(odd, items[j ^ mask], items[j]) for j in range(len(items))]
        mask *= 2
    return items


def gather_ctx(block):
    size = lax.axis_size("ctx")
    whole = block[None]
    mask = 1
    while mask < size:
        whole = jnp.concatenate([whole, swap(whole, "ctx", mask)], 0)
        mask *= 2
    return [whole]


def sum_halving(slots, axis):
    for mask in bits_down(slots.shape[0]):
        keep = slots[:mask].astype(f32)
        slots = (keep + swap(slots[mask:], axis, mask).astype(f32)).astype(slots.dtype)
    return slots[0].astype(f32)


def sum_fsdp(pieces):
    total = pieces[0].astype(f32)
    for d in range(1, len(pieces)):
        total = total + swap(pieces[d].astype(bf16), "fsdp", d).astype(f32)
    return total


def params(flops, bytes_accessed):
    return dict(
        compiler_params=pltpu.CompilerParams(vmem_limit_bytes=48 * 2**20),
        cost_estimate=pl.CostEstimate(
            flops=flops, bytes_accessed=bytes_accessed, transcendentals=0
        ),
    )


def rotate(value, cosine, sine):
    return value * cosine + pltpu.roll(value, HEAD_SIZE // 2, 1) * sine


def slot_matmul_body(n_slots, parts, depth, rope, me_ref, x_ref, *refs):
    slot_refs = refs[:n_slots]
    out_ref = refs[-1]
    total = None
    for j in range(n_slots):
        for q in range(parts):
            owner = me_ref[0] ^ (j * parts + q)
            cols = pl.ds(pl.multiple_of(owner * depth, depth), depth)
            term = jnp.dot(x_ref[:, cols], slot_refs[j][q], preferred_element_type=f32)
            total = term if total is None else total + term
    if rope:
        cosine, sine = refs[n_slots][...], refs[n_slots + 1][...]
        parts_out = [
            rotate(total[:, i * HEAD_SIZE : (i + 1) * HEAD_SIZE], cosine, sine)
            for i in range(REPEAT + 1)
        ]
        total = jnp.concatenate(parts_out + [total[:, (REPEAT + 1) * HEAD_SIZE :]], 1)
    out_ref[...] = total.astype(out_ref.dtype)


def in_order(slots, me):
    whole = jnp.concatenate(slots, 0)
    whole = whole[me ^ jnp.arange(whole.shape[0], dtype=jnp.int32)]
    return whole.reshape(-1, whole.shape[2])


def in_order(slots, me):
    whole = jnp.concatenate(slots, 0)
    whole = whole[me ^ jnp.arange(whole.shape[0], dtype=jnp.int32)]
    return whole.reshape(-1, whole.shape[2])


def slot_matmul(x, slots, me, tile, out_dtype, tables=None):
    rows = x.shape[0]
    parts, depth, width = slots[0].shape
    if depth % 128:
        total = product(x, in_order(slots, me))
        if tables is None:
            return total.astype(out_dtype)
        total = total.reshape(rows, width // UNIT, REPEAT + 2, HEAD_SIZE)
        cosine, sine = (t[:, None, None] for t in tables)
        turned = total[:, :, : REPEAT + 1]
        turned = turned * cosine + jnp.roll(turned, HEAD_SIZE // 2, -1) * sine
        total = jnp.concatenate([turned, total[:, :, REPEAT + 1 :]], 2)
        return total.reshape(rows, width).astype(out_dtype)
    extra = [] if tables is None else list(tables)
    body = functools.partial(
        slot_matmul_body, len(slots), parts, depth, tables is not None
    )
    return pl.pallas_call(
        body,
        out_shape=jax.ShapeDtypeStruct((rows, width), out_dtype),
        grid_spec=pltpu.PrefetchScalarGridSpec(
            num_scalar_prefetch=1,
            grid=(width // tile,),
            in_specs=[pl.BlockSpec(x.shape, lambda i, me: (0, 0))]
            + [pl.BlockSpec((parts, depth, tile), lambda i, me: (0, 0, i))] * len(slots)
            + [pl.BlockSpec(e.shape, lambda i, me: (0, 0)) for e in extra],
            out_specs=pl.BlockSpec((rows, tile), lambda i, me: (0, i)),
        ),
        **params(2 * rows * x.shape[1] * width, 2 * x.shape[1] * width),
    )(me, x, *slots, *extra)


def slot_matmul_t_body(n_slots, parts, depth, me_ref, x_ref, *refs):
    slot_refs = refs[:n_slots]
    out_ref, total_ref = refs[n_slots], refs[n_slots + 1]
    step = pl.program_id(0)

    @pl.when(step == 0)
    def _():
        total_ref[...] = jnp.zeros_like(total_ref)

    x = x_ref[...]
    for j in range(n_slots):
        for q in range(parts):
            owner = me_ref[0] ^ (j * parts + q)
            cols = pl.ds(pl.multiple_of(owner * depth, depth), depth)
            total_ref[:, cols] += lax.dot_general(
                x, slot_refs[j][q], (((1,), (1,)), ((), ())), preferred_element_type=f32
            )

    @pl.when(step == pl.num_programs(0) - 1)
    def _():
        out_ref[...] = total_ref[...].astype(out_ref.dtype)


def slot_matmul_t(x, slots, me, tile, out_dtype):
    rows, width = x.shape
    parts, depth, _ = slots[0].shape
    height = parts * depth * len(slots)
    if depth % 128:
        return product_t(x, in_order(slots, me)).astype(out_dtype)
    return pl.pallas_call(
        functools.partial(slot_matmul_t_body, len(slots), parts, depth),
        out_shape=jax.ShapeDtypeStruct((rows, height), out_dtype),
        grid_spec=pltpu.PrefetchScalarGridSpec(
            num_scalar_prefetch=1,
            grid=(width // tile,),
            in_specs=[pl.BlockSpec((rows, tile), lambda i, me: (0, i))]
            + [pl.BlockSpec((parts, depth, tile), lambda i, me: (0, 0, i))]
            * len(slots),
            out_specs=pl.BlockSpec((rows, height), lambda i, me: (0, 0)),
            scratch_shapes=[pltpu.VMEM((rows, height), f32)],
        ),
        **params(2 * rows * height * width, 2 * height * width),
    )(me, x, *slots)


def keys_of(slot_refs):
    def column(i):
        parts = [
            r[..., i * HEAD_SIZE : (i + 1) * HEAD_SIZE].reshape(-1, HEAD_SIZE)
            for r in slot_refs
        ]
        return parts[0] if len(parts) == 1 else jnp.concatenate(parts, 0)

    return column(0), column(1)


def scores_of(qkv_ref, keys, natural_ref, start_ref, key_natural_ref):
    blk = qkv_ref.shape[0]
    query = jnp.concatenate(
        [qkv_ref[:, i * HEAD_SIZE : (i + 1) * HEAD_SIZE] for i in range(REPEAT)], 0
    )
    scores = (
        lax.dot_general(
            query, keys, (((1,), (1,)), ((), ())), preferred_element_type=f32
        )
        * SCALE
    )
    key_natural = key_natural_ref[0]
    allowed = (key_natural >= start_ref[...]) & (key_natural <= natural_ref[...])
    allowed = jnp.concatenate([allowed] * REPEAT, 0)
    scores = jnp.where(allowed, scores, hidden_fill_value)
    best = jnp.max(scores, 1, keepdims=True)
    exps = jnp.exp(scores - best)
    return query, exps * (1.0 / jnp.sum(exps, 1, keepdims=True)), best, blk


def attend_body(n_slots, place_ref, natural_ref, start_ref, key_natural_ref, qkv_ref, *refs):
    slot_refs, (out_ref, best_ref) = refs[:n_slots], refs[n_slots:]
    keys, values = keys_of(slot_refs)
    _, probs, best, blk = scores_of(qkv_ref, keys, natural_ref, start_ref, key_natural_ref)
    heads = jnp.dot(probs.astype(bf16), values, preferred_element_type=f32)
    out_ref[...] = jnp.concatenate(
        [heads[i * blk : (i + 1) * blk] for i in range(REPEAT)], 1
    ).astype(bf16)
    tops = [
        jnp.broadcast_to(jnp.max(best[i * blk : (i + 1) * blk], 0, keepdims=True), (1, 128))
        for i in range(REPEAT)
    ]
    best_ref[0, 0] = jnp.concatenate(tops + [jnp.zeros((8 - REPEAT, 128), f32)], 0)


def attend_back_body(
    n_slots, place_ref, natural_ref, start_ref, key_natural_ref, cosine_ref, sine_ref, qkv_ref, grad_ref, *refs
):
    slot_refs, (dq_ref, *dkv_refs) = refs[:n_slots], refs[n_slots:]
    keys, values = keys_of(slot_refs)
    query, probs, _, blk = scores_of(qkv_ref, keys, natural_ref, start_ref, key_natural_ref)
    grad = jnp.concatenate(
        [grad_ref[:, i * HEAD_SIZE : (i + 1) * HEAD_SIZE] for i in range(REPEAT)], 0
    )
    low = probs.astype(bf16)
    grad_probs = lax.dot_general(
        grad, values, (((1,), (1,)), ((), ())), preferred_element_type=f32
    )
    delta = jnp.sum(low.astype(f32) * grad_probs, 1, keepdims=True)
    score_grad = (probs * (grad_probs - delta)).astype(bf16)
    query_grad = jnp.dot(score_grad, keys, preferred_element_type=f32) * SCALE
    cosine, sine = cosine_ref[...], sine_ref[...]
    dq_ref[...] = jnp.concatenate(
        [
            rotate(query_grad[i * blk : (i + 1) * blk], cosine, -sine)
            for i in range(REPEAT)
        ],
        1,
    ).astype(bf16)
    over_rows = (((0,), (0,)), ((), ()))
    key_grad = (
        lax.dot_general(score_grad, query, over_rows, preferred_element_type=f32) * SCALE
    ).astype(bf16)
    value_grad = lax.dot_general(low, grad, over_rows, preferred_element_type=f32).astype(
        bf16
    )
    both = jnp.concatenate([key_grad, value_grad], 1)
    first = 0
    for ref in dkv_refs:
        rows = math.prod(ref.shape[:-1])
        ref[...] = both[first : first + rows].reshape(ref.shape)
        first += rows


def attention_specs(slots, blk, keys, shard_heads):
    def own_place(r, h, place):
        return (r, (place[0] ^ (h // shard_heads)) * shard_heads + h % shard_heads)

    column = pl.BlockSpec((blk, 1), lambda r, h, p: (r, 0))
    return (
        [column, column, pl.BlockSpec((1, 1, keys), lambda r, h, p: (r, 0, 0))],
        pl.BlockSpec((blk, UNIT), lambda r, h, p: (r, h)),
        pl.BlockSpec((blk, REPEAT * HEAD_SIZE), lambda r, h, p: (r, h)),
        pl.BlockSpec((blk, REPEAT * HEAD_SIZE), own_place),
        pl.BlockSpec((1, 1, 8, 128), lambda r, h, p: own_place(r, h, p) + (0, 0)),
        [
            pl.BlockSpec((s.shape[0], blk, 2 * HEAD_SIZE), lambda r, h, p: (0, r, h))
            if s.ndim == 3
            else pl.BlockSpec(
                (1, s.shape[1], blk, 2 * HEAD_SIZE),
                lambda r, h, p: (h // shard_heads, 0, r, h % shard_heads),
            )
            for s in slots
        ],
    )


def attend(place, natural, start, key_natural, qkv, slots):
    rows, heads = qkv.shape[0], qkv.shape[1] // UNIT
    rounds, _, keys = key_natural.shape
    blk = rows // rounds
    meta, unit, _, placed, best, slot = attention_specs(
        slots, blk, keys, heads // lax.axis_size("fsdp")
    )
    return pl.pallas_call(
        functools.partial(attend_body, len(slots)),
        out_shape=[
            jax.ShapeDtypeStruct((rows, heads * REPEAT * HEAD_SIZE), bf16),
            jax.ShapeDtypeStruct((rounds, heads, 8, 128), f32),
        ],
        grid_spec=pltpu.PrefetchScalarGridSpec(
            num_scalar_prefetch=1,
            grid=(rounds, heads),
            in_specs=meta + [unit] + slot,
            out_specs=[placed, best],
        ),
        **params(4 * rows * keys * heads * REPEAT * HEAD_SIZE, 12 * 2**20),
    )(place, natural, start, key_natural, qkv, *slots)


def attend_back(place, natural, start, key_natural, cosine, sine, qkv, grad, slots):
    rows, heads = qkv.shape[0], qkv.shape[1] // UNIT
    rounds, _, keys = key_natural.shape
    blk = rows // rounds
    meta, unit, pair, placed, _, slot = attention_specs(
        slots, blk, keys, heads // lax.axis_size("fsdp")
    )
    table = pl.BlockSpec((blk, HEAD_SIZE), lambda r, h, p: (r, 0))
    return pl.pallas_call(
        functools.partial(attend_back_body, len(slots)),
        out_shape=[jax.ShapeDtypeStruct((rows, heads * REPEAT * HEAD_SIZE), bf16)]
        + [jax.ShapeDtypeStruct(s.shape, bf16) for s in slots],
        grid_spec=pltpu.PrefetchScalarGridSpec(
            num_scalar_prefetch=1,
            grid=(rounds, heads),
            in_specs=meta + [table, table, unit, placed] + slot,
            out_specs=[pair] + slot,
        ),
        **params(10 * rows * keys * heads * REPEAT * HEAD_SIZE, 20 * 2**20),
    )(place, natural, start, key_natural, cosine, sine, qkv, grad, *slots)


ANY = pl.BlockSpec(memory_space=pl.ANY)
VMEM = pl.BlockSpec(memory_space=pltpu.VMEM)
MESH = pl.DeviceIdType.MESH
OVER_ROWS = (((0,), (0,)), ((), ()))
OVER_COLUMNS = (((1,), (1,)), ((), ()))


def flip(place, mask):
    for bit in (1, 2, 4):
        if mask & bit:
            place = place + bit - 2 * bit * lax.rem(lax.div(place, bit), 2)
    return place


def device(ctx, fsdp):
    return {
        "ctx": flip(lax.axis_index("ctx"), ctx),
        "fsdp": flip(lax.axis_index("fsdp"), fsdp),
    }


def greet(ctx_masks, fsdp_masks):
    barrier = pltpu.get_barrier_semaphore()
    partners = [(m, 0) for m in ctx_masks] + [(0, m) for m in fsdp_masks]
    for ctx, fsdp in partners:
        pl.semaphore_signal(barrier, inc=1, device_id=device(ctx, fsdp), device_id_type=MESH)
    pl.semaphore_wait(barrier, len(partners))


class Transfers:
    def __init__(self, send, recv):
        self.send, self.recv, self.count, self.open = send, recv, 0, {}

    def start(self, src, dst, ctx=0, fsdp=0):
        number = self.count
        copy = pltpu.make_async_remote_copy(
            src_ref=src,
            dst_ref=dst,
            send_sem=self.send.at[number],
            recv_sem=self.recv.at[number],
            device_id=device(ctx, fsdp),
            device_id_type=MESH,
        )
        copy.start()
        copy_key = id(copy)
        self.open[copy_key] = copy
        self.count += 1
        return copy

    def release(self, copy):
        self.open.pop(id(copy)).wait_send()

    def finish(self):
        for copy in self.open.values():
            copy.wait_send()


def remote_call(body, outs, out_specs, in_specs, scratch, transfers, number, flops=0, moved=2**22):
    return pl.pallas_call(
        body,
        out_shape=outs,
        in_specs=in_specs,
        out_specs=out_specs,
        scratch_shapes=list(scratch)
        + [pltpu.SemaphoreType.DMA((transfers,)), pltpu.SemaphoreType.DMA((transfers,))],
        compiler_params=pltpu.CompilerParams(
            vmem_limit_bytes=60 * 2**20, collective_id=number, has_side_effects=True
        ),
        cost_estimate=pl.CostEstimate(flops=flops, bytes_accessed=moved, transcendentals=0),
    )


class PlaneGather:
    def __init__(self, transfers, slots):
        self.t, self.s = transfers, slots
        self.half = slots[0].shape[0] // 2

    def begin(self):
        s, t = self.s, self.t
        self.x = t.start(s[0], s[2], ctx=2)
        self.y = t.start(s[0], s[4], ctx=4)
        self.c = [t.start(s[0], s[1], ctx=1)]

    def middle(self):
        s, t, h = self.s, self.t, self.half
        self.x.wait_recv()
        self.low = t.start(s[2].at[:h], s[6].at[:h], ctx=4)
        self.c.append(t.start(s[2], s[3], ctx=1))
        self.y.wait_recv()
        self.high = t.start(s[4].at[h:], s[6].at[h:], ctx=2)
        self.c.append(t.start(s[4], s[5], ctx=1))

    def end(self):
        s, t = self.s, self.t
        self.low.wait_recv()
        self.high.wait_recv()
        self.c.append(t.start(s[6], s[7], ctx=1))

    def ready(self):
        for copy in self.c:
            copy.wait_recv()


class RowGather:
    def __init__(self, own, slots, send, recv):
        self.own, self.slots, self.send, self.recv = own, slots, send, recv
        place = lax.axis_index("fsdp")
        self.inner = (place == 1) | (place == 2)

    def copy(self, src, dst, number, fsdp):
        return pltpu.make_async_remote_copy(
            src_ref=src,
            dst_ref=self.slots[dst],
            send_sem=self.send.at[number],
            recv_sem=self.recv.at[dst - 1],
            device_id=device(0, fsdp),
            device_id_type=MESH,
        )

    def near(self):
        return self.copy(self.own, 1, 0, 1)

    def across(self):
        return self.copy(self.own, 3, 1, 3)

    def near_on(self):
        return self.copy(self.slots[1], 2, 2, 3)

    def across_on(self):
        return self.copy(self.slots[3], 2, 3, 1)

    def second_on(self):
        return self.copy(self.slots[2], 3, 4, 1)

    def begin(self):
        self.near().start()

        @pl.when(self.inner)
        def _():
            self.across().start()

    def first(self):
        self.near().wait_recv()

        @pl.when(self.inner)
        def _():
            self.near_on().start()
            self.across().wait_recv()
            self.across_on().start()

    def second(self):
        self.near_on().wait_recv()

        @pl.when(self.inner)
        def _():
            self.second_on().start()

    def third(self):
        @pl.when(jnp.logical_not(self.inner))
        def _():
            self.second_on().wait_recv()

    def finish(self):
        self.near().wait_send()

        @pl.when(self.inner)
        def _():
            self.across().wait_send()
            self.near_on().wait_send()
            self.across_on().wait_send()
            self.second_on().wait_send()


def probabilities(query, keys, allowed):
    scores = lax.dot_general(query, keys, OVER_COLUMNS, preferred_element_type=f32) * SCALE
    scores = jnp.where(allowed, scores, hidden_fill_value)
    best = jnp.max(scores, 1, keepdims=True)
    exps = jnp.exp(scores - best)
    return exps * (1.0 / jnp.sum(exps, 1, keepdims=True)), best


def stacked_heads(value):
    return jnp.concatenate(
        [value[:, i * HEAD_SIZE : (i + 1) * HEAD_SIZE] for i in range(REPEAT)], 0
    )


def attention_row_body(
    x_ref, gain_ref, cosine_ref, sine_ref, natural_ref, begin_ref, key_natural_ref,
    q_ref, k_ref, v_ref, o_ref, down_ref, dy_ref,
    h_out, qkv_out, attended_out, best_out, residual_out, h2_out, gain_out,
    kv_out, unit_out, output_out, down_out, dy_out,
    q_own, k_own, v_own, o_own, units, outputs, kvs, h_rel,
    own_sem, keep_sem, gain_send, gain_recv, row_send, row_recv, send, recv,
):
    me, place = lax.axis_index("ctx"), lax.axis_index("fsdp")
    rows, model = x_ref.shape
    depth = units.shape[2]
    rounds = key_natural_ref.shape[0]
    blk = rows // rounds
    heads = q_ref.shape[1] // (REPEAT * HEAD_SIZE)
    width = o_ref.shape[1]
    own = pl.ds(pl.multiple_of(me * depth, depth), depth)
    loads = [
        pltpu.make_async_copy(src, dst, own_sem.at[i])
        for i, (src, dst) in enumerate(
            ((q_ref, q_own), (k_ref, k_own), (v_ref, v_own), (o_ref, o_own))
        )
    ]
    for load in loads:
        load.start()
    gain_out[0] = gain_ref[...]
    greet((1, 2, 4), (1, 2, 3))
    gains = Transfers(gain_send, gain_recv)
    gain_copies = [gains.start(gain_ref, gain_out.at[d], fsdp=d) for d in (1, 2, 3)]
    t = Transfers(send, recv)
    unit_rows, first = [], 0
    for i, ref in enumerate((q_ref, k_ref, v_ref)):
        cols = slice(first, first + ref.shape[1])
        first += ref.shape[1]
        unit_rows.append(
            RowGather(
                ref.at[own],
                [None] + [units.at[d, 0, :, cols] for d in range(3)],
                row_send.at[i],
                row_recv.at[i],
            )
        )
    output_row = RowGather(
        o_ref.at[own], [None] + [outputs.at[d, 0] for d in range(3)], row_send.at[3], row_recv.at[3]
    )
    dy_row = RowGather(
        dy_ref, [None] + [dy_out.at[d] for d in range(3)], row_send.at[4], row_recv.at[4]
    )
    unit_plane = [None] + [
        PlaneGather(t, [units.at[d, j] for j in range(8)]) for d in range(3)
    ]
    output_plane = [None] + [
        PlaneGather(t, [outputs.at[d, j] for j in range(8)]) for d in range(3)
    ]
    down_plane = [None] + [
        PlaneGather(t, [down_out.at[d, j] for j in range(8)]) for d in range(3)
    ]
    kv_plane = [PlaneGather(t, [kvs.at[d, j] for j in range(8)]) for d in range(4)]
    for row in unit_rows:
        row.begin()

    x = x_ref[...].astype(f32)
    unit = x * lax.rsqrt(jnp.mean(x * x, 1, keepdims=True) + epsilon)
    for copy in gain_copies:
        copy.wait_recv()
    for d in range(4):
        gain_cols = pl.ds(pl.multiple_of(flip(place, d) * width, width), width)
        residual_out[:, gain_cols] = jnp.broadcast_to(gain_out[d, 0:1], (rows, width))
    h_out[...] = (unit * residual_out[...]).astype(bf16)
    for j in range(8):
        block = pl.ds(pl.multiple_of(flip(me, j) * depth, depth), depth)
        h_rel[:, j * depth : (j + 1) * depth] = h_out[:, block]
    cosine, sine = cosine_ref[...], sine_ref[...]

    def project(d):
        if d == 0:
            h = h_out[...]
            parts = [
                jnp.dot(h, w[...], preferred_element_type=f32) for w in (q_own, k_own, v_own)
            ]
            total = jnp.concatenate(parts, 1)
        else:
            weight = units[d - 1].reshape(model, units.shape[3])
            total = jnp.dot(h_rel[...], weight, preferred_element_type=f32)

        def head(i):
            return total[:, i * HEAD_SIZE : (i + 1) * HEAD_SIZE]

        for h in range(heads):
            query = [
                rotate(head(REPEAT * h + i), cosine, sine).astype(bf16) for i in range(REPEAT)
            ]
            key = rotate(head(REPEAT * heads + h), cosine, sine).astype(bf16)
            value = head((REPEAT + 1) * heads + h).astype(bf16)
            first = (d * heads + h) * UNIT
            qkv_out[:, first : first + UNIT] = jnp.concatenate(query + [key, value], 1)
            first = h * 2 * HEAD_SIZE
            kvs[d, 0, :, first : first + 2 * HEAD_SIZE] = jnp.concatenate([key, value], 1)

    def attend_heads(d):
        def step(i, carry):
            r, h = lax.div(i, heads), lax.rem(i, heads)
            here = pl.ds(pl.multiple_of(r * blk, blk), blk)
            first = pl.multiple_of(d * heads * UNIT + h * UNIT, UNIT)
            query = stacked_heads(qkv_out[here, pl.ds(first, REPEAT * HEAD_SIZE)])
            cols = pl.ds(pl.multiple_of(h * 2 * HEAD_SIZE, 2 * HEAD_SIZE), 2 * HEAD_SIZE)
            both = kvs[d, :, here, cols].reshape(8 * blk, 2 * HEAD_SIZE)
            natural = key_natural_ref[r]
            allowed = (natural >= begin_ref[here]) & (natural <= natural_ref[here])
            allowed = jnp.concatenate([allowed] * REPEAT, 0)
            probs, best = probabilities(query, both[:, :HEAD_SIZE], allowed)
            out = jnp.dot(probs.astype(bf16), both[:, HEAD_SIZE:], preferred_element_type=f32)
            spot = flip(place, d) * heads + h
            cols = pl.ds(pl.multiple_of(spot * REPEAT * HEAD_SIZE, REPEAT * HEAD_SIZE), REPEAT * HEAD_SIZE)
            attended_out[here, cols] = jnp.concatenate(
                [out[i * blk : (i + 1) * blk] for i in range(REPEAT)], 1
            ).astype(bf16)
            tops = [
                jnp.broadcast_to(jnp.max(best[i * blk : (i + 1) * blk], 0, keepdims=True), (1, 128))
                for i in range(REPEAT)
            ]
            best_out[r, spot] = jnp.concatenate(tops + [jnp.zeros((8 - REPEAT, 128), f32)], 0)
            return carry

        lax.fori_loop(0, rounds * heads, step, 0)

    keeps = []

    def keep(src, dst):
        copy = pltpu.make_async_copy(src, dst, keep_sem.at[len(keeps)])
        copy.start()
        keeps.append(copy)

    for load in loads[:3]:
        load.wait()
    project(0)
    kv_plane[0].begin()
    for row in unit_rows:
        row.first()
    unit_plane[1].begin()
    output_row.begin()
    kv_plane[0].middle()
    for row in unit_rows:
        row.second()
    unit_plane[2].begin()
    unit_plane[1].middle()
    kv_plane[0].end()
    output_row.first()
    for row in unit_rows:
        row.third()
    unit_plane[3].begin()
    downs = []
    for d in (1, 2, 3):
        row = flip(place, d) * 8 * depth + me * depth
        downs.append(
            t.start(
                down_ref.at[pl.ds(pl.multiple_of(row, depth), depth)], down_out.at[d - 1, 0], fsdp=d
            )
        )
    dy_row.begin()
    unit_plane[2].middle()
    unit_plane[1].end()
    output_row.second()
    unit_plane[1].ready()
    project(1)
    kv_plane[1].begin()
    unit_plane[3].middle()
    unit_plane[2].end()
    output_row.third()
    unit_plane[2].ready()
    project(2)
    kv_plane[2].begin()
    kv_plane[1].middle()
    unit_plane[3].end()
    kv_plane[0].ready()
    attend_heads(0)
    unit_plane[3].ready()
    project(3)
    kv_plane[3].begin()
    kv_plane[2].middle()
    kv_plane[1].end()
    output_plane[1].begin()
    dy_row.first()
    kv_plane[3].middle()
    kv_plane[2].end()
    output_plane[2].begin()
    kv_plane[1].ready()
    attend_heads(1)
    output_plane[1].middle()
    kv_plane[3].end()
    output_plane[3].begin()
    kv_plane[2].ready()
    attend_heads(2)
    output_plane[2].middle()
    output_plane[1].end()
    downs[0].wait_recv()
    down_plane[1].begin()
    dy_row.second()
    kv_plane[3].ready()
    attend_heads(3)
    output_plane[3].middle()
    output_plane[2].end()
    downs[1].wait_recv()
    down_plane[2].begin()
    output_plane[3].end()
    for j in range(8):
        block = pl.ds(pl.multiple_of(flip(me, j) * depth, depth), depth)
        h_rel[:, j * depth : (j + 1) * depth] = attended_out[:, block]
    downs[2].wait_recv()
    down_plane[3].begin()
    for d in range(3):
        keep(units.at[d], unit_out.at[d])
    for d in range(4):
        keep(kvs.at[d], kv_out.at[d])
    loads[3].wait()
    square = None
    for d in range(4):
        cols = pl.ds(pl.multiple_of(flip(place, d) * width, width), width)
        if d == 0:
            term = jnp.dot(attended_out[...], o_own[...], preferred_element_type=f32)
        else:
            output_plane[d].ready()
            weight = outputs[d - 1].reshape(model, width)
            term = jnp.dot(h_rel[...], weight, preferred_element_type=f32)
        value = x_ref[:, cols].astype(f32) + term
        residual_out[:, cols] = value
        part = jnp.sum(value * value, 1, keepdims=True)
        square = part if square is None else square + part
        if d == 1:
            down_plane[1].middle()
    scale = lax.rsqrt(square * (1.0 / model) + epsilon)
    for d in range(4):
        cols = pl.ds(pl.multiple_of(flip(place, d) * width, width), width)
        h2_out[:, cols] = (residual_out[:, cols] * scale * gain_out[d, 1:2]).astype(bf16)
    for d in range(3):
        keep(outputs.at[d], output_out.at[d])
    down_plane[2].middle()
    down_plane[1].end()
    down_plane[3].middle()
    down_plane[2].end()
    down_plane[3].end()
    dy_row.third()
    for d in (1, 2, 3):
        down_plane[d].ready()
    for copy in keeps:
        copy.wait()
    for row in unit_rows + [output_row, dy_row]:
        row.finish()
    gains.finish()
    t.finish()


def attention_row(x, gains, cosine, sine, natural, begin, key_natural, query, key, value, output, down, dy):
    rows, model = x.shape
    depth = model // 8
    width = query.shape[1] + key.shape[1] + value.shape[1]
    kv_width = key.shape[1] + value.shape[1]
    rounds = key_natural.shape[0]
    dma = pltpu.SemaphoreType.DMA

    def out(shape, dtype=bf16):
        return jax.ShapeDtypeStruct(shape, dtype)

    return remote_call(
        attention_row_body,
        [
            out((rows, model)),
            out((rows, 4 * width)),
            out((rows, model)),
            out((rounds, KEY_VALUE_HEADS, 8, 128), f32),
            out((rows, model), f32),
            out((rows, model)),
            out((4,) + gains.shape, f32),
            out((4, 8, rows, kv_width)),
            out((3, 8, depth, width)),
            out((3, 8, depth, output.shape[1])),
            out((3, 8, depth, down.shape[1])),
            out((3,) + dy.shape),
        ],
        [VMEM] * 7 + [ANY] * 5,
        [VMEM] * 7 + [ANY] * 6,
        [
            pltpu.VMEM(query.shape, bf16),
            pltpu.VMEM(key.shape, bf16),
            pltpu.VMEM(value.shape, bf16),
            pltpu.VMEM(output.shape, bf16),
            pltpu.VMEM((3, 8, depth, width), bf16),
            pltpu.VMEM((3, 8, depth, output.shape[1]), bf16),
            pltpu.VMEM((4, 8, rows, kv_width), bf16),
            pltpu.VMEM((rows, model), bf16),
            dma((4,)),
            dma((10,)),
            dma((3,)),
            dma((3,)),
            dma((5, 5)),
            dma((5, 3)),
        ],
        3 + 13 * 8,
        0,
        flops=10 * rows * model * model,
    )(x, gains, cosine, sine, natural, begin, key_natural, query, key, value, output, down, dy)


TILE = 256


def feed_forward_row_body(
    h_ref, dy_ref, dy_rest, gate_ref, up_ref, down_own, down_rest,
    hid_out, dg_out, du_out, h_out, y_out, y_rest, back_out,
    gates, ups, downs, hs, dys, y_acc, back_acc, back_send, back_land, y_send, stage,
    load_sem, down_sem, dy_sem, h_sem, stage_sem, y_sem, row_send, row_recv, send, recv,
):
    rows, model = h_ref.shape
    tiles = gates.shape[0]
    me, place = lax.axis_index("ctx"), lax.axis_index("fsdp")
    width = down_own.shape[1]

    def tile_loads(i, slot):
        cols = pl.ds(pl.multiple_of(i * TILE, TILE), TILE)
        copies = [
            pltpu.make_async_copy(gate_ref.at[:, cols], gates.at[i], load_sem.at[0, i]),
            pltpu.make_async_copy(up_ref.at[:, cols], ups.at[i], load_sem.at[1, i]),
        ]
        own_rows = pl.ds(pl.multiple_of(place * tiles * TILE + i * TILE, TILE), TILE)
        for d in range(4):
            cols = pl.ds(pl.multiple_of(flip(place, d) * width, width), width)
            src = down_own.at[own_rows] if d == 0 else down_rest.at[d - 1, slot]
            copies.append(pltpu.make_async_copy(src, downs.at[i, :, cols], down_sem.at[i, d]))
        return copies

    dy_copies = [
        pltpu.make_async_copy(dy_ref if d == 0 else dy_rest.at[d - 1], dys.at[d], dy_sem.at[d])
        for d in range(4)
    ]
    dy_copies[0].start()
    for i in range(tiles):
        for load in tile_loads(i, flip(me, i)):
            load.start()
    for load in dy_copies[1:]:
        load.start()
    greet((), (1, 2, 3))
    t = Transfers(send, recv)
    row = RowGather(h_ref, [None] + [hs.at[d] for d in range(3)], row_send, row_recv)
    row.begin()
    dy_copies[0].wait()

    def stage_copy(slot, k, part, i):
        out = (hid_out, dg_out, du_out)[k]
        cols = pl.ds(pl.multiple_of(i * TILE, TILE), TILE)
        return pltpu.make_async_copy(
            stage.at[slot, k], out.at[pl.ds(part * rows, rows), cols], stage_sem.at[slot, k]
        )

    def chunk(part, h):
        def step(i, carry):
            slot = lax.rem(i, 2)
            if part == 0:
                for load in tile_loads(i, 0):
                    load.wait()
            gate, up, down = gates[i], ups[i], downs[i]
            g = jnp.dot(h[...], gate, preferred_element_type=f32)
            u = jnp.dot(h[...], up, preferred_element_type=f32)
            grad = lax.dot_general(dys[part], down, OVER_COLUMNS, preferred_element_type=f32)
            sigmoid = jax.nn.sigmoid(g)
            silu = g * sigmoid
            hidden = (silu * u).astype(bf16)
            grad_gate = (grad * u * sigmoid * (1.0 + g * (1.0 - sigmoid))).astype(bf16)
            grad_up = (grad * silu).astype(bf16)

            @pl.when(i >= 2)
            def _():
                for k in range(3):
                    stage_copy(slot, k, part, i - 2).wait()

            stage[slot, 0] = hidden
            stage[slot, 1] = grad_gate
            stage[slot, 2] = grad_up
            for k in range(3):
                stage_copy(slot, k, part, i).start()
            y = jnp.dot(hidden, down, preferred_element_type=f32)
            back = lax.dot_general(grad_gate, gate, OVER_COLUMNS, preferred_element_type=f32)
            back += lax.dot_general(grad_up, up, OVER_COLUMNS, preferred_element_type=f32)

            @pl.when(i == 0)
            def _():
                y_acc[...] = y
                back_acc[...] = back

            @pl.when(i > 0)
            def _():
                y_acc[...] += y
                back_acc[...] += back

            return carry

        lax.fori_loop(0, tiles, step, 0)
        for i in (tiles - 2, tiles - 1):
            for k in range(3):
                stage_copy(i % 2, k, part, i).wait()

    def keep_h(part, h):
        return pltpu.make_async_copy(h, h_out.at[pl.ds(part * rows, rows)], h_sem.at[part])

    keep_h(0, h_ref).start()
    chunk(0, h_ref)
    y_out[...] = y_acc[...]
    back_out[...] = back_acc[...]
    row.first()
    backs, y_copy = [], None
    for part in (1, 2, 3):
        h = hs.at[part - 1]
        if part == 2:
            row.second()
        if part == 3:
            row.third()
        keep_h(part, h).start()
        dy_copies[part].wait()
        chunk(part, h)
        back_send[part - 1] = back_acc[...].astype(bf16)
        backs.append(t.start(back_send.at[part - 1], back_land.at[part - 1], fsdp=part))
        if y_copy is not None:
            y_copy.wait()
        y_send[...] = y_acc[...].astype(bf16)
        y_copy = pltpu.make_async_copy(y_send, y_rest.at[part - 1], y_sem.at[part - 1])
        y_copy.start()
    y_copy.wait()
    for part in range(4):
        keep_h(part, h_ref if part == 0 else hs.at[part - 1]).wait()
    for d in range(3):
        backs[d].wait_recv()
        back_out[...] += back_land[d].astype(f32)
    row.finish()
    t.finish()


def feed_forward_row(h, dy, dy_rest, gate, up, down_own, down_rest):
    rows, model = h.shape
    units = gate.shape[1]
    tiles = units // TILE
    wide = jax.ShapeDtypeStruct((4 * rows, units), bf16)
    block = pltpu.VMEM((rows, model), f32)
    dma = pltpu.SemaphoreType.DMA
    return remote_call(
        feed_forward_row_body,
        [wide, wide, wide, jax.ShapeDtypeStruct((4 * rows, model), bf16)]
        + [jax.ShapeDtypeStruct((rows, model), f32), jax.ShapeDtypeStruct((3, rows, model), bf16)]
        + [jax.ShapeDtypeStruct((rows, model), f32)],
        [ANY] * 4 + [VMEM, ANY, VMEM],
        [VMEM] + [ANY] * 6,
        [
            pltpu.VMEM((tiles, model, TILE), bf16),
            pltpu.VMEM((tiles, model, TILE), bf16),
            pltpu.VMEM((tiles, TILE, model), bf16),
            pltpu.VMEM((3, rows, model), bf16),
            pltpu.VMEM((4, rows, model), bf16),
            block,
            block,
            pltpu.VMEM((3, rows, model), bf16),
            pltpu.VMEM((3, rows, model), bf16),
            pltpu.VMEM((rows, model), bf16),
            pltpu.VMEM((2, 3, rows, TILE), bf16),
            dma((2, tiles)),
            dma((tiles, 4)),
            dma((4,)),
            dma((4,)),
            dma((2, 3)),
            dma((3,)),
            dma((5,)),
            dma((3,)),
        ],
        3,
        2,
        flops=48 * rows * model * units,
    )(h, dy, dy_rest, gate, up, down_own, down_rest)


class SmallReduce:
    MASKS = ((0, 1), (0, 2), (2, 0), (4, 0), (1, 0))

    def __init__(self, transfers, blocks, land, join):
        self.t, self.blocks, self.land, self.join = transfers, blocks, land, join

    def begin(self, step):
        ctx, fsdp = self.MASKS[step]
        self.copy = self.t.start(self.blocks.at[step], self.land.at[step], ctx=ctx, fsdp=fsdp)

    def end(self, step):
        self.copy.wait_recv()
        self.blocks[step + 1] = self.join(self.blocks[step], self.land[step])

    def on(self, step):
        if 0 <= step - 1 < 5:
            self.end(step - 1)
        if step < 5:
            self.begin(step)


def small_scratch(shape):
    return [pltpu.VMEM((6,) + shape, f32), pltpu.VMEM((5,) + shape, f32)]


class PlaneSum:
    def __init__(self, transfers, cores, far, near, sums, total):
        self.t, self.cores, self.far, self.near = transfers, cores, far, near
        self.sums, self.total = sums, total
        self.half = cores.shape[1] // 2
        self.over = {}

    def send_odd(self, j, src):
        self.over[j - 1] = self.t.start(src, self.cores.at[(j - 1) // 2], ctx=1)
        return self.over[j - 1]

    def even(self, j, value):
        t, h = self.t, self.half
        self.over[j].wait_recv()
        value = value + self.cores[j // 2].astype(f32)
        if j == 0:
            self.total[...] = value
            return
        out = self.sums.at[(6, 2, 4).index(j)]
        out[...] = value.astype(bf16)
        if j == 6:
            self.x6 = t.start(out.at[:h], self.far.at[:h], ctx=2)
            self.y6 = t.start(out.at[h:], self.far.at[h:], ctx=4)
        elif j == 2:
            self.x2 = t.start(out.at[:h], self.near.at[0, :h], ctx=2)
        else:
            self.y4 = t.start(out.at[h:], self.near.at[1, h:], ctx=4)

    def pass_on(self):
        t, h = self.t, self.half
        two, four = self.sums.at[1], self.sums.at[2]
        self.y6.wait_recv()
        two[h:] = (two[h:].astype(f32) + self.far[h:].astype(f32)).astype(bf16)
        self.x2b = t.start(two.at[h:], self.near.at[0, h:], ctx=2)
        self.x6.wait_recv()
        four[:h] = (four[:h].astype(f32) + self.far[:h].astype(f32)).astype(bf16)
        self.y4b = t.start(four.at[:h], self.near.at[1, :h], ctx=4)

    def close(self):
        for copy in (self.x2, self.x2b, self.y4, self.y4b):
            copy.wait_recv()
        return self.total[...] + self.near[0].astype(f32) + self.near[1].astype(f32)


def plane_sum_scratch(count, *shape):
    return [
        pltpu.VMEM((count, 4) + shape, bf16),
        pltpu.VMEM((count,) + shape, bf16),
        pltpu.VMEM((count, 2) + shape, bf16),
        pltpu.VMEM((count, 3) + shape, bf16),
        pltpu.VMEM((count,) + shape, f32),
    ]


def grads_body(
    h_ref, dg_ref, du_ref, hid_ref, dy_ref, dy_rest, y_rest, top_ref,
    gate_out, up_out, down_out, y_land, top_out,
    left, rights, odd, cores, far, near, sums, totals, left_sem, right_sem, dy_sem, out_sem,
    blocks, land, send, recv,
):
    me = lax.axis_index("ctx")
    rows = dy_ref.shape[0]
    depth = cores.shape[2]
    dys = [dy_ref] + [dy_rest.at[d] for d in range(3)]
    right_copies = [
        [pltpu.make_async_copy(dg_ref, rights.at[0], right_sem.at[0])],
        [pltpu.make_async_copy(du_ref, rights.at[1], right_sem.at[1])],
        [
            pltpu.make_async_copy(p, rights.at[0, i * rows : (i + 1) * rows], dy_sem.at[i])
            for i, p in enumerate(dys)
        ],
    ]
    left_copies = [
        pltpu.make_async_copy(h_ref, left, left_sem.at[0]),
        pltpu.make_async_copy(hid_ref, left, left_sem.at[1]),
    ]
    left_copies[0].start()
    right_copies[0][0].start()
    right_copies[1][0].start()
    greet((1, 2, 4), (1, 2, 3))
    t = Transfers(send, recv)
    tops = SmallReduce(t, blocks, land, jnp.maximum)
    blocks[0] = top_ref[...]
    tops.on(0)
    y_copies = []
    left_copies[0].wait()
    jobs, odd_copies, outs = [], {}, []

    def close(k):
        totals[k] = jobs[k].close()
        out = pltpu.make_async_copy(totals.at[k], (gate_out, up_out)[k], out_sem.at[k])
        out.start()
        outs.append(out)

    for k in range(3):
        job = PlaneSum(t, cores.at[k], far.at[k], near.at[k], sums.at[k], totals.at[k])
        jobs.append(job)
        if k == 2:
            for copy in [left_copies[1]] + right_copies[2]:
                copy.start()
            left_copies[1].wait()
        for copy in right_copies[k]:
            copy.wait()

        def partial(j):
            block = pl.ds(pl.multiple_of(flip(me, j) * depth, depth), depth)
            return lax.dot_general(
                left[:, block], rights[k % 2], OVER_ROWS, preferred_element_type=f32
            )

        for i, j in enumerate((7, 5, 3, 1)):
            if j in odd_copies:
                t.release(odd_copies[j])
            odd[j // 2] = partial(j).astype(bf16)
            odd_copies[j] = job.send_odd(j, odd.at[j // 2])
            if k == 0:
                tops.on(i + 1)
            if k == 0 and i == 0:
                for d in (1, 2, 3):
                    y_copies.append(t.start(y_rest.at[d - 1], y_land.at[d - 1], fsdp=d))
        if k:
            jobs[k - 1].pass_on()
        for j in (6, 2, 4, 0):
            job.even(j, partial(j))
        if k:
            close(k - 1)
    tops.on(5)
    top_out[...] = blocks[5]
    jobs[2].pass_on()
    for copy in y_copies:
        copy.wait_recv()
    down_out[...] = jobs[2].close().astype(bf16)
    for copy in outs:
        copy.wait()
    t.finish()


def grads_row(h, dg, du, hid, dy, dy_rest, y_rest, top):
    rows, model = dy.shape
    depth = model // 8
    dma = pltpu.SemaphoreType.DMA
    summed = jax.ShapeDtypeStruct((depth, dg.shape[1]), f32)
    return remote_call(
        grads_body,
        [summed, summed, jax.ShapeDtypeStruct((depth, model), bf16), jax.ShapeDtypeStruct(y_rest.shape, bf16)]
        + [jax.ShapeDtypeStruct(top.shape, f32)],
        [ANY, ANY, VMEM, ANY, VMEM],
        [ANY] * 7 + [VMEM],
        [
            pltpu.VMEM(h.shape, bf16),
            pltpu.VMEM((2,) + h.shape, bf16),
            pltpu.VMEM((4, depth, model), bf16),
        ]
        + plane_sum_scratch(3, depth, model)
        + [dma((2,)), dma((2,)), dma((4,)), dma((2,))]
        + small_scratch(top.shape),
        3 + 3 * 10 + 5,
        3,
        flops=6 * h.shape[0] * model * model,
    )(h, dg, du, hid, dy, dy_rest, y_rest, top)


def kv_sum_body(
    dkv_ref, cosine_ref, sine_ref, out_ref,
    evens, cores, far, near, sums, totals, even_sem, send, recv,
):
    slots = [dkv_ref.at[:, j] for j in range(8)]
    copies = {
        j: pltpu.make_async_copy(slots[j], evens.at[j // 2], even_sem.at[j // 2])
        for j in (6, 2, 4, 0)
    }
    for copy in copies.values():
        copy.start()
    greet((1, 2, 4), ())
    t = Transfers(send, recv)
    job = PlaneSum(t, cores.at[0], far.at[0], near.at[0], sums.at[0], totals.at[0])
    for j in (7, 3, 5, 1):
        job.send_odd(j, slots[j])
    for j in (6, 2, 4, 0):
        copies[j].wait()
        job.even(j, evens[j // 2].astype(f32))
    job.pass_on()
    total = job.close()
    cosine, sine = cosine_ref[...], -sine_ref[...]
    parts, _, width = total.shape
    for d in range(parts):
        for h in range(width // (2 * HEAD_SIZE)):
            first = 2 * h * HEAD_SIZE
            middle = first + HEAD_SIZE
            to = d * width + first
            turned = rotate(total[d, :, first:middle], cosine, sine)
            value = total[d, :, middle : middle + HEAD_SIZE]
            out_ref[:, to : to + 2 * HEAD_SIZE] = jnp.concatenate([turned, value], 1).astype(bf16)
    t.finish()


def kv_sum(dkv, cosine, sine):
    parts, _, rows, width = dkv.shape
    return remote_call(
        kv_sum_body,
        jax.ShapeDtypeStruct((rows, parts * width), bf16),
        VMEM,
        [ANY, VMEM, VMEM],
        [pltpu.VMEM((4, parts, rows, width), bf16)]
        + plane_sum_scratch(1, parts, rows, width)
        + [pltpu.SemaphoreType.DMA((4,))],
        10,
        4,
    )(dkv, cosine, sine)


def unit_grads_body(
    h_ref, dq_ref, dkv_ref, attended_ref, db_ref, gain_ref,
    query_out, key_out, value_out, output_out, gain_out,
    odd, cores, far, near, sums, totals, row_send, row_land,
    blocks, land, send, recv,
):
    me, place = lax.axis_index("ctx"), lax.axis_index("fsdp")
    depth = cores.shape[2]
    width = row_land.shape[3]
    greet((1, 2, 4), (1, 2, 3))
    t = Transfers(send, recv)
    gains = SmallReduce(t, blocks, land, jnp.add)
    blocks[0] = gain_ref[...]
    gains.on(0)
    pairs = ((attended_ref, db_ref), (h_ref, dq_ref), (h_ref, dkv_ref))
    jobs, odd_copies, over = [], {}, [None] * 3

    def columns(k, d):
        if k == 0:
            return pl.ds(pl.multiple_of(flip(place, d) * width, width), width)
        return pl.ds(d * width, width)

    def close(k):
        totals[k] = jobs[k].close()
        over[k] = []
        for d in (1, 2, 3):
            row_send[k, d - 1] = totals[k, :, columns(k, d)].astype(bf16)
            over[k].append(t.start(row_send.at[k, d - 1], row_land.at[k, d - 1], fsdp=d))

    for k in range(3):
        left, right = pairs[k]
        job = PlaneSum(t, cores.at[k], far.at[k], near.at[k], sums.at[k], totals.at[k])
        jobs.append(job)

        def partial(j):
            block = pl.ds(pl.multiple_of(flip(me, j) * depth, depth), depth)
            return lax.dot_general(
                left[:, block], right[...], OVER_ROWS, preferred_element_type=f32
            )

        for i, j in enumerate((7, 5, 3, 1)):
            if j in odd_copies:
                t.release(odd_copies[j])
            odd[j // 2] = partial(j).astype(bf16)
            odd_copies[j] = job.send_odd(j, odd.at[j // 2])
            if k == 0:
                gains.on(i + 1)
        if k:
            jobs[k - 1].pass_on()
        for j in (6, 2, 4, 0):
            job.even(j, partial(j))
        if k:
            close(k - 1)
    gains.on(5)
    gain_out[...] = blocks[5]
    jobs[2].pass_on()
    close(2)
    for k in range(3):
        total = totals[k, :, columns(k, 0)]
        for d in range(3):
            over[k][d].wait_recv()
            total = total + row_land[k, d].astype(f32)
        if k == 0:
            output_out[...] = total
        elif k == 1:
            query_out[...] = total
        else:
            for h in range(total.shape[1] // (2 * HEAD_SIZE)):
                first = 2 * h * HEAD_SIZE
                here = slice(h * HEAD_SIZE, (h + 1) * HEAD_SIZE)
                key_out[:, here] = total[:, first : first + HEAD_SIZE]
                value_out[:, here] = total[:, first + HEAD_SIZE : first + 2 * HEAD_SIZE]
    t.finish()


def unit_grads(h, dq, dkv, attended, db, gain_terms):
    rows, model = h.shape
    depth, width = model // 8, model // 4
    wide = jax.ShapeDtypeStruct((depth, width), f32)
    half = jax.ShapeDtypeStruct((depth, width // 2), f32)
    return remote_call(
        unit_grads_body,
        [wide, half, half, wide, jax.ShapeDtypeStruct(gain_terms.shape, f32)],
        [VMEM] * 5,
        [VMEM] * 6,
        [pltpu.VMEM((4, depth, model), bf16)]
        + plane_sum_scratch(3, depth, model)
        + [pltpu.VMEM((3, 3, depth, width), bf16)] * 2
        + small_scratch(gain_terms.shape),
        3 * (10 + 3) + 5,
        5,
        flops=6 * rows * model * model,
    )(h, dq, dkv, attended, db, gain_terms)


def unit_specs(depth, slots):
    def of_rest(width, first):
        return pl.BlockSpec(
            (1, slots, depth, width), lambda d, h, p: (jnp.maximum(d - 1, 0), 0, 0, first + h)
        )

    def of_own(width):
        return pl.BlockSpec(
            (slots * depth, width), lambda d, h, p: (0, jnp.where(d == 0, h, 1))
        )

    widths = ((2 * HEAD_SIZE, 0), (HEAD_SIZE, 4), (HEAD_SIZE, 6))
    return [of_own(w) for w, _ in widths] + [of_rest(w, first) for w, first in widths]


def unit_back_body(
    place_ref, dq_ref, dkv_ref, q_own, k_own, v_own, q_rest, k_rest, v_rest, out_ref
):
    d, h = pl.program_id(0), pl.program_id(1)
    grad = jnp.concatenate([dq_ref[...], dkv_ref[...]], 1)

    @pl.when((d == 0) & (h == 0))
    def _():
        out_ref[...] = jnp.zeros_like(out_ref)

    @pl.when(d == 0)
    def _():
        weight = jnp.concatenate([q_own[...], k_own[...], v_own[...]], 1)
        out_ref[...] += lax.dot_general(grad, weight, OVER_COLUMNS, preferred_element_type=f32)

    @pl.when(d > 0)
    def _():
        slots, depth = q_rest.shape[1], q_rest.shape[2]
        for j in range(slots):
            owner = place_ref[0] ^ j
            cols = pl.ds(pl.multiple_of(owner * depth, depth), depth)
            weight = jnp.concatenate([q_rest[0, j], k_rest[0, j], v_rest[0, j]], 1)
            out_ref[:, cols] += lax.dot_general(
                grad, weight, OVER_COLUMNS, preferred_element_type=f32
            )


def unit_back(places, dq, dkv, query, key, value, rest):
    rows = dq.shape[0]
    heads = query.shape[1] // (REPEAT * HEAD_SIZE)
    _, slots, depth, _ = rest.shape
    model = slots * depth
    pair = pl.BlockSpec((rows, 2 * HEAD_SIZE), lambda d, h, p: (0, d * heads + h))
    return pl.pallas_call(
        unit_back_body,
        out_shape=jax.ShapeDtypeStruct((rows, model), f32),
        grid_spec=pltpu.PrefetchScalarGridSpec(
            num_scalar_prefetch=1,
            grid=(4, heads),
            in_specs=[pair, pair] + unit_specs(depth, slots),
            out_specs=pl.BlockSpec((rows, model), lambda d, h, p: (0, 0)),
        ),
        **params(8 * rows * model * heads * UNIT, 8 * model * heads * UNIT),
    )(places, dq, dkv, query, key, value, rest, rest, rest)


def output_specs(own, rest):
    _, slots, depth, width = rest.shape
    return [
        pl.BlockSpec(own.shape, lambda d, p: (0, 0)),
        pl.BlockSpec((1, slots, depth, width), lambda d, p: (jnp.maximum(d - 1, 0), 0, 0, 0)),
    ]


def output_back_body(place_ref, db_ref, own_ref, rest_ref, out_ref, total):
    d = pl.program_id(0)
    db = db_ref[...]

    @pl.when(d == 0)
    def _():
        total[...] = lax.dot_general(db, own_ref[...], OVER_COLUMNS, preferred_element_type=f32)

    @pl.when(d > 0)
    def _():
        slots, depth = rest_ref.shape[1], rest_ref.shape[2]
        for j in range(slots):
            owner = place_ref[0] ^ j
            cols = pl.ds(pl.multiple_of(owner * depth, depth), depth)
            total[:, cols] += lax.dot_general(
                db, rest_ref[0, j], OVER_COLUMNS, preferred_element_type=f32
            )

    @pl.when(d == pl.num_programs(0) - 1)
    def _():
        out_ref[...] = total[...].astype(bf16)


def output_back(places, db, own, rest):
    rows, model = db.shape
    height, width = own.shape
    return pl.pallas_call(
        output_back_body,
        out_shape=jax.ShapeDtypeStruct((rows, height), bf16),
        grid_spec=pltpu.PrefetchScalarGridSpec(
            num_scalar_prefetch=1,
            grid=(4,),
            in_specs=[pl.BlockSpec((rows, width), lambda d, p: (0, p[1] ^ d))]
            + output_specs(own, rest),
            out_specs=pl.BlockSpec((rows, height), lambda d, p: (0, 0)),
            scratch_shapes=[pltpu.VMEM((rows, height), f32)],
        ),
        **params(2 * rows * model * height, 2 * model * height),
    )(places, db, own, rest)


def token_layout(length_row, block_slots, block_size):
    count_blocks = block_slots.shape[0]
    owner_block = jnp.argmax(
        block_slots[None, :] == jnp.arange(count_blocks, dtype=jnp.int32)[:, None], 1
    ).astype(jnp.int32)
    row_index = jnp.arange(count_blocks * block_size, dtype=jnp.int32)
    plain_order = jnp.repeat(owner_block, block_size) * block_size + row_index % block_size
    seq_ends = jnp.cumsum(length_row)
    seq_starts = seq_ends - length_row
    document_list = jnp.sum((plain_order[:, None] >= seq_ends[None, :]).astype(jnp.int32), 1)
    matches = document_list[:, None] == jnp.arange(length_row.shape[0], dtype=jnp.int32)[None, :]
    begins = jnp.sum(jnp.where(matches, seq_starts[None, :], 0), 1)
    return plain_order, begins


def rms_scale(value):
    return lax.rsqrt(jnp.mean(value * value, -1, keepdims=True) + epsilon)


def norm_back(grad_unit, unit_rows, scale_rows):
    return scale_rows * (grad_unit - unit_rows * jnp.mean(grad_unit * unit_rows, -1, keepdims=True))


def product(left, right):
    return jnp.dot(left, right, preferred_element_type=f32)


def product_t(left, right):
    return lax.dot_general(left, right, (((1,), (1,)), ((), ())), preferred_element_type=f32)


def over_rows(left, right):
    return lax.dot_general(left, right, (((0,), (0,)), ((), ())), preferred_element_type=f32)


def column_blocks(value, count, places):
    width = value.shape[1] // count
    return jnp.concatenate(
        [lax.dynamic_slice_in_dim(value, place * width, width, 1) for place in places], 1
    )


def gather_rows(piece, fsdp_place, ctx_count):
    count = lax.axis_size("fsdp")
    parts = [piece] + [swap(piece, "fsdp", d) for d in range(1, count)]
    return jnp.concatenate(by_place(parts, fsdp_place), 1)


def weight_grad_sum(left, right, me, count):
    depth = left.shape[1] // count
    full = over_rows(column_blocks(left, count, [me ^ j for j in range(count)]), right)
    return sum_halving(full.astype(bf16).reshape(count, depth, right.shape[1]), "ctx")


def down_grad_sum(hidden, grad, me, count, fsdp_count):
    bands = count // fsdp_count
    band, column = me // fsdp_count, me % fsdp_count
    depth = hidden.shape[1] // bands
    width = grad.shape[1] // fsdp_count
    left = column_blocks(hidden, bands, [band ^ j for j in range(bands)])
    right = column_blocks(grad, fsdp_count, [column ^ j for j in range(fsdp_count)])
    full = over_rows(left, right).astype(bf16).reshape(bands, depth, fsdp_count, width)
    return sum_halving(full.transpose(0, 2, 1, 3).reshape(count, depth, width), "ctx")


def clipped(weight, multiplier):
    columns = weight.shape[1]
    head_index = (
        lax.axis_index("fsdp") * columns + jnp.arange(columns, dtype=jnp.int32)
    ) // HEAD_SIZE
    matches = head_index[:, None] == jnp.arange(multiplier.shape[0], dtype=jnp.int32)[None, :]
    column_factor = jnp.sum(jnp.where(matches, multiplier[None, :], 0.0), 1)
    return (weight.astype(f32) * column_factor[None, :]).astype(bf16)


def gain_sum(term, me, place, count, fsdp_count):
    table = term.reshape(count, fsdp_count, -1)
    table = jnp.stack(by_place([table[i] for i in range(count)], me))
    mine = sum_halving(table, "ctx")
    mine = jnp.stack(by_place([mine[i] for i in range(fsdp_count)], place))
    return sum_halving(mine, "fsdp")


def attention_layout(seq_lengths, block_perm, rows):
    count, me = lax.axis_size("ctx"), lax.axis_index("ctx")
    rounds = block_perm.shape[0] // count
    blk = rows // rounds
    plain_order, begins = token_layout(seq_lengths[0], block_perm, blk)
    natural = lax.dynamic_slice_in_dim(plain_order, me * rows, rows)
    begin = lax.dynamic_slice_in_dim(begins, me * rows, rows)
    half_dim = HEAD_SIZE // 2
    exponent = jnp.arange(half_dim, dtype=f32) * (2.0 / HEAD_SIZE)
    inverse = rope_base ** (-exponent)
    angles = (natural - begin).astype(f32)[:, None] * inverse[None, :]
    cosine = jnp.concatenate([jnp.cos(angles)] * 2, 1)
    sine = jnp.concatenate([-jnp.sin(angles), jnp.sin(angles)], 1)
    order = plain_order.reshape(count, rounds, blk)
    order = jnp.stack(by_place([order[i] for i in range(count)], me), 1)
    return natural[:, None], begin[:, None], order.reshape(rounds, 1, count * blk), cosine, sine


def on_device(
    hidden_in,
    out_grad,
    seq_lengths,
    block_perm,
    first_gain,
    query_weight,
    key_matrix,
    value_matrix,
    output_weight,
    second_gain,
    gate_weight,
    up_weight,
    down_weight,
    clip_limit,
):
    rows, model = hidden_in.shape[1], hidden_in.shape[2]
    count, fsdp_count = lax.axis_size("ctx"), lax.axis_size("fsdp")
    me, place = lax.axis_index("ctx"), lax.axis_index("fsdp")
    me_ref = me.astype(jnp.int32).reshape(1)
    depth = model // count
    zero = jnp.zeros((1,), jnp.int32)
    shard_heads = KEY_VALUE_HEADS // fsdp_count

    def own_rows(weight):
        return lax.dynamic_slice_in_dim(weight, me * depth, depth, 0)

    unit_rows = jnp.concatenate(
        [
            own_rows(query_weight).reshape(depth, shard_heads, REPEAT, HEAD_SIZE),
            own_rows(key_matrix).reshape(depth, shard_heads, 1, HEAD_SIZE),
            own_rows(value_matrix).reshape(depth, shard_heads, 1, HEAD_SIZE),
        ],
        2,
    ).reshape(depth, shard_heads * UNIT)
    unit_rows = gather_rows(unit_rows, place, count)
    unit_slots = gather_ctx(unit_rows)
    gains = jnp.stack([first_gain, second_gain])
    gains = jnp.concatenate(
        by_place([gains] + [swap(gains, "fsdp", d) for d in range(1, fsdp_count)], place), 1
    ).astype(f32)
    first_full, second_full = gains[0], gains[1]
    output_rows = gather_rows(own_rows(output_weight), place, count)
    output_slots = gather_ctx(output_rows)

    hidden_width = gate_weight.shape[1]
    down_depth = hidden_width // count

    def down_piece(d):
        first = (place ^ d) * hidden_width + me * down_depth
        return lax.dynamic_slice_in_dim(down_weight, first, down_depth, 0)

    down_rows = [down_piece(0)] + [
        swap(down_piece(d), "fsdp", d) for d in range(1, fsdp_count)
    ]
    down_slots = gather_ctx(jnp.concatenate(by_place(down_rows, place), 1))

    natural_column, begin_column, key_natural, cosine, sine = attention_layout(
        seq_lengths, block_perm, rows
    )
    half_dim = HEAD_SIZE // 2

    tokens = hidden_in.reshape(rows, model).astype(f32)
    scale_one = rms_scale(tokens)
    unit_one = tokens * scale_one
    normalized = (unit_one * first_full).astype(bf16)
    qkv = slot_matmul(normalized, unit_slots, me_ref, UNIT, bf16, (cosine, sine))
    kv_local = qkv.reshape(rows, KEY_VALUE_HEADS, UNIT)[:, :, REPEAT * HEAD_SIZE :].reshape(
        rows, KEY_VALUE_HEADS * 2 * HEAD_SIZE
    )
    kv_slots = gather_ctx(kv_local)
    attended, best = attend(zero, natural_column, begin_column, key_natural, qkv, kv_slots)
    head_max = jnp.max(best[:, :, :REPEAT, 0], 0).reshape(QUERY_HEADS)
    for mask in bits_down(count):
        head_max = jnp.maximum(head_max, swap(head_max, "ctx", mask))
    for mask in bits_down(fsdp_count):
        head_max = jnp.maximum(head_max, swap(head_max, "fsdp", mask))
    residual = tokens + slot_matmul(attended, output_slots, me_ref, 512, f32)
    scale_two = rms_scale(residual)
    unit_two = residual * scale_two
    normed_two = (unit_two * second_full).astype(bf16)

    grad_out = out_grad.reshape(rows, model)
    others = range(1, fsdp_count)
    grads = [grad_out] + [swap(grad_out, "fsdp", d) for d in others]
    normed = [normed_two] + [swap(normed_two, "fsdp", d) for d in others]
    hidden_parts, gate_parts, up_parts, sums, backs = [], [], [], [], []
    for d in range(fsdp_count):
        grad_hidden = slot_matmul_t(grads[d], down_slots, me_ref, 512, f32)
        gate_act = product(normed[d], gate_weight)
        up_proj = product(normed[d], up_weight)
        sigmoid = jax.nn.sigmoid(gate_act)
        hidden = (gate_act * sigmoid * up_proj).astype(bf16)
        grad_gate = (
            grad_hidden * up_proj * sigmoid * (1.0 + gate_act * (1.0 - sigmoid))
        ).astype(bf16)
        grad_up = (grad_hidden * gate_act * sigmoid).astype(bf16)
        hidden_parts.append(hidden)
        gate_parts.append(grad_gate)
        up_parts.append(grad_up)
        backs.append(product_t(grad_gate, gate_weight) + product_t(grad_up, up_weight))
        sums.append(slot_matmul(hidden, down_slots, me_ref, 512, f32 if d == 0 else bf16))
    grad_normed_two = sum_fsdp(backs)
    result = (residual + sum_fsdp(sums)).astype(bf16)

    second_term = jnp.sum(grad_normed_two * unit_two, 0)
    grad_residual = grad_out.astype(f32) + norm_back(
        grad_normed_two * second_full, unit_two, scale_two
    )
    grad_branch = grad_residual.astype(bf16)
    head_grad = slot_matmul_t(grad_branch, output_slots, me_ref, 512, bf16)
    query_grad, *dkv_slots = attend_back(
        zero, natural_column, begin_column, key_natural, cosine, sine, qkv, head_grad, kv_slots
    )
    dkv = sum_halving(dkv_slots[0], "ctx")
    dkv = dkv.reshape(rows, KEY_VALUE_HEADS, 2, HEAD_SIZE)
    grad_key = dkv[:, :, 0]
    first, second = grad_key[..., :half_dim], grad_key[..., half_dim:]
    cos, sin = cosine[:, None, :half_dim], sine[:, None, half_dim:]
    grad_key = jnp.concatenate([first * cos + second * sin, second * cos - first * sin], -1)
    dqkv = jnp.concatenate(
        [
            query_grad.reshape(rows, KEY_VALUE_HEADS, REPEAT, HEAD_SIZE),
            grad_key[:, :, None].astype(bf16),
            dkv[:, :, 1:].astype(bf16),
        ],
        2,
    ).reshape(rows, KEY_VALUE_HEADS * UNIT)
    grad_normed_one = slot_matmul_t(dqkv, unit_slots, me_ref, 512, f32)
    first_term = jnp.sum(grad_normed_one * unit_one, 0)
    grad_input = grad_residual + norm_back(grad_normed_one * first_full, unit_one, scale_one)

    hidden_all = jnp.concatenate(hidden_parts, 0)
    normed_all = jnp.concatenate(normed, 0)
    grads_all = jnp.concatenate(grads, 0)
    down_sum = down_grad_sum(hidden_all, grads_all, me, count, fsdp_count).astype(bf16)
    bands = count // fsdp_count
    places = [
        (c * fsdp_count + f, (bands * f + c // fsdp_count) * fsdp_count + c % fsdp_count)
        for c in range(count)
        for f in range(fsdp_count)
    ]
    down_grad = lax.ppermute(down_sum, ("ctx", "fsdp"), places).astype(f32)
    gate_grad = weight_grad_sum(normed_all, jnp.concatenate(gate_parts, 0), me, count)
    up_grad = weight_grad_sum(normed_all, jnp.concatenate(up_parts, 0), me, count)

    def over_fsdp(summed):
        width = summed.shape[1] // fsdp_count
        return sum_fsdp(
            [
                lax.dynamic_slice_in_dim(summed, (place ^ d) * width, width, 1)
                for d in range(fsdp_count)
            ]
        )

    output_grad = over_fsdp(weight_grad_sum(attended, grad_branch, me, count))
    unit_grad = over_fsdp(weight_grad_sum(normalized, dqkv, me, count))
    unit_grad = unit_grad.reshape(depth, shard_heads, REPEAT + 2, HEAD_SIZE)
    query_out = unit_grad[:, :, :REPEAT].reshape(depth, -1)
    key_out = unit_grad[:, :, REPEAT].reshape(depth, -1)
    value_out = unit_grad[:, :, REPEAT + 1].reshape(depth, -1)

    first_out = gain_sum(first_term, me, place, count, fsdp_count)
    second_out = gain_sum(second_term, me, place, count, fsdp_count)
    multiplier = jnp.sqrt(clip_limit / jnp.maximum(head_max, clip_limit))
    key_ratio = jnp.min(multiplier.reshape(KEY_VALUE_HEADS, REPEAT), 1)
    return (
        result.reshape(1, rows, model),
        grad_input.astype(bf16).reshape(1, rows, model),
        first_out,
        query_out,
        key_out,
        value_out,
        output_grad,
        second_out,
        gate_grad,
        up_grad,
        down_grad,
        head_max,
        clipped(query_weight, multiplier),
        clipped(key_matrix, key_ratio),
    )


def on_row_of_chips(
    hidden_in,
    out_grad,
    seq_lengths,
    block_perm,
    first_gain,
    query_weight,
    key_matrix,
    value_matrix,
    output_weight,
    second_gain,
    gate_weight,
    up_weight,
    down_weight,
    clip_limit,
):
    rows, model = hidden_in.shape[1], hidden_in.shape[2]
    me, place = lax.axis_index("ctx"), lax.axis_index("fsdp")
    places = jnp.stack([me, place]).astype(jnp.int32)
    place_one = places[1:]
    natural, begin, key_natural, cosine, sine = attention_layout(seq_lengths, block_perm, rows)
    tokens_low = hidden_in.reshape(rows, model)
    grad_out = out_grad.reshape(rows, model)
    gains = jnp.pad(jnp.stack([first_gain, second_gain]).astype(f32), ((0, 6), (0, 0)))
    (
        normalized,
        qkv,
        attended,
        best,
        residual,
        normed_two,
        all_gains,
        kv_all,
        unit_rest,
        output_rest,
        down_rest,
        dy_rest,
    ) = attention_row(
        tokens_low,
        gains,
        cosine,
        sine,
        natural,
        begin,
        key_natural,
        query_weight,
        key_matrix,
        value_matrix,
        output_weight,
        down_weight,
        grad_out,
    )
    full = jnp.concatenate(by_place([all_gains[d] for d in range(4)], place), 1)
    first_full, second_full = full[0], full[1]
    tokens = tokens_low.astype(f32)
    scale_one = rms_scale(tokens)
    unit_one = tokens * scale_one
    scale_two = rms_scale(residual)
    unit_two = residual * scale_two
    top = jnp.max(best[:, :, :REPEAT, 0], 0)
    top = jnp.pad(top, ((0, 0), (0, 128 - REPEAT)))

    hid, dg, du, h_all, y_own, y_rest, grad_normed_two = feed_forward_row(
        normed_two, grad_out, dy_rest, gate_weight, up_weight, down_weight, down_rest
    )
    second_term = jnp.sum(grad_normed_two * unit_two, 0)
    grad_residual = grad_out.astype(f32) + norm_back(
        grad_normed_two * second_full, unit_two, scale_two
    )
    grad_branch = grad_residual.astype(bf16)
    gate_grad, up_grad, down_sum, y_land, top = grads_row(
        h_all, dg, du, hid, grad_out, dy_rest, y_rest, top
    )
    head_max = top[:, :REPEAT].reshape(QUERY_HEADS)
    result = (residual + y_own + jnp.sum(y_land.astype(f32), 0)).astype(bf16)
    width = model // 4
    moved, pieces = [], []
    for k in range(4):
        piece = lax.dynamic_slice_in_dim(down_sum, ((me % 4) ^ k) * width, width, 1)
        pieces.append(piece)
    (normalized, attended), pieces = lax.optimization_barrier(((normalized, attended), pieces))
    for k, piece in enumerate(pieces):
        pairs = [
            (c * 4 + f, (2 * f + c // 4) * 4 + (c % 4 ^ k)) for c in range(8) for f in range(4)
        ]
        moved.append(lax.ppermute(piece, ("ctx", "fsdp"), pairs))
    down_grad = jnp.concatenate(by_place(moved, place), 0).astype(f32)

    head_grad = output_back(places, grad_branch, output_weight, output_rest)
    query_grad, dkv = attend_back(
        place_one, natural, begin, key_natural, cosine, sine, qkv, head_grad, [kv_all]
    )
    dkv = kv_sum(dkv, cosine, sine)
    grad_normed_one = unit_back(
        places, query_grad, dkv, query_weight, key_matrix, value_matrix, unit_rest
    )
    first_term = jnp.sum(grad_normed_one * unit_one, 0)
    grad_input = grad_residual + norm_back(grad_normed_one * first_full, unit_one, scale_one)
    terms = jnp.concatenate([first_term, second_term]).reshape(-1, 128)
    query_out, key_out, value_out, output_out, terms = unit_grads(
        normalized, query_grad, dkv, attended, grad_branch, terms
    )
    terms = lax.dynamic_slice_in_dim(
        terms.reshape(2, -1), (me * 4 + place) * (model // 32), model // 32, 1
    )
    first_out, second_out = terms[0], terms[1]
    multiplier = jnp.sqrt(clip_limit / jnp.maximum(head_max, clip_limit))
    key_ratio = jnp.min(multiplier.reshape(KEY_VALUE_HEADS, REPEAT), 1)
    return (
        result.reshape(1, rows, model),
        grad_input.astype(bf16).reshape(1, rows, model),
        first_out,
        query_out,
        key_out,
        value_out,
        output_out,
        second_out,
        gate_grad,
        up_grad,
        down_grad,
        head_max,
        clipped(query_weight, multiplier),
        clipped(key_matrix, key_ratio),
    )


def solution(mesh):
    shard, whole = P(None, "fsdp"), P()
    token, block = P("fsdp", "ctx", None), P("ctx", "fsdp")
    gain = P(("ctx", "fsdp"))
    chips = mesh.shape["ctx"] == 8 and mesh.shape["fsdp"] == 4
    return jax.shard_map(
        on_row_of_chips if chips else on_device,
        mesh=mesh,
        in_specs=(token, token, P("fsdp", None), whole, P("fsdp"))
        + (shard,) * 4
        + (P("fsdp"),)
        + (shard,) * 3
        + (whole,),
        out_specs=(token, token, gain)
        + (block,) * 4
        + (gain,)
        + (block,) * 3
        + (whole, shard, shard),
        check_vma=False,
    )
```

```python
import functools
import math

import jax
import jax.numpy as jnp
from jax import lax
from jax.experimental import pallas as pl
from jax.experimental.pallas import tpu as pltpu
from jax.sharding import PartitionSpec as P

QUERY_HEADS = 16
KEY_VALUE_HEADS = 8
HEAD_SIZE = 128
REPEAT = QUERY_HEADS // KEY_VALUE_HEADS
UNIT = (REPEAT + 2) * HEAD_SIZE

epsilon = 1e-06
rope_base = 1000000.0
hidden_fill_value = -1e30
bf16 = jnp.bfloat16
f32 = jnp.float32
SCALE = 1.0 / math.sqrt(HEAD_SIZE)


def swap(value, axis, mask):
    size = lax.axis_size(axis)
    return lax.ppermute(value, axis, [(i, i ^ mask) for i in range(size)])


def bits_down(size):
    mask = size // 2
    while mask:
        yield mask
        mask //= 2


def by_place(items, me):
    mask = 1
    while mask < len(items):
        odd = (me & mask) != 0
        items = [jnp.where(odd, items[j ^ mask], items[j]) for j in range(len(items))]
        mask *= 2
    return items


def gather_ctx(block):
    size = lax.axis_size("ctx")
    whole = block[None]
    mask = 1
    while mask < size:
        whole = jnp.concatenate([whole, swap(whole, "ctx", mask)], 0)
        mask *= 2
    return [whole]


def sum_halving(slots, axis):
    for mask in bits_down(slots.shape[0]):
        keep = slots[:mask].astype(f32)
        slots = (keep + swap(slots[mask:], axis, mask).astype(f32)).astype(slots.dtype)
    return slots[0].astype(f32)


def sum_fsdp(pieces):
    total = pieces[0].astype(f32)
    for d in range(1, len(pieces)):
        total = total + swap(pieces[d].astype(bf16), "fsdp", d).astype(f32)
    return total


def params(flops, bytes_accessed):
    return dict(
        compiler_params=pltpu.CompilerParams(vmem_limit_bytes=48 * 2**20),
        cost_estimate=pl.CostEstimate(
            flops=flops, bytes_accessed=bytes_accessed, transcendentals=0
        ),
    )


def rotate(value, cosine, sine):
    return value * cosine + pltpu.roll(value, HEAD_SIZE // 2, 1) * sine


def slot_matmul_body(n_slots, parts, depth, rope, me_ref, x_ref, *refs):
    slot_refs = refs[:n_slots]
    out_ref = refs[-1]
    total = None
    for j in range(n_slots):
        for q in range(parts):
            owner = me_ref[0] ^ (j * parts + q)
            cols = pl.ds(pl.multiple_of(owner * depth, depth), depth)
            term = jnp.dot(x_ref[:, cols], slot_refs[j][q], preferred_element_type=f32)
            total = term if total is None else total + term
    if rope:
        cosine, sine = refs[n_slots][...], refs[n_slots + 1][...]
        parts_out = [
            rotate(total[:, i * HEAD_SIZE : (i + 1) * HEAD_SIZE], cosine, sine)
            for i in range(REPEAT + 1)
        ]
        total = jnp.concatenate(parts_out + [total[:, (REPEAT + 1) * HEAD_SIZE :]], 1)
    out_ref[...] = total.astype(out_ref.dtype)


def in_order(slots, me):
    whole = jnp.concatenate(slots, 0)
    whole = whole[me ^ jnp.arange(whole.shape[0], dtype=jnp.int32)]
    return whole.reshape(-1, whole.shape[2])


def in_order(slots, me):
    whole = jnp.concatenate(slots, 0)
    whole = whole[me ^ jnp.arange(whole.shape[0], dtype=jnp.int32)]
    return whole.reshape(-1, whole.shape[2])


def slot_matmul(x, slots, me, tile, out_dtype, tables=None):
    rows = x.shape[0]
    parts, depth, width = slots[0].shape
    if depth % 128:
        total = product(x, in_order(slots, me))
        if tables is None:
            return total.astype(out_dtype)
        total = total.reshape(rows, width // UNIT, REPEAT + 2, HEAD_SIZE)
        cosine, sine = (t[:, None, None] for t in tables)
        turned = total[:, :, : REPEAT + 1]
        turned = turned * cosine + jnp.roll(turned, HEAD_SIZE // 2, -1) * sine
        total = jnp.concatenate([turned, total[:, :, REPEAT + 1 :]], 2)
        return total.reshape(rows, width).astype(out_dtype)
    extra = [] if tables is None else list(tables)
    body = functools.partial(
        slot_matmul_body, len(slots), parts, depth, tables is not None
    )
    return pl.pallas_call(
        body,
        out_shape=jax.ShapeDtypeStruct((rows, width), out_dtype),
        grid_spec=pltpu.PrefetchScalarGridSpec(
            num_scalar_prefetch=1,
            grid=(width // tile,),
            in_specs=[pl.BlockSpec(x.shape, lambda i, me: (0, 0))]
            + [pl.BlockSpec((parts, depth, tile), lambda i, me: (0, 0, i))] * len(slots)
            + [pl.BlockSpec(e.shape, lambda i, me: (0, 0)) for e in extra],
            out_specs=pl.BlockSpec((rows, tile), lambda i, me: (0, i)),
        ),
        **params(2 * rows * x.shape[1] * width, 2 * x.shape[1] * width),
    )(me, x, *slots, *extra)


def slot_matmul_t_body(n_slots, parts, depth, me_ref, x_ref, *refs):
    slot_refs = refs[:n_slots]
    out_ref, total_ref = refs[n_slots], refs[n_slots + 1]
    step = pl.program_id(0)

    @pl.when(step == 0)
    def _():
        total_ref[...] = jnp.zeros_like(total_ref)

    x = x_ref[...]
    for j in range(n_slots):
        for q in range(parts):
            owner = me_ref[0] ^ (j * parts + q)
            cols = pl.ds(pl.multiple_of(owner * depth, depth), depth)
            total_ref[:, cols] += lax.dot_general(
                x, slot_refs[j][q], (((1,), (1,)), ((), ())), preferred_element_type=f32
            )

    @pl.when(step == pl.num_programs(0) - 1)
    def _():
        out_ref[...] = total_ref[...].astype(out_ref.dtype)


def slot_matmul_t(x, slots, me, tile, out_dtype):
    rows, width = x.shape
    parts, depth, _ = slots[0].shape
    height = parts * depth * len(slots)
    if depth % 128:
        return product_t(x, in_order(slots, me)).astype(out_dtype)
    return pl.pallas_call(
        functools.partial(slot_matmul_t_body, len(slots), parts, depth),
        out_shape=jax.ShapeDtypeStruct((rows, height), out_dtype),
        grid_spec=pltpu.PrefetchScalarGridSpec(
            num_scalar_prefetch=1,
            grid=(width // tile,),
            in_specs=[pl.BlockSpec((rows, tile), lambda i, me: (0, i))]
            + [pl.BlockSpec((parts, depth, tile), lambda i, me: (0, 0, i))]
            * len(slots),
            out_specs=pl.BlockSpec((rows, height), lambda i, me: (0, 0)),
            scratch_shapes=[pltpu.VMEM((rows, height), f32)],
        ),
        **params(2 * rows * height * width, 2 * height * width),
    )(me, x, *slots)


def keys_of(slot_refs):
    def column(i):
        parts = [
            r[..., i * HEAD_SIZE : (i + 1) * HEAD_SIZE].reshape(-1, HEAD_SIZE)
            for r in slot_refs
        ]
        return parts[0] if len(parts) == 1 else jnp.concatenate(parts, 0)

    return column(0), column(1)


def scores_of(qkv_ref, keys, natural_ref, start_ref, key_natural_ref):
    blk = qkv_ref.shape[0]
    query = jnp.concatenate(
        [qkv_ref[:, i * HEAD_SIZE : (i + 1) * HEAD_SIZE] for i in range(REPEAT)], 0
    )
    scores = (
        lax.dot_general(
            query, keys, (((1,), (1,)), ((), ())), preferred_element_type=f32
        )
        * SCALE
    )
    key_natural = key_natural_ref[0]
    allowed = (key_natural >= start_ref[...]) & (key_natural <= natural_ref[...])
    allowed = jnp.concatenate([allowed] * REPEAT, 0)
    scores = jnp.where(allowed, scores, hidden_fill_value)
    best = jnp.max(scores, 1, keepdims=True)
    exps = jnp.exp(scores - best)
    return query, exps * (1.0 / jnp.sum(exps, 1, keepdims=True)), best, blk


def attend_body(n_slots, place_ref, natural_ref, start_ref, key_natural_ref, qkv_ref, *refs):
    slot_refs, (out_ref, best_ref) = refs[:n_slots], refs[n_slots:]
    keys, values = keys_of(slot_refs)
    _, probs, best, blk = scores_of(qkv_ref, keys, natural_ref, start_ref, key_natural_ref)
    heads = jnp.dot(probs.astype(bf16), values, preferred_element_type=f32)
    out_ref[...] = jnp.concatenate(
        [heads[i * blk : (i + 1) * blk] for i in range(REPEAT)], 1
    ).astype(bf16)
    tops = [
        jnp.broadcast_to(jnp.max(best[i * blk : (i + 1) * blk], 0, keepdims=True), (1, 128))
        for i in range(REPEAT)
    ]
    best_ref[0, 0] = jnp.concatenate(tops + [jnp.zeros((8 - REPEAT, 128), f32)], 0)


def attend_back_body(
    n_slots, place_ref, natural_ref, start_ref, key_natural_ref, cosine_ref, sine_ref, qkv_ref, grad_ref, *refs
):
    slot_refs, (dq_ref, *dkv_refs) = refs[:n_slots], refs[n_slots:]
    keys, values = keys_of(slot_refs)
    query, probs, _, blk = scores_of(qkv_ref, keys, natural_ref, start_ref, key_natural_ref)
    grad = jnp.concatenate(
        [grad_ref[:, i * HEAD_SIZE : (i + 1) * HEAD_SIZE] for i in range(REPEAT)], 0
    )
    low = probs.astype(bf16)
    grad_probs = lax.dot_general(
        grad, values, (((1,), (1,)), ((), ())), preferred_element_type=f32
    )
    delta = jnp.sum(low.astype(f32) * grad_probs, 1, keepdims=True)
    score_grad = (probs * (grad_probs - delta)).astype(bf16)
    query_grad = jnp.dot(score_grad, keys, preferred_element_type=f32) * SCALE
    cosine, sine = cosine_ref[...], sine_ref[...]
    dq_ref[...] = jnp.concatenate(
        [
            rotate(query_grad[i * blk : (i + 1) * blk], cosine, -sine)
            for i in range(REPEAT)
        ],
        1,
    ).astype(bf16)
    over_rows = (((0,), (0,)), ((), ()))
    key_grad = (
        lax.dot_general(score_grad, query, over_rows, preferred_element_type=f32) * SCALE
    ).astype(bf16)
    value_grad = lax.dot_general(low, grad, over_rows, preferred_element_type=f32).astype(
        bf16
    )
    both = jnp.concatenate([key_grad, value_grad], 1)
    first = 0
    for ref in dkv_refs:
        rows = math.prod(ref.shape[:-1])
        ref[...] = both[first : first + rows].reshape(ref.shape)
        first += rows


def attention_specs(slots, blk, keys, shard_heads):
    def own_place(r, h, place):
        return (r, (place[0] ^ (h // shard_heads)) * shard_heads + h % shard_heads)

    column = pl.BlockSpec((blk, 1), lambda r, h, p: (r, 0))
    return (
        [column, column, pl.BlockSpec((1, 1, keys), lambda r, h, p: (r, 0, 0))],
        pl.BlockSpec((blk, UNIT), lambda r, h, p: (r, h)),
        pl.BlockSpec((blk, REPEAT * HEAD_SIZE), lambda r, h, p: (r, h)),
        pl.BlockSpec((blk, REPEAT * HEAD_SIZE), own_place),
        pl.BlockSpec((1, 1, 8, 128), lambda r, h, p: own_place(r, h, p) + (0, 0)),
        [
            pl.BlockSpec((s.shape[0], blk, 2 * HEAD_SIZE), lambda r, h, p: (0, r, h))
            if s.ndim == 3
            else pl.BlockSpec(
                (1, s.shape[1], blk, 2 * HEAD_SIZE),
                lambda r, h, p: (h // shard_heads, 0, r, h % shard_heads),
            )
            for s in slots
        ],
    )


def attend(place, natural, start, key_natural, qkv, slots):
    rows, heads = qkv.shape[0], qkv.shape[1] // UNIT
    rounds, _, keys = key_natural.shape
    blk = rows // rounds
    meta, unit, _, placed, best, slot = attention_specs(
        slots, blk, keys, heads // lax.axis_size("fsdp")
    )
    return pl.pallas_call(
        functools.partial(attend_body, len(slots)),
        out_shape=[
            jax.ShapeDtypeStruct((rows, heads * REPEAT * HEAD_SIZE), bf16),
            jax.ShapeDtypeStruct((rounds, heads, 8, 128), f32),
        ],
        grid_spec=pltpu.PrefetchScalarGridSpec(
            num_scalar_prefetch=1,
            grid=(rounds, heads),
            in_specs=meta + [unit] + slot,
            out_specs=[placed, best],
        ),
        **params(4 * rows * keys * heads * REPEAT * HEAD_SIZE, 12 * 2**20),
    )(place, natural, start, key_natural, qkv, *slots)


def attend_back(place, natural, start, key_natural, cosine, sine, qkv, grad, slots):
    rows, heads = qkv.shape[0], qkv.shape[1] // UNIT
    rounds, _, keys = key_natural.shape
    blk = rows // rounds
    meta, unit, pair, placed, _, slot = attention_specs(
        slots, blk, keys, heads // lax.axis_size("fsdp")
    )
    table = pl.BlockSpec((blk, HEAD_SIZE), lambda r, h, p: (r, 0))
    return pl.pallas_call(
        functools.partial(attend_back_body, len(slots)),
        out_shape=[jax.ShapeDtypeStruct((rows, heads * REPEAT * HEAD_SIZE), bf16)]
        + [jax.ShapeDtypeStruct(s.shape, bf16) for s in slots],
        grid_spec=pltpu.PrefetchScalarGridSpec(
            num_scalar_prefetch=1,
            grid=(rounds, heads),
            in_specs=meta + [table, table, unit, placed] + slot,
            out_specs=[pair] + slot,
        ),
        **params(10 * rows * keys * heads * REPEAT * HEAD_SIZE, 20 * 2**20),
    )(place, natural, start, key_natural, cosine, sine, qkv, grad, *slots)


ANY = pl.BlockSpec(memory_space=pl.ANY)
VMEM = pl.BlockSpec(memory_space=pltpu.VMEM)
MESH = pl.DeviceIdType.MESH
OVER_ROWS = (((0,), (0,)), ((), ()))
OVER_COLUMNS = (((1,), (1,)), ((), ()))


def flip(place, mask):
    for bit in (1, 2, 4):
        if mask & bit:
            place = place + bit - 2 * bit * lax.rem(lax.div(place, bit), 2)
    return place


def device(ctx, fsdp):
    return {
        "ctx": flip(lax.axis_index("ctx"), ctx),
        "fsdp": flip(lax.axis_index("fsdp"), fsdp),
    }


def greet(ctx_masks, fsdp_masks):
    barrier = pltpu.get_barrier_semaphore()
    partners = [(m, 0) for m in ctx_masks] + [(0, m) for m in fsdp_masks]
    for ctx, fsdp in partners:
        pl.semaphore_signal(barrier, inc=1, device_id=device(ctx, fsdp), device_id_type=MESH)
    pl.semaphore_wait(barrier, len(partners))


class Transfers:
    def __init__(self, send, recv):
        self.send, self.recv, self.count, self.open = send, recv, 0, {}

    def start(self, src, dst, ctx=0, fsdp=0):
        number = self.count
        copy = pltpu.make_async_remote_copy(
            src_ref=src,
            dst_ref=dst,
            send_sem=self.send.at[number],
            recv_sem=self.recv.at[number],
            device_id=device(ctx, fsdp),
            device_id_type=MESH,
        )
        copy.start()
        copy_key = id(copy)
        self.open[copy_key] = copy
        self.count += 1
        return copy

    def release(self, copy):
        self.open.pop(id(copy)).wait_send()

    def finish(self):
        for copy in self.open.values():
            copy.wait_send()


def remote_call(body, outs, out_specs, in_specs, scratch, transfers, number, flops=0, moved=2**22):
    return pl.pallas_call(
        body,
        out_shape=outs,
        in_specs=in_specs,
        out_specs=out_specs,
        scratch_shapes=list(scratch)
        + [pltpu.SemaphoreType.DMA((transfers,)), pltpu.SemaphoreType.DMA((transfers,))],
        compiler_params=pltpu.CompilerParams(
            vmem_limit_bytes=62 * 2**20, collective_id=number, has_side_effects=True
        ),
        cost_estimate=pl.CostEstimate(flops=flops, bytes_accessed=moved, transcendentals=0),
    )


class PlaneGather:
    def __init__(self, transfers, slots):
        self.t, self.s = transfers, slots
        self.half = slots[0].shape[0] // 2

    def begin(self):
        s, t = self.s, self.t
        self.x = t.start(s[0], s[2], ctx=2)
        self.y = t.start(s[0], s[4], ctx=4)
        self.c = [t.start(s[0], s[1], ctx=1)]

    def middle(self):
        s, t, h = self.s, self.t, self.half
        self.x.wait_recv()
        self.low = t.start(s[2].at[:h], s[6].at[:h], ctx=4)
        self.c.append(t.start(s[2], s[3], ctx=1))
        self.y.wait_recv()
        self.high = t.start(s[4].at[h:], s[6].at[h:], ctx=2)
        self.c.append(t.start(s[4], s[5], ctx=1))

    def end(self):
        s, t = self.s, self.t
        self.low.wait_recv()
        self.high.wait_recv()
        self.c.append(t.start(s[6], s[7], ctx=1))

    def ready(self):
        for copy in self.c:
            copy.wait_recv()


class RowGather:
    def __init__(self, own, slots, send, recv):
        self.own, self.slots, self.send, self.recv = own, slots, send, recv
        place = lax.axis_index("fsdp")
        self.inner = (place == 1) | (place == 2)

    def copy(self, src, dst, number, fsdp):
        return pltpu.make_async_remote_copy(
            src_ref=src,
            dst_ref=self.slots[dst],
            send_sem=self.send.at[number],
            recv_sem=self.recv.at[dst - 1],
            device_id=device(0, fsdp),
            device_id_type=MESH,
        )

    def near(self):
        return self.copy(self.own, 1, 0, 1)

    def across(self):
        return self.copy(self.own, 3, 1, 3)

    def near_on(self):
        return self.copy(self.slots[1], 2, 2, 3)

    def across_on(self):
        return self.copy(self.slots[3], 2, 3, 1)

    def second_on(self):
        return self.copy(self.slots[2], 3, 4, 1)

    def begin(self):
        self.near().start()

        @pl.when(self.inner)
        def _():
            self.across().start()

    def first(self):
        self.near().wait_recv()

        @pl.when(self.inner)
        def _():
            self.near_on().start()
            self.across().wait_recv()
            self.across_on().start()

    def second(self):
        self.near_on().wait_recv()

        @pl.when(self.inner)
        def _():
            self.second_on().start()

    def third(self):
        @pl.when(jnp.logical_not(self.inner))
        def _():
            self.second_on().wait_recv()

    def finish(self):
        self.near().wait_send()

        @pl.when(self.inner)
        def _():
            self.across().wait_send()
            self.near_on().wait_send()
            self.across_on().wait_send()
            self.second_on().wait_send()


def probabilities(query, keys, allowed):
    scores = lax.dot_general(query, keys, OVER_COLUMNS, preferred_element_type=f32) * SCALE
    scores = jnp.where(allowed, scores, hidden_fill_value)
    best = jnp.max(scores, 1, keepdims=True)
    exps = jnp.exp(scores - best)
    return exps * (1.0 / jnp.sum(exps, 1, keepdims=True)), best


def stacked_heads(value):
    return jnp.concatenate(
        [value[:, i * HEAD_SIZE : (i + 1) * HEAD_SIZE] for i in range(REPEAT)], 0
    )


def attention_row_body(
    x_ref, gain_ref, cosine_ref, sine_ref, natural_ref, begin_ref, key_natural_ref,
    q_ref, k_ref, v_ref, o_ref, down_ref, dy_ref,
    h_out, qkv_out, attended_out, best_out, residual_out, h2_out, gain_out,
    kv_out, unit_out, output_out, down_out, dy_out,
    q_own, k_own, v_own, o_own, units, outputs, kvs, h_rel,
    own_sem, keep_sem, gain_send, gain_recv, row_send, row_recv, send, recv,
):
    me, place = lax.axis_index("ctx"), lax.axis_index("fsdp")
    rows, model = x_ref.shape
    depth = units.shape[2]
    rounds = key_natural_ref.shape[0]
    blk = rows // rounds
    heads = q_ref.shape[1] // (REPEAT * HEAD_SIZE)
    width = o_ref.shape[1]
    own = pl.ds(pl.multiple_of(me * depth, depth), depth)
    loads = [
        pltpu.make_async_copy(src, dst, own_sem.at[i])
        for i, (src, dst) in enumerate(
            ((q_ref, q_own), (k_ref, k_own), (v_ref, v_own), (o_ref, o_own))
        )
    ]
    for load in loads:
        load.start()
    gain_out[0] = gain_ref[...]
    greet((1, 2, 4), (1, 2, 3))
    gains = Transfers(gain_send, gain_recv)
    gain_copies = [gains.start(gain_ref, gain_out.at[d], fsdp=d) for d in (1, 2, 3)]
    t = Transfers(send, recv)
    unit_rows, first = [], 0
    for i, ref in enumerate((q_ref, k_ref, v_ref)):
        cols = slice(first, first + ref.shape[1])
        first += ref.shape[1]
        unit_rows.append(
            RowGather(
                ref.at[own],
                [None] + [units.at[d, 0, :, cols] for d in range(3)],
                row_send.at[i],
                row_recv.at[i],
            )
        )
    output_row = RowGather(
        o_ref.at[own], [None] + [outputs.at[d, 0] for d in range(3)], row_send.at[3], row_recv.at[3]
    )
    dy_row = RowGather(
        dy_ref, [None] + [dy_out.at[d] for d in range(3)], row_send.at[4], row_recv.at[4]
    )
    unit_plane = [None] + [
        PlaneGather(t, [units.at[d, j] for j in range(8)]) for d in range(3)
    ]
    output_plane = [None] + [
        PlaneGather(t, [outputs.at[d, j] for j in range(8)]) for d in range(3)
    ]
    down_plane = [None] + [
        PlaneGather(t, [down_out.at[d, j] for j in range(8)]) for d in range(3)
    ]
    kv_plane = [PlaneGather(t, [kvs.at[d, j] for j in range(8)]) for d in range(4)]
    for row in unit_rows:
        row.begin()

    x = x_ref[...].astype(f32)
    unit = x * lax.rsqrt(jnp.mean(x * x, 1, keepdims=True) + epsilon)
    for copy in gain_copies:
        copy.wait_recv()
    for d in range(4):
        gain_cols = pl.ds(pl.multiple_of(flip(place, d) * width, width), width)
        residual_out[:, gain_cols] = jnp.broadcast_to(gain_out[d, 0:1], (rows, width))
    h_out[...] = (unit * residual_out[...]).astype(bf16)
    for j in range(8):
        block = pl.ds(pl.multiple_of(flip(me, j) * depth, depth), depth)
        h_rel[:, j * depth : (j + 1) * depth] = h_out[:, block]
    cosine, sine = cosine_ref[...], sine_ref[...]

    def project(d):
        if d == 0:
            h = h_out[...]
            parts = [
                jnp.dot(h, w[...], preferred_element_type=f32) for w in (q_own, k_own, v_own)
            ]
            total = jnp.concatenate(parts, 1)
        else:
            weight = units[d - 1].reshape(model, units.shape[3])
            total = jnp.dot(h_rel[...], weight, preferred_element_type=f32)

        def head(i):
            return total[:, i * HEAD_SIZE : (i + 1) * HEAD_SIZE]

        for h in range(heads):
            query = [
                rotate(head(REPEAT * h + i), cosine, sine).astype(bf16) for i in range(REPEAT)
            ]
            key = rotate(head(REPEAT * heads + h), cosine, sine).astype(bf16)
            value = head((REPEAT + 1) * heads + h).astype(bf16)
            first = (d * heads + h) * UNIT
            qkv_out[:, first : first + UNIT] = jnp.concatenate(query + [key, value], 1)
            first = h * 2 * HEAD_SIZE
            kvs[d, 0, :, first : first + 2 * HEAD_SIZE] = jnp.concatenate([key, value], 1)

    def attend_heads(d):
        def step(i, carry):
            r, h = lax.div(i, heads), lax.rem(i, heads)
            here = pl.ds(pl.multiple_of(r * blk, blk), blk)
            first = pl.multiple_of(d * heads * UNIT + h * UNIT, UNIT)
            query = stacked_heads(qkv_out[here, pl.ds(first, REPEAT * HEAD_SIZE)])
            cols = pl.ds(pl.multiple_of(h * 2 * HEAD_SIZE, 2 * HEAD_SIZE), 2 * HEAD_SIZE)
            both = kvs[d, :, here, cols].reshape(8 * blk, 2 * HEAD_SIZE)
            natural = key_natural_ref[r]
            allowed = (natural >= begin_ref[here]) & (natural <= natural_ref[here])
            allowed = jnp.concatenate([allowed] * REPEAT, 0)
            probs, best = probabilities(query, both[:, :HEAD_SIZE], allowed)
            out = jnp.dot(probs.astype(bf16), both[:, HEAD_SIZE:], preferred_element_type=f32)
            spot = flip(place, d) * heads + h
            cols = pl.ds(pl.multiple_of(spot * REPEAT * HEAD_SIZE, REPEAT * HEAD_SIZE), REPEAT * HEAD_SIZE)
            attended_out[here, cols] = jnp.concatenate(
                [out[i * blk : (i + 1) * blk] for i in range(REPEAT)], 1
            ).astype(bf16)
            tops = [
                jnp.broadcast_to(jnp.max(best[i * blk : (i + 1) * blk], 0, keepdims=True), (1, 128))
                for i in range(REPEAT)
            ]
            best_out[r, spot] = jnp.concatenate(tops + [jnp.zeros((8 - REPEAT, 128), f32)], 0)
            return carry

        lax.fori_loop(0, rounds * heads, step, 0)

    keeps = []

    def keep(src, dst):
        copy = pltpu.make_async_copy(src, dst, keep_sem.at[len(keeps)])
        copy.start()
        keeps.append(copy)

    for load in loads[:3]:
        load.wait()
    project(0)
    kv_plane[0].begin()
    for row in unit_rows:
        row.first()
    unit_plane[1].begin()
    output_row.begin()
    kv_plane[0].middle()
    for row in unit_rows:
        row.second()
    unit_plane[2].begin()
    unit_plane[1].middle()
    kv_plane[0].end()
    output_row.first()
    for row in unit_rows:
        row.third()
    unit_plane[3].begin()
    downs = []
    for d in (1, 2, 3):
        row = flip(place, d) * 8 * depth + me * depth
        downs.append(
            t.start(
                down_ref.at[pl.ds(pl.multiple_of(row, depth), depth)], down_out.at[d - 1, 0], fsdp=d
            )
        )
    dy_row.begin()
    unit_plane[2].middle()
    unit_plane[1].end()
    output_row.second()
    unit_plane[1].ready()
    project(1)
    kv_plane[1].begin()
    unit_plane[3].middle()
    unit_plane[2].end()
    output_row.third()
    unit_plane[2].ready()
    project(2)
    kv_plane[2].begin()
    kv_plane[1].middle()
    unit_plane[3].end()
    kv_plane[0].ready()
    attend_heads(0)
    unit_plane[3].ready()
    project(3)
    kv_plane[3].begin()
    kv_plane[2].middle()
    kv_plane[1].end()
    output_plane[1].begin()
    dy_row.first()
    kv_plane[3].middle()
    kv_plane[2].end()
    output_plane[2].begin()
    kv_plane[1].ready()
    attend_heads(1)
    output_plane[1].middle()
    kv_plane[3].end()
    output_plane[3].begin()
    kv_plane[2].ready()
    attend_heads(2)
    output_plane[2].middle()
    output_plane[1].end()
    downs[0].wait_recv()
    down_plane[1].begin()
    dy_row.second()
    kv_plane[3].ready()
    attend_heads(3)
    output_plane[3].middle()
    output_plane[2].end()
    downs[1].wait_recv()
    down_plane[2].begin()
    output_plane[3].end()
    for j in range(8):
        block = pl.ds(pl.multiple_of(flip(me, j) * depth, depth), depth)
        h_rel[:, j * depth : (j + 1) * depth] = attended_out[:, block]
    downs[2].wait_recv()
    down_plane[3].begin()
    for d in range(3):
        keep(units.at[d], unit_out.at[d])
    for d in range(4):
        keep(kvs.at[d], kv_out.at[d])
    loads[3].wait()
    square = None
    for d in range(4):
        cols = pl.ds(pl.multiple_of(flip(place, d) * width, width), width)
        if d == 0:
            term = jnp.dot(attended_out[...], o_own[...], preferred_element_type=f32)
        else:
            output_plane[d].ready()
            weight = outputs[d - 1].reshape(model, width)
            term = jnp.dot(h_rel[...], weight, preferred_element_type=f32)
        value = x_ref[:, cols].astype(f32) + term
        residual_out[:, cols] = value
        part = jnp.sum(value * value, 1, keepdims=True)
        square = part if square is None else square + part
        if d == 1:
            down_plane[1].middle()
    scale = lax.rsqrt(square * (1.0 / model) + epsilon)
    for d in range(4):
        cols = pl.ds(pl.multiple_of(flip(place, d) * width, width), width)
        h2_out[:, cols] = (residual_out[:, cols] * scale * gain_out[d, 1:2]).astype(bf16)
    for d in range(3):
        keep(outputs.at[d], output_out.at[d])
    down_plane[2].middle()
    down_plane[1].end()
    down_plane[3].middle()
    down_plane[2].end()
    down_plane[3].end()
    dy_row.third()
    for d in (1, 2, 3):
        down_plane[d].ready()
    for copy in keeps:
        copy.wait()
    for row in unit_rows + [output_row, dy_row]:
        row.finish()
    gains.finish()
    t.finish()


def attention_row(x, gains, cosine, sine, natural, begin, key_natural, query, key, value, output, down, dy):
    rows, model = x.shape
    depth = model // 8
    width = query.shape[1] + key.shape[1] + value.shape[1]
    kv_width = key.shape[1] + value.shape[1]
    rounds = key_natural.shape[0]
    dma = pltpu.SemaphoreType.DMA

    def out(shape, dtype=bf16):
        return jax.ShapeDtypeStruct(shape, dtype)

    return remote_call(
        attention_row_body,
        [
            out((rows, model)),
            out((rows, 4 * width)),
            out((rows, model)),
            out((rounds, KEY_VALUE_HEADS, 8, 128), f32),
            out((rows, model), f32),
            out((rows, model)),
            out((4,) + gains.shape, f32),
            out((4, 8, rows, kv_width)),
            out((3, 8, depth, width)),
            out((3, 8, depth, output.shape[1])),
            out((3, 8, depth, down.shape[1])),
            out((3,) + dy.shape),
        ],
        [VMEM] * 7 + [ANY] * 5,
        [VMEM] * 7 + [ANY] * 6,
        [
            pltpu.VMEM(query.shape, bf16),
            pltpu.VMEM(key.shape, bf16),
            pltpu.VMEM(value.shape, bf16),
            pltpu.VMEM(output.shape, bf16),
            pltpu.VMEM((3, 8, depth, width), bf16),
            pltpu.VMEM((3, 8, depth, output.shape[1]), bf16),
            pltpu.VMEM((4, 8, rows, kv_width), bf16),
            pltpu.VMEM((rows, model), bf16),
            dma((4,)),
            dma((10,)),
            dma((3,)),
            dma((3,)),
            dma((5, 5)),
            dma((5, 3)),
        ],
        3 + 13 * 8,
        0,
        flops=10 * rows * model * model,
    )(x, gains, cosine, sine, natural, begin, key_natural, query, key, value, output, down, dy)


TILE = 256


def feed_forward_row_body(
    h_ref, dy_ref, dy_rest, gate_ref, up_ref, down_own, down_rest,
    hid_out, dg_out, du_out, h_out, y_out, y_rest, back_out,
    gates, ups, downs, hs, dys, y_acc, back_acc, back_send, back_land, y_send, stage,
    load_sem, down_sem, dy_sem, h_sem, stage_sem, y_sem, row_send, row_recv, send, recv,
):
    rows, model = h_ref.shape
    tiles = gates.shape[0]
    me, place = lax.axis_index("ctx"), lax.axis_index("fsdp")
    width = down_own.shape[1]

    def tile_loads(i, slot):
        cols = pl.ds(pl.multiple_of(i * TILE, TILE), TILE)
        copies = [
            pltpu.make_async_copy(gate_ref.at[:, cols], gates.at[i], load_sem.at[0, i]),
            pltpu.make_async_copy(up_ref.at[:, cols], ups.at[i], load_sem.at[1, i]),
        ]
        own_rows = pl.ds(pl.multiple_of(place * tiles * TILE + i * TILE, TILE), TILE)
        for d in range(4):
            cols = pl.ds(pl.multiple_of(flip(place, d) * width, width), width)
            src = down_own.at[own_rows] if d == 0 else down_rest.at[d - 1, slot]
            copies.append(pltpu.make_async_copy(src, downs.at[i, :, cols], down_sem.at[i, d]))
        return copies

    dy_copies = [
        pltpu.make_async_copy(dy_ref if d == 0 else dy_rest.at[d - 1], dys.at[d], dy_sem.at[d])
        for d in range(4)
    ]
    dy_copies[0].start()
    for i in range(tiles):
        for load in tile_loads(i, flip(me, i)):
            load.start()
    for load in dy_copies[1:]:
        load.start()
    greet((), (1, 2, 3))
    t = Transfers(send, recv)
    row = RowGather(h_ref, [None] + [hs.at[d] for d in range(3)], row_send, row_recv)
    row.begin()
    dy_copies[0].wait()

    def stage_copy(slot, k, part, i):
        out = (hid_out, dg_out, du_out)[k]
        cols = pl.ds(pl.multiple_of(i * TILE, TILE), TILE)
        return pltpu.make_async_copy(
            stage.at[slot, k], out.at[pl.ds(part * rows, rows), cols], stage_sem.at[slot, k]
        )

    def chunk(part, h):
        def step(i, carry):
            slot = lax.rem(i, 2)
            if part == 0:
                for load in tile_loads(i, 0):
                    load.wait()
            gate, up, down = gates[i], ups[i], downs[i]
            g = jnp.dot(h[...], gate, preferred_element_type=f32)
            u = jnp.dot(h[...], up, preferred_element_type=f32)
            grad = lax.dot_general(dys[part], down, OVER_COLUMNS, preferred_element_type=f32)
            sigmoid = jax.nn.sigmoid(g)
            silu = g * sigmoid
            hidden = (silu * u).astype(bf16)
            grad_gate = (grad * u * sigmoid * (1.0 + g * (1.0 - sigmoid))).astype(bf16)
            grad_up = (grad * silu).astype(bf16)

            @pl.when(i >= 2)
            def _():
                for k in range(3):
                    stage_copy(slot, k, part, i - 2).wait()

            stage[slot, 0] = hidden
            stage[slot, 1] = grad_gate
            stage[slot, 2] = grad_up
            for k in range(3):
                stage_copy(slot, k, part, i).start()
            y = jnp.dot(hidden, down, preferred_element_type=f32)
            back = lax.dot_general(grad_gate, gate, OVER_COLUMNS, preferred_element_type=f32)
            back += lax.dot_general(grad_up, up, OVER_COLUMNS, preferred_element_type=f32)

            @pl.when(i == 0)
            def _():
                y_acc[...] = y
                back_acc[...] = back

            @pl.when(i > 0)
            def _():
                y_acc[...] += y
                back_acc[...] += back

            return carry

        lax.fori_loop(0, tiles, step, 0)
        for i in (tiles - 2, tiles - 1):
            for k in range(3):
                stage_copy(i % 2, k, part, i).wait()

    def keep_h(part, h):
        return pltpu.make_async_copy(h, h_out.at[pl.ds(part * rows, rows)], h_sem.at[part])

    keep_h(0, h_ref).start()
    chunk(0, h_ref)
    y_out[...] = y_acc[...]
    back_out[...] = back_acc[...]
    row.first()
    backs, y_copy = [], None
    for part in (1, 2, 3):
        h = hs.at[part - 1]
        if part == 2:
            row.second()
        if part == 3:
            row.third()
        keep_h(part, h).start()
        dy_copies[part].wait()
        chunk(part, h)
        back_send[part - 1] = back_acc[...].astype(bf16)
        backs.append(t.start(back_send.at[part - 1], back_land.at[part - 1], fsdp=part))
        if y_copy is not None:
            y_copy.wait()
        y_send[...] = y_acc[...].astype(bf16)
        y_copy = pltpu.make_async_copy(y_send, y_rest.at[part - 1], y_sem.at[part - 1])
        y_copy.start()
    y_copy.wait()
    for part in range(4):
        keep_h(part, h_ref if part == 0 else hs.at[part - 1]).wait()
    for d in range(3):
        backs[d].wait_recv()
        back_out[...] += back_land[d].astype(f32)
    row.finish()
    t.finish()


def feed_forward_row(h, dy, dy_rest, gate, up, down_own, down_rest):
    rows, model = h.shape
    units = gate.shape[1]
    tiles = units // TILE
    wide = jax.ShapeDtypeStruct((4 * rows, units), bf16)
    block = pltpu.VMEM((rows, model), f32)
    dma = pltpu.SemaphoreType.DMA
    return remote_call(
        feed_forward_row_body,
        [wide, wide, wide, jax.ShapeDtypeStruct((4 * rows, model), bf16)]
        + [jax.ShapeDtypeStruct((rows, model), f32), jax.ShapeDtypeStruct((3, rows, model), bf16)]
        + [jax.ShapeDtypeStruct((rows, model), f32)],
        [ANY] * 4 + [VMEM, ANY, VMEM],
        [VMEM] + [ANY] * 6,
        [
            pltpu.VMEM((tiles, model, TILE), bf16),
            pltpu.VMEM((tiles, model, TILE), bf16),
            pltpu.VMEM((tiles, TILE, model), bf16),
            pltpu.VMEM((3, rows, model), bf16),
            pltpu.VMEM((4, rows, model), bf16),
            block,
            block,
            pltpu.VMEM((3, rows, model), bf16),
            pltpu.VMEM((3, rows, model), bf16),
            pltpu.VMEM((rows, model), bf16),
            pltpu.VMEM((2, 3, rows, TILE), bf16),
            dma((2, tiles)),
            dma((tiles, 4)),
            dma((4,)),
            dma((4,)),
            dma((2, 3)),
            dma((3,)),
            dma((5,)),
            dma((3,)),
        ],
        3,
        2,
        flops=48 * rows * model * units,
    )(h, dy, dy_rest, gate, up, down_own, down_rest)


class SmallReduce:
    MASKS = ((0, 1), (0, 2), (2, 0), (4, 0), (1, 0))

    def __init__(self, transfers, blocks, land, join):
        self.t, self.blocks, self.land, self.join = transfers, blocks, land, join

    def begin(self, step):
        ctx, fsdp = self.MASKS[step]
        self.copy = self.t.start(self.blocks.at[step], self.land.at[step], ctx=ctx, fsdp=fsdp)

    def end(self, step):
        self.copy.wait_recv()
        self.blocks[step + 1] = self.join(self.blocks[step], self.land[step])

    def on(self, step):
        if 0 <= step - 1 < 5:
            self.end(step - 1)
        if step < 5:
            self.begin(step)


def small_scratch(shape):
    return [pltpu.VMEM((6,) + shape, f32), pltpu.VMEM((5,) + shape, f32)]


class PlaneSum:
    def __init__(self, transfers, cores, far, near, sums, total):
        self.t, self.cores, self.far, self.near = transfers, cores, far, near
        self.sums, self.total = sums, total
        self.half = cores.shape[1] // 2
        self.over = {}

    def send_odd(self, j, src):
        self.over[j - 1] = self.t.start(src, self.cores.at[(j - 1) // 2], ctx=1)
        return self.over[j - 1]

    def even(self, j, value):
        t, h = self.t, self.half
        self.over[j].wait_recv()
        value = value + self.cores[j // 2].astype(f32)
        if j == 0:
            self.total[...] = value
            return
        out = self.sums.at[(6, 2, 4).index(j)]
        out[...] = value.astype(bf16)
        if j == 6:
            self.x6 = t.start(out.at[:h], self.far.at[:h], ctx=2)
            self.y6 = t.start(out.at[h:], self.far.at[h:], ctx=4)
        elif j == 2:
            self.x2 = t.start(out.at[:h], self.near.at[0, :h], ctx=2)
        else:
            self.y4 = t.start(out.at[h:], self.near.at[1, h:], ctx=4)

    def pass_on(self):
        t, h = self.t, self.half
        two, four = self.sums.at[1], self.sums.at[2]
        self.y6.wait_recv()
        two[h:] = (two[h:].astype(f32) + self.far[h:].astype(f32)).astype(bf16)
        self.x2b = t.start(two.at[h:], self.near.at[0, h:], ctx=2)
        self.x6.wait_recv()
        four[:h] = (four[:h].astype(f32) + self.far[:h].astype(f32)).astype(bf16)
        self.y4b = t.start(four.at[:h], self.near.at[1, :h], ctx=4)

    def close(self):
        for copy in (self.x2, self.x2b, self.y4, self.y4b):
            copy.wait_recv()
        return self.total[...] + self.near[0].astype(f32) + self.near[1].astype(f32)


def plane_sum_scratch(count, *shape):
    return [
        pltpu.VMEM((count, 4) + shape, bf16),
        pltpu.VMEM((count,) + shape, bf16),
        pltpu.VMEM((count, 2) + shape, bf16),
        pltpu.VMEM((count, 3) + shape, bf16),
        pltpu.VMEM((count,) + shape, f32),
    ]


def grads_body(
    h_ref, dg_ref, du_ref, hid_ref, dy_ref, dy_rest, y_rest, top_ref,
    gate_out, up_out, down_out, y_land, top_out,
    left, rights, odd, cores, far, near, sums, totals, left_sem, right_sem, dy_sem, out_sem,
    blocks, land, send, recv,
):
    me = lax.axis_index("ctx")
    rows = dy_ref.shape[0]
    depth = cores.shape[2]
    dys = [dy_ref] + [dy_rest.at[d] for d in range(3)]
    right_copies = [
        [pltpu.make_async_copy(dg_ref, rights.at[0], right_sem.at[0])],
        [pltpu.make_async_copy(du_ref, rights.at[1], right_sem.at[1])],
        [
            pltpu.make_async_copy(p, rights.at[0, i * rows : (i + 1) * rows], dy_sem.at[i])
            for i, p in enumerate(dys)
        ],
    ]
    left_copies = [
        pltpu.make_async_copy(h_ref, left, left_sem.at[0]),
        pltpu.make_async_copy(hid_ref, left, left_sem.at[1]),
    ]
    left_copies[0].start()
    right_copies[0][0].start()
    right_copies[1][0].start()
    greet((1, 2, 4), (1, 2, 3))
    t = Transfers(send, recv)
    tops = SmallReduce(t, blocks, land, jnp.maximum)
    blocks[0] = top_ref[...]
    tops.on(0)
    y_copies = []
    left_copies[0].wait()
    jobs, odd_copies, outs = [], {}, []

    def close(k):
        totals[k] = jobs[k].close()
        out = pltpu.make_async_copy(totals.at[k], (gate_out, up_out)[k], out_sem.at[k])
        out.start()
        outs.append(out)

    for k in range(3):
        job = PlaneSum(t, cores.at[k], far.at[k], near.at[k], sums.at[k], totals.at[k])
        jobs.append(job)
        if k == 2:
            for copy in [left_copies[1]] + right_copies[2]:
                copy.start()
            left_copies[1].wait()
        for copy in right_copies[k]:
            copy.wait()

        def partial(j):
            block = pl.ds(pl.multiple_of(flip(me, j) * depth, depth), depth)
            return lax.dot_general(
                left[:, block], rights[k % 2], OVER_ROWS, preferred_element_type=f32
            )

        for i, j in enumerate((7, 5, 3, 1)):
            if j in odd_copies:
                t.release(odd_copies[j])
            odd[j // 2] = partial(j).astype(bf16)
            odd_copies[j] = job.send_odd(j, odd.at[j // 2])
            if k == 0:
                tops.on(i + 1)
            if k == 0 and i == 0:
                for d in (1, 2, 3):
                    y_copies.append(t.start(y_rest.at[d - 1], y_land.at[d - 1], fsdp=d))
        if k:
            jobs[k - 1].pass_on()
        for j in (6, 2, 4, 0):
            job.even(j, partial(j))
        if k:
            close(k - 1)
    tops.on(5)
    top_out[...] = blocks[5]
    jobs[2].pass_on()
    for copy in y_copies:
        copy.wait_recv()
    down_out[...] = jobs[2].close().astype(bf16)
    for copy in outs:
        copy.wait()
    t.finish()


def grads_row(h, dg, du, hid, dy, dy_rest, y_rest, top):
    rows, model = dy.shape
    depth = model // 8
    dma = pltpu.SemaphoreType.DMA
    summed = jax.ShapeDtypeStruct((depth, dg.shape[1]), f32)
    return remote_call(
        grads_body,
        [summed, summed, jax.ShapeDtypeStruct((depth, model), bf16), jax.ShapeDtypeStruct(y_rest.shape, bf16)]
        + [jax.ShapeDtypeStruct(top.shape, f32)],
        [ANY, ANY, VMEM, ANY, VMEM],
        [ANY] * 7 + [VMEM],
        [
            pltpu.VMEM(h.shape, bf16),
            pltpu.VMEM((2,) + h.shape, bf16),
            pltpu.VMEM((4, depth, model), bf16),
        ]
        + plane_sum_scratch(3, depth, model)
        + [dma((2,)), dma((2,)), dma((4,)), dma((2,))]
        + small_scratch(top.shape),
        3 + 3 * 10 + 5,
        3,
        flops=6 * h.shape[0] * model * model,
    )(h, dg, du, hid, dy, dy_rest, y_rest, top)


class RowSum:
    def __init__(self, transfers, total, sent, landed, columns):
        self.total, self.landed, self.columns = total, landed, columns
        self.over = []
        for d in (1, 2, 3):
            sent[d - 1] = total[:, columns(d)].astype(bf16)
            self.over.append(transfers.start(sent.at[d - 1], landed.at[d - 1], fsdp=d))

    def close(self):
        total = self.total[:, self.columns(0)]
        for d in range(3):
            self.over[d].wait_recv()
            total = total + self.landed[d].astype(f32)
        return total


def attention_back_body(
    db_ref, attended_ref, qkv_ref, cosine_ref, sine_ref, natural_ref, begin_ref, key_natural_ref,
    kv_ref, o_ref, output_rest,
    dq_out, dkv_out, output_out,
    kvs, o_own, outputs, head_grad, odd,
    cores, far, near, sums, totals,
    kv_cores, kv_far, kv_near, kv_sums, kv_totals,
    row_send, row_land, load_sem, send, recv,
):
    me, place = lax.axis_index("ctx"), lax.axis_index("fsdp")
    rows, model = db_ref.shape
    depth = cores.shape[2]
    width = o_own.shape[1]
    rounds = key_natural_ref.shape[0]
    blk = rows // rounds
    heads = kvs.shape[3] // (2 * HEAD_SIZE)
    loads = [
        pltpu.make_async_copy(src, dst, load_sem.at[i])
        for i, (src, dst) in enumerate(((o_ref, o_own), (output_rest, outputs), (kv_ref, kvs)))
    ]
    for load in loads:
        load.start()
    greet((1, 2, 4), (1, 2, 3))
    t = Transfers(send, recv)

    def of_slot(j):
        return pl.ds(pl.multiple_of(flip(me, j) * depth, depth), depth)

    def shard(d):
        return pl.ds(pl.multiple_of(flip(place, d) * width, width), width)

    job = PlaneSum(t, cores.at[0], far.at[0], near.at[0], sums.at[0], totals.at[0])

    def partial(j):
        return lax.dot_general(
            attended_ref[:, of_slot(j)], db_ref[...], OVER_ROWS, preferred_element_type=f32
        )

    for j in (7, 5, 3, 1):
        odd[j // 2] = partial(j).astype(bf16)
        job.send_odd(j, odd.at[j // 2])
    for j in (6, 2, 4, 0):
        job.even(j, partial(j))

    loads[0].wait()
    loads[1].wait()
    for j in range(8):
        total = lax.dot_general(
            db_ref[:, shard(0)], o_own[of_slot(j)], OVER_COLUMNS, preferred_element_type=f32
        )
        for d in (1, 2, 3):
            total += lax.dot_general(
                db_ref[:, shard(d)], outputs[d - 1, j], OVER_COLUMNS, preferred_element_type=f32
            )
        head_grad[:, of_slot(j)] = total.astype(bf16)
    loads[2].wait()
    cosine, sine = cosine_ref[...], -sine_ref[...]

    def attend_heads(d):
        def step(i, carry):
            r, h = lax.div(i, heads), lax.rem(i, heads)
            here = pl.ds(pl.multiple_of(r * blk, blk), blk)
            first = pl.multiple_of(d * heads * UNIT + h * UNIT, UNIT)
            query = stacked_heads(qkv_ref[here, pl.ds(first, REPEAT * HEAD_SIZE)])
            cols = pl.ds(pl.multiple_of(h * 2 * HEAD_SIZE, 2 * HEAD_SIZE), 2 * HEAD_SIZE)
            both = kvs[d, :, here, cols].reshape(8 * blk, 2 * HEAD_SIZE)
            keys, values = both[:, :HEAD_SIZE], both[:, HEAD_SIZE:]
            natural = key_natural_ref[r]
            allowed = (natural >= begin_ref[here]) & (natural <= natural_ref[here])
            allowed = jnp.concatenate([allowed] * REPEAT, 0)
            spot = flip(place, d) * heads + h
            spot_cols = pl.ds(
                pl.multiple_of(spot * REPEAT * HEAD_SIZE, REPEAT * HEAD_SIZE), REPEAT * HEAD_SIZE
            )
            grad = stacked_heads(head_grad[here, spot_cols])
            probs, _ = probabilities(query, keys, allowed)
            low = probs.astype(bf16)
            grad_probs = lax.dot_general(grad, values, OVER_COLUMNS, preferred_element_type=f32)
            delta = jnp.sum(low.astype(f32) * grad_probs, 1, keepdims=True)
            score_grad = (probs * (grad_probs - delta)).astype(bf16)
            query_grad = jnp.dot(score_grad, keys, preferred_element_type=f32) * SCALE
            turn = cosine_ref[here], -sine_ref[here]
            first = pl.multiple_of((d * heads + h) * REPEAT * HEAD_SIZE, REPEAT * HEAD_SIZE)
            dq_out[here, pl.ds(first, REPEAT * HEAD_SIZE)] = jnp.concatenate(
                [rotate(query_grad[i * blk : (i + 1) * blk], *turn) for i in range(REPEAT)], 1
            ).astype(bf16)
            key_grad = lax.dot_general(score_grad, query, OVER_ROWS, preferred_element_type=f32)
            value_grad = lax.dot_general(low, grad, OVER_ROWS, preferred_element_type=f32)
            both = jnp.concatenate([key_grad * SCALE, value_grad], 1).astype(bf16)
            kvs[d, :, here, cols] = both.reshape(8, blk, 2 * HEAD_SIZE)
            return carry

        lax.fori_loop(0, rounds * heads, step, 0)

    kv_jobs = [
        PlaneSum(t, kv_cores.at[k], kv_far.at[k], kv_near.at[k], kv_sums.at[k], kv_totals.at[k])
        for k in range(2)
    ]

    def send_half(k):
        half = pl.ds(2 * k, 2)
        for j in (7, 3, 5, 1):
            kv_jobs[k].send_odd(j, kvs.at[half, j])
        for j in (6, 2, 4, 0):
            kv_jobs[k].even(j, kvs[half, j].astype(f32))

    def take_half(k):
        total = kv_jobs[k].close()
        for i in range(2):
            for h in range(heads):
                first = 2 * h * HEAD_SIZE
                middle = first + HEAD_SIZE
                to = ((2 * k + i) * heads + h) * 2 * HEAD_SIZE
                turned = rotate(total[i, :, first:middle], cosine, sine)
                value = total[i, :, middle : middle + HEAD_SIZE]
                dkv_out[:, to : to + 2 * HEAD_SIZE] = jnp.concatenate([turned, value], 1).astype(bf16)

    attend_heads(0)
    job.pass_on()
    attend_heads(1)
    send_half(0)
    attend_heads(2)
    kv_jobs[0].pass_on()
    attend_heads(3)
    send_half(1)
    totals[0] = job.close()
    row = RowSum(t, totals.at[0], row_send, row_land, shard)
    kv_jobs[1].pass_on()
    take_half(0)
    output_out[...] = row.close()
    take_half(1)
    t.finish()


def attention_back(db, attended, qkv, cosine, sine, natural, begin, key_natural, kv, output, output_rest):
    rows, model = db.shape
    depth, width = model // 8, output.shape[1]
    kv_width = kv.shape[3]
    return remote_call(
        attention_back_body,
        [
            jax.ShapeDtypeStruct((rows, model), bf16),
            jax.ShapeDtypeStruct((rows, 4 * kv_width), bf16),
            jax.ShapeDtypeStruct((depth, width), f32),
        ],
        [VMEM] * 3,
        [VMEM] * 8 + [ANY] * 3,
        [
            pltpu.VMEM(kv.shape, bf16),
            pltpu.VMEM(output.shape, bf16),
            pltpu.VMEM(output_rest.shape, bf16),
            pltpu.VMEM((rows, model), bf16),
            pltpu.VMEM((4, depth, model), bf16),
        ]
        + plane_sum_scratch(1, depth, model)
        + plane_sum_scratch(2, 2, rows, kv_width)
        + [pltpu.VMEM((3, depth, width), bf16)] * 2
        + [pltpu.SemaphoreType.DMA((3,))],
        3 * 10 + 3,
        4,
        flops=20 * rows * model * model,
    )(db, attended, qkv, cosine, sine, natural, begin, key_natural, kv, output, output_rest)


def unit_grads_body(
    h_ref, dq_ref, dkv_ref, x_ref, term_ref, q_ref, k_ref, v_ref, unit_rest,
    query_out, key_out, value_out, back_out, gain_out,
    odd, q_own, k_own, v_own, units, cores, far, near, sums, totals, row_send, row_land,
    blocks, land, load_sem, unit_sem, send, recv,
):
    me = lax.axis_index("ctx")
    depth = cores.shape[2]
    width = row_land.shape[3]
    heads = k_own.shape[1] // HEAD_SIZE
    loads = [
        pltpu.make_async_copy(src, dst, load_sem.at[i])
        for i, (src, dst) in enumerate(((q_ref, q_own), (k_ref, k_own), (v_ref, v_own)))
    ]
    unit_loads = [
        pltpu.make_async_copy(unit_rest.at[d], units.at[d % 2], unit_sem.at[d]) for d in range(3)
    ]
    for load in loads + unit_loads[:2]:
        load.start()
    greet((1, 2, 4), (1, 2, 3))
    t = Transfers(send, recv)
    jobs, odd_copies = [], {}

    def of_slot(j):
        return pl.ds(pl.multiple_of(flip(me, j) * depth, depth), depth)

    for k, right in enumerate((dq_ref, dkv_ref)):
        job = PlaneSum(t, cores.at[k], far.at[k], near.at[k], sums.at[k], totals.at[k])
        jobs.append(job)

        def partial(j):
            return lax.dot_general(
                h_ref[:, of_slot(j)], right[...], OVER_ROWS, preferred_element_type=f32
            )

        for j in (7, 5, 3, 1):
            if j in odd_copies:
                t.release(odd_copies[j])
            odd[j // 2] = partial(j).astype(bf16)
            odd_copies[j] = job.send_odd(j, odd.at[j // 2])
        for j in (6, 2, 4, 0):
            job.even(j, partial(j))

    def grads(d):
        query = dq_ref[:, d * width : (d + 1) * width]
        pairs = dkv_ref[:, d * width : (d + 1) * width]
        parts = [pairs[:, i * HEAD_SIZE : (i + 1) * HEAD_SIZE] for i in range(2 * heads)]
        return jnp.concatenate([query] + parts[::2] + parts[1::2], 1)

    def back(d):
        grad = grads(d)
        for j in range(8):
            cols = of_slot(j)
            if d == 0:
                weight = jnp.concatenate([w[cols] for w in (q_own, k_own, v_own)], 1)
                back_out[:, cols] = lax.dot_general(
                    grad, weight, OVER_COLUMNS, preferred_element_type=f32
                )
            else:
                back_out[:, cols] += lax.dot_general(
                    grad, units[(d - 1) % 2, j], OVER_COLUMNS, preferred_element_type=f32
                )

    for load in loads:
        load.wait()
    back(0)
    jobs[0].pass_on()
    unit_loads[0].wait()
    back(1)
    unit_loads[2].start()
    unit_loads[1].wait()
    back(2)
    jobs[1].pass_on()
    unit_loads[2].wait()
    back(3)
    x = x_ref[...].astype(f32)
    unit = x * lax.rsqrt(jnp.mean(x * x, 1, keepdims=True) + epsilon)
    gains = SmallReduce(t, blocks, land, jnp.add)
    blocks[0] = jnp.concatenate(
        [jnp.sum(back_out[...] * unit, 0, keepdims=True), term_ref[1:8]], 0
    )
    gains.on(0)

    def columns(d):
        return pl.ds(d * width, width)

    totals[0] = jobs[0].close()
    gains.on(1)
    first = RowSum(t, totals.at[0], row_send.at[0], row_land.at[0], columns)
    gains.on(2)
    totals[1] = jobs[1].close()
    second = RowSum(t, totals.at[1], row_send.at[1], row_land.at[1], columns)
    gains.on(3)
    gains.on(4)
    query_out[...] = first.close()
    gains.on(5)
    gain_out[...] = blocks[5]
    total = second.close()
    for h in range(heads):
        start = 2 * h * HEAD_SIZE
        here = slice(h * HEAD_SIZE, (h + 1) * HEAD_SIZE)
        key_out[:, here] = total[:, start : start + HEAD_SIZE]
        value_out[:, here] = total[:, start + HEAD_SIZE : start + 2 * HEAD_SIZE]
    t.finish()


def unit_grads(h, dq, dkv, x, terms, query, key, value, rest):
    rows, model = h.shape
    depth, width = model // 8, model // 4
    wide = jax.ShapeDtypeStruct((depth, width), f32)
    half = jax.ShapeDtypeStruct((depth, width // 2), f32)
    dma = pltpu.SemaphoreType.DMA
    return remote_call(
        unit_grads_body,
        [wide, half, half, jax.ShapeDtypeStruct((rows, model), f32)]
        + [jax.ShapeDtypeStruct(terms.shape, f32)],
        [VMEM] * 5,
        [VMEM] * 5 + [ANY] * 4,
        [
            pltpu.VMEM((4, depth, model), bf16),
            pltpu.VMEM(query.shape, bf16),
            pltpu.VMEM(key.shape, bf16),
            pltpu.VMEM(value.shape, bf16),
            pltpu.VMEM((2,) + rest.shape[1:], bf16),
        ]
        + plane_sum_scratch(2, depth, model)
        + [pltpu.VMEM((2, 3, depth, width), bf16)] * 2
        + small_scratch(terms.shape)
        + [dma((3,)), dma((3,))],
        2 * (10 + 3) + 5,
        5,
        flops=12 * rows * model * model,
    )(h, dq, dkv, x, terms, query, key, value, rest)


def token_layout(length_row, block_slots, block_size):
    count_blocks = block_slots.shape[0]
    owner_block = jnp.argmax(
        block_slots[None, :] == jnp.arange(count_blocks, dtype=jnp.int32)[:, None], 1
    ).astype(jnp.int32)
    row_index = jnp.arange(count_blocks * block_size, dtype=jnp.int32)
    plain_order = jnp.repeat(owner_block, block_size) * block_size + row_index % block_size
    seq_ends = jnp.cumsum(length_row)
    seq_starts = seq_ends - length_row
    document_list = jnp.sum((plain_order[:, None] >= seq_ends[None, :]).astype(jnp.int32), 1)
    matches = document_list[:, None] == jnp.arange(length_row.shape[0], dtype=jnp.int32)[None, :]
    begins = jnp.sum(jnp.where(matches, seq_starts[None, :], 0), 1)
    return plain_order, begins


def rms_scale(value):
    return lax.rsqrt(jnp.mean(value * value, -1, keepdims=True) + epsilon)


def norm_back(grad_unit, unit_rows, scale_rows):
    return scale_rows * (grad_unit - unit_rows * jnp.mean(grad_unit * unit_rows, -1, keepdims=True))


def product(left, right):
    return jnp.dot(left, right, preferred_element_type=f32)


def product_t(left, right):
    return lax.dot_general(left, right, (((1,), (1,)), ((), ())), preferred_element_type=f32)


def over_rows(left, right):
    return lax.dot_general(left, right, (((0,), (0,)), ((), ())), preferred_element_type=f32)


def column_blocks(value, count, places):
    width = value.shape[1] // count
    return jnp.concatenate(
        [lax.dynamic_slice_in_dim(value, place * width, width, 1) for place in places], 1
    )


def gather_rows(piece, fsdp_place, ctx_count):
    count = lax.axis_size("fsdp")
    parts = [piece] + [swap(piece, "fsdp", d) for d in range(1, count)]
    return jnp.concatenate(by_place(parts, fsdp_place), 1)


def weight_grad_sum(left, right, me, count):
    depth = left.shape[1] // count
    full = over_rows(column_blocks(left, count, [me ^ j for j in range(count)]), right)
    return sum_halving(full.astype(bf16).reshape(count, depth, right.shape[1]), "ctx")


def down_grad_sum(hidden, grad, me, count, fsdp_count):
    bands = count // fsdp_count
    band, column = me // fsdp_count, me % fsdp_count
    depth = hidden.shape[1] // bands
    width = grad.shape[1] // fsdp_count
    left = column_blocks(hidden, bands, [band ^ j for j in range(bands)])
    right = column_blocks(grad, fsdp_count, [column ^ j for j in range(fsdp_count)])
    full = over_rows(left, right).astype(bf16).reshape(bands, depth, fsdp_count, width)
    return sum_halving(full.transpose(0, 2, 1, 3).reshape(count, depth, width), "ctx")


def clipped(weight, multiplier):
    columns = weight.shape[1]
    head_index = (
        lax.axis_index("fsdp") * columns + jnp.arange(columns, dtype=jnp.int32)
    ) // HEAD_SIZE
    matches = head_index[:, None] == jnp.arange(multiplier.shape[0], dtype=jnp.int32)[None, :]
    column_factor = jnp.sum(jnp.where(matches, multiplier[None, :], 0.0), 1)
    return (weight.astype(f32) * column_factor[None, :]).astype(bf16)


def gain_sum(term, me, place, count, fsdp_count):
    table = term.reshape(count, fsdp_count, -1)
    table = jnp.stack(by_place([table[i] for i in range(count)], me))
    mine = sum_halving(table, "ctx")
    mine = jnp.stack(by_place([mine[i] for i in range(fsdp_count)], place))
    return sum_halving(mine, "fsdp")


def attention_layout(seq_lengths, block_perm, rows):
    count, me = lax.axis_size("ctx"), lax.axis_index("ctx")
    rounds = block_perm.shape[0] // count
    blk = rows // rounds
    plain_order, begins = token_layout(seq_lengths[0], block_perm, blk)
    natural = lax.dynamic_slice_in_dim(plain_order, me * rows, rows)
    begin = lax.dynamic_slice_in_dim(begins, me * rows, rows)
    half_dim = HEAD_SIZE // 2
    exponent = jnp.arange(half_dim, dtype=f32) * (2.0 / HEAD_SIZE)
    inverse = rope_base ** (-exponent)
    angles = (natural - begin).astype(f32)[:, None] * inverse[None, :]
    cosine = jnp.concatenate([jnp.cos(angles)] * 2, 1)
    sine = jnp.concatenate([-jnp.sin(angles), jnp.sin(angles)], 1)
    order = plain_order.reshape(count, rounds, blk)
    order = jnp.stack(by_place([order[i] for i in range(count)], me), 1)
    return natural[:, None], begin[:, None], order.reshape(rounds, 1, count * blk), cosine, sine


def on_device(
    hidden_in,
    out_grad,
    seq_lengths,
    block_perm,
    first_gain,
    query_weight,
    key_matrix,
    value_matrix,
    output_weight,
    second_gain,
    gate_weight,
    up_weight,
    down_weight,
    clip_limit,
):
    rows, model = hidden_in.shape[1], hidden_in.shape[2]
    count, fsdp_count = lax.axis_size("ctx"), lax.axis_size("fsdp")
    me, place = lax.axis_index("ctx"), lax.axis_index("fsdp")
    me_ref = me.astype(jnp.int32).reshape(1)
    depth = model // count
    zero = jnp.zeros((1,), jnp.int32)
    shard_heads = KEY_VALUE_HEADS // fsdp_count

    def own_rows(weight):
        return lax.dynamic_slice_in_dim(weight, me * depth, depth, 0)

    unit_rows = jnp.concatenate(
        [
            own_rows(query_weight).reshape(depth, shard_heads, REPEAT, HEAD_SIZE),
            own_rows(key_matrix).reshape(depth, shard_heads, 1, HEAD_SIZE),
            own_rows(value_matrix).reshape(depth, shard_heads, 1, HEAD_SIZE),
        ],
        2,
    ).reshape(depth, shard_heads * UNIT)
    unit_rows = gather_rows(unit_rows, place, count)
    unit_slots = gather_ctx(unit_rows)
    gains = jnp.stack([first_gain, second_gain])
    gains = jnp.concatenate(
        by_place([gains] + [swap(gains, "fsdp", d) for d in range(1, fsdp_count)], place), 1
    ).astype(f32)
    first_full, second_full = gains[0], gains[1]
    output_rows = gather_rows(own_rows(output_weight), place, count)
    output_slots = gather_ctx(output_rows)

    hidden_width = gate_weight.shape[1]
    down_depth = hidden_width // count

    def down_piece(d):
        first = (place ^ d) * hidden_width + me * down_depth
        return lax.dynamic_slice_in_dim(down_weight, first, down_depth, 0)

    down_rows = [down_piece(0)] + [
        swap(down_piece(d), "fsdp", d) for d in range(1, fsdp_count)
    ]
    down_slots = gather_ctx(jnp.concatenate(by_place(down_rows, place), 1))

    natural_column, begin_column, key_natural, cosine, sine = attention_layout(
        seq_lengths, block_perm, rows
    )
    half_dim = HEAD_SIZE // 2

    tokens = hidden_in.reshape(rows, model).astype(f32)
    scale_one = rms_scale(tokens)
    unit_one = tokens * scale_one
    normalized = (unit_one * first_full).astype(bf16)
    qkv = slot_matmul(normalized, unit_slots, me_ref, UNIT, bf16, (cosine, sine))
    kv_local = qkv.reshape(rows, KEY_VALUE_HEADS, UNIT)[:, :, REPEAT * HEAD_SIZE :].reshape(
        rows, KEY_VALUE_HEADS * 2 * HEAD_SIZE
    )
    kv_slots = gather_ctx(kv_local)
    attended, best = attend(zero, natural_column, begin_column, key_natural, qkv, kv_slots)
    head_max = jnp.max(best[:, :, :REPEAT, 0], 0).reshape(QUERY_HEADS)
    for mask in bits_down(count):
        head_max = jnp.maximum(head_max, swap(head_max, "ctx", mask))
    for mask in bits_down(fsdp_count):
        head_max = jnp.maximum(head_max, swap(head_max, "fsdp", mask))
    residual = tokens + slot_matmul(attended, output_slots, me_ref, 512, f32)
    scale_two = rms_scale(residual)
    unit_two = residual * scale_two
    normed_two = (unit_two * second_full).astype(bf16)

    grad_out = out_grad.reshape(rows, model)
    others = range(1, fsdp_count)
    grads = [grad_out] + [swap(grad_out, "fsdp", d) for d in others]
    normed = [normed_two] + [swap(normed_two, "fsdp", d) for d in others]
    hidden_parts, gate_parts, up_parts, sums, backs = [], [], [], [], []
    for d in range(fsdp_count):
        grad_hidden = slot_matmul_t(grads[d], down_slots, me_ref, 512, f32)
        gate_act = product(normed[d], gate_weight)
        up_proj = product(normed[d], up_weight)
        sigmoid = jax.nn.sigmoid(gate_act)
        hidden = (gate_act * sigmoid * up_proj).astype(bf16)
        grad_gate = (
            grad_hidden * up_proj * sigmoid * (1.0 + gate_act * (1.0 - sigmoid))
        ).astype(bf16)
        grad_up = (grad_hidden * gate_act * sigmoid).astype(bf16)
        hidden_parts.append(hidden)
        gate_parts.append(grad_gate)
        up_parts.append(grad_up)
        backs.append(product_t(grad_gate, gate_weight) + product_t(grad_up, up_weight))
        sums.append(slot_matmul(hidden, down_slots, me_ref, 512, f32 if d == 0 else bf16))
    grad_normed_two = sum_fsdp(backs)
    result = (residual + sum_fsdp(sums)).astype(bf16)

    second_term = jnp.sum(grad_normed_two * unit_two, 0)
    grad_residual = grad_out.astype(f32) + norm_back(
        grad_normed_two * second_full, unit_two, scale_two
    )
    grad_branch = grad_residual.astype(bf16)
    head_grad = slot_matmul_t(grad_branch, output_slots, me_ref, 512, bf16)
    query_grad, *dkv_slots = attend_back(
        zero, natural_column, begin_column, key_natural, cosine, sine, qkv, head_grad, kv_slots
    )
    dkv = sum_halving(dkv_slots[0], "ctx")
    dkv = dkv.reshape(rows, KEY_VALUE_HEADS, 2, HEAD_SIZE)
    grad_key = dkv[:, :, 0]
    first, second = grad_key[..., :half_dim], grad_key[..., half_dim:]
    cos, sin = cosine[:, None, :half_dim], sine[:, None, half_dim:]
    grad_key = jnp.concatenate([first * cos + second * sin, second * cos - first * sin], -1)
    dqkv = jnp.concatenate(
        [
            query_grad.reshape(rows, KEY_VALUE_HEADS, REPEAT, HEAD_SIZE),
            grad_key[:, :, None].astype(bf16),
            dkv[:, :, 1:].astype(bf16),
        ],
        2,
    ).reshape(rows, KEY_VALUE_HEADS * UNIT)
    grad_normed_one = slot_matmul_t(dqkv, unit_slots, me_ref, 512, f32)
    first_term = jnp.sum(grad_normed_one * unit_one, 0)
    grad_input = grad_residual + norm_back(grad_normed_one * first_full, unit_one, scale_one)

    hidden_all = jnp.concatenate(hidden_parts, 0)
    normed_all = jnp.concatenate(normed, 0)
    grads_all = jnp.concatenate(grads, 0)
    down_sum = down_grad_sum(hidden_all, grads_all, me, count, fsdp_count).astype(bf16)
    bands = count // fsdp_count
    places = [
        (c * fsdp_count + f, (bands * f + c // fsdp_count) * fsdp_count + c % fsdp_count)
        for c in range(count)
        for f in range(fsdp_count)
    ]
    down_grad = lax.ppermute(down_sum, ("ctx", "fsdp"), places).astype(f32)
    gate_grad = weight_grad_sum(normed_all, jnp.concatenate(gate_parts, 0), me, count)
    up_grad = weight_grad_sum(normed_all, jnp.concatenate(up_parts, 0), me, count)

    def over_fsdp(summed):
        width = summed.shape[1] // fsdp_count
        return sum_fsdp(
            [
                lax.dynamic_slice_in_dim(summed, (place ^ d) * width, width, 1)
                for d in range(fsdp_count)
            ]
        )

    output_grad = over_fsdp(weight_grad_sum(attended, grad_branch, me, count))
    unit_grad = over_fsdp(weight_grad_sum(normalized, dqkv, me, count))
    unit_grad = unit_grad.reshape(depth, shard_heads, REPEAT + 2, HEAD_SIZE)
    query_out = unit_grad[:, :, :REPEAT].reshape(depth, -1)
    key_out = unit_grad[:, :, REPEAT].reshape(depth, -1)
    value_out = unit_grad[:, :, REPEAT + 1].reshape(depth, -1)

    first_out = gain_sum(first_term, me, place, count, fsdp_count)
    second_out = gain_sum(second_term, me, place, count, fsdp_count)
    multiplier = jnp.sqrt(clip_limit / jnp.maximum(head_max, clip_limit))
    key_ratio = jnp.min(multiplier.reshape(KEY_VALUE_HEADS, REPEAT), 1)
    return (
        result.reshape(1, rows, model),
        grad_input.astype(bf16).reshape(1, rows, model),
        first_out,
        query_out,
        key_out,
        value_out,
        output_grad,
        second_out,
        gate_grad,
        up_grad,
        down_grad,
        head_max,
        clipped(query_weight, multiplier),
        clipped(key_matrix, key_ratio),
    )


def on_row_of_chips(
    hidden_in,
    out_grad,
    seq_lengths,
    block_perm,
    first_gain,
    query_weight,
    key_matrix,
    value_matrix,
    output_weight,
    second_gain,
    gate_weight,
    up_weight,
    down_weight,
    clip_limit,
):
    rows, model = hidden_in.shape[1], hidden_in.shape[2]
    me, place = lax.axis_index("ctx"), lax.axis_index("fsdp")
    natural, begin, key_natural, cosine, sine = attention_layout(seq_lengths, block_perm, rows)
    tokens_low = hidden_in.reshape(rows, model)
    grad_out = out_grad.reshape(rows, model)
    gains = jnp.pad(jnp.stack([first_gain, second_gain]).astype(f32), ((0, 6), (0, 0)))
    (
        normalized,
        qkv,
        attended,
        best,
        residual,
        normed_two,
        all_gains,
        kv_all,
        unit_rest,
        output_rest,
        down_rest,
        dy_rest,
    ) = attention_row(
        tokens_low,
        gains,
        cosine,
        sine,
        natural,
        begin,
        key_natural,
        query_weight,
        key_matrix,
        value_matrix,
        output_weight,
        down_weight,
        grad_out,
    )
    full = jnp.concatenate(by_place([all_gains[d] for d in range(4)], place), 1)
    first_full, second_full = full[0], full[1]
    tokens = tokens_low.astype(f32)
    scale_one = rms_scale(tokens)
    unit_one = tokens * scale_one
    scale_two = rms_scale(residual)
    unit_two = residual * scale_two
    top = jnp.max(best[:, :, :REPEAT, 0], 0)
    top = jnp.pad(top, ((0, 0), (0, 128 - REPEAT)))

    hid, dg, du, h_all, y_own, y_rest, grad_normed_two = feed_forward_row(
        normed_two, grad_out, dy_rest, gate_weight, up_weight, down_weight, down_rest
    )
    second_term = jnp.sum(grad_normed_two * unit_two, 0)
    grad_residual = grad_out.astype(f32) + norm_back(
        grad_normed_two * second_full, unit_two, scale_two
    )
    grad_branch = grad_residual.astype(bf16)
    gate_grad, up_grad, down_sum, y_land, top = grads_row(
        h_all, dg, du, hid, grad_out, dy_rest, y_rest, top
    )
    head_max = top[:, :REPEAT].reshape(QUERY_HEADS)
    result = (residual + y_own + jnp.sum(y_land.astype(f32), 0)).astype(bf16)
    width = model // 4
    moved, pieces = [], []
    for k in range(4):
        piece = lax.dynamic_slice_in_dim(down_sum, ((me % 4) ^ k) * width, width, 1)
        pieces.append(piece)
    attended, pieces = lax.optimization_barrier((attended, pieces))
    for k, piece in enumerate(pieces):
        pairs = [
            (c * 4 + f, (2 * f + c // 4) * 4 + (c % 4 ^ k)) for c in range(8) for f in range(4)
        ]
        moved.append(lax.ppermute(piece, ("ctx", "fsdp"), pairs))
    down_grad = jnp.concatenate(by_place(moved, place), 0).astype(f32)

    query_grad, dkv, output_out = attention_back(
        grad_branch,
        attended,
        qkv,
        cosine,
        sine,
        natural,
        begin,
        key_natural,
        kv_all,
        output_weight,
        output_rest,
    )
    terms = jnp.pad(second_term[None], ((1, 6), (0, 0)))
    query_out, key_out, value_out, grad_normed_one, terms = unit_grads(
        normalized,
        query_grad,
        dkv,
        tokens_low,
        terms,
        query_weight,
        key_matrix,
        value_matrix,
        unit_rest,
    )
    grad_input = grad_residual + norm_back(grad_normed_one * first_full, unit_one, scale_one)
    terms = lax.dynamic_slice_in_dim(
        terms[:2], (me * 4 + place) * (model // 32), model // 32, 1
    )
    first_out, second_out = terms[0], terms[1]
    multiplier = jnp.sqrt(clip_limit / jnp.maximum(head_max, clip_limit))
    key_ratio = jnp.min(multiplier.reshape(KEY_VALUE_HEADS, REPEAT), 1)
    return (
        result.reshape(1, rows, model),
        grad_input.astype(bf16).reshape(1, rows, model),
        first_out,
        query_out,
        key_out,
        value_out,
        output_out,
        second_out,
        gate_grad,
        up_grad,
        down_grad,
        head_max,
        clipped(query_weight, multiplier),
        clipped(key_matrix, key_ratio),
    )


def solution(mesh):
    shard, whole = P(None, "fsdp"), P()
    token, block = P("fsdp", "ctx", None), P("ctx", "fsdp")
    gain = P(("ctx", "fsdp"))
    chips = mesh.shape["ctx"] == 8 and mesh.shape["fsdp"] == 4
    return jax.shard_map(
        on_row_of_chips if chips else on_device,
        mesh=mesh,
        in_specs=(token, token, P("fsdp", None), whole, P("fsdp"))
        + (shard,) * 4
        + (P("fsdp"),)
        + (shard,) * 3
        + (whole,),
        out_specs=(token, token, gain)
        + (block,) * 4
        + (gain,)
        + (block,) * 3
        + (whole, shard, shard),
        check_vma=False,
    )
```

```python
import functools
import math

import jax
import jax.numpy as jnp
from jax import lax
from jax.experimental import pallas as pl
from jax.experimental.pallas import tpu as pltpu
from jax.sharding import PartitionSpec as P

QUERY_HEADS = 16
KEY_VALUE_HEADS = 8
HEAD_SIZE = 128
REPEAT = QUERY_HEADS // KEY_VALUE_HEADS
UNIT = (REPEAT + 2) * HEAD_SIZE

epsilon = 1e-06
rope_base = 1000000.0
hidden_fill_value = -1e30
bf16 = jnp.bfloat16
f32 = jnp.float32
SCALE = 1.0 / math.sqrt(HEAD_SIZE)


def swap(value, axis, mask):
    size = lax.axis_size(axis)
    return lax.ppermute(value, axis, [(i, i ^ mask) for i in range(size)])


def bits_down(size):
    mask = size // 2
    while mask:
        yield mask
        mask //= 2


def by_place(items, me):
    mask = 1
    while mask < len(items):
        odd = (me & mask) != 0
        items = [jnp.where(odd, items[j ^ mask], items[j]) for j in range(len(items))]
        mask *= 2
    return items


def gather_ctx(block):
    size = lax.axis_size("ctx")
    whole = block[None]
    mask = 1
    while mask < size:
        whole = jnp.concatenate([whole, swap(whole, "ctx", mask)], 0)
        mask *= 2
    return [whole]


def sum_halving(slots, axis):
    for mask in bits_down(slots.shape[0]):
        keep = slots[:mask].astype(f32)
        slots = (keep + swap(slots[mask:], axis, mask).astype(f32)).astype(slots.dtype)
    return slots[0].astype(f32)


def sum_fsdp(pieces):
    total = pieces[0].astype(f32)
    for d in range(1, len(pieces)):
        total = total + swap(pieces[d].astype(bf16), "fsdp", d).astype(f32)
    return total


def params(flops, bytes_accessed):
    return dict(
        compiler_params=pltpu.CompilerParams(vmem_limit_bytes=48 * 2**20),
        cost_estimate=pl.CostEstimate(
            flops=flops, bytes_accessed=bytes_accessed, transcendentals=0
        ),
    )


def rotate(value, cosine, sine):
    return value * cosine + pltpu.roll(value, HEAD_SIZE // 2, 1) * sine


def slot_matmul_body(n_slots, parts, depth, rope, me_ref, x_ref, *refs):
    slot_refs = refs[:n_slots]
    out_ref = refs[-1]
    total = None
    for j in range(n_slots):
        for q in range(parts):
            owner = me_ref[0] ^ (j * parts + q)
            cols = pl.ds(pl.multiple_of(owner * depth, depth), depth)
            term = jnp.dot(x_ref[:, cols], slot_refs[j][q], preferred_element_type=f32)
            total = term if total is None else total + term
    if rope:
        cosine, sine = refs[n_slots][...], refs[n_slots + 1][...]
        parts_out = [
            rotate(total[:, i * HEAD_SIZE : (i + 1) * HEAD_SIZE], cosine, sine)
            for i in range(REPEAT + 1)
        ]
        total = jnp.concatenate(parts_out + [total[:, (REPEAT + 1) * HEAD_SIZE :]], 1)
    out_ref[...] = total.astype(out_ref.dtype)


def in_order(slots, me):
    whole = jnp.concatenate(slots, 0)
    whole = whole[me ^ jnp.arange(whole.shape[0], dtype=jnp.int32)]
    return whole.reshape(-1, whole.shape[2])


def in_order(slots, me):
    whole = jnp.concatenate(slots, 0)
    whole = whole[me ^ jnp.arange(whole.shape[0], dtype=jnp.int32)]
    return whole.reshape(-1, whole.shape[2])


def slot_matmul(x, slots, me, tile, out_dtype, tables=None):
    rows = x.shape[0]
    parts, depth, width = slots[0].shape
    if depth % 128:
        total = product(x, in_order(slots, me))
        if tables is None:
            return total.astype(out_dtype)
        total = total.reshape(rows, width // UNIT, REPEAT + 2, HEAD_SIZE)
        cosine, sine = (t[:, None, None] for t in tables)
        turned = total[:, :, : REPEAT + 1]
        turned = turned * cosine + jnp.roll(turned, HEAD_SIZE // 2, -1) * sine
        total = jnp.concatenate([turned, total[:, :, REPEAT + 1 :]], 2)
        return total.reshape(rows, width).astype(out_dtype)
    extra = [] if tables is None else list(tables)
    body = functools.partial(
        slot_matmul_body, len(slots), parts, depth, tables is not None
    )
    return pl.pallas_call(
        body,
        out_shape=jax.ShapeDtypeStruct((rows, width), out_dtype),
        grid_spec=pltpu.PrefetchScalarGridSpec(
            num_scalar_prefetch=1,
            grid=(width // tile,),
            in_specs=[pl.BlockSpec(x.shape, lambda i, me: (0, 0))]
            + [pl.BlockSpec((parts, depth, tile), lambda i, me: (0, 0, i))] * len(slots)
            + [pl.BlockSpec(e.shape, lambda i, me: (0, 0)) for e in extra],
            out_specs=pl.BlockSpec((rows, tile), lambda i, me: (0, i)),
        ),
        **params(2 * rows * x.shape[1] * width, 2 * x.shape[1] * width),
    )(me, x, *slots, *extra)


def slot_matmul_t_body(n_slots, parts, depth, me_ref, x_ref, *refs):
    slot_refs = refs[:n_slots]
    out_ref, total_ref = refs[n_slots], refs[n_slots + 1]
    step = pl.program_id(0)

    @pl.when(step == 0)
    def _():
        total_ref[...] = jnp.zeros_like(total_ref)

    x = x_ref[...]
    for j in range(n_slots):
        for q in range(parts):
            owner = me_ref[0] ^ (j * parts + q)
            cols = pl.ds(pl.multiple_of(owner * depth, depth), depth)
            total_ref[:, cols] += lax.dot_general(
                x, slot_refs[j][q], (((1,), (1,)), ((), ())), preferred_element_type=f32
            )

    @pl.when(step == pl.num_programs(0) - 1)
    def _():
        out_ref[...] = total_ref[...].astype(out_ref.dtype)


def slot_matmul_t(x, slots, me, tile, out_dtype):
    rows, width = x.shape
    parts, depth, _ = slots[0].shape
    height = parts * depth * len(slots)
    if depth % 128:
        return product_t(x, in_order(slots, me)).astype(out_dtype)
    return pl.pallas_call(
        functools.partial(slot_matmul_t_body, len(slots), parts, depth),
        out_shape=jax.ShapeDtypeStruct((rows, height), out_dtype),
        grid_spec=pltpu.PrefetchScalarGridSpec(
            num_scalar_prefetch=1,
            grid=(width // tile,),
            in_specs=[pl.BlockSpec((rows, tile), lambda i, me: (0, i))]
            + [pl.BlockSpec((parts, depth, tile), lambda i, me: (0, 0, i))]
            * len(slots),
            out_specs=pl.BlockSpec((rows, height), lambda i, me: (0, 0)),
            scratch_shapes=[pltpu.VMEM((rows, height), f32)],
        ),
        **params(2 * rows * height * width, 2 * height * width),
    )(me, x, *slots)


def keys_of(slot_refs):
    def column(i):
        parts = [
            r[..., i * HEAD_SIZE : (i + 1) * HEAD_SIZE].reshape(-1, HEAD_SIZE)
            for r in slot_refs
        ]
        return parts[0] if len(parts) == 1 else jnp.concatenate(parts, 0)

    return column(0), column(1)


def scores_of(qkv_ref, keys, natural_ref, start_ref, key_natural_ref):
    blk = qkv_ref.shape[0]
    query = jnp.concatenate(
        [qkv_ref[:, i * HEAD_SIZE : (i + 1) * HEAD_SIZE] for i in range(REPEAT)], 0
    )
    scores = (
        lax.dot_general(
            query, keys, (((1,), (1,)), ((), ())), preferred_element_type=f32
        )
        * SCALE
    )
    key_natural = key_natural_ref[0]
    allowed = (key_natural >= start_ref[...]) & (key_natural <= natural_ref[...])
    allowed = jnp.concatenate([allowed] * REPEAT, 0)
    scores = jnp.where(allowed, scores, hidden_fill_value)
    best = jnp.max(scores, 1, keepdims=True)
    exps = jnp.exp(scores - best)
    return query, exps * (1.0 / jnp.sum(exps, 1, keepdims=True)), best, blk


def attend_body(n_slots, place_ref, natural_ref, start_ref, key_natural_ref, qkv_ref, *refs):
    slot_refs, (out_ref, best_ref) = refs[:n_slots], refs[n_slots:]
    keys, values = keys_of(slot_refs)
    _, probs, best, blk = scores_of(qkv_ref, keys, natural_ref, start_ref, key_natural_ref)
    heads = jnp.dot(probs.astype(bf16), values, preferred_element_type=f32)
    out_ref[...] = jnp.concatenate(
        [heads[i * blk : (i + 1) * blk] for i in range(REPEAT)], 1
    ).astype(bf16)
    tops = [
        jnp.broadcast_to(jnp.max(best[i * blk : (i + 1) * blk], 0, keepdims=True), (1, 128))
        for i in range(REPEAT)
    ]
    best_ref[0, 0] = jnp.concatenate(tops + [jnp.zeros((8 - REPEAT, 128), f32)], 0)


def attend_back_body(
    n_slots, place_ref, natural_ref, start_ref, key_natural_ref, cosine_ref, sine_ref, qkv_ref, grad_ref, *refs
):
    slot_refs, (dq_ref, *dkv_refs) = refs[:n_slots], refs[n_slots:]
    keys, values = keys_of(slot_refs)
    query, probs, _, blk = scores_of(qkv_ref, keys, natural_ref, start_ref, key_natural_ref)
    grad = jnp.concatenate(
        [grad_ref[:, i * HEAD_SIZE : (i + 1) * HEAD_SIZE] for i in range(REPEAT)], 0
    )
    low = probs.astype(bf16)
    grad_probs = lax.dot_general(
        grad, values, (((1,), (1,)), ((), ())), preferred_element_type=f32
    )
    delta = jnp.sum(low.astype(f32) * grad_probs, 1, keepdims=True)
    score_grad = (probs * (grad_probs - delta)).astype(bf16)
    query_grad = jnp.dot(score_grad, keys, preferred_element_type=f32) * SCALE
    cosine, sine = cosine_ref[...], sine_ref[...]
    dq_ref[...] = jnp.concatenate(
        [
            rotate(query_grad[i * blk : (i + 1) * blk], cosine, -sine)
            for i in range(REPEAT)
        ],
        1,
    ).astype(bf16)
    over_rows = (((0,), (0,)), ((), ()))
    key_grad = (
        lax.dot_general(score_grad, query, over_rows, preferred_element_type=f32) * SCALE
    ).astype(bf16)
    value_grad = lax.dot_general(low, grad, over_rows, preferred_element_type=f32).astype(
        bf16
    )
    both = jnp.concatenate([key_grad, value_grad], 1)
    first = 0
    for ref in dkv_refs:
        rows = math.prod(ref.shape[:-1])
        ref[...] = both[first : first + rows].reshape(ref.shape)
        first += rows


def attention_specs(slots, blk, keys, shard_heads):
    def own_place(r, h, place):
        return (r, (place[0] ^ (h // shard_heads)) * shard_heads + h % shard_heads)

    column = pl.BlockSpec((blk, 1), lambda r, h, p: (r, 0))
    return (
        [column, column, pl.BlockSpec((1, 1, keys), lambda r, h, p: (r, 0, 0))],
        pl.BlockSpec((blk, UNIT), lambda r, h, p: (r, h)),
        pl.BlockSpec((blk, REPEAT * HEAD_SIZE), lambda r, h, p: (r, h)),
        pl.BlockSpec((blk, REPEAT * HEAD_SIZE), own_place),
        pl.BlockSpec((1, 1, 8, 128), lambda r, h, p: own_place(r, h, p) + (0, 0)),
        [
            pl.BlockSpec((s.shape[0], blk, 2 * HEAD_SIZE), lambda r, h, p: (0, r, h))
            if s.ndim == 3
            else pl.BlockSpec(
                (1, s.shape[1], blk, 2 * HEAD_SIZE),
                lambda r, h, p: (h // shard_heads, 0, r, h % shard_heads),
            )
            for s in slots
        ],
    )


def attend(place, natural, start, key_natural, qkv, slots):
    rows, heads = qkv.shape[0], qkv.shape[1] // UNIT
    rounds, _, keys = key_natural.shape
    blk = rows // rounds
    meta, unit, _, placed, best, slot = attention_specs(
        slots, blk, keys, heads // lax.axis_size("fsdp")
    )
    return pl.pallas_call(
        functools.partial(attend_body, len(slots)),
        out_shape=[
            jax.ShapeDtypeStruct((rows, heads * REPEAT * HEAD_SIZE), bf16),
            jax.ShapeDtypeStruct((rounds, heads, 8, 128), f32),
        ],
        grid_spec=pltpu.PrefetchScalarGridSpec(
            num_scalar_prefetch=1,
            grid=(rounds, heads),
            in_specs=meta + [unit] + slot,
            out_specs=[placed, best],
        ),
        **params(4 * rows * keys * heads * REPEAT * HEAD_SIZE, 12 * 2**20),
    )(place, natural, start, key_natural, qkv, *slots)


def attend_back(place, natural, start, key_natural, cosine, sine, qkv, grad, slots):
    rows, heads = qkv.shape[0], qkv.shape[1] // UNIT
    rounds, _, keys = key_natural.shape
    blk = rows // rounds
    meta, unit, pair, placed, _, slot = attention_specs(
        slots, blk, keys, heads // lax.axis_size("fsdp")
    )
    table = pl.BlockSpec((blk, HEAD_SIZE), lambda r, h, p: (r, 0))
    return pl.pallas_call(
        functools.partial(attend_back_body, len(slots)),
        out_shape=[jax.ShapeDtypeStruct((rows, heads * REPEAT * HEAD_SIZE), bf16)]
        + [jax.ShapeDtypeStruct(s.shape, bf16) for s in slots],
        grid_spec=pltpu.PrefetchScalarGridSpec(
            num_scalar_prefetch=1,
            grid=(rounds, heads),
            in_specs=meta + [table, table, unit, placed] + slot,
            out_specs=[pair] + slot,
        ),
        **params(10 * rows * keys * heads * REPEAT * HEAD_SIZE, 20 * 2**20),
    )(place, natural, start, key_natural, cosine, sine, qkv, grad, *slots)


ANY = pl.BlockSpec(memory_space=pl.ANY)
VMEM = pl.BlockSpec(memory_space=pltpu.VMEM)
MESH = pl.DeviceIdType.MESH
TILE = 256
OVER_ROWS = (((0,), (0,)), ((), ()))
OVER_COLUMNS = (((1,), (1,)), ((), ()))


def flip(place, mask):
    for bit in (1, 2, 4):
        if mask & bit:
            place = place + bit - 2 * bit * lax.rem(lax.div(place, bit), 2)
    return place


def device(ctx, fsdp):
    return {
        "ctx": flip(lax.axis_index("ctx"), ctx),
        "fsdp": flip(lax.axis_index("fsdp"), fsdp),
    }


def greet(ctx_masks, fsdp_masks):
    barrier = pltpu.get_barrier_semaphore()
    partners = [(m, 0) for m in ctx_masks] + [(0, m) for m in fsdp_masks]
    for ctx, fsdp in partners:
        pl.semaphore_signal(barrier, inc=1, device_id=device(ctx, fsdp), device_id_type=MESH)
    pl.semaphore_wait(barrier, len(partners))


def stretch(place, size):
    first = place * size
    return pl.ds(first if isinstance(place, int) else pl.multiple_of(first, size), size)


class Transfers:
    def __init__(self, send, recv):
        self.send, self.recv, self.count, self.open = send, recv, 0, {}

    def start(self, src, dst, ctx=0, fsdp=0, now=True):
        copy = Transfer(self, self.count, src, dst, ctx, fsdp)
        if now:
            copy.made().start()
        self.open[self.count] = copy
        self.count += 1
        return copy

    def release(self, copy):
        self.open.pop(copy.number).made().wait_send()

    def finish(self):
        for copy in list(self.open.values()):
            self.release(copy)


def part_of(ref):
    return ref[0].at[ref[1]] if isinstance(ref, tuple) else ref


class Transfer:
    def __init__(self, transfers, number, src, dst, ctx, fsdp):
        self.t, self.number, self.src, self.dst = transfers, number, src, dst
        self.ctx, self.fsdp = ctx, fsdp

    def made(self):
        return pltpu.make_async_remote_copy(
            src_ref=part_of(self.src),
            dst_ref=part_of(self.dst),
            send_sem=self.t.send.at[self.number],
            recv_sem=self.t.recv.at[self.number],
            device_id=device(self.ctx, self.fsdp),
            device_id_type=MESH,
        )

    def wait_recv(self):
        self.made().wait_recv()


def remote_call(body, outs, out_specs, in_specs, scratch, transfers, number, flops=0, moved=2**22):
    return pl.pallas_call(
        body,
        out_shape=outs,
        in_specs=in_specs,
        out_specs=out_specs,
        scratch_shapes=list(scratch)
        + [pltpu.SemaphoreType.DMA((transfers,)), pltpu.SemaphoreType.DMA((transfers,))],
        compiler_params=pltpu.CompilerParams(
            vmem_limit_bytes=62 * 2**20, collective_id=number, has_side_effects=True
        ),
        cost_estimate=pl.CostEstimate(flops=flops, bytes_accessed=moved, transcendentals=0),
    )


class PlaneGather:
    def __init__(self, transfers, slots):
        self.t, self.s = transfers, slots
        self.half = slots[0].shape[0] // 2

    def begin(self):
        s, t = self.s, self.t
        self.x = t.start(s[0], s[2], ctx=2)
        self.y = t.start(s[0], s[4], ctx=4)
        self.c = [t.start(s[0], s[1], ctx=1)]

    def middle(self):
        s, t, h = self.s, self.t, self.half
        self.x.wait_recv()
        self.low = t.start(s[2].at[:h], s[6].at[:h], ctx=4)
        self.c.append(t.start(s[2], s[3], ctx=1))
        self.y.wait_recv()
        self.high = t.start(s[4].at[h:], s[6].at[h:], ctx=2)
        self.c.append(t.start(s[4], s[5], ctx=1))

    def end(self):
        s, t = self.s, self.t
        self.low.wait_recv()
        self.high.wait_recv()
        self.c.append(t.start(s[6], s[7], ctx=1))

    def ready(self):
        for copy in self.c:
            copy.wait_recv()


class RowGather:
    def __init__(self, own, slots, send, recv):
        self.own, self.slots, self.send, self.recv = own, slots, send, recv
        place = lax.axis_index("fsdp")
        self.inner = (place == 1) | (place == 2)

    def copy(self, src, dst, number, fsdp):
        return pltpu.make_async_remote_copy(
            src_ref=src,
            dst_ref=self.slots[dst],
            send_sem=self.send.at[number],
            recv_sem=self.recv.at[dst - 1],
            device_id=device(0, fsdp),
            device_id_type=MESH,
        )

    def near(self):
        return self.copy(self.own, 1, 0, 1)

    def across(self):
        return self.copy(self.own, 3, 1, 3)

    def near_on(self):
        return self.copy(self.slots[1], 2, 2, 3)

    def across_on(self):
        return self.copy(self.slots[3], 2, 3, 1)

    def second_on(self):
        return self.copy(self.slots[2], 3, 4, 1)

    def begin(self):
        self.near().start()

        @pl.when(self.inner)
        def _():
            self.across().start()

    def first(self):
        self.near().wait_recv()

        @pl.when(self.inner)
        def _():
            self.near_on().start()
            self.across().wait_recv()
            self.across_on().start()

    def second(self):
        self.near_on().wait_recv()

        @pl.when(self.inner)
        def _():
            self.second_on().start()

    def third(self):
        @pl.when(jnp.logical_not(self.inner))
        def _():
            self.second_on().wait_recv()

    def finish(self):
        self.near().wait_send()

        @pl.when(self.inner)
        def _():
            self.across().wait_send()
            self.near_on().wait_send()
            self.across_on().wait_send()
            self.second_on().wait_send()


def probabilities(query, keys, allowed):
    scores = lax.dot_general(query, keys, OVER_COLUMNS, preferred_element_type=f32) * SCALE
    scores = jnp.where(allowed, scores, hidden_fill_value)
    best = jnp.max(scores, 1, keepdims=True)
    exps = jnp.exp(scores - best)
    return exps * (1.0 / jnp.sum(exps, 1, keepdims=True)), best


def stacked_heads(value):
    return jnp.concatenate(
        [value[:, i * HEAD_SIZE : (i + 1) * HEAD_SIZE] for i in range(REPEAT)], 0
    )


def attention_row_body(
    x_ref, gain_ref, cosine_ref, sine_ref, natural_ref, begin_ref, key_natural_ref,
    q_ref, k_ref, v_ref, o_ref, down_ref, dy_ref,
    h_out, qkv_out, attended_out, best_out, residual_out, h2_out, gain_out,
    kv_out, unit_out, output_out, down_out, dy_out,
    q_own, k_own, v_own, o_own, units, outputs, kvs, h_rel,
    own_sem, keep_sem, gain_send, gain_recv, row_send, row_recv, send, recv,
):
    me, place = lax.axis_index("ctx"), lax.axis_index("fsdp")
    rows, model = x_ref.shape
    depth = units.shape[2]
    rounds = key_natural_ref.shape[0]
    blk = rows // rounds
    heads = q_ref.shape[1] // (REPEAT * HEAD_SIZE)
    width = o_ref.shape[1]
    own = pl.ds(pl.multiple_of(me * depth, depth), depth)
    loads = [
        pltpu.make_async_copy(src, dst, own_sem.at[i])
        for i, (src, dst) in enumerate(
            ((q_ref, q_own), (k_ref, k_own), (v_ref, v_own), (o_ref, o_own))
        )
    ]
    for load in loads:
        load.start()
    gain_out[0] = gain_ref[...]
    greet((1, 2, 4), (1, 2, 3))
    gains = Transfers(gain_send, gain_recv)
    gain_copies = [gains.start(gain_ref, gain_out.at[d], fsdp=d) for d in (1, 2, 3)]
    t = Transfers(send, recv)
    unit_rows, first = [], 0
    for i, ref in enumerate((q_ref, k_ref, v_ref)):
        cols = slice(first, first + ref.shape[1])
        first += ref.shape[1]
        unit_rows.append(
            RowGather(
                ref.at[own],
                [None] + [units.at[d, 0, :, cols] for d in range(3)],
                row_send.at[i],
                row_recv.at[i],
            )
        )
    output_row = RowGather(
        o_ref.at[own], [None] + [outputs.at[d, 0] for d in range(3)], row_send.at[3], row_recv.at[3]
    )
    dy_row = RowGather(
        dy_ref, [None] + [dy_out.at[d] for d in range(3)], row_send.at[4], row_recv.at[4]
    )
    unit_plane = [None] + [
        PlaneGather(t, [units.at[d, j] for j in range(8)]) for d in range(3)
    ]
    output_plane = [None] + [
        PlaneGather(t, [outputs.at[d, j] for j in range(8)]) for d in range(3)
    ]
    down_plane = [None] + [
        PlaneGather(t, [down_out.at[d, j] for j in range(8)]) for d in range(3)
    ]
    kv_plane = [PlaneGather(t, [kvs.at[d, j] for j in range(8)]) for d in range(4)]
    for row in unit_rows:
        row.begin()

    x = x_ref[...].astype(f32)
    unit = x * lax.rsqrt(jnp.mean(x * x, 1, keepdims=True) + epsilon)
    for copy in gain_copies:
        copy.wait_recv()
    for d in range(4):
        gain_cols = pl.ds(pl.multiple_of(flip(place, d) * width, width), width)
        residual_out[:, gain_cols] = jnp.broadcast_to(gain_out[d, 0:1], (rows, width))
    h_out[...] = (unit * residual_out[...]).astype(bf16)
    for j in range(8):
        block = pl.ds(pl.multiple_of(flip(me, j) * depth, depth), depth)
        h_rel[:, j * depth : (j + 1) * depth] = h_out[:, block]
    cosine, sine = cosine_ref[...], sine_ref[...]

    def project(d):
        if d == 0:
            h = h_out[...]
            parts = [
                jnp.dot(h, w[...], preferred_element_type=f32) for w in (q_own, k_own, v_own)
            ]
            total = jnp.concatenate(parts, 1)
        else:
            weight = units[d - 1].reshape(model, units.shape[3])
            total = jnp.dot(h_rel[...], weight, preferred_element_type=f32)

        def head(i):
            return total[:, i * HEAD_SIZE : (i + 1) * HEAD_SIZE]

        for h in range(heads):
            query = [
                rotate(head(REPEAT * h + i), cosine, sine).astype(bf16) for i in range(REPEAT)
            ]
            key = rotate(head(REPEAT * heads + h), cosine, sine).astype(bf16)
            value = head((REPEAT + 1) * heads + h).astype(bf16)
            first = (d * heads + h) * UNIT
            qkv_out[:, first : first + UNIT] = jnp.concatenate(query + [key, value], 1)
            first = h * 2 * HEAD_SIZE
            kvs[d, 0, :, first : first + 2 * HEAD_SIZE] = jnp.concatenate([key, value], 1)

    def attend_heads(d):
        def step(i, carry):
            r, h = lax.div(i, heads), lax.rem(i, heads)
            here = pl.ds(pl.multiple_of(r * blk, blk), blk)
            first = pl.multiple_of(d * heads * UNIT + h * UNIT, UNIT)
            query = stacked_heads(qkv_out[here, pl.ds(first, REPEAT * HEAD_SIZE)])
            cols = pl.ds(pl.multiple_of(h * 2 * HEAD_SIZE, 2 * HEAD_SIZE), 2 * HEAD_SIZE)
            both = kvs[d, :, here, cols].reshape(8 * blk, 2 * HEAD_SIZE)
            natural = key_natural_ref[r]
            allowed = (natural >= begin_ref[here]) & (natural <= natural_ref[here])
            allowed = jnp.concatenate([allowed] * REPEAT, 0)
            probs, best = probabilities(query, both[:, :HEAD_SIZE], allowed)
            out = jnp.dot(probs.astype(bf16), both[:, HEAD_SIZE:], preferred_element_type=f32)
            spot = flip(place, d) * heads + h
            cols = pl.ds(pl.multiple_of(spot * REPEAT * HEAD_SIZE, REPEAT * HEAD_SIZE), REPEAT * HEAD_SIZE)
            attended_out[here, cols] = jnp.concatenate(
                [out[i * blk : (i + 1) * blk] for i in range(REPEAT)], 1
            ).astype(bf16)
            tops = [
                jnp.broadcast_to(jnp.max(best[i * blk : (i + 1) * blk], 0, keepdims=True), (1, 128))
                for i in range(REPEAT)
            ]
            best_out[r, spot] = jnp.concatenate(tops + [jnp.zeros((8 - REPEAT, 128), f32)], 0)
            return carry

        lax.fori_loop(0, rounds * heads, step, 0)

    keeps = []

    def keep(src, dst):
        copy = pltpu.make_async_copy(src, dst, keep_sem.at[len(keeps)])
        copy.start()
        keeps.append(copy)

    for load in loads[:3]:
        load.wait()
    project(0)
    kv_plane[0].begin()
    for row in unit_rows:
        row.first()
    unit_plane[1].begin()
    output_row.begin()
    kv_plane[0].middle()
    for row in unit_rows:
        row.second()
    unit_plane[2].begin()
    unit_plane[1].middle()
    kv_plane[0].end()
    output_row.first()
    for row in unit_rows:
        row.third()
    unit_plane[3].begin()
    downs = []
    for d in (1, 2, 3):
        row = flip(place, d) * 8 * depth + me * depth
        downs.append(
            t.start(
                down_ref.at[pl.ds(pl.multiple_of(row, depth), depth)], down_out.at[d - 1, 0], fsdp=d
            )
        )
    dy_row.begin()
    unit_plane[2].middle()
    unit_plane[1].end()
    output_row.second()
    unit_plane[1].ready()
    project(1)
    kv_plane[1].begin()
    unit_plane[3].middle()
    unit_plane[2].end()
    output_row.third()
    unit_plane[2].ready()
    project(2)
    kv_plane[2].begin()
    kv_plane[1].middle()
    unit_plane[3].end()
    kv_plane[0].ready()
    attend_heads(0)
    unit_plane[3].ready()
    project(3)
    kv_plane[3].begin()
    kv_plane[2].middle()
    kv_plane[1].end()
    output_plane[1].begin()
    dy_row.first()
    kv_plane[3].middle()
    kv_plane[2].end()
    output_plane[2].begin()
    kv_plane[1].ready()
    attend_heads(1)
    output_plane[1].middle()
    kv_plane[3].end()
    output_plane[3].begin()
    kv_plane[2].ready()
    attend_heads(2)
    output_plane[2].middle()
    output_plane[1].end()
    downs[0].wait_recv()
    down_plane[1].begin()
    dy_row.second()
    kv_plane[3].ready()
    attend_heads(3)
    output_plane[3].middle()
    output_plane[2].end()
    downs[1].wait_recv()
    down_plane[2].begin()
    output_plane[3].end()
    for j in range(8):
        block = pl.ds(pl.multiple_of(flip(me, j) * depth, depth), depth)
        h_rel[:, j * depth : (j + 1) * depth] = attended_out[:, block]
    downs[2].wait_recv()
    down_plane[3].begin()
    for d in range(3):
        keep(units.at[d], unit_out.at[d])
    for d in range(4):
        keep(kvs.at[d], kv_out.at[d])
    loads[3].wait()
    square = None
    for d in range(4):
        cols = pl.ds(pl.multiple_of(flip(place, d) * width, width), width)
        if d == 0:
            term = jnp.dot(attended_out[...], o_own[...], preferred_element_type=f32)
        else:
            output_plane[d].ready()
            weight = outputs[d - 1].reshape(model, width)
            term = jnp.dot(h_rel[...], weight, preferred_element_type=f32)
        value = x_ref[:, cols].astype(f32) + term
        residual_out[:, cols] = value
        part = jnp.sum(value * value, 1, keepdims=True)
        square = part if square is None else square + part
        if d == 1:
            down_plane[1].middle()
    scale = lax.rsqrt(square * (1.0 / model) + epsilon)
    for d in range(4):
        cols = pl.ds(pl.multiple_of(flip(place, d) * width, width), width)
        h2_out[:, cols] = (residual_out[:, cols] * scale * gain_out[d, 1:2]).astype(bf16)
    for d in range(3):
        keep(outputs.at[d], output_out.at[d])
    down_plane[2].middle()
    down_plane[1].end()
    down_plane[3].middle()
    down_plane[2].end()
    down_plane[3].end()
    dy_row.third()
    for d in (1, 2, 3):
        down_plane[d].ready()
    for copy in keeps:
        copy.wait()
    for row in unit_rows + [output_row, dy_row]:
        row.finish()
    gains.finish()
    t.finish()


def attention_row(x, gains, cosine, sine, natural, begin, key_natural, query, key, value, output, down, dy):
    rows, model = x.shape
    depth = model // 8
    width = query.shape[1] + key.shape[1] + value.shape[1]
    kv_width = key.shape[1] + value.shape[1]
    rounds = key_natural.shape[0]
    dma = pltpu.SemaphoreType.DMA

    def out(shape, dtype=bf16):
        return jax.ShapeDtypeStruct(shape, dtype)

    return remote_call(
        attention_row_body,
        [
            out((rows, model)),
            out((rows, 4 * width)),
            out((rows, model)),
            out((rounds, KEY_VALUE_HEADS, 8, 128), f32),
            out((rows, model), f32),
            out((rows, model)),
            out((4,) + gains.shape, f32),
            out((4, 8, rows, kv_width)),
            out((3, 8, depth, width)),
            out((3, 8, depth, output.shape[1])),
            out((3, 8, depth, down.shape[1])),
            out((3,) + dy.shape),
        ],
        [VMEM] * 7 + [ANY] * 5,
        [VMEM] * 7 + [ANY] * 6,
        [
            pltpu.VMEM(query.shape, bf16),
            pltpu.VMEM(key.shape, bf16),
            pltpu.VMEM(value.shape, bf16),
            pltpu.VMEM(output.shape, bf16),
            pltpu.VMEM((3, 8, depth, width), bf16),
            pltpu.VMEM((3, 8, depth, output.shape[1]), bf16),
            pltpu.VMEM((4, 8, rows, kv_width), bf16),
            pltpu.VMEM((rows, model), bf16),
            dma((4,)),
            dma((10,)),
            dma((3,)),
            dma((3,)),
            dma((5, 5)),
            dma((5, 3)),
        ],
        3 + 13 * 8,
        0,
        flops=10 * rows * model * model,
    )(x, gains, cosine, sine, natural, begin, key_natural, query, key, value, output, down, dy)


class SmallReduce:
    def __init__(self, transfers, blocks, land, join, masks):
        self.t, self.blocks, self.land, self.join = transfers, blocks, land, join
        self.masks = masks

    def begin(self, step):
        ctx, fsdp = self.masks[step]
        self.copy = self.t.start(
            (self.blocks, step), (self.land, step), ctx=ctx, fsdp=fsdp
        )

    def end(self, step):
        self.copy.wait_recv()
        self.blocks[step + 1] = self.join(self.blocks[step], self.land[step])

    def on(self, step):
        if 0 <= step - 1 < 5:
            self.end(step - 1)
        if step < 5:
            self.begin(step)


def small_scratch(shape):
    return [pltpu.VMEM((6,) + shape, f32), pltpu.VMEM((5,) + shape, f32)]


class PlaneSum:
    def __init__(self, transfers, cores, far, near, sums, total, fetch=None):
        self.t, self.cores, self.far, self.near = transfers, cores, far, near
        self.sums, self.total, self.fetch = sums, total, fetch
        self.half = cores.shape[1] // 2
        self.over = {}

    def arrive(self, j):
        self.over[j].wait_recv()
        if self.fetch is not None:
            place, sems = self.fetch
            slot = (j // 2) % 2
            self.copy = pltpu.make_async_copy(
                self.cores.at[j // 2], place.at[slot], sems.at[slot]
            )
            self.copy.start()

    def send_odd(self, j, src):
        self.over[j - 1] = self.t.start(src, self.cores.at[(j - 1) // 2], ctx=1)
        return self.over[j - 1]

    def even(self, j, value):
        t, h = self.t, self.half
        if self.fetch is None:
            value = value + self.cores[j // 2].astype(f32)
        else:
            self.copy.wait()
            value = value + self.fetch[0][(j // 2) % 2].astype(f32)
        if j == 0:
            self.total[...] = value
            return
        out = self.sums.at[(6, 2, 4).index(j)]
        out[...] = value.astype(bf16)
        if j == 6:
            self.x6 = t.start(out.at[:h], self.far.at[:h], ctx=2)
            self.y6 = t.start(out.at[h:], self.far.at[h:], ctx=4)
        elif j == 2:
            self.x2 = t.start(out.at[:h], self.near.at[0, :h], ctx=2)
        else:
            self.y4 = t.start(out.at[h:], self.near.at[1, h:], ctx=4)

    def pass_on(self):
        t, h = self.t, self.half
        two, four = self.sums.at[1], self.sums.at[2]
        self.y6.wait_recv()
        two[h:] = (two[h:].astype(f32) + self.far[h:].astype(f32)).astype(bf16)
        self.x2b = t.start(two.at[h:], self.near.at[0, h:], ctx=2)
        self.x6.wait_recv()
        four[:h] = (four[:h].astype(f32) + self.far[:h].astype(f32)).astype(bf16)
        self.y4b = t.start(four.at[:h], self.near.at[1, :h], ctx=4)

    def close(self):
        for copy in (self.x2, self.x2b, self.y4, self.y4b):
            copy.wait_recv()
        return self.total[...] + self.near[0].astype(f32) + self.near[1].astype(f32)


def plane_sum_scratch(count, *shape):
    return [
        pltpu.VMEM((count, 4) + shape, bf16),
        pltpu.VMEM((count,) + shape, bf16),
        pltpu.VMEM((count, 2) + shape, bf16),
        pltpu.VMEM((count, 3) + shape, bf16),
        pltpu.VMEM((count,) + shape, f32),
    ]


def feed_forward_row_body(
    h_ref, dy_ref, dy_rest, gate_ref, up_ref, down_own, down_rest, top_ref,
    hid_out, dg_out, du_out, h_out, y_out, y_rest, back_out,
    cores, y_land, gate_out, up_out, down_out, top_out,
    hs, back_send, back_land, far, near, blocks, land,
    load_sem, down_sem, dy_sem, h_sem, stage_sem, y_sem, left_sem, right_sem, core_sem, out_sem,
    row_send, row_recv, send, recv,
):
    greet((1, 2, 4), (1, 2, 3))
    t = Transfers(send, recv)
    row = RowGather(h_ref, [None] + [hs.at[d] for d in range(3)], row_send, row_recv)
    row.begin()
    blocks[0] = top_ref[...]
    tops = SmallReduce(
        t, blocks, land, jnp.maximum, ((2, 0), (4, 0), (1, 0), (0, 1), (0, 2))
    )
    rows, model = h_ref.shape
    tiles = gate_ref.shape[1] // TILE
    backs = []

    def forward(gates, ups, downs, dys, y_acc, back_acc, y_send, stage):
        feed_forward_parts(
            t, row, tops, backs,
            h_ref, dy_ref, dy_rest, gate_ref, up_ref, down_own, down_rest,
            hid_out, dg_out, du_out, h_out, y_out, y_rest, back_out,
            gates, ups, downs, hs, dys, y_acc, back_acc, back_send, back_land, y_send, stage,
            load_sem, down_sem, dy_sem, h_sem, stage_sem, y_sem,
        )

    block = pltpu.VMEM((rows, model), f32)
    pl.run_scoped(
        forward,
        pltpu.VMEM((tiles, model, TILE), bf16),
        pltpu.VMEM((tiles, model, TILE), bf16),
        pltpu.VMEM((tiles, TILE, model), bf16),
        pltpu.VMEM((4, rows, model), bf16),
        block,
        block,
        pltpu.VMEM((rows, model), bf16),
        pltpu.VMEM((2, 3, rows, TILE), bf16),
    )
    y_copy = t.start((y_rest, 0), y_land, fsdp=1)

    def grads(left, rights, odd, sums, totals, fetched):
        feed_forward_grads(
            t, h_out, dg_out, du_out, hid_out, dy_ref, dy_rest,
            gate_out, up_out, down_out,
            left, rights, odd, cores, far, near, sums, totals, fetched,
            left_sem, right_sem, dy_sem, core_sem, out_sem,
        )
        t.finish()

    depth = model // 8
    pl.run_scoped(
        grads,
        pltpu.VMEM((4 * rows, model), bf16),
        pltpu.VMEM((2, 4 * rows, model), bf16),
        pltpu.VMEM((4, depth, model), bf16),
        pltpu.VMEM((3, 3, depth, model), bf16),
        pltpu.VMEM((3, depth, model), f32),
        pltpu.VMEM((2, depth, model), bf16),
    )
    for d in range(3):
        backs[d].wait_recv()
        back_out[...] += back_land[d].astype(f32)
    tops.on(5)
    top_out[...] = blocks[5]
    y_copy.wait_recv()
    row.finish()
    t.finish()


def feed_forward_parts(
    t, row, tops, backs,
    h_ref, dy_ref, dy_rest, gate_ref, up_ref, down_own, down_rest,
    hid_out, dg_out, du_out, h_out, y_out, y_rest, back_out,
    gates, ups, downs, hs, dys, y_acc, back_acc, back_send, back_land, y_send, stage,
    load_sem, down_sem, dy_sem, h_sem, stage_sem, y_sem,
):
    rows, model = h_ref.shape
    tiles = gates.shape[0]
    me, place = lax.axis_index("ctx"), lax.axis_index("fsdp")
    width = down_own.shape[1]

    def tile_loads(i, slot):
        cols = stretch(i, TILE)
        copies = [
            pltpu.make_async_copy(gate_ref.at[:, cols], gates.at[i], load_sem.at[0, i]),
            pltpu.make_async_copy(up_ref.at[:, cols], ups.at[i], load_sem.at[1, i]),
        ]
        own_rows = stretch(place * tiles + i, TILE)
        for d in range(4):
            cols = stretch(flip(place, d), width)
            src = down_own.at[own_rows] if d == 0 else down_rest.at[d - 1, slot]
            copies.append(pltpu.make_async_copy(src, downs.at[i, :, cols], down_sem.at[i, d]))
        return copies

    dy_copies = [
        pltpu.make_async_copy(dy_ref if d == 0 else dy_rest.at[d - 1], dys.at[d], dy_sem.at[d])
        for d in range(4)
    ]
    dy_copies[0].start()
    for i in range(tiles):
        for load in tile_loads(i, flip(me, i)):
            load.start()
    for load in dy_copies[1:]:
        load.start()
    dy_copies[0].wait()

    def stage_copy(slot, k, part, i):
        out = (hid_out, dg_out, du_out)[k]
        cols = stretch(i, TILE)
        return pltpu.make_async_copy(
            stage.at[slot, k], out.at[pl.ds(part * rows, rows), cols], stage_sem.at[slot, k]
        )

    def chunk(part, h):
        def step(i, carry):
            slot = lax.rem(i, 2)
            if part == 0:
                for load in tile_loads(i, 0):
                    load.wait()
            gate, up, down = gates[i], ups[i], downs[i]
            g = jnp.dot(h[...], gate, preferred_element_type=f32)
            u = jnp.dot(h[...], up, preferred_element_type=f32)
            grad = lax.dot_general(dys[part], down, OVER_COLUMNS, preferred_element_type=f32)
            sigmoid = jax.nn.sigmoid(g)
            silu = g * sigmoid
            hidden = (silu * u).astype(bf16)
            grad_gate = (grad * u * sigmoid * (1.0 + g * (1.0 - sigmoid))).astype(bf16)
            grad_up = (grad * silu).astype(bf16)

            @pl.when(i >= 2)
            def _():
                for k in range(3):
                    stage_copy(slot, k, part, i - 2).wait()

            stage[slot, 0] = hidden
            stage[slot, 1] = grad_gate
            stage[slot, 2] = grad_up
            for k in range(3):
                stage_copy(slot, k, part, i).start()
            y = jnp.dot(hidden, down, preferred_element_type=f32)
            back = lax.dot_general(grad_gate, gate, OVER_COLUMNS, preferred_element_type=f32)
            back += lax.dot_general(grad_up, up, OVER_COLUMNS, preferred_element_type=f32)

            @pl.when(i == 0)
            def _():
                y_acc[...] = y
                back_acc[...] = back

            @pl.when(i > 0)
            def _():
                y_acc[...] += y
                back_acc[...] += back

            return carry

        lax.fori_loop(0, tiles, step, 0)
        for i in (tiles - 2, tiles - 1):
            for k in range(3):
                stage_copy(i % 2, k, part, i).wait()

    def keep_h(part, h):
        return pltpu.make_async_copy(h, h_out.at[pl.ds(part * rows, rows)], h_sem.at[part])

    keep_h(0, h_ref).start()
    tops.on(0)
    chunk(0, h_ref)
    y_copy = pltpu.make_async_copy(y_acc, y_out, y_sem.at[3])
    y_copy.start()
    back_out[...] = back_acc[...]
    row.first()
    tops.on(1)
    y_copy.wait()
    y_copy = None
    for part in (1, 2, 3):
        h = hs.at[part - 1]
        if part == 2:
            row.second()
        if part == 3:
            row.third()
        keep_h(part, h).start()
        dy_copies[part].wait()
        chunk(part, h)
        back_send[part - 1] = back_acc[...].astype(bf16)
        backs.append(
            t.start((back_send, part - 1), (back_land, part - 1), fsdp=part, now=part > 1)
        )
        if part != 2:
            @pl.when(row.inner == (part == 3))
            def _():
                backs[0].made().start()

        if y_copy is not None:
            y_copy.wait()
        y_send[...] = y_acc[...].astype(bf16)
        y_copy = pltpu.make_async_copy(y_send, y_rest.at[part - 1], y_sem.at[part - 1])
        y_copy.start()
        tops.on(part + 1)
    y_copy.wait()
    for part in range(4):
        keep_h(part, h_ref if part == 0 else hs.at[part - 1]).wait()


def feed_forward_grads(
    t, h_ref, dg_ref, du_ref, hid_ref, dy_ref, dy_rest,
    gate_out, up_out, down_out,
    left, rights, odd, cores, far, near, sums, totals, fetched,
    left_sem, right_sem, dy_sem, core_sem, out_sem,
):
    me = lax.axis_index("ctx")
    rows = dy_ref.shape[0]
    depth = far.shape[1]
    dys = [dy_ref] + [dy_rest.at[d] for d in range(3)]
    right_copies = [
        [pltpu.make_async_copy(dg_ref, rights.at[0], right_sem.at[0])],
        [pltpu.make_async_copy(du_ref, rights.at[1], right_sem.at[1])],
        [
            pltpu.make_async_copy(p, rights.at[0, i * rows : (i + 1) * rows], dy_sem.at[i])
            for i, p in enumerate(dys)
        ],
    ]
    left_copies = [
        pltpu.make_async_copy(h_ref, left, left_sem.at[0]),
        pltpu.make_async_copy(hid_ref, left, left_sem.at[1]),
    ]
    left_copies[0].start()
    right_copies[0][0].start()
    right_copies[1][0].start()
    left_copies[0].wait()
    jobs, odd_copies, outs = [], {}, []

    def close(k):
        totals[k] = jobs[k].close()
        out = pltpu.make_async_copy(totals.at[k], (gate_out, up_out)[k], out_sem.at[k])
        out.start()
        outs.append(out)

    for k in range(3):
        job = PlaneSum(
            t, cores.at[k], far.at[k], near.at[k], sums.at[k], totals.at[k], (fetched, core_sem)
        )
        jobs.append(job)
        if k == 2:
            for copy in [left_copies[1]] + right_copies[2]:
                copy.start()
            left_copies[1].wait()
        for copy in right_copies[k]:
            copy.wait()

        def partial(j):
            block = stretch(flip(me, j), depth)
            return lax.dot_general(
                left[:, block], rights[k % 2], OVER_ROWS, preferred_element_type=f32
            )

        for j in (7, 5, 3, 1):
            if j in odd_copies:
                t.release(odd_copies[j])
            odd[j // 2] = partial(j).astype(bf16)
            odd_copies[j] = job.send_odd(j, odd.at[j // 2])
        if k:
            jobs[k - 1].pass_on()
        for j in (6, 2, 4, 0):
            job.arrive(j)
            job.even(j, partial(j))
        if k:
            close(k - 1)
    jobs[2].pass_on()
    down_out[...] = jobs[2].close().astype(bf16)
    for copy in outs:
        copy.wait()


def feed_forward_row(h, dy, dy_rest, gate, up, down_own, down_rest, top):
    rows, model = h.shape
    units = gate.shape[1]
    tiles = units // TILE
    depth = model // 8
    wide = jax.ShapeDtypeStruct((4 * rows, units), bf16)
    low = jax.ShapeDtypeStruct((rows, model), bf16)
    high = jax.ShapeDtypeStruct((rows, model), f32)
    summed = jax.ShapeDtypeStruct((depth, units), f32)
    dma = pltpu.SemaphoreType.DMA
    return remote_call(
        feed_forward_row_body,
        [wide, wide, wide, jax.ShapeDtypeStruct((4 * rows, model), bf16)]
        + [high, jax.ShapeDtypeStruct((3, rows, model), bf16), high]
        + [jax.ShapeDtypeStruct((3, 4, depth, model), bf16), low, summed, summed]
        + [jax.ShapeDtypeStruct((depth, model), bf16), jax.ShapeDtypeStruct(top.shape, f32)],
        [ANY] * 6 + [VMEM] + [ANY] * 4 + [VMEM] * 2,
        [VMEM] + [ANY] * 6 + [VMEM],
        [
            pltpu.VMEM((3, rows, model), bf16),
            pltpu.VMEM((3, rows, model), bf16),
            pltpu.VMEM((3, rows, model), bf16),
            pltpu.VMEM((3, depth, model), bf16),
            pltpu.VMEM((3, 2, depth, model), bf16),
        ]
        + small_scratch(top.shape)
        + [
            dma((2, tiles)),
            dma((tiles, 4)),
            dma((4,)),
            dma((4,)),
            dma((2, 3)),
            dma((4,)),
            dma((2,)),
            dma((2,)),
            dma((2,)),
            dma((2,)),
            dma((5,)),
            dma((3,)),
        ],
        3 + 5 + 1 + 3 * 10,
        2,
        flops=54 * rows * model * units,
    )(h, dy, dy_rest, gate, up, down_own, down_rest, top)


class RowSum:
    def __init__(self, transfers, total, sent, landed, columns):
        self.total, self.landed, self.columns = total, landed, columns
        self.over = []
        for d in (1, 2, 3):
            sent[d - 1] = total[:, columns(d)].astype(bf16)
            self.over.append(transfers.start(sent.at[d - 1], landed.at[d - 1], fsdp=d))

    def close(self):
        total = self.total[:, self.columns(0)]
        for d in range(3):
            self.over[d].wait_recv()
            total = total + self.landed[d].astype(f32)
        return total


def attention_back_body(
    db_ref, attended_ref, qkv_ref, cosine_ref, sine_ref, natural_ref, begin_ref, key_natural_ref,
    kv_ref, o_ref, output_rest, y_ref,
    dq_out, dkv_out, output_out, y_land,
    kvs, o_own, outputs, head_grad, odd,
    cores, far, near, sums, totals,
    kv_cores, kv_far, kv_near, kv_sums, kv_totals,
    row_send, row_land, load_sem, send, recv,
):
    me, place = lax.axis_index("ctx"), lax.axis_index("fsdp")
    rows, model = db_ref.shape
    depth = cores.shape[2]
    width = o_own.shape[1]
    rounds = key_natural_ref.shape[0]
    blk = rows // rounds
    heads = kvs.shape[3] // (2 * HEAD_SIZE)
    loads = [
        pltpu.make_async_copy(src, dst, load_sem.at[i])
        for i, (src, dst) in enumerate(((o_ref, o_own), (output_rest, outputs), (kv_ref, kvs)))
    ]
    for load in loads:
        load.start()
    greet((1, 2, 4), (1, 2, 3))
    t = Transfers(send, recv)

    def of_slot(j):
        return pl.ds(pl.multiple_of(flip(me, j) * depth, depth), depth)

    def shard(d):
        return pl.ds(pl.multiple_of(flip(place, d) * width, width), width)

    y_copy = t.start(y_ref.at[1], y_land, fsdp=2)
    job = PlaneSum(t, cores.at[0], far.at[0], near.at[0], sums.at[0], totals.at[0])

    def partial(j):
        return lax.dot_general(
            attended_ref[:, of_slot(j)], db_ref[...], OVER_ROWS, preferred_element_type=f32
        )

    for j in (7, 5, 3, 1):
        odd[j // 2] = partial(j).astype(bf16)
        job.send_odd(j, odd.at[j // 2])
    for j in (6, 2, 4, 0):
        job.arrive(j)
        job.even(j, partial(j))

    loads[0].wait()
    loads[1].wait()
    for j in range(8):
        total = lax.dot_general(
            db_ref[:, shard(0)], o_own[of_slot(j)], OVER_COLUMNS, preferred_element_type=f32
        )
        for d in (1, 2, 3):
            total += lax.dot_general(
                db_ref[:, shard(d)], outputs[d - 1, j], OVER_COLUMNS, preferred_element_type=f32
            )
        head_grad[:, of_slot(j)] = total.astype(bf16)
    loads[2].wait()
    cosine, sine = cosine_ref[...], -sine_ref[...]

    def attend_heads(d):
        def step(i, carry):
            r, h = lax.div(i, heads), lax.rem(i, heads)
            here = pl.ds(pl.multiple_of(r * blk, blk), blk)
            first = pl.multiple_of(d * heads * UNIT + h * UNIT, UNIT)
            query = stacked_heads(qkv_ref[here, pl.ds(first, REPEAT * HEAD_SIZE)])
            cols = pl.ds(pl.multiple_of(h * 2 * HEAD_SIZE, 2 * HEAD_SIZE), 2 * HEAD_SIZE)
            both = kvs[d, :, here, cols].reshape(8 * blk, 2 * HEAD_SIZE)
            keys, values = both[:, :HEAD_SIZE], both[:, HEAD_SIZE:]
            natural = key_natural_ref[r]
            allowed = (natural >= begin_ref[here]) & (natural <= natural_ref[here])
            allowed = jnp.concatenate([allowed] * REPEAT, 0)
            spot = flip(place, d) * heads + h
            spot_cols = pl.ds(
                pl.multiple_of(spot * REPEAT * HEAD_SIZE, REPEAT * HEAD_SIZE), REPEAT * HEAD_SIZE
            )
            grad = stacked_heads(head_grad[here, spot_cols])
            probs, _ = probabilities(query, keys, allowed)
            low = probs.astype(bf16)
            grad_probs = lax.dot_general(grad, values, OVER_COLUMNS, preferred_element_type=f32)
            delta = jnp.sum(low.astype(f32) * grad_probs, 1, keepdims=True)
            score_grad = (probs * (grad_probs - delta)).astype(bf16)
            query_grad = jnp.dot(score_grad, keys, preferred_element_type=f32) * SCALE
            turn = cosine_ref[here], -sine_ref[here]
            first = pl.multiple_of((d * heads + h) * REPEAT * HEAD_SIZE, REPEAT * HEAD_SIZE)
            dq_out[here, pl.ds(first, REPEAT * HEAD_SIZE)] = jnp.concatenate(
                [rotate(query_grad[i * blk : (i + 1) * blk], *turn) for i in range(REPEAT)], 1
            ).astype(bf16)
            key_grad = lax.dot_general(score_grad, query, OVER_ROWS, preferred_element_type=f32)
            value_grad = lax.dot_general(low, grad, OVER_ROWS, preferred_element_type=f32)
            both = jnp.concatenate([key_grad * SCALE, value_grad], 1).astype(bf16)
            kvs[d, :, here, cols] = both.reshape(8, blk, 2 * HEAD_SIZE)
            return carry

        lax.fori_loop(0, rounds * heads, step, 0)

    kv_jobs = [
        PlaneSum(t, kv_cores.at[k], kv_far.at[k], kv_near.at[k], kv_sums.at[k], kv_totals.at[k])
        for k in range(2)
    ]

    def send_half(k):
        half = pl.ds(2 * k, 2)
        for j in (7, 3, 5, 1):
            kv_jobs[k].send_odd(j, kvs.at[half, j])
        for j in (6, 2, 4, 0):
            kv_jobs[k].arrive(j)
            kv_jobs[k].even(j, kvs[half, j].astype(f32))

    def take_half(k):
        total = kv_jobs[k].close()
        for i in range(2):
            for h in range(heads):
                first = 2 * h * HEAD_SIZE
                middle = first + HEAD_SIZE
                to = ((2 * k + i) * heads + h) * 2 * HEAD_SIZE
                turned = rotate(total[i, :, first:middle], cosine, sine)
                value = total[i, :, middle : middle + HEAD_SIZE]
                dkv_out[:, to : to + 2 * HEAD_SIZE] = jnp.concatenate([turned, value], 1).astype(bf16)

    attend_heads(0)
    job.pass_on()
    attend_heads(1)
    send_half(0)
    attend_heads(2)
    kv_jobs[0].pass_on()
    attend_heads(3)
    send_half(1)
    totals[0] = job.close()
    row = RowSum(t, totals.at[0], row_send, row_land, shard)
    kv_jobs[1].pass_on()
    take_half(0)
    output_out[...] = row.close()
    take_half(1)
    y_copy.wait_recv()
    t.finish()


def attention_back(db, attended, qkv, cosine, sine, natural, begin, key_natural, kv, output, output_rest, y_rest):
    rows, model = db.shape
    depth, width = model // 8, output.shape[1]
    kv_width = kv.shape[3]
    return remote_call(
        attention_back_body,
        [
            jax.ShapeDtypeStruct((rows, model), bf16),
            jax.ShapeDtypeStruct((rows, 4 * kv_width), bf16),
            jax.ShapeDtypeStruct((depth, width), f32),
            jax.ShapeDtypeStruct((rows, model), bf16),
        ],
        [VMEM] * 3 + [ANY],
        [VMEM] * 8 + [ANY] * 4,
        [
            pltpu.VMEM(kv.shape, bf16),
            pltpu.VMEM(output.shape, bf16),
            pltpu.VMEM(output_rest.shape, bf16),
            pltpu.VMEM((rows, model), bf16),
            pltpu.VMEM((4, depth, model), bf16),
        ]
        + plane_sum_scratch(1, depth, model)
        + plane_sum_scratch(2, 2, rows, kv_width)
        + [pltpu.VMEM((3, depth, width), bf16)] * 2
        + [pltpu.SemaphoreType.DMA((3,))],
        3 * 10 + 3 + 1,
        4,
        flops=20 * rows * model * model,
    )(db, attended, qkv, cosine, sine, natural, begin, key_natural, kv, output, output_rest, y_rest)


def unit_grads_body(
    h_ref, dq_ref, dkv_ref, x_ref, term_ref, q_ref, k_ref, v_ref, unit_rest, y_ref,
    query_out, key_out, value_out, back_out, gain_out, y_land,
    odd, q_own, k_own, v_own, units, cores, far, near, sums, totals, row_send, row_land,
    blocks, land, load_sem, unit_sem, send, recv,
):
    me = lax.axis_index("ctx")
    depth = cores.shape[2]
    width = row_land.shape[3]
    heads = k_own.shape[1] // HEAD_SIZE
    loads = [
        pltpu.make_async_copy(src, dst, load_sem.at[i])
        for i, (src, dst) in enumerate(((q_ref, q_own), (k_ref, k_own), (v_ref, v_own)))
    ]
    unit_loads = [
        pltpu.make_async_copy(unit_rest.at[d], units.at[d % 2], unit_sem.at[d]) for d in range(3)
    ]
    for load in loads + unit_loads[:2]:
        load.start()
    greet((1, 2, 4), (1, 2, 3))
    t = Transfers(send, recv)
    y_copy = t.start(y_ref.at[2], y_land, fsdp=3)
    jobs, odd_copies = [], {}

    def of_slot(j):
        return pl.ds(pl.multiple_of(flip(me, j) * depth, depth), depth)

    for k, right in enumerate((dq_ref, dkv_ref)):
        job = PlaneSum(t, cores.at[k], far.at[k], near.at[k], sums.at[k], totals.at[k])
        jobs.append(job)

        def partial(j):
            return lax.dot_general(
                h_ref[:, of_slot(j)], right[...], OVER_ROWS, preferred_element_type=f32
            )

        for j in (7, 5, 3, 1):
            if j in odd_copies:
                t.release(odd_copies[j])
            odd[j // 2] = partial(j).astype(bf16)
            odd_copies[j] = job.send_odd(j, odd.at[j // 2])
        for j in (6, 2, 4, 0):
            job.arrive(j)
            job.even(j, partial(j))

    def grads(d):
        query = dq_ref[:, d * width : (d + 1) * width]
        pairs = dkv_ref[:, d * width : (d + 1) * width]
        parts = [pairs[:, i * HEAD_SIZE : (i + 1) * HEAD_SIZE] for i in range(2 * heads)]
        return jnp.concatenate([query] + parts[::2] + parts[1::2], 1)

    def back(d):
        grad = grads(d)
        for j in range(8):
            cols = of_slot(j)
            if d == 0:
                weight = jnp.concatenate([w[cols] for w in (q_own, k_own, v_own)], 1)
                back_out[:, cols] = lax.dot_general(
                    grad, weight, OVER_COLUMNS, preferred_element_type=f32
                )
            else:
                back_out[:, cols] += lax.dot_general(
                    grad, units[(d - 1) % 2, j], OVER_COLUMNS, preferred_element_type=f32
                )

    for load in loads:
        load.wait()
    back(0)
    jobs[0].pass_on()
    unit_loads[0].wait()
    back(1)
    unit_loads[2].start()
    unit_loads[1].wait()
    back(2)
    jobs[1].pass_on()
    unit_loads[2].wait()
    back(3)
    x = x_ref[...].astype(f32)
    unit = x * lax.rsqrt(jnp.mean(x * x, 1, keepdims=True) + epsilon)
    gains = SmallReduce(
        t, blocks, land, jnp.add, ((0, 1), (0, 2), (2, 0), (4, 0), (1, 0))
    )
    blocks[0] = jnp.concatenate(
        [jnp.sum(back_out[...] * unit, 0, keepdims=True), term_ref[1:8]], 0
    )
    gains.on(0)

    def columns(d):
        return pl.ds(d * width, width)

    totals[0] = jobs[0].close()
    gains.on(1)
    first = RowSum(t, totals.at[0], row_send.at[0], row_land.at[0], columns)
    gains.on(2)
    totals[1] = jobs[1].close()
    second = RowSum(t, totals.at[1], row_send.at[1], row_land.at[1], columns)
    gains.on(3)
    gains.on(4)
    query_out[...] = first.close()
    gains.on(5)
    gain_out[...] = blocks[5]
    total = second.close()
    for h in range(heads):
        start = 2 * h * HEAD_SIZE
        here = slice(h * HEAD_SIZE, (h + 1) * HEAD_SIZE)
        key_out[:, here] = total[:, start : start + HEAD_SIZE]
        value_out[:, here] = total[:, start + HEAD_SIZE : start + 2 * HEAD_SIZE]
    y_copy.wait_recv()
    t.finish()


def unit_grads(h, dq, dkv, x, terms, query, key, value, rest, y_rest):
    rows, model = h.shape
    depth, width = model // 8, model // 4
    wide = jax.ShapeDtypeStruct((depth, width), f32)
    half = jax.ShapeDtypeStruct((depth, width // 2), f32)
    dma = pltpu.SemaphoreType.DMA
    return remote_call(
        unit_grads_body,
        [wide, half, half, jax.ShapeDtypeStruct((rows, model), f32)]
        + [jax.ShapeDtypeStruct(terms.shape, f32), jax.ShapeDtypeStruct((rows, model), bf16)],
        [VMEM] * 5 + [ANY],
        [VMEM] * 5 + [ANY] * 5,
        [
            pltpu.VMEM((4, depth, model), bf16),
            pltpu.VMEM(query.shape, bf16),
            pltpu.VMEM(key.shape, bf16),
            pltpu.VMEM(value.shape, bf16),
            pltpu.VMEM((2,) + rest.shape[1:], bf16),
        ]
        + plane_sum_scratch(2, depth, model)
        + [pltpu.VMEM((2, 3, depth, width), bf16)] * 2
        + small_scratch(terms.shape)
        + [dma((3,)), dma((3,))],
        2 * (10 + 3) + 5 + 1,
        5,
        flops=12 * rows * model * model,
    )(h, dq, dkv, x, terms, query, key, value, rest, y_rest)


def token_layout(length_row, block_slots, block_size):
    count_blocks = block_slots.shape[0]
    owner_block = jnp.argmax(
        block_slots[None, :] == jnp.arange(count_blocks, dtype=jnp.int32)[:, None], 1
    ).astype(jnp.int32)
    row_index = jnp.arange(count_blocks * block_size, dtype=jnp.int32)
    plain_order = jnp.repeat(owner_block, block_size) * block_size + row_index % block_size
    seq_ends = jnp.cumsum(length_row)
    seq_starts = seq_ends - length_row
    document_list = jnp.sum((plain_order[:, None] >= seq_ends[None, :]).astype(jnp.int32), 1)
    matches = document_list[:, None] == jnp.arange(length_row.shape[0], dtype=jnp.int32)[None, :]
    begins = jnp.sum(jnp.where(matches, seq_starts[None, :], 0), 1)
    return plain_order, begins


def rms_scale(value):
    return lax.rsqrt(jnp.mean(value * value, -1, keepdims=True) + epsilon)


def norm_back(grad_unit, unit_rows, scale_rows):
    return scale_rows * (grad_unit - unit_rows * jnp.mean(grad_unit * unit_rows, -1, keepdims=True))


def product(left, right):
    return jnp.dot(left, right, preferred_element_type=f32)


def product_t(left, right):
    return lax.dot_general(left, right, (((1,), (1,)), ((), ())), preferred_element_type=f32)


def over_rows(left, right):
    return lax.dot_general(left, right, (((0,), (0,)), ((), ())), preferred_element_type=f32)


def column_blocks(value, count, places):
    width = value.shape[1] // count
    return jnp.concatenate(
        [lax.dynamic_slice_in_dim(value, place * width, width, 1) for place in places], 1
    )


def gather_rows(piece, fsdp_place, ctx_count):
    count = lax.axis_size("fsdp")
    parts = [piece] + [swap(piece, "fsdp", d) for d in range(1, count)]
    return jnp.concatenate(by_place(parts, fsdp_place), 1)


def weight_grad_sum(left, right, me, count):
    depth = left.shape[1] // count
    full = over_rows(column_blocks(left, count, [me ^ j for j in range(count)]), right)
    return sum_halving(full.astype(bf16).reshape(count, depth, right.shape[1]), "ctx")


def down_grad_sum(hidden, grad, me, count, fsdp_count):
    bands = count // fsdp_count
    band, column = me // fsdp_count, me % fsdp_count
    depth = hidden.shape[1] // bands
    width = grad.shape[1] // fsdp_count
    left = column_blocks(hidden, bands, [band ^ j for j in range(bands)])
    right = column_blocks(grad, fsdp_count, [column ^ j for j in range(fsdp_count)])
    full = over_rows(left, right).astype(bf16).reshape(bands, depth, fsdp_count, width)
    return sum_halving(full.transpose(0, 2, 1, 3).reshape(count, depth, width), "ctx")


def clipped(weight, multiplier):
    columns = weight.shape[1]
    head_index = (
        lax.axis_index("fsdp") * columns + jnp.arange(columns, dtype=jnp.int32)
    ) // HEAD_SIZE
    matches = head_index[:, None] == jnp.arange(multiplier.shape[0], dtype=jnp.int32)[None, :]
    column_factor = jnp.sum(jnp.where(matches, multiplier[None, :], 0.0), 1)
    return (weight.astype(f32) * column_factor[None, :]).astype(bf16)


def gain_sum(term, me, place, count, fsdp_count):
    table = term.reshape(count, fsdp_count, -1)
    table = jnp.stack(by_place([table[i] for i in range(count)], me))
    mine = sum_halving(table, "ctx")
    mine = jnp.stack(by_place([mine[i] for i in range(fsdp_count)], place))
    return sum_halving(mine, "fsdp")


def attention_layout(seq_lengths, block_perm, rows):
    count, me = lax.axis_size("ctx"), lax.axis_index("ctx")
    rounds = block_perm.shape[0] // count
    blk = rows // rounds
    plain_order, begins = token_layout(seq_lengths[0], block_perm, blk)
    natural = lax.dynamic_slice_in_dim(plain_order, me * rows, rows)
    begin = lax.dynamic_slice_in_dim(begins, me * rows, rows)
    half_dim = HEAD_SIZE // 2
    exponent = jnp.arange(half_dim, dtype=f32) * (2.0 / HEAD_SIZE)
    inverse = rope_base ** (-exponent)
    angles = (natural - begin).astype(f32)[:, None] * inverse[None, :]
    cosine = jnp.concatenate([jnp.cos(angles)] * 2, 1)
    sine = jnp.concatenate([-jnp.sin(angles), jnp.sin(angles)], 1)
    order = plain_order.reshape(count, rounds, blk)
    order = jnp.stack(by_place([order[i] for i in range(count)], me), 1)
    return natural[:, None], begin[:, None], order.reshape(rounds, 1, count * blk), cosine, sine


def on_device(
    hidden_in,
    out_grad,
    seq_lengths,
    block_perm,
    first_gain,
    query_weight,
    key_matrix,
    value_matrix,
    output_weight,
    second_gain,
    gate_weight,
    up_weight,
    down_weight,
    clip_limit,
):
    rows, model = hidden_in.shape[1], hidden_in.shape[2]
    count, fsdp_count = lax.axis_size("ctx"), lax.axis_size("fsdp")
    me, place = lax.axis_index("ctx"), lax.axis_index("fsdp")
    me_ref = me.astype(jnp.int32).reshape(1)
    depth = model // count
    zero = jnp.zeros((1,), jnp.int32)
    shard_heads = KEY_VALUE_HEADS // fsdp_count

    def own_rows(weight):
        return lax.dynamic_slice_in_dim(weight, me * depth, depth, 0)

    unit_rows = jnp.concatenate(
        [
            own_rows(query_weight).reshape(depth, shard_heads, REPEAT, HEAD_SIZE),
            own_rows(key_matrix).reshape(depth, shard_heads, 1, HEAD_SIZE),
            own_rows(value_matrix).reshape(depth, shard_heads, 1, HEAD_SIZE),
        ],
        2,
    ).reshape(depth, shard_heads * UNIT)
    unit_rows = gather_rows(unit_rows, place, count)
    unit_slots = gather_ctx(unit_rows)
    gains = jnp.stack([first_gain, second_gain])
    gains = jnp.concatenate(
        by_place([gains] + [swap(gains, "fsdp", d) for d in range(1, fsdp_count)], place), 1
    ).astype(f32)
    first_full, second_full = gains[0], gains[1]
    output_rows = gather_rows(own_rows(output_weight), place, count)
    output_slots = gather_ctx(output_rows)

    hidden_width = gate_weight.shape[1]
    down_depth = hidden_width // count

    def down_piece(d):
        first = (place ^ d) * hidden_width + me * down_depth
        return lax.dynamic_slice_in_dim(down_weight, first, down_depth, 0)

    down_rows = [down_piece(0)] + [
        swap(down_piece(d), "fsdp", d) for d in range(1, fsdp_count)
    ]
    down_slots = gather_ctx(jnp.concatenate(by_place(down_rows, place), 1))

    natural_column, begin_column, key_natural, cosine, sine = attention_layout(
        seq_lengths, block_perm, rows
    )
    half_dim = HEAD_SIZE // 2

    tokens = hidden_in.reshape(rows, model).astype(f32)
    scale_one = rms_scale(tokens)
    unit_one = tokens * scale_one
    normalized = (unit_one * first_full).astype(bf16)
    qkv = slot_matmul(normalized, unit_slots, me_ref, UNIT, bf16, (cosine, sine))
    kv_local = qkv.reshape(rows, KEY_VALUE_HEADS, UNIT)[:, :, REPEAT * HEAD_SIZE :].reshape(
        rows, KEY_VALUE_HEADS * 2 * HEAD_SIZE
    )
    kv_slots = gather_ctx(kv_local)
    attended, best = attend(zero, natural_column, begin_column, key_natural, qkv, kv_slots)
    head_max = jnp.max(best[:, :, :REPEAT, 0], 0).reshape(QUERY_HEADS)
    for mask in bits_down(count):
        head_max = jnp.maximum(head_max, swap(head_max, "ctx", mask))
    for mask in bits_down(fsdp_count):
        head_max = jnp.maximum(head_max, swap(head_max, "fsdp", mask))
    residual = tokens + slot_matmul(attended, output_slots, me_ref, 512, f32)
    scale_two = rms_scale(residual)
    unit_two = residual * scale_two
    normed_two = (unit_two * second_full).astype(bf16)

    grad_out = out_grad.reshape(rows, model)
    others = range(1, fsdp_count)
    grads = [grad_out] + [swap(grad_out, "fsdp", d) for d in others]
    normed = [normed_two] + [swap(normed_two, "fsdp", d) for d in others]
    hidden_parts, gate_parts, up_parts, sums, backs = [], [], [], [], []
    for d in range(fsdp_count):
        grad_hidden = slot_matmul_t(grads[d], down_slots, me_ref, 512, f32)
        gate_act = product(normed[d], gate_weight)
        up_proj = product(normed[d], up_weight)
        sigmoid = jax.nn.sigmoid(gate_act)
        hidden = (gate_act * sigmoid * up_proj).astype(bf16)
        grad_gate = (
            grad_hidden * up_proj * sigmoid * (1.0 + gate_act * (1.0 - sigmoid))
        ).astype(bf16)
        grad_up = (grad_hidden * gate_act * sigmoid).astype(bf16)
        hidden_parts.append(hidden)
        gate_parts.append(grad_gate)
        up_parts.append(grad_up)
        backs.append(product_t(grad_gate, gate_weight) + product_t(grad_up, up_weight))
        sums.append(slot_matmul(hidden, down_slots, me_ref, 512, f32 if d == 0 else bf16))
    grad_normed_two = sum_fsdp(backs)
    result = (residual + sum_fsdp(sums)).astype(bf16)

    second_term = jnp.sum(grad_normed_two * unit_two, 0)
    grad_residual = grad_out.astype(f32) + norm_back(
        grad_normed_two * second_full, unit_two, scale_two
    )
    grad_branch = grad_residual.astype(bf16)
    head_grad = slot_matmul_t(grad_branch, output_slots, me_ref, 512, bf16)
    query_grad, *dkv_slots = attend_back(
        zero, natural_column, begin_column, key_natural, cosine, sine, qkv, head_grad, kv_slots
    )
    dkv = sum_halving(dkv_slots[0], "ctx")
    dkv = dkv.reshape(rows, KEY_VALUE_HEADS, 2, HEAD_SIZE)
    grad_key = dkv[:, :, 0]
    first, second = grad_key[..., :half_dim], grad_key[..., half_dim:]
    cos, sin = cosine[:, None, :half_dim], sine[:, None, half_dim:]
    grad_key = jnp.concatenate([first * cos + second * sin, second * cos - first * sin], -1)
    dqkv = jnp.concatenate(
        [
            query_grad.reshape(rows, KEY_VALUE_HEADS, REPEAT, HEAD_SIZE),
            grad_key[:, :, None].astype(bf16),
            dkv[:, :, 1:].astype(bf16),
        ],
        2,
    ).reshape(rows, KEY_VALUE_HEADS * UNIT)
    grad_normed_one = slot_matmul_t(dqkv, unit_slots, me_ref, 512, f32)
    first_term = jnp.sum(grad_normed_one * unit_one, 0)
    grad_input = grad_residual + norm_back(grad_normed_one * first_full, unit_one, scale_one)

    hidden_all = jnp.concatenate(hidden_parts, 0)
    normed_all = jnp.concatenate(normed, 0)
    grads_all = jnp.concatenate(grads, 0)
    down_sum = down_grad_sum(hidden_all, grads_all, me, count, fsdp_count).astype(bf16)
    bands = count // fsdp_count
    places = [
        (c * fsdp_count + f, (bands * f + c // fsdp_count) * fsdp_count + c % fsdp_count)
        for c in range(count)
        for f in range(fsdp_count)
    ]
    down_grad = lax.ppermute(down_sum, ("ctx", "fsdp"), places).astype(f32)
    gate_grad = weight_grad_sum(normed_all, jnp.concatenate(gate_parts, 0), me, count)
    up_grad = weight_grad_sum(normed_all, jnp.concatenate(up_parts, 0), me, count)

    def over_fsdp(summed):
        width = summed.shape[1] // fsdp_count
        return sum_fsdp(
            [
                lax.dynamic_slice_in_dim(summed, (place ^ d) * width, width, 1)
                for d in range(fsdp_count)
            ]
        )

    output_grad = over_fsdp(weight_grad_sum(attended, grad_branch, me, count))
    unit_grad = over_fsdp(weight_grad_sum(normalized, dqkv, me, count))
    unit_grad = unit_grad.reshape(depth, shard_heads, REPEAT + 2, HEAD_SIZE)
    query_out = unit_grad[:, :, :REPEAT].reshape(depth, -1)
    key_out = unit_grad[:, :, REPEAT].reshape(depth, -1)
    value_out = unit_grad[:, :, REPEAT + 1].reshape(depth, -1)

    first_out = gain_sum(first_term, me, place, count, fsdp_count)
    second_out = gain_sum(second_term, me, place, count, fsdp_count)
    multiplier = jnp.sqrt(clip_limit / jnp.maximum(head_max, clip_limit))
    key_ratio = jnp.min(multiplier.reshape(KEY_VALUE_HEADS, REPEAT), 1)
    return (
        result.reshape(1, rows, model),
        grad_input.astype(bf16).reshape(1, rows, model),
        first_out,
        query_out,
        key_out,
        value_out,
        output_grad,
        second_out,
        gate_grad,
        up_grad,
        down_grad,
        head_max,
        clipped(query_weight, multiplier),
        clipped(key_matrix, key_ratio),
    )


def on_row_of_chips(
    hidden_in,
    out_grad,
    seq_lengths,
    block_perm,
    first_gain,
    query_weight,
    key_matrix,
    value_matrix,
    output_weight,
    second_gain,
    gate_weight,
    up_weight,
    down_weight,
    clip_limit,
):
    rows, model = hidden_in.shape[1], hidden_in.shape[2]
    me, place = lax.axis_index("ctx"), lax.axis_index("fsdp")
    natural, begin, key_natural, cosine, sine = attention_layout(seq_lengths, block_perm, rows)
    tokens_low = hidden_in.reshape(rows, model)
    grad_out = out_grad.reshape(rows, model)
    gains = jnp.pad(jnp.stack([first_gain, second_gain]).astype(f32), ((0, 6), (0, 0)))
    (
        normalized,
        qkv,
        attended,
        best,
        residual,
        normed_two,
        all_gains,
        kv_all,
        unit_rest,
        output_rest,
        down_rest,
        dy_rest,
    ) = attention_row(
        tokens_low,
        gains,
        cosine,
        sine,
        natural,
        begin,
        key_natural,
        query_weight,
        key_matrix,
        value_matrix,
        output_weight,
        down_weight,
        grad_out,
    )
    full = jnp.concatenate(by_place([all_gains[d] for d in range(4)], place), 1)
    first_full, second_full = full[0], full[1]
    tokens = tokens_low.astype(f32)
    scale_one = rms_scale(tokens)
    unit_one = tokens * scale_one
    scale_two = rms_scale(residual)
    unit_two = residual * scale_two
    top = jnp.max(best[:, :, :REPEAT, 0], 0)
    top = jnp.pad(top, ((0, 0), (0, 128 - REPEAT)))

    _, _, _, _, y_own, y_rest, grad_normed_two, _, y_near, gate_grad, up_grad, down_sum, top = (
        feed_forward_row(
            normed_two,
            grad_out,
            dy_rest,
            gate_weight,
            up_weight,
            down_weight,
            down_rest,
            top,
        )
    )
    head_max = top[:, :REPEAT].reshape(QUERY_HEADS)
    second_term = jnp.sum(grad_normed_two * unit_two, 0)
    grad_residual = grad_out.astype(f32) + norm_back(
        grad_normed_two * second_full, unit_two, scale_two
    )
    grad_branch = grad_residual.astype(bf16)
    width = model // 4
    moved, pieces = [], []
    for k in range(4):
        piece = lax.dynamic_slice_in_dim(down_sum, ((me % 4) ^ k) * width, width, 1)
        pieces.append(piece)
    attended, pieces = lax.optimization_barrier((attended, pieces))
    for k, piece in enumerate(pieces):
        pairs = [
            (c * 4 + f, (2 * f + c // 4) * 4 + (c % 4 ^ k)) for c in range(8) for f in range(4)
        ]
        moved.append(lax.ppermute(piece, ("ctx", "fsdp"), pairs))
    down_grad = jnp.concatenate(by_place(moved, place), 0).astype(f32)

    query_grad, dkv, output_out, y_second = attention_back(
        grad_branch,
        attended,
        qkv,
        cosine,
        sine,
        natural,
        begin,
        key_natural,
        kv_all,
        output_weight,
        output_rest,
        y_rest,
    )
    terms = jnp.pad(second_term[None], ((1, 6), (0, 0)))
    query_out, key_out, value_out, grad_normed_one, terms, y_third = unit_grads(
        normalized,
        query_grad,
        dkv,
        tokens_low,
        terms,
        query_weight,
        key_matrix,
        value_matrix,
        unit_rest,
        y_rest,
    )
    landed = y_near.astype(f32) + y_second.astype(f32) + y_third.astype(f32)
    result = (residual + y_own + landed).astype(bf16)
    grad_input = grad_residual + norm_back(grad_normed_one * first_full, unit_one, scale_one)
    terms = lax.dynamic_slice_in_dim(
        terms[:2], (me * 4 + place) * (model // 32), model // 32, 1
    )
    first_out, second_out = terms[0], terms[1]
    multiplier = jnp.sqrt(clip_limit / jnp.maximum(head_max, clip_limit))
    key_ratio = jnp.min(multiplier.reshape(KEY_VALUE_HEADS, REPEAT), 1)
    return (
        result.reshape(1, rows, model),
        grad_input.astype(bf16).reshape(1, rows, model),
        first_out,
        query_out,
        key_out,
        value_out,
        output_out,
        second_out,
        gate_grad,
        up_grad,
        down_grad,
        head_max,
        clipped(query_weight, multiplier),
        clipped(key_matrix, key_ratio),
    )


def solution(mesh):
    shard, whole = P(None, "fsdp"), P()
    token, block = P("fsdp", "ctx", None), P("ctx", "fsdp")
    gain = P(("ctx", "fsdp"))
    chips = mesh.shape["ctx"] == 8 and mesh.shape["fsdp"] == 4
    return jax.shard_map(
        on_row_of_chips if chips else on_device,
        mesh=mesh,
        in_specs=(token, token, P("fsdp", None), whole, P("fsdp"))
        + (shard,) * 4
        + (P("fsdp"),)
        + (shard,) * 3
        + (whole,),
        out_specs=(token, token, gain)
        + (block,) * 4
        + (gain,)
        + (block,) * 3
        + (whole, shard, shard),
        check_vma=False,
    )
```

```python
import functools
import math

import jax
import jax.numpy as jnp
from jax import lax
from jax.experimental import pallas as pl
from jax.experimental.pallas import tpu as pltpu
from jax.sharding import PartitionSpec as P

QUERY_HEADS = 16
KEY_VALUE_HEADS = 8
HEAD_SIZE = 128
REPEAT = QUERY_HEADS // KEY_VALUE_HEADS
UNIT = (REPEAT + 2) * HEAD_SIZE

epsilon = 1e-06
rope_base = 1000000.0
hidden_fill_value = -1e30
bf16 = jnp.bfloat16
f32 = jnp.float32
SCALE = 1.0 / math.sqrt(HEAD_SIZE)


def swap(value, axis, mask):
    size = lax.axis_size(axis)
    return lax.ppermute(value, axis, [(i, i ^ mask) for i in range(size)])


def bits_down(size):
    mask = size // 2
    while mask:
        yield mask
        mask //= 2


def by_place(items, me):
    mask = 1
    while mask < len(items):
        odd = (me & mask) != 0
        items = [jnp.where(odd, items[j ^ mask], items[j]) for j in range(len(items))]
        mask *= 2
    return items


def gather_ctx(block):
    size = lax.axis_size("ctx")
    whole = block[None]
    mask = 1
    while mask < size:
        whole = jnp.concatenate([whole, swap(whole, "ctx", mask)], 0)
        mask *= 2
    return [whole]


def sum_halving(slots, axis):
    for mask in bits_down(slots.shape[0]):
        keep = slots[:mask].astype(f32)
        slots = (keep + swap(slots[mask:], axis, mask).astype(f32)).astype(slots.dtype)
    return slots[0].astype(f32)


def sum_fsdp(pieces):
    total = pieces[0].astype(f32)
    for d in range(1, len(pieces)):
        total = total + swap(pieces[d].astype(bf16), "fsdp", d).astype(f32)
    return total


def params(flops, bytes_accessed):
    return dict(
        compiler_params=pltpu.CompilerParams(vmem_limit_bytes=48 * 2**20),
        cost_estimate=pl.CostEstimate(
            flops=flops, bytes_accessed=bytes_accessed, transcendentals=0
        ),
    )


def rotate(value, cosine, sine):
    return value * cosine + pltpu.roll(value, HEAD_SIZE // 2, 1) * sine


def slot_matmul_body(n_slots, parts, depth, rope, me_ref, x_ref, *refs):
    slot_refs = refs[:n_slots]
    out_ref = refs[-1]
    total = None
    for j in range(n_slots):
        for q in range(parts):
            owner = me_ref[0] ^ (j * parts + q)
            cols = pl.ds(pl.multiple_of(owner * depth, depth), depth)
            term = jnp.dot(x_ref[:, cols], slot_refs[j][q], preferred_element_type=f32)
            total = term if total is None else total + term
    if rope:
        cosine, sine = refs[n_slots][...], refs[n_slots + 1][...]
        parts_out = [
            rotate(total[:, i * HEAD_SIZE : (i + 1) * HEAD_SIZE], cosine, sine)
            for i in range(REPEAT + 1)
        ]
        total = jnp.concatenate(parts_out + [total[:, (REPEAT + 1) * HEAD_SIZE :]], 1)
    out_ref[...] = total.astype(out_ref.dtype)


def in_order(slots, me):
    whole = jnp.concatenate(slots, 0)
    whole = whole[me ^ jnp.arange(whole.shape[0], dtype=jnp.int32)]
    return whole.reshape(-1, whole.shape[2])


def in_order(slots, me):
    whole = jnp.concatenate(slots, 0)
    whole = whole[me ^ jnp.arange(whole.shape[0], dtype=jnp.int32)]
    return whole.reshape(-1, whole.shape[2])


def slot_matmul(x, slots, me, tile, out_dtype, tables=None):
    rows = x.shape[0]
    parts, depth, width = slots[0].shape
    if depth % 128:
        total = product(x, in_order(slots, me))
        if tables is None:
            return total.astype(out_dtype)
        total = total.reshape(rows, width // UNIT, REPEAT + 2, HEAD_SIZE)
        cosine, sine = (t[:, None, None] for t in tables)
        turned = total[:, :, : REPEAT + 1]
        turned = turned * cosine + jnp.roll(turned, HEAD_SIZE // 2, -1) * sine
        total = jnp.concatenate([turned, total[:, :, REPEAT + 1 :]], 2)
        return total.reshape(rows, width).astype(out_dtype)
    extra = [] if tables is None else list(tables)
    body = functools.partial(
        slot_matmul_body, len(slots), parts, depth, tables is not None
    )
    return pl.pallas_call(
        body,
        out_shape=jax.ShapeDtypeStruct((rows, width), out_dtype),
        grid_spec=pltpu.PrefetchScalarGridSpec(
            num_scalar_prefetch=1,
            grid=(width // tile,),
            in_specs=[pl.BlockSpec(x.shape, lambda i, me: (0, 0))]
            + [pl.BlockSpec((parts, depth, tile), lambda i, me: (0, 0, i))] * len(slots)
            + [pl.BlockSpec(e.shape, lambda i, me: (0, 0)) for e in extra],
            out_specs=pl.BlockSpec((rows, tile), lambda i, me: (0, i)),
        ),
        **params(2 * rows * x.shape[1] * width, 2 * x.shape[1] * width),
    )(me, x, *slots, *extra)


def slot_matmul_t_body(n_slots, parts, depth, me_ref, x_ref, *refs):
    slot_refs = refs[:n_slots]
    out_ref, total_ref = refs[n_slots], refs[n_slots + 1]
    step = pl.program_id(0)

    @pl.when(step == 0)
    def _():
        total_ref[...] = jnp.zeros_like(total_ref)

    x = x_ref[...]
    for j in range(n_slots):
        for q in range(parts):
            owner = me_ref[0] ^ (j * parts + q)
            cols = pl.ds(pl.multiple_of(owner * depth, depth), depth)
            total_ref[:, cols] += lax.dot_general(
                x, slot_refs[j][q], (((1,), (1,)), ((), ())), preferred_element_type=f32
            )

    @pl.when(step == pl.num_programs(0) - 1)
    def _():
        out_ref[...] = total_ref[...].astype(out_ref.dtype)


def slot_matmul_t(x, slots, me, tile, out_dtype):
    rows, width = x.shape
    parts, depth, _ = slots[0].shape
    height = parts * depth * len(slots)
    if depth % 128:
        return product_t(x, in_order(slots, me)).astype(out_dtype)
    return pl.pallas_call(
        functools.partial(slot_matmul_t_body, len(slots), parts, depth),
        out_shape=jax.ShapeDtypeStruct((rows, height), out_dtype),
        grid_spec=pltpu.PrefetchScalarGridSpec(
            num_scalar_prefetch=1,
            grid=(width // tile,),
            in_specs=[pl.BlockSpec((rows, tile), lambda i, me: (0, i))]
            + [pl.BlockSpec((parts, depth, tile), lambda i, me: (0, 0, i))]
            * len(slots),
            out_specs=pl.BlockSpec((rows, height), lambda i, me: (0, 0)),
            scratch_shapes=[pltpu.VMEM((rows, height), f32)],
        ),
        **params(2 * rows * height * width, 2 * height * width),
    )(me, x, *slots)


def keys_of(slot_refs):
    def column(i):
        parts = [
            r[..., i * HEAD_SIZE : (i + 1) * HEAD_SIZE].reshape(-1, HEAD_SIZE)
            for r in slot_refs
        ]
        return parts[0] if len(parts) == 1 else jnp.concatenate(parts, 0)

    return column(0), column(1)


def scores_of(qkv_ref, keys, natural_ref, start_ref, key_natural_ref):
    blk = qkv_ref.shape[0]
    query = jnp.concatenate(
        [qkv_ref[:, i * HEAD_SIZE : (i + 1) * HEAD_SIZE] for i in range(REPEAT)], 0
    )
    scores = (
        lax.dot_general(
            query, keys, (((1,), (1,)), ((), ())), preferred_element_type=f32
        )
        * SCALE
    )
    key_natural = key_natural_ref[0]
    allowed = (key_natural >= start_ref[...]) & (key_natural <= natural_ref[...])
    allowed = jnp.concatenate([allowed] * REPEAT, 0)
    scores = jnp.where(allowed, scores, hidden_fill_value)
    best = jnp.max(scores, 1, keepdims=True)
    exps = jnp.exp(scores - best)
    return query, exps * (1.0 / jnp.sum(exps, 1, keepdims=True)), best, blk


def attend_body(n_slots, place_ref, natural_ref, start_ref, key_natural_ref, qkv_ref, *refs):
    slot_refs, (out_ref, best_ref) = refs[:n_slots], refs[n_slots:]
    keys, values = keys_of(slot_refs)
    _, probs, best, blk = scores_of(qkv_ref, keys, natural_ref, start_ref, key_natural_ref)
    heads = jnp.dot(probs.astype(bf16), values, preferred_element_type=f32)
    out_ref[...] = jnp.concatenate(
        [heads[i * blk : (i + 1) * blk] for i in range(REPEAT)], 1
    ).astype(bf16)
    tops = [
        jnp.broadcast_to(jnp.max(best[i * blk : (i + 1) * blk], 0, keepdims=True), (1, 128))
        for i in range(REPEAT)
    ]
    best_ref[0, 0] = jnp.concatenate(tops + [jnp.zeros((8 - REPEAT, 128), f32)], 0)


def attend_back_body(
    n_slots, place_ref, natural_ref, start_ref, key_natural_ref, cosine_ref, sine_ref, qkv_ref, grad_ref, *refs
):
    slot_refs, (dq_ref, *dkv_refs) = refs[:n_slots], refs[n_slots:]
    keys, values = keys_of(slot_refs)
    query, probs, _, blk = scores_of(qkv_ref, keys, natural_ref, start_ref, key_natural_ref)
    grad = jnp.concatenate(
        [grad_ref[:, i * HEAD_SIZE : (i + 1) * HEAD_SIZE] for i in range(REPEAT)], 0
    )
    low = probs.astype(bf16)
    grad_probs = lax.dot_general(
        grad, values, (((1,), (1,)), ((), ())), preferred_element_type=f32
    )
    delta = jnp.sum(low.astype(f32) * grad_probs, 1, keepdims=True)
    score_grad = (probs * (grad_probs - delta)).astype(bf16)
    query_grad = jnp.dot(score_grad, keys, preferred_element_type=f32) * SCALE
    cosine, sine = cosine_ref[...], sine_ref[...]
    dq_ref[...] = jnp.concatenate(
        [
            rotate(query_grad[i * blk : (i + 1) * blk], cosine, -sine)
            for i in range(REPEAT)
        ],
        1,
    ).astype(bf16)
    over_rows = (((0,), (0,)), ((), ()))
    key_grad = (
        lax.dot_general(score_grad, query, over_rows, preferred_element_type=f32) * SCALE
    ).astype(bf16)
    value_grad = lax.dot_general(low, grad, over_rows, preferred_element_type=f32).astype(
        bf16
    )
    both = jnp.concatenate([key_grad, value_grad], 1)
    first = 0
    for ref in dkv_refs:
        rows = math.prod(ref.shape[:-1])
        ref[...] = both[first : first + rows].reshape(ref.shape)
        first += rows


def attention_specs(slots, blk, keys, shard_heads):
    def own_place(r, h, place):
        return (r, (place[0] ^ (h // shard_heads)) * shard_heads + h % shard_heads)

    column = pl.BlockSpec((blk, 1), lambda r, h, p: (r, 0))
    return (
        [column, column, pl.BlockSpec((1, 1, keys), lambda r, h, p: (r, 0, 0))],
        pl.BlockSpec((blk, UNIT), lambda r, h, p: (r, h)),
        pl.BlockSpec((blk, REPEAT * HEAD_SIZE), lambda r, h, p: (r, h)),
        pl.BlockSpec((blk, REPEAT * HEAD_SIZE), own_place),
        pl.BlockSpec((1, 1, 8, 128), lambda r, h, p: own_place(r, h, p) + (0, 0)),
        [
            pl.BlockSpec((s.shape[0], blk, 2 * HEAD_SIZE), lambda r, h, p: (0, r, h))
            if s.ndim == 3
            else pl.BlockSpec(
                (1, s.shape[1], blk, 2 * HEAD_SIZE),
                lambda r, h, p: (h // shard_heads, 0, r, h % shard_heads),
            )
            for s in slots
        ],
    )


def attend(place, natural, start, key_natural, qkv, slots):
    rows, heads = qkv.shape[0], qkv.shape[1] // UNIT
    rounds, _, keys = key_natural.shape
    blk = rows // rounds
    meta, unit, _, placed, best, slot = attention_specs(
        slots, blk, keys, heads // lax.axis_size("fsdp")
    )
    return pl.pallas_call(
        functools.partial(attend_body, len(slots)),
        out_shape=[
            jax.ShapeDtypeStruct((rows, heads * REPEAT * HEAD_SIZE), bf16),
            jax.ShapeDtypeStruct((rounds, heads, 8, 128), f32),
        ],
        grid_spec=pltpu.PrefetchScalarGridSpec(
            num_scalar_prefetch=1,
            grid=(rounds, heads),
            in_specs=meta + [unit] + slot,
            out_specs=[placed, best],
        ),
        **params(4 * rows * keys * heads * REPEAT * HEAD_SIZE, 12 * 2**20),
    )(place, natural, start, key_natural, qkv, *slots)


def attend_back(place, natural, start, key_natural, cosine, sine, qkv, grad, slots):
    rows, heads = qkv.shape[0], qkv.shape[1] // UNIT
    rounds, _, keys = key_natural.shape
    blk = rows // rounds
    meta, unit, pair, placed, _, slot = attention_specs(
        slots, blk, keys, heads // lax.axis_size("fsdp")
    )
    table = pl.BlockSpec((blk, HEAD_SIZE), lambda r, h, p: (r, 0))
    return pl.pallas_call(
        functools.partial(attend_back_body, len(slots)),
        out_shape=[jax.ShapeDtypeStruct((rows, heads * REPEAT * HEAD_SIZE), bf16)]
        + [jax.ShapeDtypeStruct(s.shape, bf16) for s in slots],
        grid_spec=pltpu.PrefetchScalarGridSpec(
            num_scalar_prefetch=1,
            grid=(rounds, heads),
            in_specs=meta + [table, table, unit, placed] + slot,
            out_specs=[pair] + slot,
        ),
        **params(10 * rows * keys * heads * REPEAT * HEAD_SIZE, 20 * 2**20),
    )(place, natural, start, key_natural, cosine, sine, qkv, grad, *slots)


ANY = pl.BlockSpec(memory_space=pl.ANY)
VMEM = pl.BlockSpec(memory_space=pltpu.VMEM)
MESH = pl.DeviceIdType.MESH
TILE = 256
OVER_ROWS = (((0,), (0,)), ((), ()))
OVER_COLUMNS = (((1,), (1,)), ((), ()))


def flip(place, mask):
    for bit in (1, 2, 4):
        if mask & bit:
            place = place + bit - 2 * bit * lax.rem(lax.div(place, bit), 2)
    return place


def device(ctx, fsdp):
    return {
        "ctx": flip(lax.axis_index("ctx"), ctx),
        "fsdp": flip(lax.axis_index("fsdp"), fsdp),
    }


def greet(ctx_masks, fsdp_masks):
    barrier = pltpu.get_barrier_semaphore()
    partners = [(m, 0) for m in ctx_masks] + [(0, m) for m in fsdp_masks]
    for ctx, fsdp in partners:
        pl.semaphore_signal(barrier, inc=1, device_id=device(ctx, fsdp), device_id_type=MESH)
    pl.semaphore_wait(barrier, len(partners))


def stretch(place, size):
    first = place * size
    return pl.ds(first if isinstance(place, int) else pl.multiple_of(first, size), size)


class Transfers:
    def __init__(self, send, recv):
        self.send, self.recv, self.count, self.open = send, recv, 0, {}

    def start(self, src, dst, ctx=0, fsdp=0, now=True):
        copy = Transfer(self, self.count, src, dst, ctx, fsdp)
        if now:
            copy.made().start()
        self.open[self.count] = copy
        self.count += 1
        return copy

    def release(self, copy):
        self.open.pop(copy.number).made().wait_send()

    def finish(self):
        for copy in list(self.open.values()):
            self.release(copy)


def part_of(ref):
    return ref[0].at[ref[1]] if isinstance(ref, tuple) else ref


class Transfer:
    def __init__(self, transfers, number, src, dst, ctx, fsdp):
        self.t, self.number, self.src, self.dst = transfers, number, src, dst
        self.ctx, self.fsdp = ctx, fsdp

    def made(self):
        return pltpu.make_async_remote_copy(
            src_ref=part_of(self.src),
            dst_ref=part_of(self.dst),
            send_sem=self.t.send.at[self.number],
            recv_sem=self.t.recv.at[self.number],
            device_id=device(self.ctx, self.fsdp),
            device_id_type=MESH,
        )

    def wait_recv(self):
        self.made().wait_recv()


def remote_call(body, outs, out_specs, in_specs, scratch, transfers, number, flops=0, moved=2**22):
    return pl.pallas_call(
        body,
        out_shape=outs,
        in_specs=in_specs,
        out_specs=out_specs,
        scratch_shapes=list(scratch)
        + [pltpu.SemaphoreType.DMA((transfers,)), pltpu.SemaphoreType.DMA((transfers,))],
        compiler_params=pltpu.CompilerParams(
            vmem_limit_bytes=62 * 2**20, collective_id=number, has_side_effects=True
        ),
        cost_estimate=pl.CostEstimate(flops=flops, bytes_accessed=moved, transcendentals=0),
    )


class PlaneGather:
    def __init__(self, transfers, slots):
        self.t, self.s = transfers, slots
        self.half = slots[0].shape[0] // 2

    def begin(self):
        s, t = self.s, self.t
        self.x = t.start(s[0], s[2], ctx=2)
        self.y = t.start(s[0], s[4], ctx=4)
        self.c = [t.start(s[0], s[1], ctx=1)]

    def middle(self):
        s, t, h = self.s, self.t, self.half
        self.x.wait_recv()
        self.low = t.start(s[2].at[:h], s[6].at[:h], ctx=4)
        self.c.append(t.start(s[2], s[3], ctx=1))
        self.y.wait_recv()
        self.high = t.start(s[4].at[h:], s[6].at[h:], ctx=2)
        self.c.append(t.start(s[4], s[5], ctx=1))

    def end(self):
        s, t = self.s, self.t
        self.low.wait_recv()
        self.high.wait_recv()
        self.c.append(t.start(s[6], s[7], ctx=1))

    def ready(self):
        for copy in self.c:
            copy.wait_recv()


class RowGather:
    def __init__(self, own, slots, send, recv):
        self.own, self.slots, self.send, self.recv = own, slots, send, recv
        place = lax.axis_index("fsdp")
        self.inner = (place == 1) | (place == 2)

    def copy(self, src, dst, number, fsdp):
        return pltpu.make_async_remote_copy(
            src_ref=src,
            dst_ref=self.slots[dst],
            send_sem=self.send.at[number],
            recv_sem=self.recv.at[dst - 1],
            device_id=device(0, fsdp),
            device_id_type=MESH,
        )

    def near(self):
        return self.copy(self.own, 1, 0, 1)

    def across(self):
        return self.copy(self.own, 3, 1, 3)

    def near_on(self):
        return self.copy(self.slots[1], 2, 2, 3)

    def across_on(self):
        return self.copy(self.slots[3], 2, 3, 1)

    def second_on(self):
        return self.copy(self.slots[2], 3, 4, 1)

    def begin(self):
        self.near().start()

        @pl.when(self.inner)
        def _():
            self.across().start()

    def first(self):
        self.near().wait_recv()

        @pl.when(self.inner)
        def _():
            self.near_on().start()
            self.across().wait_recv()
            self.across_on().start()

    def second(self):
        self.near_on().wait_recv()

        @pl.when(self.inner)
        def _():
            self.second_on().start()

    def third(self):
        @pl.when(jnp.logical_not(self.inner))
        def _():
            self.second_on().wait_recv()

    def finish(self):
        self.near().wait_send()

        @pl.when(self.inner)
        def _():
            self.across().wait_send()
            self.near_on().wait_send()
            self.across_on().wait_send()
            self.second_on().wait_send()


def probabilities(query, keys, allowed):
    scores = lax.dot_general(query, keys, OVER_COLUMNS, preferred_element_type=f32) * SCALE
    scores = jnp.where(allowed, scores, hidden_fill_value)
    best = jnp.max(scores, 1, keepdims=True)
    exps = jnp.exp(scores - best)
    return exps * (1.0 / jnp.sum(exps, 1, keepdims=True)), best


def stacked_heads(value):
    return jnp.concatenate(
        [value[:, i * HEAD_SIZE : (i + 1) * HEAD_SIZE] for i in range(REPEAT)], 0
    )


def attention_row_body(
    x_ref, gain_ref, cosine_ref, sine_ref, natural_ref, begin_ref, key_natural_ref,
    q_ref, k_ref, v_ref, o_ref, down_ref, dy_ref,
    h_out, qkv_out, attended_out, best_out, residual_out, h2_out, gain_out,
    kv_out, unit_out, output_out, down_out, dy_out,
    q_own, k_own, v_own, o_own, units, outputs, kvs, h_rel,
    own_sem, keep_sem, gain_send, gain_recv, row_send, row_recv, send, recv,
):
    me, place = lax.axis_index("ctx"), lax.axis_index("fsdp")
    rows, model = x_ref.shape
    depth = units.shape[2]
    rounds = key_natural_ref.shape[0]
    blk = rows // rounds
    heads = q_ref.shape[1] // (REPEAT * HEAD_SIZE)
    width = o_ref.shape[1]
    own = pl.ds(pl.multiple_of(me * depth, depth), depth)
    loads = [
        pltpu.make_async_copy(src, dst, own_sem.at[i])
        for i, (src, dst) in enumerate(
            ((q_ref, q_own), (k_ref, k_own), (v_ref, v_own), (o_ref, o_own))
        )
    ]
    for load in loads:
        load.start()
    gain_out[0] = gain_ref[...]
    greet((1, 2, 4), (1, 2, 3))
    gains = Transfers(gain_send, gain_recv)
    gain_copies = [gains.start(gain_ref, gain_out.at[d], fsdp=d) for d in (1, 2, 3)]
    t = Transfers(send, recv)
    unit_rows, first = [], 0
    for i, ref in enumerate((q_ref, k_ref, v_ref)):
        cols = slice(first, first + ref.shape[1])
        first += ref.shape[1]
        unit_rows.append(
            RowGather(
                ref.at[own],
                [None] + [units.at[d, 0, :, cols] for d in range(3)],
                row_send.at[i],
                row_recv.at[i],
            )
        )
    output_row = RowGather(
        o_ref.at[own], [None] + [outputs.at[d, 0] for d in range(3)], row_send.at[3], row_recv.at[3]
    )
    dy_row = RowGather(
        dy_ref, [None] + [dy_out.at[d] for d in range(3)], row_send.at[4], row_recv.at[4]
    )
    unit_plane = [None] + [
        PlaneGather(t, [units.at[d, j] for j in range(8)]) for d in range(3)
    ]
    output_plane = [None] + [
        PlaneGather(t, [outputs.at[d, j] for j in range(8)]) for d in range(3)
    ]
    down_plane = [None] + [
        PlaneGather(t, [down_out.at[d, j] for j in range(8)]) for d in range(3)
    ]
    kv_plane = [PlaneGather(t, [kvs.at[d, j] for j in range(8)]) for d in range(4)]
    for row in unit_rows:
        row.begin()

    x = x_ref[...].astype(f32)
    unit = x * lax.rsqrt(jnp.mean(x * x, 1, keepdims=True) + epsilon)
    for copy in gain_copies:
        copy.wait_recv()
    for d in range(4):
        gain_cols = pl.ds(pl.multiple_of(flip(place, d) * width, width), width)
        residual_out[:, gain_cols] = jnp.broadcast_to(gain_out[d, 0:1], (rows, width))
    h_out[...] = (unit * residual_out[...]).astype(bf16)
    for j in range(8):
        block = pl.ds(pl.multiple_of(flip(me, j) * depth, depth), depth)
        h_rel[:, j * depth : (j + 1) * depth] = h_out[:, block]
    cosine, sine = cosine_ref[...], sine_ref[...]

    def project(d):
        if d == 0:
            h = h_out[...]
            parts = [
                jnp.dot(h, w[...], preferred_element_type=f32) for w in (q_own, k_own, v_own)
            ]
            total = jnp.concatenate(parts, 1)
        else:
            weight = units[d - 1].reshape(model, units.shape[3])
            total = jnp.dot(h_rel[...], weight, preferred_element_type=f32)

        def head(i):
            return total[:, i * HEAD_SIZE : (i + 1) * HEAD_SIZE]

        for h in range(heads):
            query = [
                rotate(head(REPEAT * h + i), cosine, sine).astype(bf16) for i in range(REPEAT)
            ]
            key = rotate(head(REPEAT * heads + h), cosine, sine).astype(bf16)
            value = head((REPEAT + 1) * heads + h).astype(bf16)
            first = (d * heads + h) * UNIT
            qkv_out[:, first : first + UNIT] = jnp.concatenate(query + [key, value], 1)
            first = h * 2 * HEAD_SIZE
            kvs[d, 0, :, first : first + 2 * HEAD_SIZE] = jnp.concatenate([key, value], 1)

    def attend_heads(d):
        def step(i, carry):
            r, h = lax.div(i, heads), lax.rem(i, heads)
            here = pl.ds(pl.multiple_of(r * blk, blk), blk)
            first = pl.multiple_of(d * heads * UNIT + h * UNIT, UNIT)
            query = stacked_heads(qkv_out[here, pl.ds(first, REPEAT * HEAD_SIZE)])
            cols = pl.ds(pl.multiple_of(h * 2 * HEAD_SIZE, 2 * HEAD_SIZE), 2 * HEAD_SIZE)
            both = kvs[d, :, here, cols].reshape(8 * blk, 2 * HEAD_SIZE)
            natural = key_natural_ref[r]
            allowed = (natural >= begin_ref[here]) & (natural <= natural_ref[here])
            allowed = jnp.concatenate([allowed] * REPEAT, 0)
            probs, best = probabilities(query, both[:, :HEAD_SIZE], allowed)
            out = jnp.dot(probs.astype(bf16), both[:, HEAD_SIZE:], preferred_element_type=f32)
            spot = flip(place, d) * heads + h
            cols = pl.ds(pl.multiple_of(spot * REPEAT * HEAD_SIZE, REPEAT * HEAD_SIZE), REPEAT * HEAD_SIZE)
            attended_out[here, cols] = jnp.concatenate(
                [out[i * blk : (i + 1) * blk] for i in range(REPEAT)], 1
            ).astype(bf16)
            tops = [
                jnp.broadcast_to(jnp.max(best[i * blk : (i + 1) * blk], 0, keepdims=True), (1, 128))
                for i in range(REPEAT)
            ]
            best_out[r, spot] = jnp.concatenate(tops + [jnp.zeros((8 - REPEAT, 128), f32)], 0)
            return carry

        lax.fori_loop(0, rounds * heads, step, 0)

    keeps = []

    def keep(src, dst):
        copy = pltpu.make_async_copy(src, dst, keep_sem.at[len(keeps)])
        copy.start()
        keeps.append(copy)

    for load in loads[:3]:
        load.wait()
    project(0)
    kv_plane[0].begin()
    for row in unit_rows:
        row.first()
    unit_plane[1].begin()
    output_row.begin()
    kv_plane[0].middle()
    for row in unit_rows:
        row.second()
    unit_plane[2].begin()
    unit_plane[1].middle()
    kv_plane[0].end()
    output_row.first()
    for row in unit_rows:
        row.third()
    unit_plane[3].begin()
    downs = []
    for d in (1, 2, 3):
        row = flip(place, d) * 8 * depth + me * depth
        downs.append(
            t.start(
                down_ref.at[pl.ds(pl.multiple_of(row, depth), depth)], down_out.at[d - 1, 0], fsdp=d
            )
        )
    dy_row.begin()
    unit_plane[2].middle()
    unit_plane[1].end()
    output_row.second()
    unit_plane[1].ready()
    project(1)
    kv_plane[1].begin()
    unit_plane[3].middle()
    unit_plane[2].end()
    output_row.third()
    unit_plane[2].ready()
    project(2)
    kv_plane[2].begin()
    kv_plane[1].middle()
    unit_plane[3].end()
    kv_plane[0].ready()
    attend_heads(0)
    unit_plane[3].ready()
    project(3)
    kv_plane[3].begin()
    kv_plane[2].middle()
    kv_plane[1].end()
    output_plane[1].begin()
    dy_row.first()
    kv_plane[3].middle()
    kv_plane[2].end()
    output_plane[2].begin()
    kv_plane[1].ready()
    attend_heads(1)
    output_plane[1].middle()
    kv_plane[3].end()
    output_plane[3].begin()
    kv_plane[2].ready()
    attend_heads(2)
    output_plane[2].middle()
    output_plane[1].end()
    downs[0].wait_recv()
    down_plane[1].begin()
    dy_row.second()
    kv_plane[3].ready()
    attend_heads(3)
    output_plane[3].middle()
    output_plane[2].end()
    downs[1].wait_recv()
    down_plane[2].begin()
    output_plane[3].end()
    for j in range(8):
        block = pl.ds(pl.multiple_of(flip(me, j) * depth, depth), depth)
        h_rel[:, j * depth : (j + 1) * depth] = attended_out[:, block]
    downs[2].wait_recv()
    down_plane[3].begin()
    for d in range(3):
        keep(units.at[d], unit_out.at[d])
    for d in range(4):
        keep(kvs.at[d], kv_out.at[d])
    loads[3].wait()
    square = None
    for d in range(4):
        cols = pl.ds(pl.multiple_of(flip(place, d) * width, width), width)
        if d == 0:
            term = jnp.dot(attended_out[...], o_own[...], preferred_element_type=f32)
        else:
            output_plane[d].ready()
            weight = outputs[d - 1].reshape(model, width)
            term = jnp.dot(h_rel[...], weight, preferred_element_type=f32)
        value = x_ref[:, cols].astype(f32) + term
        residual_out[:, cols] = value
        part = jnp.sum(value * value, 1, keepdims=True)
        square = part if square is None else square + part
        if d == 1:
            down_plane[1].middle()
    scale = lax.rsqrt(square * (1.0 / model) + epsilon)
    for d in range(4):
        cols = pl.ds(pl.multiple_of(flip(place, d) * width, width), width)
        h2_out[:, cols] = (residual_out[:, cols] * scale * gain_out[d, 1:2]).astype(bf16)
    for d in range(3):
        keep(outputs.at[d], output_out.at[d])
    down_plane[2].middle()
    down_plane[1].end()
    down_plane[3].middle()
    down_plane[2].end()
    down_plane[3].end()
    dy_row.third()
    for d in (1, 2, 3):
        down_plane[d].ready()
    for copy in keeps:
        copy.wait()
    for row in unit_rows + [output_row, dy_row]:
        row.finish()
    gains.finish()
    t.finish()


def attention_row(x, gains, cosine, sine, natural, begin, key_natural, query, key, value, output, down, dy):
    rows, model = x.shape
    depth = model // 8
    width = query.shape[1] + key.shape[1] + value.shape[1]
    kv_width = key.shape[1] + value.shape[1]
    rounds = key_natural.shape[0]
    dma = pltpu.SemaphoreType.DMA

    def out(shape, dtype=bf16):
        return jax.ShapeDtypeStruct(shape, dtype)

    return remote_call(
        attention_row_body,
        [
            out((rows, model)),
            out((rows, 4 * width)),
            out((rows, model)),
            out((rounds, KEY_VALUE_HEADS, 8, 128), f32),
            out((rows, model), f32),
            out((rows, model)),
            out((4,) + gains.shape, f32),
            out((4, 8, rows, kv_width)),
            out((3, 8, depth, width)),
            out((3, 8, depth, output.shape[1])),
            out((3, 8, depth, down.shape[1])),
            out((3,) + dy.shape),
        ],
        [VMEM] * 7 + [ANY] * 5,
        [VMEM] * 7 + [ANY] * 6,
        [
            pltpu.VMEM(query.shape, bf16),
            pltpu.VMEM(key.shape, bf16),
            pltpu.VMEM(value.shape, bf16),
            pltpu.VMEM(output.shape, bf16),
            pltpu.VMEM((3, 8, depth, width), bf16),
            pltpu.VMEM((3, 8, depth, output.shape[1]), bf16),
            pltpu.VMEM((4, 8, rows, kv_width), bf16),
            pltpu.VMEM((rows, model), bf16),
            dma((4,)),
            dma((10,)),
            dma((3,)),
            dma((3,)),
            dma((5, 5)),
            dma((5, 3)),
        ],
        3 + 13 * 8,
        0,
        flops=10 * rows * model * model,
    )(x, gains, cosine, sine, natural, begin, key_natural, query, key, value, output, down, dy)


SLOTS = (7, 3, 6, 5, 2, 1, 4, 0)


class SmallReduce:
    def __init__(self, transfers, blocks, land, join, masks):
        self.t, self.blocks, self.land, self.join = transfers, blocks, land, join
        self.masks = masks

    def begin(self, step):
        ctx, fsdp = self.masks[step]
        self.copy = self.t.start(
            (self.blocks, step), (self.land, step), ctx=ctx, fsdp=fsdp
        )

    def end(self, step):
        self.copy.wait_recv()
        self.blocks[step + 1] = self.join(self.blocks[step], self.land[step])

    def on(self, step):
        if 0 <= step - 1 < 5:
            self.end(step - 1)
        if step < 5:
            self.begin(step)


def small_scratch(shape):
    return [pltpu.VMEM((6,) + shape, f32), pltpu.VMEM((5,) + shape, f32)]


class PlaneSum:
    def __init__(self, transfers, cores, far, near, sums, total, fetch=None):
        self.t, self.cores, self.far, self.near = transfers, cores, far, near
        self.sums, self.total, self.fetch = sums, total, fetch
        self.half = cores.shape[1] // 2
        self.over = {}

    def arrive(self, j):
        self.over[j].wait_recv()
        if self.fetch is not None:
            place, sems = self.fetch
            slot = (j // 2) % 2
            self.copy = pltpu.make_async_copy(
                self.cores.at[j // 2], place.at[slot], sems.at[slot]
            )
            self.copy.start()

    def send_odd(self, j, src):
        self.over[j - 1] = self.t.start(src, self.cores.at[(j - 1) // 2], ctx=1)
        return self.over[j - 1]

    def even(self, j, value):
        t, h = self.t, self.half
        if self.fetch is None:
            value = value + self.cores[j // 2].astype(f32)
        else:
            self.copy.wait()
            value = value + self.fetch[0][(j // 2) % 2].astype(f32)
        if j == 0:
            self.total[...] = value
            return
        out = self.sums.at[(6, 2, 4).index(j)]
        out[...] = value.astype(bf16)
        if j == 6:
            self.x6 = t.start(out.at[:h], self.far.at[:h], ctx=2)
            self.y6 = t.start(out.at[h:], self.far.at[h:], ctx=4)
        elif j == 2:
            self.x2 = t.start(out.at[:h], self.near.at[0, :h], ctx=2)
        else:
            self.y4 = t.start(out.at[h:], self.near.at[1, h:], ctx=4)

    def pass_on(self):
        t, h = self.t, self.half
        two, four = self.sums.at[1], self.sums.at[2]
        self.y6.wait_recv()
        two[h:] = (two[h:].astype(f32) + self.far[h:].astype(f32)).astype(bf16)
        self.x2b = t.start(two.at[h:], self.near.at[0, h:], ctx=2)
        self.x6.wait_recv()
        four[:h] = (four[:h].astype(f32) + self.far[:h].astype(f32)).astype(bf16)
        self.y4b = t.start(four.at[:h], self.near.at[1, :h], ctx=4)

    def close(self):
        for copy in (self.x2, self.x2b, self.y4, self.y4b):
            copy.wait_recv()
        return self.total[...] + self.near[0].astype(f32) + self.near[1].astype(f32)


def plane_sum_scratch(count, *shape):
    return [
        pltpu.VMEM((count, 4) + shape, bf16),
        pltpu.VMEM((count,) + shape, bf16),
        pltpu.VMEM((count, 2) + shape, bf16),
        pltpu.VMEM((count, 3) + shape, bf16),
        pltpu.VMEM((count,) + shape, f32),
    ]


def feed_forward_row_body(
    h_ref, dy_ref, dy_rest, gate_ref, up_ref, down_own, down_rest, top_ref,
    hid_out, dg_out, du_out, h_out, y_out, y_rest, back_out,
    cores, y_land, gate_out, up_out, down_out, top_out,
    hs, back_send, back_land, far, near, blocks, land,
    load_sem, down_sem, dy_sem, h_sem, stage_sem, y_sem, left_sem, right_sem, core_sem, out_sem,
    row_send, row_recv, send, recv,
):
    greet((1, 2, 4), (1, 2, 3))
    t = Transfers(send, recv)
    row = RowGather(h_ref, [None] + [hs.at[d] for d in range(3)], row_send, row_recv)
    row.begin()
    blocks[0] = top_ref[...]
    tops = SmallReduce(
        t, blocks, land, jnp.maximum, ((2, 0), (4, 0), (1, 0), (0, 1), (0, 2))
    )
    rows, model = h_ref.shape
    tiles = gate_ref.shape[1] // TILE
    backs = []

    def forward(gates, ups, downs, dys, y_acc, back_acc, y_send, stage):
        feed_forward_parts(
            t, row, tops, backs,
            h_ref, dy_ref, dy_rest, gate_ref, up_ref, down_own, down_rest,
            hid_out, dg_out, du_out, h_out, y_out, y_rest, back_out,
            gates, ups, downs, hs, dys, y_acc, back_acc, back_send, back_land, y_send, stage,
            load_sem, down_sem, dy_sem, h_sem, stage_sem, y_sem,
        )

    block = pltpu.VMEM((rows, model), f32)
    pl.run_scoped(
        forward,
        pltpu.VMEM((tiles, model, TILE), bf16),
        pltpu.VMEM((tiles, model, TILE), bf16),
        pltpu.VMEM((tiles, TILE, model), bf16),
        pltpu.VMEM((4, rows, model), bf16),
        block,
        block,
        pltpu.VMEM((rows, model), bf16),
        pltpu.VMEM((2, 3, rows, TILE), bf16),
    )
    y_copy = t.start((y_rest, 0), y_land, fsdp=1)

    def grads(left, rights, odd, sums, totals, fetched):
        feed_forward_grads(
            t, h_out, dg_out, du_out, hid_out, dy_ref, dy_rest,
            gate_out, up_out, down_out,
            left, rights, odd, cores, far, near, sums, totals, fetched,
            left_sem, right_sem, dy_sem, core_sem, out_sem,
        )
        t.finish()

    depth = model // 8
    pl.run_scoped(
        grads,
        pltpu.VMEM((4 * rows, model), bf16),
        pltpu.VMEM((2, 4 * rows, model), bf16),
        pltpu.VMEM((4, depth, model // 2), bf16),
        pltpu.VMEM((6, 3, depth, model // 2), bf16),
        pltpu.VMEM((6, depth, model // 2), f32),
        pltpu.VMEM((2, depth, model // 2), bf16),
    )
    for d in range(3):
        backs[d].wait_recv()
        back_out[...] += back_land[d].astype(f32)
    tops.on(5)
    top_out[...] = blocks[5]
    y_copy.wait_recv()
    row.finish()
    t.finish()


def feed_forward_parts(
    t, row, tops, backs,
    h_ref, dy_ref, dy_rest, gate_ref, up_ref, down_own, down_rest,
    hid_out, dg_out, du_out, h_out, y_out, y_rest, back_out,
    gates, ups, downs, hs, dys, y_acc, back_acc, back_send, back_land, y_send, stage,
    load_sem, down_sem, dy_sem, h_sem, stage_sem, y_sem,
):
    rows, model = h_ref.shape
    tiles = gates.shape[0]
    me, place = lax.axis_index("ctx"), lax.axis_index("fsdp")
    width = down_own.shape[1]

    def tile_loads(i, slot):
        cols = stretch(i, TILE)
        copies = [
            pltpu.make_async_copy(gate_ref.at[:, cols], gates.at[i], load_sem.at[0, i]),
            pltpu.make_async_copy(up_ref.at[:, cols], ups.at[i], load_sem.at[1, i]),
        ]
        own_rows = stretch(place * tiles + i, TILE)
        for d in range(4):
            cols = stretch(flip(place, d), width)
            src = down_own.at[own_rows] if d == 0 else down_rest.at[d - 1, slot]
            copies.append(pltpu.make_async_copy(src, downs.at[i, :, cols], down_sem.at[i, d]))
        return copies

    dy_copies = [
        pltpu.make_async_copy(dy_ref if d == 0 else dy_rest.at[d - 1], dys.at[d], dy_sem.at[d])
        for d in range(4)
    ]
    dy_copies[0].start()
    for i in range(tiles):
        for load in tile_loads(i, flip(me, i)):
            load.start()
    for load in dy_copies[1:]:
        load.start()
    dy_copies[0].wait()

    def stage_copy(slot, k, part, i):
        out = (hid_out, dg_out, du_out)[k]
        cols = stretch(i, TILE)
        return pltpu.make_async_copy(
            stage.at[slot, k], out.at[pl.ds(part * rows, rows), cols], stage_sem.at[slot, k]
        )

    def chunk(part, h):
        def step(i, carry):
            slot = lax.rem(i, 2)
            if part == 0:
                for load in tile_loads(i, 0):
                    load.wait()
            gate, up, down = gates[i], ups[i], downs[i]
            g = jnp.dot(h[...], gate, preferred_element_type=f32)
            u = jnp.dot(h[...], up, preferred_element_type=f32)
            grad = lax.dot_general(dys[part], down, OVER_COLUMNS, preferred_element_type=f32)
            sigmoid = jax.nn.sigmoid(g)
            silu = g * sigmoid
            hidden = (silu * u).astype(bf16)
            grad_gate = (grad * u * sigmoid * (1.0 + g * (1.0 - sigmoid))).astype(bf16)
            grad_up = (grad * silu).astype(bf16)

            @pl.when(i >= 2)
            def _():
                for k in range(3):
                    stage_copy(slot, k, part, i - 2).wait()

            stage[slot, 0] = hidden
            stage[slot, 1] = grad_gate
            stage[slot, 2] = grad_up
            for k in range(3):
                stage_copy(slot, k, part, i).start()
            y = jnp.dot(hidden, down, preferred_element_type=f32)
            back = lax.dot_general(grad_gate, gate, OVER_COLUMNS, preferred_element_type=f32)
            back += lax.dot_general(grad_up, up, OVER_COLUMNS, preferred_element_type=f32)

            @pl.when(i == 0)
            def _():
                y_acc[...] = y
                back_acc[...] = back

            @pl.when(i > 0)
            def _():
                y_acc[...] += y
                back_acc[...] += back

            return carry

        lax.fori_loop(0, tiles, step, 0)
        for i in (tiles - 2, tiles - 1):
            for k in range(3):
                stage_copy(i % 2, k, part, i).wait()

    def keep_h(part, h):
        return pltpu.make_async_copy(h, h_out.at[pl.ds(part * rows, rows)], h_sem.at[part])

    keep_h(0, h_ref).start()
    tops.on(0)
    chunk(0, h_ref)
    y_copy = pltpu.make_async_copy(y_acc, y_out, y_sem.at[3])
    y_copy.start()
    back_out[...] = back_acc[...]
    row.first()
    tops.on(1)
    y_copy.wait()
    y_copy = None
    for part in (1, 2, 3):
        h = hs.at[part - 1]
        if part == 2:
            row.second()
        if part == 3:
            row.third()
        keep_h(part, h).start()
        dy_copies[part].wait()
        chunk(part, h)
        back_send[part - 1] = back_acc[...].astype(bf16)
        backs.append(
            t.start((back_send, part - 1), (back_land, part - 1), fsdp=part, now=part > 1)
        )
        if part != 2:
            @pl.when(row.inner == (part == 3))
            def _():
                backs[0].made().start()

        if y_copy is not None:
            y_copy.wait()
        y_send[...] = y_acc[...].astype(bf16)
        y_copy = pltpu.make_async_copy(y_send, y_rest.at[part - 1], y_sem.at[part - 1])
        y_copy.start()
        tops.on(part + 1)
    y_copy.wait()
    for part in range(4):
        keep_h(part, h_ref if part == 0 else hs.at[part - 1]).wait()


def feed_forward_grads(
    t, h_ref, dg_ref, du_ref, hid_ref, dy_ref, dy_rest,
    gate_out, up_out, down_out,
    left, rights, odd, cores, far, near, sums, totals, fetched,
    left_sem, right_sem, dy_sem, core_sem, out_sem,
):
    me = lax.axis_index("ctx")
    rows = dy_ref.shape[0]
    depth = far.shape[1]
    dys = [dy_ref] + [dy_rest.at[d] for d in range(3)]
    right_copies = [
        [pltpu.make_async_copy(dg_ref, rights.at[0], right_sem.at[0])],
        [pltpu.make_async_copy(du_ref, rights.at[1], right_sem.at[1])],
        [
            pltpu.make_async_copy(p, rights.at[0, i * rows : (i + 1) * rows], dy_sem.at[i])
            for i, p in enumerate(dys)
        ],
    ]
    left_copies = [
        pltpu.make_async_copy(h_ref, left, left_sem.at[0]),
        pltpu.make_async_copy(hid_ref, left, left_sem.at[1]),
    ]
    left_copies[0].start()
    right_copies[0][0].start()
    right_copies[1][0].start()
    left_copies[0].wait()
    half = far.shape[2]
    count = far.shape[0]
    jobs, odd_copies, outs = [], {}, []

    def close(n):
        cols = slice((n % 2) * half, (n % 2 + 1) * half)
        if n < 4:
            totals[n] = jobs[n].close()
            out = pltpu.make_async_copy(
                totals.at[n], (gate_out, up_out)[n // 2].at[:, cols], out_sem.at[n]
            )
            out.start()
            outs.append(out)
        else:
            down_out[:, cols] = jobs[n].close().astype(bf16)

    for n in range(count):
        k = n // 2
        cols = slice((n % 2) * half, (n % 2 + 1) * half)
        job = PlaneSum(
            t, cores.at[n], far.at[n], near.at[n], sums.at[n], totals.at[n], (fetched, core_sem)
        )
        jobs.append(job)
        if n == 2:
            for copy in right_copies[2]:
                copy.start()
        if n == 4:
            left_copies[1].start()
            left_copies[1].wait()
        if n % 2 == 0:
            for copy in right_copies[k]:
                copy.wait()

        def partial(j):
            return lax.dot_general(
                left[:, stretch(flip(me, j), depth)],
                rights[k % 2, :, cols],
                OVER_ROWS,
                preferred_element_type=f32,
            )

        for i, j in enumerate(SLOTS):
            if i == 2 and n:
                jobs[n - 1].pass_on()
            if j % 2:
                if j in odd_copies:
                    t.release(odd_copies[j])
                odd[j // 2] = partial(j).astype(bf16)
                odd_copies[j] = job.send_odd(j, odd.at[j // 2])
            else:
                job.arrive(j)
                job.even(j, partial(j))
        if n:
            close(n - 1)
    jobs[count - 1].pass_on()
    close(count - 1)
    for copy in outs:
        copy.wait()


def feed_forward_row(h, dy, dy_rest, gate, up, down_own, down_rest, top):
    rows, model = h.shape
    units = gate.shape[1]
    tiles = units // TILE
    depth = model // 8
    wide = jax.ShapeDtypeStruct((4 * rows, units), bf16)
    low = jax.ShapeDtypeStruct((rows, model), bf16)
    high = jax.ShapeDtypeStruct((rows, model), f32)
    summed = jax.ShapeDtypeStruct((depth, units), f32)
    dma = pltpu.SemaphoreType.DMA
    return remote_call(
        feed_forward_row_body,
        [wide, wide, wide, jax.ShapeDtypeStruct((4 * rows, model), bf16)]
        + [high, jax.ShapeDtypeStruct((3, rows, model), bf16), high]
        + [jax.ShapeDtypeStruct((6, 4, depth, model // 2), bf16), low, summed, summed]
        + [jax.ShapeDtypeStruct((depth, model), bf16), jax.ShapeDtypeStruct(top.shape, f32)],
        [ANY] * 6 + [VMEM] + [ANY] * 4 + [VMEM] * 2,
        [VMEM] + [ANY] * 6 + [VMEM],
        [
            pltpu.VMEM((3, rows, model), bf16),
            pltpu.VMEM((3, rows, model), bf16),
            pltpu.VMEM((3, rows, model), bf16),
            pltpu.VMEM((6, depth, model // 2), bf16),
            pltpu.VMEM((6, 2, depth, model // 2), bf16),
        ]
        + small_scratch(top.shape)
        + [
            dma((2, tiles)),
            dma((tiles, 4)),
            dma((4,)),
            dma((4,)),
            dma((2, 3)),
            dma((4,)),
            dma((2,)),
            dma((2,)),
            dma((2,)),
            dma((4,)),
            dma((5,)),
            dma((3,)),
        ],
        3 + 5 + 1 + 6 * 10,
        2,
        flops=54 * rows * model * units,
    )(h, dy, dy_rest, gate, up, down_own, down_rest, top)


class RowSum:
    def __init__(self, transfers, total, sent, landed, columns):
        self.total, self.landed, self.columns = total, landed, columns
        self.over = []
        for d in (1, 2, 3):
            sent[d - 1] = total[:, columns(d)].astype(bf16)
            self.over.append(transfers.start(sent.at[d - 1], landed.at[d - 1], fsdp=d))

    def close(self):
        total = self.total[:, self.columns(0)]
        for d in range(3):
            self.over[d].wait_recv()
            total = total + self.landed[d].astype(f32)
        return total


def attention_back_body(
    db_ref, attended_ref, qkv_ref, cosine_ref, sine_ref, natural_ref, begin_ref, key_natural_ref,
    kv_ref, o_ref, output_rest, y_ref,
    dq_out, dkv_out, output_out, y_land,
    kvs, o_own, outputs, head_grad, odd,
    cores, far, near, sums, totals,
    kv_cores, kv_far, kv_near, kv_sums, kv_totals,
    row_send, row_land, load_sem, send, recv,
):
    me, place = lax.axis_index("ctx"), lax.axis_index("fsdp")
    rows, model = db_ref.shape
    depth = cores.shape[2]
    width = o_own.shape[1]
    rounds = key_natural_ref.shape[0]
    blk = rows // rounds
    heads = kvs.shape[3] // (2 * HEAD_SIZE)
    loads = [
        pltpu.make_async_copy(src, dst, load_sem.at[i])
        for i, (src, dst) in enumerate(((o_ref, o_own), (output_rest, outputs), (kv_ref, kvs)))
    ]
    for load in loads:
        load.start()
    greet((1, 2, 4), (1, 2, 3))
    t = Transfers(send, recv)

    def of_slot(j):
        return pl.ds(pl.multiple_of(flip(me, j) * depth, depth), depth)

    def shard(d):
        return pl.ds(pl.multiple_of(flip(place, d) * width, width), width)

    y_copy = t.start(y_ref.at[1], y_land, fsdp=2)
    job = PlaneSum(t, cores.at[0], far.at[0], near.at[0], sums.at[0], totals.at[0])

    def partial(j):
        return lax.dot_general(
            attended_ref[:, of_slot(j)], db_ref[...], OVER_ROWS, preferred_element_type=f32
        )

    for j in SLOTS:
        if j % 2:
            odd[j // 2] = partial(j).astype(bf16)
            job.send_odd(j, odd.at[j // 2])
        else:
            job.arrive(j)
            job.even(j, partial(j))

    loads[0].wait()
    loads[1].wait()
    for j in range(8):
        total = lax.dot_general(
            db_ref[:, shard(0)], o_own[of_slot(j)], OVER_COLUMNS, preferred_element_type=f32
        )
        for d in (1, 2, 3):
            total += lax.dot_general(
                db_ref[:, shard(d)], outputs[d - 1, j], OVER_COLUMNS, preferred_element_type=f32
            )
        head_grad[:, of_slot(j)] = total.astype(bf16)
    loads[2].wait()
    cosine, sine = cosine_ref[...], -sine_ref[...]

    def attend_heads(d):
        def step(i, carry):
            r, h = lax.div(i, heads), lax.rem(i, heads)
            here = pl.ds(pl.multiple_of(r * blk, blk), blk)
            first = pl.multiple_of(d * heads * UNIT + h * UNIT, UNIT)
            query = stacked_heads(qkv_ref[here, pl.ds(first, REPEAT * HEAD_SIZE)])
            cols = pl.ds(pl.multiple_of(h * 2 * HEAD_SIZE, 2 * HEAD_SIZE), 2 * HEAD_SIZE)
            both = kvs[d, :, here, cols].reshape(8 * blk, 2 * HEAD_SIZE)
            keys, values = both[:, :HEAD_SIZE], both[:, HEAD_SIZE:]
            natural = key_natural_ref[r]
            allowed = (natural >= begin_ref[here]) & (natural <= natural_ref[here])
            allowed = jnp.concatenate([allowed] * REPEAT, 0)
            spot = flip(place, d) * heads + h
            spot_cols = pl.ds(
                pl.multiple_of(spot * REPEAT * HEAD_SIZE, REPEAT * HEAD_SIZE), REPEAT * HEAD_SIZE
            )
            grad = stacked_heads(head_grad[here, spot_cols])
            probs, _ = probabilities(query, keys, allowed)
            low = probs.astype(bf16)
            grad_probs = lax.dot_general(grad, values, OVER_COLUMNS, preferred_element_type=f32)
            delta = jnp.sum(low.astype(f32) * grad_probs, 1, keepdims=True)
            score_grad = (probs * (grad_probs - delta)).astype(bf16)
            query_grad = jnp.dot(score_grad, keys, preferred_element_type=f32) * SCALE
            turn = cosine_ref[here], -sine_ref[here]
            first = pl.multiple_of((d * heads + h) * REPEAT * HEAD_SIZE, REPEAT * HEAD_SIZE)
            dq_out[here, pl.ds(first, REPEAT * HEAD_SIZE)] = jnp.concatenate(
                [rotate(query_grad[i * blk : (i + 1) * blk], *turn) for i in range(REPEAT)], 1
            ).astype(bf16)
            key_grad = lax.dot_general(score_grad, query, OVER_ROWS, preferred_element_type=f32)
            value_grad = lax.dot_general(low, grad, OVER_ROWS, preferred_element_type=f32)
            both = jnp.concatenate([key_grad * SCALE, value_grad], 1).astype(bf16)
            kvs[d, :, here, cols] = both.reshape(8, blk, 2 * HEAD_SIZE)
            return carry

        lax.fori_loop(0, rounds * heads, step, 0)

    kv_jobs = [
        PlaneSum(t, kv_cores.at[k], kv_far.at[k], kv_near.at[k], kv_sums.at[k], kv_totals.at[k])
        for k in range(2)
    ]

    def send_half(k):
        half = pl.ds(2 * k, 2)
        for j in (7, 3, 5, 1):
            kv_jobs[k].send_odd(j, kvs.at[half, j])
        for j in (6, 2, 4, 0):
            kv_jobs[k].arrive(j)
            kv_jobs[k].even(j, kvs[half, j].astype(f32))

    def take_half(k):
        total = kv_jobs[k].close()
        for i in range(2):
            for h in range(heads):
                first = 2 * h * HEAD_SIZE
                middle = first + HEAD_SIZE
                to = ((2 * k + i) * heads + h) * 2 * HEAD_SIZE
                turned = rotate(total[i, :, first:middle], cosine, sine)
                value = total[i, :, middle : middle + HEAD_SIZE]
                dkv_out[:, to : to + 2 * HEAD_SIZE] = jnp.concatenate([turned, value], 1).astype(bf16)

    attend_heads(0)
    job.pass_on()
    attend_heads(1)
    send_half(0)
    attend_heads(2)
    kv_jobs[0].pass_on()
    attend_heads(3)
    send_half(1)
    totals[0] = job.close()
    row = RowSum(t, totals.at[0], row_send, row_land, shard)
    kv_jobs[1].pass_on()
    take_half(0)
    output_out[...] = row.close()
    take_half(1)
    y_copy.wait_recv()
    t.finish()


def attention_back(db, attended, qkv, cosine, sine, natural, begin, key_natural, kv, output, output_rest, y_rest):
    rows, model = db.shape
    depth, width = model // 8, output.shape[1]
    kv_width = kv.shape[3]
    return remote_call(
        attention_back_body,
        [
            jax.ShapeDtypeStruct((rows, model), bf16),
            jax.ShapeDtypeStruct((rows, 4 * kv_width), bf16),
            jax.ShapeDtypeStruct((depth, width), f32),
            jax.ShapeDtypeStruct((rows, model), bf16),
        ],
        [VMEM] * 3 + [ANY],
        [VMEM] * 8 + [ANY] * 4,
        [
            pltpu.VMEM(kv.shape, bf16),
            pltpu.VMEM(output.shape, bf16),
            pltpu.VMEM(output_rest.shape, bf16),
            pltpu.VMEM((rows, model), bf16),
            pltpu.VMEM((4, depth, model), bf16),
        ]
        + plane_sum_scratch(1, depth, model)
        + plane_sum_scratch(2, 2, rows, kv_width)
        + [pltpu.VMEM((3, depth, width), bf16)] * 2
        + [pltpu.SemaphoreType.DMA((3,))],
        3 * 10 + 3 + 1,
        4,
        flops=20 * rows * model * model,
    )(db, attended, qkv, cosine, sine, natural, begin, key_natural, kv, output, output_rest, y_rest)


def unit_grads_body(
    h_ref, dq_ref, dkv_ref, x_ref, term_ref, q_ref, k_ref, v_ref, unit_rest, y_ref,
    query_out, key_out, value_out, back_out, gain_out, y_land,
    odd, q_own, k_own, v_own, units, cores, far, near, sums, totals, row_send, row_land,
    blocks, land, load_sem, unit_sem, send, recv,
):
    me = lax.axis_index("ctx")
    depth = cores.shape[2]
    width = row_land.shape[3]
    heads = k_own.shape[1] // HEAD_SIZE
    loads = [
        pltpu.make_async_copy(src, dst, load_sem.at[i])
        for i, (src, dst) in enumerate(((q_ref, q_own), (k_ref, k_own), (v_ref, v_own)))
    ]
    unit_loads = [
        pltpu.make_async_copy(unit_rest.at[d], units.at[d % 2], unit_sem.at[d]) for d in range(3)
    ]
    for load in loads + unit_loads[:2]:
        load.start()
    greet((1, 2, 4), (1, 2, 3))
    t = Transfers(send, recv)
    y_copy = t.start(y_ref.at[2], y_land, fsdp=3)
    jobs, odd_copies = [], {}

    def of_slot(j):
        return pl.ds(pl.multiple_of(flip(me, j) * depth, depth), depth)

    half = cores.shape[3]
    order = ((1, 1), (0, 1), (0, 0), (1, 0))
    over = []

    def close(n):
        k, p = order[n]
        totals[n] = jobs[n].close()
        for d in (2 * p, 2 * p + 1):
            if d:
                first = (d % 2) * width
                row_send[k, d - 1] = totals[n, :, first : first + width].astype(bf16)
                over.append(t.start(row_send.at[k, d - 1], row_land.at[k, d - 1], fsdp=d))

    for n, (k, p) in enumerate(order):
        right = (dq_ref, dkv_ref)[k]
        job = PlaneSum(t, cores.at[n], far.at[n], near.at[n], sums.at[n], totals.at[n])
        jobs.append(job)

        def partial(j):
            return lax.dot_general(
                h_ref[:, of_slot(j)],
                right[:, p * half : (p + 1) * half],
                OVER_ROWS,
                preferred_element_type=f32,
            )

        for j in SLOTS:
            if j % 2:
                if j in odd_copies:
                    t.release(odd_copies[j])
                odd[j // 2] = partial(j).astype(bf16)
                odd_copies[j] = job.send_odd(j, odd.at[j // 2])
            else:
                job.arrive(j)
                job.even(j, partial(j))
        if n:
            jobs[n - 1].pass_on()
        if n > 1:
            close(n - 2)

    def grads(d):
        query = dq_ref[:, d * width : (d + 1) * width]
        pairs = dkv_ref[:, d * width : (d + 1) * width]
        parts = [pairs[:, i * HEAD_SIZE : (i + 1) * HEAD_SIZE] for i in range(2 * heads)]
        return jnp.concatenate([query] + parts[::2] + parts[1::2], 1)

    def back(d):
        grad = grads(d)
        for j in range(8):
            cols = of_slot(j)
            if d == 0:
                weight = jnp.concatenate([w[cols] for w in (q_own, k_own, v_own)], 1)
                back_out[:, cols] = lax.dot_general(
                    grad, weight, OVER_COLUMNS, preferred_element_type=f32
                )
            else:
                back_out[:, cols] += lax.dot_general(
                    grad, units[(d - 1) % 2, j], OVER_COLUMNS, preferred_element_type=f32
                )

    for load in loads:
        load.wait()
    back(0)
    jobs[3].pass_on()
    unit_loads[0].wait()
    back(1)
    unit_loads[2].start()
    unit_loads[1].wait()
    back(2)
    unit_loads[2].wait()
    back(3)
    x = x_ref[...].astype(f32)
    unit = x * lax.rsqrt(jnp.mean(x * x, 1, keepdims=True) + epsilon)
    gains = SmallReduce(
        t, blocks, land, jnp.add, ((0, 1), (0, 2), (2, 0), (4, 0), (1, 0))
    )
    blocks[0] = jnp.concatenate(
        [jnp.sum(back_out[...] * unit, 0, keepdims=True), term_ref[1:8]], 0
    )
    gains.on(0)
    close(2)
    gains.on(1)
    gains.on(2)
    close(3)
    gains.on(3)
    gains.on(4)
    gains.on(5)
    gain_out[...] = blocks[5]
    for copy in over:
        copy.wait_recv()

    def whole(n, k):
        total = totals[n, :, :width]
        for d in range(3):
            total = total + row_land[k, d].astype(f32)
        return total

    query_out[...] = whole(2, 0)
    total = whole(3, 1)
    for h in range(heads):
        start = 2 * h * HEAD_SIZE
        here = slice(h * HEAD_SIZE, (h + 1) * HEAD_SIZE)
        key_out[:, here] = total[:, start : start + HEAD_SIZE]
        value_out[:, here] = total[:, start + HEAD_SIZE : start + 2 * HEAD_SIZE]
    y_copy.wait_recv()
    t.finish()


def unit_grads(h, dq, dkv, x, terms, query, key, value, rest, y_rest):
    rows, model = h.shape
    depth, width = model // 8, model // 4
    wide = jax.ShapeDtypeStruct((depth, width), f32)
    half = jax.ShapeDtypeStruct((depth, width // 2), f32)
    dma = pltpu.SemaphoreType.DMA
    return remote_call(
        unit_grads_body,
        [wide, half, half, jax.ShapeDtypeStruct((rows, model), f32)]
        + [jax.ShapeDtypeStruct(terms.shape, f32), jax.ShapeDtypeStruct((rows, model), bf16)],
        [VMEM] * 5 + [ANY],
        [VMEM] * 5 + [ANY] * 5,
        [
            pltpu.VMEM((4, depth, model // 2), bf16),
            pltpu.VMEM(query.shape, bf16),
            pltpu.VMEM(key.shape, bf16),
            pltpu.VMEM(value.shape, bf16),
            pltpu.VMEM((2,) + rest.shape[1:], bf16),
        ]
        + plane_sum_scratch(4, depth, model // 2)
        + [pltpu.VMEM((2, 3, depth, width), bf16)] * 2
        + small_scratch(terms.shape)
        + [dma((3,)), dma((3,))],
        4 * 10 + 6 + 5 + 1,
        5,
        flops=12 * rows * model * model,
    )(h, dq, dkv, x, terms, query, key, value, rest, y_rest)


def token_layout(length_row, block_slots, block_size):
    count_blocks = block_slots.shape[0]
    owner_block = jnp.argmax(
        block_slots[None, :] == jnp.arange(count_blocks, dtype=jnp.int32)[:, None], 1
    ).astype(jnp.int32)
    row_index = jnp.arange(count_blocks * block_size, dtype=jnp.int32)
    plain_order = jnp.repeat(owner_block, block_size) * block_size + row_index % block_size
    seq_ends = jnp.cumsum(length_row)
    seq_starts = seq_ends - length_row
    document_list = jnp.sum((plain_order[:, None] >= seq_ends[None, :]).astype(jnp.int32), 1)
    matches = document_list[:, None] == jnp.arange(length_row.shape[0], dtype=jnp.int32)[None, :]
    begins = jnp.sum(jnp.where(matches, seq_starts[None, :], 0), 1)
    return plain_order, begins


def rms_scale(value):
    return lax.rsqrt(jnp.mean(value * value, -1, keepdims=True) + epsilon)


def norm_back(grad_unit, unit_rows, scale_rows):
    return scale_rows * (grad_unit - unit_rows * jnp.mean(grad_unit * unit_rows, -1, keepdims=True))


def product(left, right):
    return jnp.dot(left, right, preferred_element_type=f32)


def product_t(left, right):
    return lax.dot_general(left, right, (((1,), (1,)), ((), ())), preferred_element_type=f32)


def over_rows(left, right):
    return lax.dot_general(left, right, (((0,), (0,)), ((), ())), preferred_element_type=f32)


def column_blocks(value, count, places):
    width = value.shape[1] // count
    return jnp.concatenate(
        [lax.dynamic_slice_in_dim(value, place * width, width, 1) for place in places], 1
    )


def gather_rows(piece, fsdp_place, ctx_count):
    count = lax.axis_size("fsdp")
    parts = [piece] + [swap(piece, "fsdp", d) for d in range(1, count)]
    return jnp.concatenate(by_place(parts, fsdp_place), 1)


def weight_grad_sum(left, right, me, count):
    depth = left.shape[1] // count
    full = over_rows(column_blocks(left, count, [me ^ j for j in range(count)]), right)
    return sum_halving(full.astype(bf16).reshape(count, depth, right.shape[1]), "ctx")


def down_grad_sum(hidden, grad, me, count, fsdp_count):
    bands = count // fsdp_count
    band, column = me // fsdp_count, me % fsdp_count
    depth = hidden.shape[1] // bands
    width = grad.shape[1] // fsdp_count
    left = column_blocks(hidden, bands, [band ^ j for j in range(bands)])
    right = column_blocks(grad, fsdp_count, [column ^ j for j in range(fsdp_count)])
    full = over_rows(left, right).astype(bf16).reshape(bands, depth, fsdp_count, width)
    return sum_halving(full.transpose(0, 2, 1, 3).reshape(count, depth, width), "ctx")


def clipped(weight, multiplier):
    columns = weight.shape[1]
    head_index = (
        lax.axis_index("fsdp") * columns + jnp.arange(columns, dtype=jnp.int32)
    ) // HEAD_SIZE
    matches = head_index[:, None] == jnp.arange(multiplier.shape[0], dtype=jnp.int32)[None, :]
    column_factor = jnp.sum(jnp.where(matches, multiplier[None, :], 0.0), 1)
    return (weight.astype(f32) * column_factor[None, :]).astype(bf16)


def gain_sum(term, me, place, count, fsdp_count):
    table = term.reshape(count, fsdp_count, -1)
    table = jnp.stack(by_place([table[i] for i in range(count)], me))
    mine = sum_halving(table, "ctx")
    mine = jnp.stack(by_place([mine[i] for i in range(fsdp_count)], place))
    return sum_halving(mine, "fsdp")


def attention_layout(seq_lengths, block_perm, rows):
    count, me = lax.axis_size("ctx"), lax.axis_index("ctx")
    rounds = block_perm.shape[0] // count
    blk = rows // rounds
    plain_order, begins = token_layout(seq_lengths[0], block_perm, blk)
    natural = lax.dynamic_slice_in_dim(plain_order, me * rows, rows)
    begin = lax.dynamic_slice_in_dim(begins, me * rows, rows)
    half_dim = HEAD_SIZE // 2
    exponent = jnp.arange(half_dim, dtype=f32) * (2.0 / HEAD_SIZE)
    inverse = rope_base ** (-exponent)
    angles = (natural - begin).astype(f32)[:, None] * inverse[None, :]
    cosine = jnp.concatenate([jnp.cos(angles)] * 2, 1)
    sine = jnp.concatenate([-jnp.sin(angles), jnp.sin(angles)], 1)
    order = plain_order.reshape(count, rounds, blk)
    order = jnp.stack(by_place([order[i] for i in range(count)], me), 1)
    return natural[:, None], begin[:, None], order.reshape(rounds, 1, count * blk), cosine, sine


def on_device(
    hidden_in,
    out_grad,
    seq_lengths,
    block_perm,
    first_gain,
    query_weight,
    key_matrix,
    value_matrix,
    output_weight,
    second_gain,
    gate_weight,
    up_weight,
    down_weight,
    clip_limit,
):
    rows, model = hidden_in.shape[1], hidden_in.shape[2]
    count, fsdp_count = lax.axis_size("ctx"), lax.axis_size("fsdp")
    me, place = lax.axis_index("ctx"), lax.axis_index("fsdp")
    me_ref = me.astype(jnp.int32).reshape(1)
    depth = model // count
    zero = jnp.zeros((1,), jnp.int32)
    shard_heads = KEY_VALUE_HEADS // fsdp_count

    def own_rows(weight):
        return lax.dynamic_slice_in_dim(weight, me * depth, depth, 0)

    unit_rows = jnp.concatenate(
        [
            own_rows(query_weight).reshape(depth, shard_heads, REPEAT, HEAD_SIZE),
            own_rows(key_matrix).reshape(depth, shard_heads, 1, HEAD_SIZE),
            own_rows(value_matrix).reshape(depth, shard_heads, 1, HEAD_SIZE),
        ],
        2,
    ).reshape(depth, shard_heads * UNIT)
    unit_rows = gather_rows(unit_rows, place, count)
    unit_slots = gather_ctx(unit_rows)
    gains = jnp.stack([first_gain, second_gain])
    gains = jnp.concatenate(
        by_place([gains] + [swap(gains, "fsdp", d) for d in range(1, fsdp_count)], place), 1
    ).astype(f32)
    first_full, second_full = gains[0], gains[1]
    output_rows = gather_rows(own_rows(output_weight), place, count)
    output_slots = gather_ctx(output_rows)

    hidden_width = gate_weight.shape[1]
    down_depth = hidden_width // count

    def down_piece(d):
        first = (place ^ d) * hidden_width + me * down_depth
        return lax.dynamic_slice_in_dim(down_weight, first, down_depth, 0)

    down_rows = [down_piece(0)] + [
        swap(down_piece(d), "fsdp", d) for d in range(1, fsdp_count)
    ]
    down_slots = gather_ctx(jnp.concatenate(by_place(down_rows, place), 1))

    natural_column, begin_column, key_natural, cosine, sine = attention_layout(
        seq_lengths, block_perm, rows
    )
    half_dim = HEAD_SIZE // 2

    tokens = hidden_in.reshape(rows, model).astype(f32)
    scale_one = rms_scale(tokens)
    unit_one = tokens * scale_one
    normalized = (unit_one * first_full).astype(bf16)
    qkv = slot_matmul(normalized, unit_slots, me_ref, UNIT, bf16, (cosine, sine))
    kv_local = qkv.reshape(rows, KEY_VALUE_HEADS, UNIT)[:, :, REPEAT * HEAD_SIZE :].reshape(
        rows, KEY_VALUE_HEADS * 2 * HEAD_SIZE
    )
    kv_slots = gather_ctx(kv_local)
    attended, best = attend(zero, natural_column, begin_column, key_natural, qkv, kv_slots)
    head_max = jnp.max(best[:, :, :REPEAT, 0], 0).reshape(QUERY_HEADS)
    for mask in bits_down(count):
        head_max = jnp.maximum(head_max, swap(head_max, "ctx", mask))
    for mask in bits_down(fsdp_count):
        head_max = jnp.maximum(head_max, swap(head_max, "fsdp", mask))
    residual = tokens + slot_matmul(attended, output_slots, me_ref, 512, f32)
    scale_two = rms_scale(residual)
    unit_two = residual * scale_two
    normed_two = (unit_two * second_full).astype(bf16)

    grad_out = out_grad.reshape(rows, model)
    others = range(1, fsdp_count)
    grads = [grad_out] + [swap(grad_out, "fsdp", d) for d in others]
    normed = [normed_two] + [swap(normed_two, "fsdp", d) for d in others]
    hidden_parts, gate_parts, up_parts, sums, backs = [], [], [], [], []
    for d in range(fsdp_count):
        grad_hidden = slot_matmul_t(grads[d], down_slots, me_ref, 512, f32)
        gate_act = product(normed[d], gate_weight)
        up_proj = product(normed[d], up_weight)
        sigmoid = jax.nn.sigmoid(gate_act)
        hidden = (gate_act * sigmoid * up_proj).astype(bf16)
        grad_gate = (
            grad_hidden * up_proj * sigmoid * (1.0 + gate_act * (1.0 - sigmoid))
        ).astype(bf16)
        grad_up = (grad_hidden * gate_act * sigmoid).astype(bf16)
        hidden_parts.append(hidden)
        gate_parts.append(grad_gate)
        up_parts.append(grad_up)
        backs.append(product_t(grad_gate, gate_weight) + product_t(grad_up, up_weight))
        sums.append(slot_matmul(hidden, down_slots, me_ref, 512, f32 if d == 0 else bf16))
    grad_normed_two = sum_fsdp(backs)
    result = (residual + sum_fsdp(sums)).astype(bf16)

    second_term = jnp.sum(grad_normed_two * unit_two, 0)
    grad_residual = grad_out.astype(f32) + norm_back(
        grad_normed_two * second_full, unit_two, scale_two
    )
    grad_branch = grad_residual.astype(bf16)
    head_grad = slot_matmul_t(grad_branch, output_slots, me_ref, 512, bf16)
    query_grad, *dkv_slots = attend_back(
        zero, natural_column, begin_column, key_natural, cosine, sine, qkv, head_grad, kv_slots
    )
    dkv = sum_halving(dkv_slots[0], "ctx")
    dkv = dkv.reshape(rows, KEY_VALUE_HEADS, 2, HEAD_SIZE)
    grad_key = dkv[:, :, 0]
    first, second = grad_key[..., :half_dim], grad_key[..., half_dim:]
    cos, sin = cosine[:, None, :half_dim], sine[:, None, half_dim:]
    grad_key = jnp.concatenate([first * cos + second * sin, second * cos - first * sin], -1)
    dqkv = jnp.concatenate(
        [
            query_grad.reshape(rows, KEY_VALUE_HEADS, REPEAT, HEAD_SIZE),
            grad_key[:, :, None].astype(bf16),
            dkv[:, :, 1:].astype(bf16),
        ],
        2,
    ).reshape(rows, KEY_VALUE_HEADS * UNIT)
    grad_normed_one = slot_matmul_t(dqkv, unit_slots, me_ref, 512, f32)
    first_term = jnp.sum(grad_normed_one * unit_one, 0)
    grad_input = grad_residual + norm_back(grad_normed_one * first_full, unit_one, scale_one)

    hidden_all = jnp.concatenate(hidden_parts, 0)
    normed_all = jnp.concatenate(normed, 0)
    grads_all = jnp.concatenate(grads, 0)
    down_sum = down_grad_sum(hidden_all, grads_all, me, count, fsdp_count).astype(bf16)
    bands = count // fsdp_count
    places = [
        (c * fsdp_count + f, (bands * f + c // fsdp_count) * fsdp_count + c % fsdp_count)
        for c in range(count)
        for f in range(fsdp_count)
    ]
    down_grad = lax.ppermute(down_sum, ("ctx", "fsdp"), places).astype(f32)
    gate_grad = weight_grad_sum(normed_all, jnp.concatenate(gate_parts, 0), me, count)
    up_grad = weight_grad_sum(normed_all, jnp.concatenate(up_parts, 0), me, count)

    def over_fsdp(summed):
        width = summed.shape[1] // fsdp_count
        return sum_fsdp(
            [
                lax.dynamic_slice_in_dim(summed, (place ^ d) * width, width, 1)
                for d in range(fsdp_count)
            ]
        )

    output_grad = over_fsdp(weight_grad_sum(attended, grad_branch, me, count))
    unit_grad = over_fsdp(weight_grad_sum(normalized, dqkv, me, count))
    unit_grad = unit_grad.reshape(depth, shard_heads, REPEAT + 2, HEAD_SIZE)
    query_out = unit_grad[:, :, :REPEAT].reshape(depth, -1)
    key_out = unit_grad[:, :, REPEAT].reshape(depth, -1)
    value_out = unit_grad[:, :, REPEAT + 1].reshape(depth, -1)

    first_out = gain_sum(first_term, me, place, count, fsdp_count)
    second_out = gain_sum(second_term, me, place, count, fsdp_count)
    multiplier = jnp.sqrt(clip_limit / jnp.maximum(head_max, clip_limit))
    key_ratio = jnp.min(multiplier.reshape(KEY_VALUE_HEADS, REPEAT), 1)
    return (
        result.reshape(1, rows, model),
        grad_input.astype(bf16).reshape(1, rows, model),
        first_out,
        query_out,
        key_out,
        value_out,
        output_grad,
        second_out,
        gate_grad,
        up_grad,
        down_grad,
        head_max,
        clipped(query_weight, multiplier),
        clipped(key_matrix, key_ratio),
    )


def on_row_of_chips(
    hidden_in,
    out_grad,
    seq_lengths,
    block_perm,
    first_gain,
    query_weight,
    key_matrix,
    value_matrix,
    output_weight,
    second_gain,
    gate_weight,
    up_weight,
    down_weight,
    clip_limit,
):
    rows, model = hidden_in.shape[1], hidden_in.shape[2]
    me, place = lax.axis_index("ctx"), lax.axis_index("fsdp")
    natural, begin, key_natural, cosine, sine = attention_layout(seq_lengths, block_perm, rows)
    tokens_low = hidden_in.reshape(rows, model)
    grad_out = out_grad.reshape(rows, model)
    gains = jnp.pad(jnp.stack([first_gain, second_gain]).astype(f32), ((0, 6), (0, 0)))
    (
        normalized,
        qkv,
        attended,
        best,
        residual,
        normed_two,
        all_gains,
        kv_all,
        unit_rest,
        output_rest,
        down_rest,
        dy_rest,
    ) = attention_row(
        tokens_low,
        gains,
        cosine,
        sine,
        natural,
        begin,
        key_natural,
        query_weight,
        key_matrix,
        value_matrix,
        output_weight,
        down_weight,
        grad_out,
    )
    full = jnp.concatenate(by_place([all_gains[d] for d in range(4)], place), 1)
    first_full, second_full = full[0], full[1]
    tokens = tokens_low.astype(f32)
    scale_one = rms_scale(tokens)
    unit_one = tokens * scale_one
    scale_two = rms_scale(residual)
    unit_two = residual * scale_two
    top = jnp.max(best[:, :, :REPEAT, 0], 0)
    top = jnp.pad(top, ((0, 0), (0, 128 - REPEAT)))

    _, _, _, _, y_own, y_rest, grad_normed_two, _, y_near, gate_grad, up_grad, down_sum, top = (
        feed_forward_row(
            normed_two,
            grad_out,
            dy_rest,
            gate_weight,
            up_weight,
            down_weight,
            down_rest,
            top,
        )
    )
    head_max = top[:, :REPEAT].reshape(QUERY_HEADS)
    second_term = jnp.sum(grad_normed_two * unit_two, 0)
    grad_residual = grad_out.astype(f32) + norm_back(
        grad_normed_two * second_full, unit_two, scale_two
    )
    grad_branch = grad_residual.astype(bf16)
    width = model // 4
    moved, pieces = [], []
    for k in range(4):
        piece = lax.dynamic_slice_in_dim(down_sum, ((me % 4) ^ k) * width, width, 1)
        pieces.append(piece)
    attended, pieces = lax.optimization_barrier((attended, pieces))
    for k, piece in enumerate(pieces):
        pairs = [
            (c * 4 + f, (2 * f + c // 4) * 4 + (c % 4 ^ k)) for c in range(8) for f in range(4)
        ]
        moved.append(lax.ppermute(piece, ("ctx", "fsdp"), pairs))
    down_grad = jnp.concatenate(by_place(moved, place), 0).astype(f32)

    query_grad, dkv, output_out, y_second = attention_back(
        grad_branch,
        attended,
        qkv,
        cosine,
        sine,
        natural,
        begin,
        key_natural,
        kv_all,
        output_weight,
        output_rest,
        y_rest,
    )
    terms = jnp.pad(second_term[None], ((1, 6), (0, 0)))
    query_out, key_out, value_out, grad_normed_one, terms, y_third = unit_grads(
        normalized,
        query_grad,
        dkv,
        tokens_low,
        terms,
        query_weight,
        key_matrix,
        value_matrix,
        unit_rest,
        y_rest,
    )
    landed = y_near.astype(f32) + y_second.astype(f32) + y_third.astype(f32)
    result = (residual + y_own + landed).astype(bf16)
    grad_input = grad_residual + norm_back(grad_normed_one * first_full, unit_one, scale_one)
    terms = lax.dynamic_slice_in_dim(
        terms[:2], (me * 4 + place) * (model // 32), model // 32, 1
    )
    first_out, second_out = terms[0], terms[1]
    multiplier = jnp.sqrt(clip_limit / jnp.maximum(head_max, clip_limit))
    key_ratio = jnp.min(multiplier.reshape(KEY_VALUE_HEADS, REPEAT), 1)
    return (
        result.reshape(1, rows, model),
        grad_input.astype(bf16).reshape(1, rows, model),
        first_out,
        query_out,
        key_out,
        value_out,
        output_out,
        second_out,
        gate_grad,
        up_grad,
        down_grad,
        head_max,
        clipped(query_weight, multiplier),
        clipped(key_matrix, key_ratio),
    )


def solution(mesh):
    shard, whole = P(None, "fsdp"), P()
    token, block = P("fsdp", "ctx", None), P("ctx", "fsdp")
    gain = P(("ctx", "fsdp"))
    chips = mesh.shape["ctx"] == 8 and mesh.shape["fsdp"] == 4
    return jax.shard_map(
        on_row_of_chips if chips else on_device,
        mesh=mesh,
        in_specs=(token, token, P("fsdp", None), whole, P("fsdp"))
        + (shard,) * 4
        + (P("fsdp"),)
        + (shard,) * 3
        + (whole,),
        out_specs=(token, token, gain)
        + (block,) * 4
        + (gain,)
        + (block,) * 3
        + (whole, shard, shard),
        check_vma=False,
    )
```

```python
import functools
import math

import jax
import jax.numpy as jnp
from jax import lax
from jax.experimental import pallas as pl
from jax.experimental.pallas import tpu as pltpu
from jax.sharding import PartitionSpec as P

QUERY_HEADS = 16
KEY_VALUE_HEADS = 8
HEAD_SIZE = 128
REPEAT = QUERY_HEADS // KEY_VALUE_HEADS
UNIT = (REPEAT + 2) * HEAD_SIZE

epsilon = 1e-06
rope_base = 1000000.0
hidden_fill_value = -1e30
bf16 = jnp.bfloat16
f32 = jnp.float32
SCALE = 1.0 / math.sqrt(HEAD_SIZE)


def swap(value, axis, mask):
    size = lax.axis_size(axis)
    return lax.ppermute(value, axis, [(i, i ^ mask) for i in range(size)])


def bits_down(size):
    mask = size // 2
    while mask:
        yield mask
        mask //= 2


def by_place(items, me):
    mask = 1
    while mask < len(items):
        odd = (me & mask) != 0
        items = [jnp.where(odd, items[j ^ mask], items[j]) for j in range(len(items))]
        mask *= 2
    return items


def gather_ctx(block):
    size = lax.axis_size("ctx")
    whole = block[None]
    mask = 1
    while mask < size:
        whole = jnp.concatenate([whole, swap(whole, "ctx", mask)], 0)
        mask *= 2
    return [whole]


def sum_halving(slots, axis):
    for mask in bits_down(slots.shape[0]):
        keep = slots[:mask].astype(f32)
        slots = (keep + swap(slots[mask:], axis, mask).astype(f32)).astype(slots.dtype)
    return slots[0].astype(f32)


def sum_fsdp(pieces):
    total = pieces[0].astype(f32)
    for d in range(1, len(pieces)):
        total = total + swap(pieces[d].astype(bf16), "fsdp", d).astype(f32)
    return total


def params(flops, bytes_accessed):
    return dict(
        compiler_params=pltpu.CompilerParams(vmem_limit_bytes=48 * 2**20),
        cost_estimate=pl.CostEstimate(
            flops=flops, bytes_accessed=bytes_accessed, transcendentals=0
        ),
    )


def rotate(value, cosine, sine):
    return value * cosine + pltpu.roll(value, HEAD_SIZE // 2, 1) * sine


def slot_matmul_body(n_slots, parts, depth, rope, me_ref, x_ref, *refs):
    slot_refs = refs[:n_slots]
    out_ref = refs[-1]
    total = None
    for j in range(n_slots):
        for q in range(parts):
            owner = me_ref[0] ^ (j * parts + q)
            cols = pl.ds(pl.multiple_of(owner * depth, depth), depth)
            term = jnp.dot(x_ref[:, cols], slot_refs[j][q], preferred_element_type=f32)
            total = term if total is None else total + term
    if rope:
        cosine, sine = refs[n_slots][...], refs[n_slots + 1][...]
        parts_out = [
            rotate(total[:, i * HEAD_SIZE : (i + 1) * HEAD_SIZE], cosine, sine)
            for i in range(REPEAT + 1)
        ]
        total = jnp.concatenate(parts_out + [total[:, (REPEAT + 1) * HEAD_SIZE :]], 1)
    out_ref[...] = total.astype(out_ref.dtype)


def in_order(slots, me):
    whole = jnp.concatenate(slots, 0)
    whole = whole[me ^ jnp.arange(whole.shape[0], dtype=jnp.int32)]
    return whole.reshape(-1, whole.shape[2])


def in_order(slots, me):
    whole = jnp.concatenate(slots, 0)
    whole = whole[me ^ jnp.arange(whole.shape[0], dtype=jnp.int32)]
    return whole.reshape(-1, whole.shape[2])


def slot_matmul(x, slots, me, tile, out_dtype, tables=None):
    rows = x.shape[0]
    parts, depth, width = slots[0].shape
    if depth % 128:
        total = product(x, in_order(slots, me))
        if tables is None:
            return total.astype(out_dtype)
        total = total.reshape(rows, width // UNIT, REPEAT + 2, HEAD_SIZE)
        cosine, sine = (t[:, None, None] for t in tables)
        turned = total[:, :, : REPEAT + 1]
        turned = turned * cosine + jnp.roll(turned, HEAD_SIZE // 2, -1) * sine
        total = jnp.concatenate([turned, total[:, :, REPEAT + 1 :]], 2)
        return total.reshape(rows, width).astype(out_dtype)
    extra = [] if tables is None else list(tables)
    body = functools.partial(
        slot_matmul_body, len(slots), parts, depth, tables is not None
    )
    return pl.pallas_call(
        body,
        out_shape=jax.ShapeDtypeStruct((rows, width), out_dtype),
        grid_spec=pltpu.PrefetchScalarGridSpec(
            num_scalar_prefetch=1,
            grid=(width // tile,),
            in_specs=[pl.BlockSpec(x.shape, lambda i, me: (0, 0))]
            + [pl.BlockSpec((parts, depth, tile), lambda i, me: (0, 0, i))] * len(slots)
            + [pl.BlockSpec(e.shape, lambda i, me: (0, 0)) for e in extra],
            out_specs=pl.BlockSpec((rows, tile), lambda i, me: (0, i)),
        ),
        **params(2 * rows * x.shape[1] * width, 2 * x.shape[1] * width),
    )(me, x, *slots, *extra)


def slot_matmul_t_body(n_slots, parts, depth, me_ref, x_ref, *refs):
    slot_refs = refs[:n_slots]
    out_ref, total_ref = refs[n_slots], refs[n_slots + 1]
    step = pl.program_id(0)

    @pl.when(step == 0)
    def _():
        total_ref[...] = jnp.zeros_like(total_ref)

    x = x_ref[...]
    for j in range(n_slots):
        for q in range(parts):
            owner = me_ref[0] ^ (j * parts + q)
            cols = pl.ds(pl.multiple_of(owner * depth, depth), depth)
            total_ref[:, cols] += lax.dot_general(
                x, slot_refs[j][q], (((1,), (1,)), ((), ())), preferred_element_type=f32
            )

    @pl.when(step == pl.num_programs(0) - 1)
    def _():
        out_ref[...] = total_ref[...].astype(out_ref.dtype)


def slot_matmul_t(x, slots, me, tile, out_dtype):
    rows, width = x.shape
    parts, depth, _ = slots[0].shape
    height = parts * depth * len(slots)
    if depth % 128:
        return product_t(x, in_order(slots, me)).astype(out_dtype)
    return pl.pallas_call(
        functools.partial(slot_matmul_t_body, len(slots), parts, depth),
        out_shape=jax.ShapeDtypeStruct((rows, height), out_dtype),
        grid_spec=pltpu.PrefetchScalarGridSpec(
            num_scalar_prefetch=1,
            grid=(width // tile,),
            in_specs=[pl.BlockSpec((rows, tile), lambda i, me: (0, i))]
            + [pl.BlockSpec((parts, depth, tile), lambda i, me: (0, 0, i))]
            * len(slots),
            out_specs=pl.BlockSpec((rows, height), lambda i, me: (0, 0)),
            scratch_shapes=[pltpu.VMEM((rows, height), f32)],
        ),
        **params(2 * rows * height * width, 2 * height * width),
    )(me, x, *slots)


def keys_of(slot_refs):
    def column(i):
        parts = [
            r[..., i * HEAD_SIZE : (i + 1) * HEAD_SIZE].reshape(-1, HEAD_SIZE)
            for r in slot_refs
        ]
        return parts[0] if len(parts) == 1 else jnp.concatenate(parts, 0)

    return column(0), column(1)


def scores_of(qkv_ref, keys, natural_ref, start_ref, key_natural_ref):
    blk = qkv_ref.shape[0]
    query = jnp.concatenate(
        [qkv_ref[:, i * HEAD_SIZE : (i + 1) * HEAD_SIZE] for i in range(REPEAT)], 0
    )
    scores = (
        lax.dot_general(
            query, keys, (((1,), (1,)), ((), ())), preferred_element_type=f32
        )
        * SCALE
    )
    key_natural = key_natural_ref[0]
    allowed = (key_natural >= start_ref[...]) & (key_natural <= natural_ref[...])
    allowed = jnp.concatenate([allowed] * REPEAT, 0)
    scores = jnp.where(allowed, scores, hidden_fill_value)
    best = jnp.max(scores, 1, keepdims=True)
    exps = jnp.exp(scores - best)
    return query, exps * (1.0 / jnp.sum(exps, 1, keepdims=True)), best, blk


def attend_body(n_slots, place_ref, natural_ref, start_ref, key_natural_ref, qkv_ref, *refs):
    slot_refs, (out_ref, best_ref) = refs[:n_slots], refs[n_slots:]
    keys, values = keys_of(slot_refs)
    _, probs, best, blk = scores_of(qkv_ref, keys, natural_ref, start_ref, key_natural_ref)
    heads = jnp.dot(probs.astype(bf16), values, preferred_element_type=f32)
    out_ref[...] = jnp.concatenate(
        [heads[i * blk : (i + 1) * blk] for i in range(REPEAT)], 1
    ).astype(bf16)
    tops = [
        jnp.broadcast_to(jnp.max(best[i * blk : (i + 1) * blk], 0, keepdims=True), (1, 128))
        for i in range(REPEAT)
    ]
    best_ref[0, 0] = jnp.concatenate(tops + [jnp.zeros((8 - REPEAT, 128), f32)], 0)


def attend_back_body(
    n_slots, place_ref, natural_ref, start_ref, key_natural_ref, cosine_ref, sine_ref, qkv_ref, grad_ref, *refs
):
    slot_refs, (dq_ref, *dkv_refs) = refs[:n_slots], refs[n_slots:]
    keys, values = keys_of(slot_refs)
    query, probs, _, blk = scores_of(qkv_ref, keys, natural_ref, start_ref, key_natural_ref)
    grad = jnp.concatenate(
        [grad_ref[:, i * HEAD_SIZE : (i + 1) * HEAD_SIZE] for i in range(REPEAT)], 0
    )
    low = probs.astype(bf16)
    grad_probs = lax.dot_general(
        grad, values, (((1,), (1,)), ((), ())), preferred_element_type=f32
    )
    delta = jnp.sum(low.astype(f32) * grad_probs, 1, keepdims=True)
    score_grad = (probs * (grad_probs - delta)).astype(bf16)
    query_grad = jnp.dot(score_grad, keys, preferred_element_type=f32) * SCALE
    cosine, sine = cosine_ref[...], sine_ref[...]
    dq_ref[...] = jnp.concatenate(
        [
            rotate(query_grad[i * blk : (i + 1) * blk], cosine, -sine)
            for i in range(REPEAT)
        ],
        1,
    ).astype(bf16)
    over_rows = (((0,), (0,)), ((), ()))
    key_grad = (
        lax.dot_general(score_grad, query, over_rows, preferred_element_type=f32) * SCALE
    ).astype(bf16)
    value_grad = lax.dot_general(low, grad, over_rows, preferred_element_type=f32).astype(
        bf16
    )
    both = jnp.concatenate([key_grad, value_grad], 1)
    first = 0
    for ref in dkv_refs:
        rows = math.prod(ref.shape[:-1])
        ref[...] = both[first : first + rows].reshape(ref.shape)
        first += rows


def attention_specs(slots, blk, keys, shard_heads):
    def own_place(r, h, place):
        return (r, (place[0] ^ (h // shard_heads)) * shard_heads + h % shard_heads)

    column = pl.BlockSpec((blk, 1), lambda r, h, p: (r, 0))
    return (
        [column, column, pl.BlockSpec((1, 1, keys), lambda r, h, p: (r, 0, 0))],
        pl.BlockSpec((blk, UNIT), lambda r, h, p: (r, h)),
        pl.BlockSpec((blk, REPEAT * HEAD_SIZE), lambda r, h, p: (r, h)),
        pl.BlockSpec((blk, REPEAT * HEAD_SIZE), own_place),
        pl.BlockSpec((1, 1, 8, 128), lambda r, h, p: own_place(r, h, p) + (0, 0)),
        [
            pl.BlockSpec((s.shape[0], blk, 2 * HEAD_SIZE), lambda r, h, p: (0, r, h))
            if s.ndim == 3
            else pl.BlockSpec(
                (1, s.shape[1], blk, 2 * HEAD_SIZE),
                lambda r, h, p: (h // shard_heads, 0, r, h % shard_heads),
            )
            for s in slots
        ],
    )


def attend(place, natural, start, key_natural, qkv, slots):
    rows, heads = qkv.shape[0], qkv.shape[1] // UNIT
    rounds, _, keys = key_natural.shape
    blk = rows // rounds
    meta, unit, _, placed, best, slot = attention_specs(
        slots, blk, keys, heads // lax.axis_size("fsdp")
    )
    return pl.pallas_call(
        functools.partial(attend_body, len(slots)),
        out_shape=[
            jax.ShapeDtypeStruct((rows, heads * REPEAT * HEAD_SIZE), bf16),
            jax.ShapeDtypeStruct((rounds, heads, 8, 128), f32),
        ],
        grid_spec=pltpu.PrefetchScalarGridSpec(
            num_scalar_prefetch=1,
            grid=(rounds, heads),
            in_specs=meta + [unit] + slot,
            out_specs=[placed, best],
        ),
        **params(4 * rows * keys * heads * REPEAT * HEAD_SIZE, 12 * 2**20),
    )(place, natural, start, key_natural, qkv, *slots)


def attend_back(place, natural, start, key_natural, cosine, sine, qkv, grad, slots):
    rows, heads = qkv.shape[0], qkv.shape[1] // UNIT
    rounds, _, keys = key_natural.shape
    blk = rows // rounds
    meta, unit, pair, placed, _, slot = attention_specs(
        slots, blk, keys, heads // lax.axis_size("fsdp")
    )
    table = pl.BlockSpec((blk, HEAD_SIZE), lambda r, h, p: (r, 0))
    return pl.pallas_call(
        functools.partial(attend_back_body, len(slots)),
        out_shape=[jax.ShapeDtypeStruct((rows, heads * REPEAT * HEAD_SIZE), bf16)]
        + [jax.ShapeDtypeStruct(s.shape, bf16) for s in slots],
        grid_spec=pltpu.PrefetchScalarGridSpec(
            num_scalar_prefetch=1,
            grid=(rounds, heads),
            in_specs=meta + [table, table, unit, placed] + slot,
            out_specs=[pair] + slot,
        ),
        **params(10 * rows * keys * heads * REPEAT * HEAD_SIZE, 20 * 2**20),
    )(place, natural, start, key_natural, cosine, sine, qkv, grad, *slots)


ANY = pl.BlockSpec(memory_space=pl.ANY)
VMEM = pl.BlockSpec(memory_space=pltpu.VMEM)
MESH = pl.DeviceIdType.MESH
TILE = 256
OVER_ROWS = (((0,), (0,)), ((), ()))
OVER_COLUMNS = (((1,), (1,)), ((), ()))


def flip(place, mask):
    for bit in (1, 2, 4):
        if mask & bit:
            place = place + bit - 2 * bit * lax.rem(lax.div(place, bit), 2)
    return place


def device(ctx, fsdp):
    return {
        "ctx": flip(lax.axis_index("ctx"), ctx),
        "fsdp": flip(lax.axis_index("fsdp"), fsdp),
    }


def greet(ctx_masks, fsdp_masks):
    barrier = pltpu.get_barrier_semaphore()
    partners = [(m, 0) for m in ctx_masks] + [(0, m) for m in fsdp_masks]
    for ctx, fsdp in partners:
        pl.semaphore_signal(barrier, inc=1, device_id=device(ctx, fsdp), device_id_type=MESH)
    pl.semaphore_wait(barrier, len(partners))


def stretch(place, size):
    first = place * size
    return pl.ds(first if isinstance(place, int) else pl.multiple_of(first, size), size)


class Transfers:
    def __init__(self, send, recv):
        self.send, self.recv, self.count, self.open = send, recv, 0, {}

    def start(self, src, dst, ctx=0, fsdp=0, now=True):
        copy = Transfer(self, self.count, src, dst, ctx, fsdp)
        if now:
            copy.made().start()
        self.open[self.count] = copy
        self.count += 1
        return copy

    def release(self, copy):
        self.open.pop(copy.number).made().wait_send()

    def finish(self):
        for copy in list(self.open.values()):
            self.release(copy)


def part_of(ref):
    return ref[0].at[ref[1]] if isinstance(ref, tuple) else ref


class Transfer:
    def __init__(self, transfers, number, src, dst, ctx, fsdp):
        self.t, self.number, self.src, self.dst = transfers, number, src, dst
        self.ctx, self.fsdp = ctx, fsdp

    def made(self):
        return pltpu.make_async_remote_copy(
            src_ref=part_of(self.src),
            dst_ref=part_of(self.dst),
            send_sem=self.t.send.at[self.number],
            recv_sem=self.t.recv.at[self.number],
            device_id=device(self.ctx, self.fsdp),
            device_id_type=MESH,
        )

    def wait_recv(self):
        self.made().wait_recv()


def remote_call(body, outs, out_specs, in_specs, scratch, transfers, number, flops=0, moved=2**22):
    return pl.pallas_call(
        body,
        out_shape=outs,
        in_specs=in_specs,
        out_specs=out_specs,
        scratch_shapes=list(scratch)
        + [pltpu.SemaphoreType.DMA((transfers,)), pltpu.SemaphoreType.DMA((transfers,))],
        compiler_params=pltpu.CompilerParams(
            vmem_limit_bytes=62 * 2**20, collective_id=number, has_side_effects=True
        ),
        cost_estimate=pl.CostEstimate(flops=flops, bytes_accessed=moved, transcendentals=0),
    )


class PlaneGather:
    def __init__(self, transfers, slots):
        self.t, self.s = transfers, slots
        self.half = slots[0].shape[0] // 2

    def begin(self):
        s, t = self.s, self.t
        self.x = t.start(s[0], s[2], ctx=2)
        self.y = t.start(s[0], s[4], ctx=4)
        self.c = [t.start(s[0], s[1], ctx=1)]

    def middle(self):
        s, t, h = self.s, self.t, self.half
        self.x.wait_recv()
        self.low = t.start(s[2].at[:h], s[6].at[:h], ctx=4)
        self.c.append(t.start(s[2], s[3], ctx=1))
        self.y.wait_recv()
        self.high = t.start(s[4].at[h:], s[6].at[h:], ctx=2)
        self.c.append(t.start(s[4], s[5], ctx=1))

    def end(self):
        s, t = self.s, self.t
        self.low.wait_recv()
        self.high.wait_recv()
        self.c.append(t.start(s[6], s[7], ctx=1))

    def ready(self):
        for copy in self.c:
            copy.wait_recv()


class RowGather:
    def __init__(self, own, slots, send, recv):
        self.own, self.slots, self.send, self.recv = own, slots, send, recv
        place = lax.axis_index("fsdp")
        self.inner = (place == 1) | (place == 2)

    def copy(self, src, dst, number, fsdp):
        return pltpu.make_async_remote_copy(
            src_ref=src,
            dst_ref=self.slots[dst],
            send_sem=self.send.at[number],
            recv_sem=self.recv.at[dst - 1],
            device_id=device(0, fsdp),
            device_id_type=MESH,
        )

    def near(self):
        return self.copy(self.own, 1, 0, 1)

    def across(self):
        return self.copy(self.own, 3, 1, 3)

    def near_on(self):
        return self.copy(self.slots[1], 2, 2, 3)

    def across_on(self):
        return self.copy(self.slots[3], 2, 3, 1)

    def second_on(self):
        return self.copy(self.slots[2], 3, 4, 1)

    def begin(self):
        self.near().start()

        @pl.when(self.inner)
        def _():
            self.across().start()

    def first(self):
        self.near().wait_recv()

        @pl.when(self.inner)
        def _():
            self.near_on().start()
            self.across().wait_recv()
            self.across_on().start()

    def second(self):
        self.near_on().wait_recv()

        @pl.when(self.inner)
        def _():
            self.second_on().start()

    def third(self):
        @pl.when(jnp.logical_not(self.inner))
        def _():
            self.second_on().wait_recv()

    def finish(self):
        self.near().wait_send()

        @pl.when(self.inner)
        def _():
            self.across().wait_send()
            self.near_on().wait_send()
            self.across_on().wait_send()
            self.second_on().wait_send()


def probabilities(query, keys, allowed):
    scores = lax.dot_general(query, keys, OVER_COLUMNS, preferred_element_type=f32) * SCALE
    scores = jnp.where(allowed, scores, hidden_fill_value)
    best = jnp.max(scores, 1, keepdims=True)
    exps = jnp.exp(scores - best)
    return exps * (1.0 / jnp.sum(exps, 1, keepdims=True)), best


def stacked_heads(value):
    return jnp.concatenate(
        [value[:, i * HEAD_SIZE : (i + 1) * HEAD_SIZE] for i in range(REPEAT)], 0
    )


def attention_row_body(
    x_ref, gain_ref, cosine_ref, sine_ref, natural_ref, begin_ref, key_natural_ref,
    q_ref, k_ref, v_ref, o_ref, down_ref, dy_ref,
    h_out, qkv_out, attended_out, best_out, residual_out, h2_out, gain_out,
    kv_out, unit_out, output_out, down_out, dy_out,
    q_own, k_own, v_own, o_own, units, outputs, kvs, h_rel,
    own_sem, keep_sem, gain_send, gain_recv, row_send, row_recv, send, recv,
):
    me, place = lax.axis_index("ctx"), lax.axis_index("fsdp")
    rows, model = x_ref.shape
    depth = units.shape[2]
    rounds = key_natural_ref.shape[0]
    blk = rows // rounds
    heads = q_ref.shape[1] // (REPEAT * HEAD_SIZE)
    width = o_ref.shape[1]
    own = pl.ds(pl.multiple_of(me * depth, depth), depth)
    loads = [
        pltpu.make_async_copy(src, dst, own_sem.at[i])
        for i, (src, dst) in enumerate(
            ((q_ref, q_own), (k_ref, k_own), (v_ref, v_own), (o_ref, o_own))
        )
    ]
    for load in loads:
        load.start()
    gain_out[0] = gain_ref[...]
    greet((1, 2, 4), (1, 2, 3))
    gains = Transfers(gain_send, gain_recv)
    gain_copies = [gains.start(gain_ref, gain_out.at[d], fsdp=d) for d in (1, 2, 3)]
    t = Transfers(send, recv)
    unit_rows, first = [], 0
    for i, ref in enumerate((q_ref, k_ref, v_ref)):
        cols = slice(first, first + ref.shape[1])
        first += ref.shape[1]
        unit_rows.append(
            RowGather(
                ref.at[own],
                [None] + [units.at[d, 0, :, cols] for d in range(3)],
                row_send.at[i],
                row_recv.at[i],
            )
        )
    output_row = RowGather(
        o_ref.at[own], [None] + [outputs.at[d, 0] for d in range(3)], row_send.at[3], row_recv.at[3]
    )
    dy_row = RowGather(
        dy_ref, [None] + [dy_out.at[d] for d in range(3)], row_send.at[4], row_recv.at[4]
    )
    unit_plane = [None] + [
        PlaneGather(t, [units.at[d, j] for j in range(8)]) for d in range(3)
    ]
    output_plane = [None] + [
        PlaneGather(t, [outputs.at[d, j] for j in range(8)]) for d in range(3)
    ]
    down_plane = [None] + [
        PlaneGather(t, [down_out.at[d, j] for j in range(8)]) for d in range(3)
    ]
    kv_plane = [PlaneGather(t, [kvs.at[d, j] for j in range(8)]) for d in range(4)]
    for row in unit_rows:
        row.begin()

    x = x_ref[...].astype(f32)
    unit = x * lax.rsqrt(jnp.mean(x * x, 1, keepdims=True) + epsilon)
    for copy in gain_copies:
        copy.wait_recv()
    for d in range(4):
        gain_cols = pl.ds(pl.multiple_of(flip(place, d) * width, width), width)
        residual_out[:, gain_cols] = jnp.broadcast_to(gain_out[d, 0:1], (rows, width))
    h_out[...] = (unit * residual_out[...]).astype(bf16)
    for j in range(8):
        block = pl.ds(pl.multiple_of(flip(me, j) * depth, depth), depth)
        h_rel[:, j * depth : (j + 1) * depth] = h_out[:, block]
    cosine, sine = cosine_ref[...], sine_ref[...]

    def project(d):
        if d == 0:
            h = h_out[...]
            parts = [
                jnp.dot(h, w[...], preferred_element_type=f32) for w in (q_own, k_own, v_own)
            ]
            total = jnp.concatenate(parts, 1)
        else:
            weight = units[d - 1].reshape(model, units.shape[3])
            total = jnp.dot(h_rel[...], weight, preferred_element_type=f32)

        def head(i):
            return total[:, i * HEAD_SIZE : (i + 1) * HEAD_SIZE]

        for h in range(heads):
            query = [
                rotate(head(REPEAT * h + i), cosine, sine).astype(bf16) for i in range(REPEAT)
            ]
            key = rotate(head(REPEAT * heads + h), cosine, sine).astype(bf16)
            value = head((REPEAT + 1) * heads + h).astype(bf16)
            first = (d * heads + h) * UNIT
            qkv_out[:, first : first + UNIT] = jnp.concatenate(query + [key, value], 1)
            first = h * 2 * HEAD_SIZE
            kvs[d, 0, :, first : first + 2 * HEAD_SIZE] = jnp.concatenate([key, value], 1)

    def attend_heads(d):
        def step(i, carry):
            r, h = lax.div(i, heads), lax.rem(i, heads)
            here = pl.ds(pl.multiple_of(r * blk, blk), blk)
            first = pl.multiple_of(d * heads * UNIT + h * UNIT, UNIT)
            query = stacked_heads(qkv_out[here, pl.ds(first, REPEAT * HEAD_SIZE)])
            cols = pl.ds(pl.multiple_of(h * 2 * HEAD_SIZE, 2 * HEAD_SIZE), 2 * HEAD_SIZE)
            both = kvs[d, :, here, cols].reshape(8 * blk, 2 * HEAD_SIZE)
            natural = key_natural_ref[r]
            allowed = (natural >= begin_ref[here]) & (natural <= natural_ref[here])
            allowed = jnp.concatenate([allowed] * REPEAT, 0)
            probs, best = probabilities(query, both[:, :HEAD_SIZE], allowed)
            out = jnp.dot(probs.astype(bf16), both[:, HEAD_SIZE:], preferred_element_type=f32)
            spot = flip(place, d) * heads + h
            cols = pl.ds(pl.multiple_of(spot * REPEAT * HEAD_SIZE, REPEAT * HEAD_SIZE), REPEAT * HEAD_SIZE)
            attended_out[here, cols] = jnp.concatenate(
                [out[i * blk : (i + 1) * blk] for i in range(REPEAT)], 1
            ).astype(bf16)
            tops = [
                jnp.broadcast_to(jnp.max(best[i * blk : (i + 1) * blk], 0, keepdims=True), (1, 128))
                for i in range(REPEAT)
            ]
            best_out[r, spot] = jnp.concatenate(tops + [jnp.zeros((8 - REPEAT, 128), f32)], 0)
            return carry

        lax.fori_loop(0, rounds * heads, step, 0)

    keeps = []

    def keep(src, dst):
        copy = pltpu.make_async_copy(src, dst, keep_sem.at[len(keeps)])
        copy.start()
        keeps.append(copy)

    for load in loads[:3]:
        load.wait()
    project(0)
    kv_plane[0].begin()
    for row in unit_rows:
        row.first()
    unit_plane[1].begin()
    output_row.begin()
    kv_plane[0].middle()
    for row in unit_rows:
        row.second()
    unit_plane[2].begin()
    unit_plane[1].middle()
    kv_plane[0].end()
    output_row.first()
    for row in unit_rows:
        row.third()
    dy_row.begin()
    unit_plane[3].begin()
    downs = []
    for d in (1, 2, 3):
        row = flip(place, d) * 8 * depth + me * depth
        downs.append(
            t.start(
                down_ref.at[pl.ds(pl.multiple_of(row, depth), depth)], down_out.at[d - 1, 0], fsdp=d
            )
        )
    unit_plane[2].middle()
    unit_plane[1].end()
    output_row.second()
    unit_plane[1].ready()
    project(1)
    kv_plane[1].begin()
    unit_plane[3].middle()
    unit_plane[2].end()
    output_row.third()
    unit_plane[2].ready()
    project(2)
    kv_plane[2].begin()
    kv_plane[1].middle()
    unit_plane[3].end()
    kv_plane[0].ready()
    attend_heads(0)
    dy_row.first()
    unit_plane[3].ready()
    project(3)
    kv_plane[3].begin()
    kv_plane[2].middle()
    kv_plane[1].end()
    output_plane[1].begin()
    kv_plane[3].middle()
    kv_plane[2].end()
    output_plane[2].begin()
    kv_plane[1].ready()
    attend_heads(1)
    output_plane[1].middle()
    kv_plane[3].end()
    output_plane[3].begin()
    kv_plane[2].ready()
    attend_heads(2)
    dy_row.second()
    output_plane[2].middle()
    output_plane[1].end()
    downs[0].wait_recv()
    down_plane[1].begin()
    kv_plane[3].ready()
    attend_heads(3)
    output_plane[3].middle()
    output_plane[2].end()
    downs[1].wait_recv()
    down_plane[2].begin()
    output_plane[3].end()
    for j in range(8):
        block = pl.ds(pl.multiple_of(flip(me, j) * depth, depth), depth)
        h_rel[:, j * depth : (j + 1) * depth] = attended_out[:, block]
    downs[2].wait_recv()
    down_plane[3].begin()
    for d in range(3):
        keep(units.at[d], unit_out.at[d])
    for d in range(4):
        keep(kvs.at[d], kv_out.at[d])
    loads[3].wait()
    square = None
    for d in range(4):
        cols = pl.ds(pl.multiple_of(flip(place, d) * width, width), width)
        if d == 0:
            term = jnp.dot(attended_out[...], o_own[...], preferred_element_type=f32)
        else:
            output_plane[d].ready()
            weight = outputs[d - 1].reshape(model, width)
            term = jnp.dot(h_rel[...], weight, preferred_element_type=f32)
        value = x_ref[:, cols].astype(f32) + term
        residual_out[:, cols] = value
        part = jnp.sum(value * value, 1, keepdims=True)
        square = part if square is None else square + part
        if d == 1:
            down_plane[1].middle()
    scale = lax.rsqrt(square * (1.0 / model) + epsilon)
    for d in range(4):
        cols = pl.ds(pl.multiple_of(flip(place, d) * width, width), width)
        h2_out[:, cols] = (residual_out[:, cols] * scale * gain_out[d, 1:2]).astype(bf16)
    for d in range(3):
        keep(outputs.at[d], output_out.at[d])
    down_plane[2].middle()
    down_plane[1].end()
    down_plane[3].middle()
    down_plane[2].end()
    down_plane[3].end()
    dy_row.third()
    for d in (1, 2, 3):
        down_plane[d].ready()
    for copy in keeps:
        copy.wait()
    for row in unit_rows + [output_row, dy_row]:
        row.finish()
    gains.finish()
    t.finish()


def attention_row(x, gains, cosine, sine, natural, begin, key_natural, query, key, value, output, down, dy):
    rows, model = x.shape
    depth = model // 8
    width = query.shape[1] + key.shape[1] + value.shape[1]
    kv_width = key.shape[1] + value.shape[1]
    rounds = key_natural.shape[0]
    dma = pltpu.SemaphoreType.DMA

    def out(shape, dtype=bf16):
        return jax.ShapeDtypeStruct(shape, dtype)

    return remote_call(
        attention_row_body,
        [
            out((rows, model)),
            out((rows, 4 * width)),
            out((rows, model)),
            out((rounds, KEY_VALUE_HEADS, 8, 128), f32),
            out((rows, model), f32),
            out((rows, model)),
            out((4,) + gains.shape, f32),
            out((4, 8, rows, kv_width)),
            out((3, 8, depth, width)),
            out((3, 8, depth, output.shape[1])),
            out((3, 8, depth, down.shape[1])),
            out((3,) + dy.shape),
        ],
        [VMEM] * 7 + [ANY] * 5,
        [VMEM] * 7 + [ANY] * 6,
        [
            pltpu.VMEM(query.shape, bf16),
            pltpu.VMEM(key.shape, bf16),
            pltpu.VMEM(value.shape, bf16),
            pltpu.VMEM(output.shape, bf16),
            pltpu.VMEM((3, 8, depth, width), bf16),
            pltpu.VMEM((3, 8, depth, output.shape[1]), bf16),
            pltpu.VMEM((4, 8, rows, kv_width), bf16),
            pltpu.VMEM((rows, model), bf16),
            dma((4,)),
            dma((10,)),
            dma((3,)),
            dma((3,)),
            dma((5, 5)),
            dma((5, 3)),
        ],
        3 + 13 * 8,
        0,
        flops=10 * rows * model * model,
    )(x, gains, cosine, sine, natural, begin, key_natural, query, key, value, output, down, dy)


SLOTS = (7, 3, 6, 5, 2, 1, 4, 0)


class SmallReduce:
    def __init__(self, transfers, blocks, land, join, masks):
        self.t, self.blocks, self.land, self.join = transfers, blocks, land, join
        self.masks = masks

    def begin(self, step):
        ctx, fsdp = self.masks[step]
        self.copy = self.t.start(
            (self.blocks, step), (self.land, step), ctx=ctx, fsdp=fsdp
        )

    def end(self, step):
        self.copy.wait_recv()
        self.blocks[step + 1] = self.join(self.blocks[step], self.land[step])

    def on(self, step):
        if 0 <= step - 1 < 5:
            self.end(step - 1)
        if step < 5:
            self.begin(step)


def small_scratch(shape):
    return [pltpu.VMEM((6,) + shape, f32), pltpu.VMEM((5,) + shape, f32)]


class PlaneSum:
    def __init__(self, transfers, cores, far, near, sums, total, fetch=None):
        self.t, self.cores, self.far, self.near = transfers, cores, far, near
        self.sums, self.total, self.fetch = sums, total, fetch
        self.half = cores.shape[1] // 2
        self.over = {}

    def arrive(self, j):
        self.over[j].wait_recv()
        if self.fetch is not None:
            place, sems = self.fetch
            slot = (j // 2) % 2
            self.copy = pltpu.make_async_copy(
                self.cores.at[j // 2], place.at[slot], sems.at[slot]
            )
            self.copy.start()

    def send_odd(self, j, src):
        self.over[j - 1] = self.t.start(src, self.cores.at[(j - 1) // 2], ctx=1)
        return self.over[j - 1]

    def even(self, j, value):
        t, h = self.t, self.half
        if self.fetch is None:
            value = value + self.cores[j // 2].astype(f32)
        else:
            self.copy.wait()
            value = value + self.fetch[0][(j // 2) % 2].astype(f32)
        if j == 0:
            self.total[...] = value
            return
        out = self.sums.at[(6, 2, 4).index(j)]
        out[...] = value.astype(bf16)
        if j == 6:
            self.x6 = t.start(out.at[:h], self.far.at[:h], ctx=2)
            self.y6 = t.start(out.at[h:], self.far.at[h:], ctx=4)
        elif j == 2:
            self.x2 = t.start(out.at[:h], self.near.at[0, :h], ctx=2)
        else:
            self.y4 = t.start(out.at[h:], self.near.at[1, h:], ctx=4)

    def pass_on(self):
        t, h = self.t, self.half
        two, four = self.sums.at[1], self.sums.at[2]
        self.y6.wait_recv()
        two[h:] = (two[h:].astype(f32) + self.far[h:].astype(f32)).astype(bf16)
        self.x2b = t.start(two.at[h:], self.near.at[0, h:], ctx=2)
        self.x6.wait_recv()
        four[:h] = (four[:h].astype(f32) + self.far[:h].astype(f32)).astype(bf16)
        self.y4b = t.start(four.at[:h], self.near.at[1, :h], ctx=4)

    def close(self):
        for copy in (self.x2, self.x2b, self.y4, self.y4b):
            copy.wait_recv()
        return self.total[...] + self.near[0].astype(f32) + self.near[1].astype(f32)


def plane_sum_scratch(count, *shape):
    return [
        pltpu.VMEM((count, 4) + shape, bf16),
        pltpu.VMEM((count,) + shape, bf16),
        pltpu.VMEM((count, 2) + shape, bf16),
        pltpu.VMEM((count, 3) + shape, bf16),
        pltpu.VMEM((count,) + shape, f32),
    ]


def feed_forward_row_body(
    h_ref, dy_ref, dy_rest, gate_ref, up_ref, down_own, down_rest, top_ref,
    hid_out, dg_out, du_out, h_out, y_out, y_rest, back_out,
    cores, y_land, gate_out, up_out, down_out, top_out,
    hs, back_send, back_land, far, near, blocks, land,
    load_sem, down_sem, dy_sem, h_sem, stage_sem, y_sem, left_sem, right_sem, core_sem, out_sem,
    row_send, row_recv, send, recv,
):
    greet((1, 2, 4), (1, 2, 3))
    t = Transfers(send, recv)
    row = RowGather(h_ref, [None] + [hs.at[d] for d in range(3)], row_send, row_recv)
    row.begin()
    blocks[0] = top_ref[...]
    tops = SmallReduce(
        t, blocks, land, jnp.maximum, ((2, 0), (4, 0), (1, 0), (0, 1), (0, 2))
    )
    rows, model = h_ref.shape
    tiles = gate_ref.shape[1] // TILE
    backs = []

    def forward(gates, ups, downs, dys, y_acc, back_acc, y_send, stage):
        feed_forward_parts(
            t, row, tops, backs,
            h_ref, dy_ref, dy_rest, gate_ref, up_ref, down_own, down_rest,
            hid_out, dg_out, du_out, h_out, y_out, y_rest, back_out,
            gates, ups, downs, hs, dys, y_acc, back_acc, back_send, back_land, y_send, stage,
            load_sem, down_sem, dy_sem, h_sem, stage_sem, y_sem,
        )

    block = pltpu.VMEM((rows, model), f32)
    pl.run_scoped(
        forward,
        pltpu.VMEM((tiles, model, TILE), bf16),
        pltpu.VMEM((tiles, model, TILE), bf16),
        pltpu.VMEM((tiles, TILE, model), bf16),
        pltpu.VMEM((4, rows, model), bf16),
        block,
        block,
        pltpu.VMEM((rows, model), bf16),
        pltpu.VMEM((2, 3, rows, TILE), bf16),
    )
    y_copies = [
        t.start((y_rest, d - 1), (y_land, d // 2), fsdp=d) for d in (1, 3)
    ]

    def grads(left, rights, odd, sums, totals, fetched):
        feed_forward_grads(
            t, h_out, dg_out, du_out, hid_out, dy_ref, dy_rest,
            gate_out, up_out, down_out,
            left, rights, odd, cores, far, near, sums, totals, fetched,
            left_sem, right_sem, dy_sem, core_sem, out_sem,
        )
        t.finish()

    depth = model // 8
    pl.run_scoped(
        grads,
        pltpu.VMEM((4 * rows, model), bf16),
        pltpu.VMEM((2, 4 * rows, model), bf16),
        pltpu.VMEM((4, depth, model // 2), bf16),
        pltpu.VMEM((6, 3, depth, model // 2), bf16),
        pltpu.VMEM((6, depth, model // 2), f32),
        pltpu.VMEM((2, depth, model // 2), bf16),
    )
    for d in range(3):
        backs[d].wait_recv()
        back_out[...] += back_land[d].astype(f32)
    tops.on(5)
    top_out[...] = blocks[5]
    for copy in y_copies:
        copy.wait_recv()
    row.finish()
    t.finish()


def feed_forward_parts(
    t, row, tops, backs,
    h_ref, dy_ref, dy_rest, gate_ref, up_ref, down_own, down_rest,
    hid_out, dg_out, du_out, h_out, y_out, y_rest, back_out,
    gates, ups, downs, hs, dys, y_acc, back_acc, back_send, back_land, y_send, stage,
    load_sem, down_sem, dy_sem, h_sem, stage_sem, y_sem,
):
    rows, model = h_ref.shape
    tiles = gates.shape[0]
    me, place = lax.axis_index("ctx"), lax.axis_index("fsdp")
    width = down_own.shape[1]

    def tile_loads(i, slot):
        cols = stretch(i, TILE)
        copies = [
            pltpu.make_async_copy(gate_ref.at[:, cols], gates.at[i], load_sem.at[0, i]),
            pltpu.make_async_copy(up_ref.at[:, cols], ups.at[i], load_sem.at[1, i]),
        ]
        own_rows = stretch(place * tiles + i, TILE)
        for d in range(4):
            cols = stretch(flip(place, d), width)
            src = down_own.at[own_rows] if d == 0 else down_rest.at[d - 1, slot]
            copies.append(pltpu.make_async_copy(src, downs.at[i, :, cols], down_sem.at[i, d]))
        return copies

    dy_copies = [
        pltpu.make_async_copy(dy_ref if d == 0 else dy_rest.at[d - 1], dys.at[d], dy_sem.at[d])
        for d in range(4)
    ]
    dy_copies[0].start()
    for i in range(tiles):
        for load in tile_loads(i, flip(me, i)):
            load.start()
    for load in dy_copies[1:]:
        load.start()
    dy_copies[0].wait()

    def stage_copy(slot, k, part, i):
        out = (hid_out, dg_out, du_out)[k]
        cols = stretch(i, TILE)
        return pltpu.make_async_copy(
            stage.at[slot, k], out.at[pl.ds(part * rows, rows), cols], stage_sem.at[slot, k]
        )

    def chunk(part, h):
        def step(i, carry):
            slot = lax.rem(i, 2)
            if part == 0:
                for load in tile_loads(i, 0):
                    load.wait()
            gate, up, down = gates[i], ups[i], downs[i]
            g = jnp.dot(h[...], gate, preferred_element_type=f32)
            u = jnp.dot(h[...], up, preferred_element_type=f32)
            grad = lax.dot_general(dys[part], down, OVER_COLUMNS, preferred_element_type=f32)
            sigmoid = jax.nn.sigmoid(g)
            silu = g * sigmoid
            hidden = (silu * u).astype(bf16)
            grad_gate = (grad * u * sigmoid * (1.0 + g * (1.0 - sigmoid))).astype(bf16)
            grad_up = (grad * silu).astype(bf16)

            @pl.when(i >= 2)
            def _():
                for k in range(3):
                    stage_copy(slot, k, part, i - 2).wait()

            stage[slot, 0] = hidden
            stage[slot, 1] = grad_gate
            stage[slot, 2] = grad_up
            for k in range(3):
                stage_copy(slot, k, part, i).start()
            y = jnp.dot(hidden, down, preferred_element_type=f32)
            back = lax.dot_general(grad_gate, gate, OVER_COLUMNS, preferred_element_type=f32)
            back += lax.dot_general(grad_up, up, OVER_COLUMNS, preferred_element_type=f32)

            @pl.when(i == 0)
            def _():
                y_acc[...] = y
                back_acc[...] = back

            @pl.when(i > 0)
            def _():
                y_acc[...] += y
                back_acc[...] += back

            return carry

        lax.fori_loop(0, tiles, step, 0)
        for i in (tiles - 2, tiles - 1):
            for k in range(3):
                stage_copy(i % 2, k, part, i).wait()

    def keep_h(part, h):
        return pltpu.make_async_copy(h, h_out.at[pl.ds(part * rows, rows)], h_sem.at[part])

    keep_h(0, h_ref).start()
    tops.on(0)
    chunk(0, h_ref)
    y_copy = pltpu.make_async_copy(y_acc, y_out, y_sem.at[3])
    y_copy.start()
    back_out[...] = back_acc[...]
    row.first()
    tops.on(1)
    y_copy.wait()
    y_copy = None
    for part in (1, 2, 3):
        h = hs.at[part - 1]
        if part == 2:
            row.second()
        if part == 3:
            row.third()
        keep_h(part, h).start()
        dy_copies[part].wait()
        chunk(part, h)
        back_send[part - 1] = back_acc[...].astype(bf16)
        backs.append(
            t.start((back_send, part - 1), (back_land, part - 1), fsdp=part, now=part > 1)
        )
        if part != 2:
            @pl.when(row.inner == (part == 3))
            def _():
                backs[0].made().start()

        if y_copy is not None:
            y_copy.wait()
        y_send[...] = y_acc[...].astype(bf16)
        y_copy = pltpu.make_async_copy(y_send, y_rest.at[part - 1], y_sem.at[part - 1])
        y_copy.start()
        tops.on(part + 1)
    y_copy.wait()
    for part in range(4):
        keep_h(part, h_ref if part == 0 else hs.at[part - 1]).wait()


def feed_forward_grads(
    t, h_ref, dg_ref, du_ref, hid_ref, dy_ref, dy_rest,
    gate_out, up_out, down_out,
    left, rights, odd, cores, far, near, sums, totals, fetched,
    left_sem, right_sem, dy_sem, core_sem, out_sem,
):
    me = lax.axis_index("ctx")
    rows = dy_ref.shape[0]
    depth = far.shape[1]
    dys = [dy_ref] + [dy_rest.at[d] for d in range(3)]
    right_copies = [
        [pltpu.make_async_copy(dg_ref, rights.at[0], right_sem.at[0])],
        [pltpu.make_async_copy(du_ref, rights.at[1], right_sem.at[1])],
        [
            pltpu.make_async_copy(p, rights.at[0, i * rows : (i + 1) * rows], dy_sem.at[i])
            for i, p in enumerate(dys)
        ],
    ]
    left_copies = [
        pltpu.make_async_copy(h_ref, left, left_sem.at[0]),
        pltpu.make_async_copy(hid_ref, left, left_sem.at[1]),
    ]
    left_copies[0].start()
    right_copies[0][0].start()
    right_copies[1][0].start()
    left_copies[0].wait()
    half = far.shape[2]
    count = far.shape[0]
    jobs, odd_copies, outs = [], {}, []

    def close(n):
        cols = slice((n % 2) * half, (n % 2 + 1) * half)
        if n < 4:
            totals[n] = jobs[n].close()
            out = pltpu.make_async_copy(
                totals.at[n], (gate_out, up_out)[n // 2].at[:, cols], out_sem.at[n]
            )
            out.start()
            outs.append(out)
        else:
            down_out[:, cols] = jobs[n].close().astype(bf16)

    for n in range(count):
        k = n // 2
        cols = slice((n % 2) * half, (n % 2 + 1) * half)
        job = PlaneSum(
            t, cores.at[n], far.at[n], near.at[n], sums.at[n], totals.at[n], (fetched, core_sem)
        )
        jobs.append(job)
        if n == 2:
            for copy in right_copies[2]:
                copy.start()
        if n == 4:
            left_copies[1].start()
            left_copies[1].wait()
        if n % 2 == 0:
            for copy in right_copies[k]:
                copy.wait()

        def partial(j):
            return lax.dot_general(
                left[:, stretch(flip(me, j), depth)],
                rights[k % 2, :, cols],
                OVER_ROWS,
                preferred_element_type=f32,
            )

        for i, j in enumerate(SLOTS):
            if i == 2 and n:
                jobs[n - 1].pass_on()
            if j % 2:
                if j in odd_copies:
                    t.release(odd_copies[j])
                odd[j // 2] = partial(j).astype(bf16)
                odd_copies[j] = job.send_odd(j, odd.at[j // 2])
            else:
                job.arrive(j)
                job.even(j, partial(j))
        if n:
            close(n - 1)
    jobs[count - 1].pass_on()
    close(count - 1)
    for copy in outs:
        copy.wait()


def feed_forward_row(h, dy, dy_rest, gate, up, down_own, down_rest, top):
    rows, model = h.shape
    units = gate.shape[1]
    tiles = units // TILE
    depth = model // 8
    wide = jax.ShapeDtypeStruct((4 * rows, units), bf16)
    high = jax.ShapeDtypeStruct((rows, model), f32)
    summed = jax.ShapeDtypeStruct((depth, units), f32)
    dma = pltpu.SemaphoreType.DMA
    return remote_call(
        feed_forward_row_body,
        [wide, wide, wide, jax.ShapeDtypeStruct((4 * rows, model), bf16)]
        + [high, jax.ShapeDtypeStruct((3, rows, model), bf16), high]
        + [jax.ShapeDtypeStruct((6, 4, depth, model // 2), bf16)]
        + [jax.ShapeDtypeStruct((2, rows, model), bf16), summed, summed]
        + [jax.ShapeDtypeStruct((depth, model), bf16), jax.ShapeDtypeStruct(top.shape, f32)],
        [ANY] * 6 + [VMEM] + [ANY] * 4 + [VMEM] * 2,
        [VMEM] + [ANY] * 6 + [VMEM],
        [
            pltpu.VMEM((3, rows, model), bf16),
            pltpu.VMEM((3, rows, model), bf16),
            pltpu.VMEM((3, rows, model), bf16),
            pltpu.VMEM((6, depth, model // 2), bf16),
            pltpu.VMEM((6, 2, depth, model // 2), bf16),
        ]
        + small_scratch(top.shape)
        + [
            dma((2, tiles)),
            dma((tiles, 4)),
            dma((4,)),
            dma((4,)),
            dma((2, 3)),
            dma((4,)),
            dma((2,)),
            dma((2,)),
            dma((2,)),
            dma((4,)),
            dma((5,)),
            dma((3,)),
        ],
        3 + 5 + 2 + 6 * 10,
        2,
        flops=54 * rows * model * units,
    )(h, dy, dy_rest, gate, up, down_own, down_rest, top)


class RowSum:
    def __init__(self, transfers, total, sent, landed, columns):
        self.total, self.landed, self.columns = total, landed, columns
        self.over = []
        for d in (1, 2, 3):
            sent[d - 1] = total[:, columns(d)].astype(bf16)
            self.over.append(transfers.start(sent.at[d - 1], landed.at[d - 1], fsdp=d))

    def close(self):
        total = self.total[:, self.columns(0)]
        for d in range(3):
            self.over[d].wait_recv()
            total = total + self.landed[d].astype(f32)
        return total


def attention_back_body(
    db_ref, attended_ref, qkv_ref, cosine_ref, sine_ref, natural_ref, begin_ref, key_natural_ref,
    kv_ref, o_ref, output_rest, y_ref,
    dq_out, dkv_out, output_out, y_land,
    kvs, o_own, outputs, head_grad, odd,
    cores, far, near, sums, totals,
    kv_cores, kv_far, kv_near, kv_sums, kv_totals,
    row_send, row_land, load_sem, send, recv,
):
    me, place = lax.axis_index("ctx"), lax.axis_index("fsdp")
    rows, model = db_ref.shape
    depth = cores.shape[2]
    width = o_own.shape[1]
    rounds = key_natural_ref.shape[0]
    blk = rows // rounds
    heads = kvs.shape[3] // (2 * HEAD_SIZE)
    loads = [
        pltpu.make_async_copy(src, dst, load_sem.at[i])
        for i, (src, dst) in enumerate(((o_ref, o_own), (output_rest, outputs), (kv_ref, kvs)))
    ]
    for load in loads:
        load.start()
    greet((1, 2, 4), (1, 2, 3))
    t = Transfers(send, recv)

    def of_slot(j):
        return pl.ds(pl.multiple_of(flip(me, j) * depth, depth), depth)

    def shard(d):
        return pl.ds(pl.multiple_of(flip(place, d) * width, width), width)

    y_copy = t.start(y_ref.at[1], y_land, fsdp=2)
    job = PlaneSum(t, cores.at[0], far.at[0], near.at[0], sums.at[0], totals.at[0])

    def partial(j):
        return lax.dot_general(
            attended_ref[:, of_slot(j)], db_ref[...], OVER_ROWS, preferred_element_type=f32
        )

    for j in SLOTS:
        if j % 2:
            odd[j // 2] = partial(j).astype(bf16)
            job.send_odd(j, odd.at[j // 2])
        else:
            job.arrive(j)
            job.even(j, partial(j))

    loads[0].wait()
    loads[1].wait()
    for j in range(8):
        total = lax.dot_general(
            db_ref[:, shard(0)], o_own[of_slot(j)], OVER_COLUMNS, preferred_element_type=f32
        )
        for d in (1, 2, 3):
            total += lax.dot_general(
                db_ref[:, shard(d)], outputs[d - 1, j], OVER_COLUMNS, preferred_element_type=f32
            )
        head_grad[:, of_slot(j)] = total.astype(bf16)
    loads[2].wait()
    cosine, sine = cosine_ref[...], -sine_ref[...]

    def attend_heads(d):
        def step(i, carry):
            r, h = lax.div(i, heads), lax.rem(i, heads)
            here = pl.ds(pl.multiple_of(r * blk, blk), blk)
            first = pl.multiple_of(d * heads * UNIT + h * UNIT, UNIT)
            query = stacked_heads(qkv_ref[here, pl.ds(first, REPEAT * HEAD_SIZE)])
            cols = pl.ds(pl.multiple_of(h * 2 * HEAD_SIZE, 2 * HEAD_SIZE), 2 * HEAD_SIZE)
            both = kvs[d, :, here, cols].reshape(8 * blk, 2 * HEAD_SIZE)
            keys, values = both[:, :HEAD_SIZE], both[:, HEAD_SIZE:]
            natural = key_natural_ref[r]
            allowed = (natural >= begin_ref[here]) & (natural <= natural_ref[here])
            allowed = jnp.concatenate([allowed] * REPEAT, 0)
            spot = flip(place, d) * heads + h
            spot_cols = pl.ds(
                pl.multiple_of(spot * REPEAT * HEAD_SIZE, REPEAT * HEAD_SIZE), REPEAT * HEAD_SIZE
            )
            grad = stacked_heads(head_grad[here, spot_cols])
            probs, _ = probabilities(query, keys, allowed)
            low = probs.astype(bf16)
            grad_probs = lax.dot_general(grad, values, OVER_COLUMNS, preferred_element_type=f32)
            delta = jnp.sum(low.astype(f32) * grad_probs, 1, keepdims=True)
            score_grad = (probs * (grad_probs - delta)).astype(bf16)
            query_grad = jnp.dot(score_grad, keys, preferred_element_type=f32) * SCALE
            turn = cosine_ref[here], -sine_ref[here]
            first = pl.multiple_of((d * heads + h) * REPEAT * HEAD_SIZE, REPEAT * HEAD_SIZE)
            dq_out[here, pl.ds(first, REPEAT * HEAD_SIZE)] = jnp.concatenate(
                [rotate(query_grad[i * blk : (i + 1) * blk], *turn) for i in range(REPEAT)], 1
            ).astype(bf16)
            key_grad = lax.dot_general(score_grad, query, OVER_ROWS, preferred_element_type=f32)
            value_grad = lax.dot_general(low, grad, OVER_ROWS, preferred_element_type=f32)
            both = jnp.concatenate([key_grad * SCALE, value_grad], 1).astype(bf16)
            kvs[d, :, here, cols] = both.reshape(8, blk, 2 * HEAD_SIZE)
            return carry

        lax.fori_loop(0, rounds * heads, step, 0)

    kv_jobs = [
        PlaneSum(t, kv_cores.at[k], kv_far.at[k], kv_near.at[k], kv_sums.at[k], kv_totals.at[k])
        for k in range(2)
    ]

    def send_half(k):
        half = pl.ds(2 * k, 2)
        for j in (7, 3, 5, 1):
            kv_jobs[k].send_odd(j, kvs.at[half, j])
        for j in (6, 2, 4, 0):
            kv_jobs[k].arrive(j)
            kv_jobs[k].even(j, kvs[half, j].astype(f32))

    def take_half(k):
        total = kv_jobs[k].close()
        for i in range(2):
            for h in range(heads):
                first = 2 * h * HEAD_SIZE
                middle = first + HEAD_SIZE
                to = ((2 * k + i) * heads + h) * 2 * HEAD_SIZE
                turned = rotate(total[i, :, first:middle], cosine, sine)
                value = total[i, :, middle : middle + HEAD_SIZE]
                dkv_out[:, to : to + 2 * HEAD_SIZE] = jnp.concatenate([turned, value], 1).astype(bf16)

    attend_heads(0)
    job.pass_on()
    attend_heads(1)
    send_half(0)
    attend_heads(2)
    kv_jobs[0].pass_on()
    attend_heads(3)
    send_half(1)
    totals[0] = job.close()
    row = RowSum(t, totals.at[0], row_send, row_land, shard)
    kv_jobs[1].pass_on()
    take_half(0)
    output_out[...] = row.close()
    take_half(1)
    y_copy.wait_recv()
    t.finish()


def attention_back(db, attended, qkv, cosine, sine, natural, begin, key_natural, kv, output, output_rest, y_rest):
    rows, model = db.shape
    depth, width = model // 8, output.shape[1]
    kv_width = kv.shape[3]
    return remote_call(
        attention_back_body,
        [
            jax.ShapeDtypeStruct((rows, model), bf16),
            jax.ShapeDtypeStruct((rows, 4 * kv_width), bf16),
            jax.ShapeDtypeStruct((depth, width), f32),
            jax.ShapeDtypeStruct((rows, model), bf16),
        ],
        [VMEM] * 3 + [ANY],
        [VMEM] * 8 + [ANY] * 4,
        [
            pltpu.VMEM(kv.shape, bf16),
            pltpu.VMEM(output.shape, bf16),
            pltpu.VMEM(output_rest.shape, bf16),
            pltpu.VMEM((rows, model), bf16),
            pltpu.VMEM((4, depth, model), bf16),
        ]
        + plane_sum_scratch(1, depth, model)
        + plane_sum_scratch(2, 2, rows, kv_width)
        + [pltpu.VMEM((3, depth, width), bf16)] * 2
        + [pltpu.SemaphoreType.DMA((3,))],
        3 * 10 + 3 + 1,
        4,
        flops=20 * rows * model * model,
    )(db, attended, qkv, cosine, sine, natural, begin, key_natural, kv, output, output_rest, y_rest)


def unit_grads_body(
    h_ref, dq_ref, dkv_ref, x_ref, term_ref, q_ref, k_ref, v_ref, unit_rest,
    query_out, key_out, value_out, back_out, gain_out,
    odd, q_own, k_own, v_own, units, cores, far, near, sums, totals, row_send, row_land,
    blocks, land, load_sem, unit_sem, send, recv,
):
    me = lax.axis_index("ctx")
    depth = cores.shape[2]
    width = row_land.shape[3]
    heads = k_own.shape[1] // HEAD_SIZE
    loads = [
        pltpu.make_async_copy(src, dst, load_sem.at[i])
        for i, (src, dst) in enumerate(((q_ref, q_own), (k_ref, k_own), (v_ref, v_own)))
    ]
    unit_loads = [
        pltpu.make_async_copy(unit_rest.at[d], units.at[d % 2], unit_sem.at[d]) for d in range(3)
    ]
    for load in loads + unit_loads[:2]:
        load.start()
    greet((1, 2, 4), (1, 2, 3))
    t = Transfers(send, recv)
    jobs, odd_copies = [], {}

    def of_slot(j):
        return pl.ds(pl.multiple_of(flip(me, j) * depth, depth), depth)

    half = cores.shape[3]
    order = ((1, 1), (0, 1), (0, 0), (1, 0))
    over = []

    def close(n):
        k, p = order[n]
        totals[n] = jobs[n].close()
        for d in (2 * p, 2 * p + 1):
            if d:
                first = (d % 2) * width
                row_send[k, d - 1] = totals[n, :, first : first + width].astype(bf16)
                over.append(t.start(row_send.at[k, d - 1], row_land.at[k, d - 1], fsdp=d))

    for n, (k, p) in enumerate(order):
        right = (dq_ref, dkv_ref)[k]
        job = PlaneSum(t, cores.at[n], far.at[n], near.at[n], sums.at[n], totals.at[n])
        jobs.append(job)

        def partial(j):
            return lax.dot_general(
                h_ref[:, of_slot(j)],
                right[:, p * half : (p + 1) * half],
                OVER_ROWS,
                preferred_element_type=f32,
            )

        for j in SLOTS:
            if j % 2:
                if j in odd_copies:
                    t.release(odd_copies[j])
                odd[j // 2] = partial(j).astype(bf16)
                odd_copies[j] = job.send_odd(j, odd.at[j // 2])
            else:
                job.arrive(j)
                job.even(j, partial(j))
        if n:
            jobs[n - 1].pass_on()
        if n > 1:
            close(n - 2)

    def grads(d):
        query = dq_ref[:, d * width : (d + 1) * width]
        pairs = dkv_ref[:, d * width : (d + 1) * width]
        parts = [pairs[:, i * HEAD_SIZE : (i + 1) * HEAD_SIZE] for i in range(2 * heads)]
        return jnp.concatenate([query] + parts[::2] + parts[1::2], 1)

    def back(d):
        grad = grads(d)
        for j in range(8):
            cols = of_slot(j)
            if d == 0:
                weight = jnp.concatenate([w[cols] for w in (q_own, k_own, v_own)], 1)
                back_out[:, cols] = lax.dot_general(
                    grad, weight, OVER_COLUMNS, preferred_element_type=f32
                )
            else:
                back_out[:, cols] += lax.dot_general(
                    grad, units[(d - 1) % 2, j], OVER_COLUMNS, preferred_element_type=f32
                )

    for load in loads:
        load.wait()
    back(0)
    jobs[3].pass_on()
    unit_loads[0].wait()
    back(1)
    unit_loads[2].start()
    unit_loads[1].wait()
    back(2)
    unit_loads[2].wait()
    back(3)
    x = x_ref[...].astype(f32)
    unit = x * lax.rsqrt(jnp.mean(x * x, 1, keepdims=True) + epsilon)
    gains = SmallReduce(
        t, blocks, land, jnp.add, ((0, 1), (0, 2), (2, 0), (4, 0), (1, 0))
    )
    blocks[0] = jnp.concatenate(
        [jnp.sum(back_out[...] * unit, 0, keepdims=True), term_ref[1:8]], 0
    )
    gains.on(0)
    close(2)
    gains.on(1)
    gains.on(2)
    close(3)
    gains.on(3)
    gains.on(4)
    gains.on(5)
    gain_out[...] = blocks[5]
    for copy in over:
        copy.wait_recv()

    def whole(n, k):
        total = totals[n, :, :width]
        for d in range(3):
            total = total + row_land[k, d].astype(f32)
        return total

    query_out[...] = whole(2, 0)
    total = whole(3, 1)
    for h in range(heads):
        start = 2 * h * HEAD_SIZE
        here = slice(h * HEAD_SIZE, (h + 1) * HEAD_SIZE)
        key_out[:, here] = total[:, start : start + HEAD_SIZE]
        value_out[:, here] = total[:, start + HEAD_SIZE : start + 2 * HEAD_SIZE]
    t.finish()


def unit_grads(h, dq, dkv, x, terms, query, key, value, rest):
    rows, model = h.shape
    depth, width = model // 8, model // 4
    wide = jax.ShapeDtypeStruct((depth, width), f32)
    half = jax.ShapeDtypeStruct((depth, width // 2), f32)
    dma = pltpu.SemaphoreType.DMA
    return remote_call(
        unit_grads_body,
        [wide, half, half, jax.ShapeDtypeStruct((rows, model), f32)]
        + [jax.ShapeDtypeStruct(terms.shape, f32)],
        [VMEM] * 5,
        [VMEM] * 5 + [ANY] * 4,
        [
            pltpu.VMEM((4, depth, model // 2), bf16),
            pltpu.VMEM(query.shape, bf16),
            pltpu.VMEM(key.shape, bf16),
            pltpu.VMEM(value.shape, bf16),
            pltpu.VMEM((2,) + rest.shape[1:], bf16),
        ]
        + plane_sum_scratch(4, depth, model // 2)
        + [pltpu.VMEM((2, 3, depth, width), bf16)] * 2
        + small_scratch(terms.shape)
        + [dma((3,)), dma((3,))],
        4 * 10 + 6 + 5,
        5,
        flops=12 * rows * model * model,
    )(h, dq, dkv, x, terms, query, key, value, rest)


def token_layout(length_row, block_slots, block_size):
    count_blocks = block_slots.shape[0]
    owner_block = jnp.argmax(
        block_slots[None, :] == jnp.arange(count_blocks, dtype=jnp.int32)[:, None], 1
    ).astype(jnp.int32)
    row_index = jnp.arange(count_blocks * block_size, dtype=jnp.int32)
    plain_order = jnp.repeat(owner_block, block_size) * block_size + row_index % block_size
    seq_ends = jnp.cumsum(length_row)
    seq_starts = seq_ends - length_row
    document_list = jnp.sum((plain_order[:, None] >= seq_ends[None, :]).astype(jnp.int32), 1)
    matches = document_list[:, None] == jnp.arange(length_row.shape[0], dtype=jnp.int32)[None, :]
    begins = jnp.sum(jnp.where(matches, seq_starts[None, :], 0), 1)
    return plain_order, begins


def rms_scale(value):
    return lax.rsqrt(jnp.mean(value * value, -1, keepdims=True) + epsilon)


def norm_back(grad_unit, unit_rows, scale_rows):
    return scale_rows * (grad_unit - unit_rows * jnp.mean(grad_unit * unit_rows, -1, keepdims=True))


def product(left, right):
    return jnp.dot(left, right, preferred_element_type=f32)


def product_t(left, right):
    return lax.dot_general(left, right, (((1,), (1,)), ((), ())), preferred_element_type=f32)


def over_rows(left, right):
    return lax.dot_general(left, right, (((0,), (0,)), ((), ())), preferred_element_type=f32)


def column_blocks(value, count, places):
    width = value.shape[1] // count
    return jnp.concatenate(
        [lax.dynamic_slice_in_dim(value, place * width, width, 1) for place in places], 1
    )


def gather_rows(piece, fsdp_place, ctx_count):
    count = lax.axis_size("fsdp")
    parts = [piece] + [swap(piece, "fsdp", d) for d in range(1, count)]
    return jnp.concatenate(by_place(parts, fsdp_place), 1)


def weight_grad_sum(left, right, me, count):
    depth = left.shape[1] // count
    full = over_rows(column_blocks(left, count, [me ^ j for j in range(count)]), right)
    return sum_halving(full.astype(bf16).reshape(count, depth, right.shape[1]), "ctx")


def down_grad_sum(hidden, grad, me, count, fsdp_count):
    bands = count // fsdp_count
    band, column = me // fsdp_count, me % fsdp_count
    depth = hidden.shape[1] // bands
    width = grad.shape[1] // fsdp_count
    left = column_blocks(hidden, bands, [band ^ j for j in range(bands)])
    right = column_blocks(grad, fsdp_count, [column ^ j for j in range(fsdp_count)])
    full = over_rows(left, right).astype(bf16).reshape(bands, depth, fsdp_count, width)
    return sum_halving(full.transpose(0, 2, 1, 3).reshape(count, depth, width), "ctx")


def clipped(weight, multiplier):
    columns = weight.shape[1]
    head_index = (
        lax.axis_index("fsdp") * columns + jnp.arange(columns, dtype=jnp.int32)
    ) // HEAD_SIZE
    matches = head_index[:, None] == jnp.arange(multiplier.shape[0], dtype=jnp.int32)[None, :]
    column_factor = jnp.sum(jnp.where(matches, multiplier[None, :], 0.0), 1)
    return (weight.astype(f32) * column_factor[None, :]).astype(bf16)


def gain_sum(term, me, place, count, fsdp_count):
    table = term.reshape(count, fsdp_count, -1)
    table = jnp.stack(by_place([table[i] for i in range(count)], me))
    mine = sum_halving(table, "ctx")
    mine = jnp.stack(by_place([mine[i] for i in range(fsdp_count)], place))
    return sum_halving(mine, "fsdp")


def attention_layout(seq_lengths, block_perm, rows):
    count, me = lax.axis_size("ctx"), lax.axis_index("ctx")
    rounds = block_perm.shape[0] // count
    blk = rows // rounds
    plain_order, begins = token_layout(seq_lengths[0], block_perm, blk)
    natural = lax.dynamic_slice_in_dim(plain_order, me * rows, rows)
    begin = lax.dynamic_slice_in_dim(begins, me * rows, rows)
    half_dim = HEAD_SIZE // 2
    exponent = jnp.arange(half_dim, dtype=f32) * (2.0 / HEAD_SIZE)
    inverse = rope_base ** (-exponent)
    angles = (natural - begin).astype(f32)[:, None] * inverse[None, :]
    cosine = jnp.concatenate([jnp.cos(angles)] * 2, 1)
    sine = jnp.concatenate([-jnp.sin(angles), jnp.sin(angles)], 1)
    order = plain_order.reshape(count, rounds, blk)
    order = jnp.stack(by_place([order[i] for i in range(count)], me), 1)
    return natural[:, None], begin[:, None], order.reshape(rounds, 1, count * blk), cosine, sine


def on_device(
    hidden_in,
    out_grad,
    seq_lengths,
    block_perm,
    first_gain,
    query_weight,
    key_matrix,
    value_matrix,
    output_weight,
    second_gain,
    gate_weight,
    up_weight,
    down_weight,
    clip_limit,
):
    rows, model = hidden_in.shape[1], hidden_in.shape[2]
    count, fsdp_count = lax.axis_size("ctx"), lax.axis_size("fsdp")
    me, place = lax.axis_index("ctx"), lax.axis_index("fsdp")
    me_ref = me.astype(jnp.int32).reshape(1)
    depth = model // count
    zero = jnp.zeros((1,), jnp.int32)
    shard_heads = KEY_VALUE_HEADS // fsdp_count

    def own_rows(weight):
        return lax.dynamic_slice_in_dim(weight, me * depth, depth, 0)

    unit_rows = jnp.concatenate(
        [
            own_rows(query_weight).reshape(depth, shard_heads, REPEAT, HEAD_SIZE),
            own_rows(key_matrix).reshape(depth, shard_heads, 1, HEAD_SIZE),
            own_rows(value_matrix).reshape(depth, shard_heads, 1, HEAD_SIZE),
        ],
        2,
    ).reshape(depth, shard_heads * UNIT)
    unit_rows = gather_rows(unit_rows, place, count)
    unit_slots = gather_ctx(unit_rows)
    gains = jnp.stack([first_gain, second_gain])
    gains = jnp.concatenate(
        by_place([gains] + [swap(gains, "fsdp", d) for d in range(1, fsdp_count)], place), 1
    ).astype(f32)
    first_full, second_full = gains[0], gains[1]
    output_rows = gather_rows(own_rows(output_weight), place, count)
    output_slots = gather_ctx(output_rows)

    hidden_width = gate_weight.shape[1]
    down_depth = hidden_width // count

    def down_piece(d):
        first = (place ^ d) * hidden_width + me * down_depth
        return lax.dynamic_slice_in_dim(down_weight, first, down_depth, 0)

    down_rows = [down_piece(0)] + [
        swap(down_piece(d), "fsdp", d) for d in range(1, fsdp_count)
    ]
    down_slots = gather_ctx(jnp.concatenate(by_place(down_rows, place), 1))

    natural_column, begin_column, key_natural, cosine, sine = attention_layout(
        seq_lengths, block_perm, rows
    )
    half_dim = HEAD_SIZE // 2

    tokens = hidden_in.reshape(rows, model).astype(f32)
    scale_one = rms_scale(tokens)
    unit_one = tokens * scale_one
    normalized = (unit_one * first_full).astype(bf16)
    qkv = slot_matmul(normalized, unit_slots, me_ref, UNIT, bf16, (cosine, sine))
    kv_local = qkv.reshape(rows, KEY_VALUE_HEADS, UNIT)[:, :, REPEAT * HEAD_SIZE :].reshape(
        rows, KEY_VALUE_HEADS * 2 * HEAD_SIZE
    )
    kv_slots = gather_ctx(kv_local)
    attended, best = attend(zero, natural_column, begin_column, key_natural, qkv, kv_slots)
    head_max = jnp.max(best[:, :, :REPEAT, 0], 0).reshape(QUERY_HEADS)
    for mask in bits_down(count):
        head_max = jnp.maximum(head_max, swap(head_max, "ctx", mask))
    for mask in bits_down(fsdp_count):
        head_max = jnp.maximum(head_max, swap(head_max, "fsdp", mask))
    residual = tokens + slot_matmul(attended, output_slots, me_ref, 512, f32)
    scale_two = rms_scale(residual)
    unit_two = residual * scale_two
    normed_two = (unit_two * second_full).astype(bf16)

    grad_out = out_grad.reshape(rows, model)
    others = range(1, fsdp_count)
    grads = [grad_out] + [swap(grad_out, "fsdp", d) for d in others]
    normed = [normed_two] + [swap(normed_two, "fsdp", d) for d in others]
    hidden_parts, gate_parts, up_parts, sums, backs = [], [], [], [], []
    for d in range(fsdp_count):
        grad_hidden = slot_matmul_t(grads[d], down_slots, me_ref, 512, f32)
        gate_act = product(normed[d], gate_weight)
        up_proj = product(normed[d], up_weight)
        sigmoid = jax.nn.sigmoid(gate_act)
        hidden = (gate_act * sigmoid * up_proj).astype(bf16)
        grad_gate = (
            grad_hidden * up_proj * sigmoid * (1.0 + gate_act * (1.0 - sigmoid))
        ).astype(bf16)
        grad_up = (grad_hidden * gate_act * sigmoid).astype(bf16)
        hidden_parts.append(hidden)
        gate_parts.append(grad_gate)
        up_parts.append(grad_up)
        backs.append(product_t(grad_gate, gate_weight) + product_t(grad_up, up_weight))
        sums.append(slot_matmul(hidden, down_slots, me_ref, 512, f32 if d == 0 else bf16))
    grad_normed_two = sum_fsdp(backs)
    result = (residual + sum_fsdp(sums)).astype(bf16)

    second_term = jnp.sum(grad_normed_two * unit_two, 0)
    grad_residual = grad_out.astype(f32) + norm_back(
        grad_normed_two * second_full, unit_two, scale_two
    )
    grad_branch = grad_residual.astype(bf16)
    head_grad = slot_matmul_t(grad_branch, output_slots, me_ref, 512, bf16)
    query_grad, *dkv_slots = attend_back(
        zero, natural_column, begin_column, key_natural, cosine, sine, qkv, head_grad, kv_slots
    )
    dkv = sum_halving(dkv_slots[0], "ctx")
    dkv = dkv.reshape(rows, KEY_VALUE_HEADS, 2, HEAD_SIZE)
    grad_key = dkv[:, :, 0]
    first, second = grad_key[..., :half_dim], grad_key[..., half_dim:]
    cos, sin = cosine[:, None, :half_dim], sine[:, None, half_dim:]
    grad_key = jnp.concatenate([first * cos + second * sin, second * cos - first * sin], -1)
    dqkv = jnp.concatenate(
        [
            query_grad.reshape(rows, KEY_VALUE_HEADS, REPEAT, HEAD_SIZE),
            grad_key[:, :, None].astype(bf16),
            dkv[:, :, 1:].astype(bf16),
        ],
        2,
    ).reshape(rows, KEY_VALUE_HEADS * UNIT)
    grad_normed_one = slot_matmul_t(dqkv, unit_slots, me_ref, 512, f32)
    first_term = jnp.sum(grad_normed_one * unit_one, 0)
    grad_input = grad_residual + norm_back(grad_normed_one * first_full, unit_one, scale_one)

    hidden_all = jnp.concatenate(hidden_parts, 0)
    normed_all = jnp.concatenate(normed, 0)
    grads_all = jnp.concatenate(grads, 0)
    down_sum = down_grad_sum(hidden_all, grads_all, me, count, fsdp_count).astype(bf16)
    bands = count // fsdp_count
    places = [
        (c * fsdp_count + f, (bands * f + c // fsdp_count) * fsdp_count + c % fsdp_count)
        for c in range(count)
        for f in range(fsdp_count)
    ]
    down_grad = lax.ppermute(down_sum, ("ctx", "fsdp"), places).astype(f32)
    gate_grad = weight_grad_sum(normed_all, jnp.concatenate(gate_parts, 0), me, count)
    up_grad = weight_grad_sum(normed_all, jnp.concatenate(up_parts, 0), me, count)

    def over_fsdp(summed):
        width = summed.shape[1] // fsdp_count
        return sum_fsdp(
            [
                lax.dynamic_slice_in_dim(summed, (place ^ d) * width, width, 1)
                for d in range(fsdp_count)
            ]
        )

    output_grad = over_fsdp(weight_grad_sum(attended, grad_branch, me, count))
    unit_grad = over_fsdp(weight_grad_sum(normalized, dqkv, me, count))
    unit_grad = unit_grad.reshape(depth, shard_heads, REPEAT + 2, HEAD_SIZE)
    query_out = unit_grad[:, :, :REPEAT].reshape(depth, -1)
    key_out = unit_grad[:, :, REPEAT].reshape(depth, -1)
    value_out = unit_grad[:, :, REPEAT + 1].reshape(depth, -1)

    first_out = gain_sum(first_term, me, place, count, fsdp_count)
    second_out = gain_sum(second_term, me, place, count, fsdp_count)
    multiplier = jnp.sqrt(clip_limit / jnp.maximum(head_max, clip_limit))
    key_ratio = jnp.min(multiplier.reshape(KEY_VALUE_HEADS, REPEAT), 1)
    return (
        result.reshape(1, rows, model),
        grad_input.astype(bf16).reshape(1, rows, model),
        first_out,
        query_out,
        key_out,
        value_out,
        output_grad,
        second_out,
        gate_grad,
        up_grad,
        down_grad,
        head_max,
        clipped(query_weight, multiplier),
        clipped(key_matrix, key_ratio),
    )


def on_row_of_chips(
    hidden_in,
    out_grad,
    seq_lengths,
    block_perm,
    first_gain,
    query_weight,
    key_matrix,
    value_matrix,
    output_weight,
    second_gain,
    gate_weight,
    up_weight,
    down_weight,
    clip_limit,
):
    rows, model = hidden_in.shape[1], hidden_in.shape[2]
    me, place = lax.axis_index("ctx"), lax.axis_index("fsdp")
    natural, begin, key_natural, cosine, sine = attention_layout(seq_lengths, block_perm, rows)
    tokens_low = hidden_in.reshape(rows, model)
    grad_out = out_grad.reshape(rows, model)
    gains = jnp.pad(jnp.stack([first_gain, second_gain]).astype(f32), ((0, 6), (0, 0)))
    (
        normalized,
        qkv,
        attended,
        best,
        residual,
        normed_two,
        all_gains,
        kv_all,
        unit_rest,
        output_rest,
        down_rest,
        dy_rest,
    ) = attention_row(
        tokens_low,
        gains,
        cosine,
        sine,
        natural,
        begin,
        key_natural,
        query_weight,
        key_matrix,
        value_matrix,
        output_weight,
        down_weight,
        grad_out,
    )
    full = jnp.concatenate(by_place([all_gains[d] for d in range(4)], place), 1)
    first_full, second_full = full[0], full[1]
    tokens = tokens_low.astype(f32)
    scale_one = rms_scale(tokens)
    unit_one = tokens * scale_one
    scale_two = rms_scale(residual)
    unit_two = residual * scale_two
    top = jnp.max(best[:, :, :REPEAT, 0], 0)
    top = jnp.pad(top, ((0, 0), (0, 128 - REPEAT)))

    _, _, _, _, y_own, y_rest, grad_normed_two, _, y_near, gate_grad, up_grad, down_sum, top = (
        feed_forward_row(
            normed_two,
            grad_out,
            dy_rest,
            gate_weight,
            up_weight,
            down_weight,
            down_rest,
            top,
        )
    )
    head_max = top[:, :REPEAT].reshape(QUERY_HEADS)
    second_term = jnp.sum(grad_normed_two * unit_two, 0)
    grad_residual = grad_out.astype(f32) + norm_back(
        grad_normed_two * second_full, unit_two, scale_two
    )
    grad_branch = grad_residual.astype(bf16)
    width = model // 4
    moved, pieces = [], []
    for k in range(4):
        piece = lax.dynamic_slice_in_dim(down_sum, ((me % 4) ^ k) * width, width, 1)
        pieces.append(piece)
    attended, pieces = lax.optimization_barrier((attended, pieces))
    for k, piece in enumerate(pieces):
        pairs = [
            (c * 4 + f, (2 * f + c // 4) * 4 + (c % 4 ^ k)) for c in range(8) for f in range(4)
        ]
        moved.append(lax.ppermute(piece, ("ctx", "fsdp"), pairs))
    down_grad = jnp.concatenate(by_place(moved, place), 0).astype(f32)

    query_grad, dkv, output_out, y_second = attention_back(
        grad_branch,
        attended,
        qkv,
        cosine,
        sine,
        natural,
        begin,
        key_natural,
        kv_all,
        output_weight,
        output_rest,
        y_rest,
    )
    terms = jnp.pad(second_term[None], ((1, 6), (0, 0)))
    query_out, key_out, value_out, grad_normed_one, terms = unit_grads(
        normalized,
        query_grad,
        dkv,
        tokens_low,
        terms,
        query_weight,
        key_matrix,
        value_matrix,
        unit_rest,
    )
    landed = y_near[0].astype(f32) + y_second.astype(f32) + y_near[1].astype(f32)
    result = (residual + y_own + landed).astype(bf16)
    grad_input = grad_residual + norm_back(grad_normed_one * first_full, unit_one, scale_one)
    terms = lax.dynamic_slice_in_dim(
        terms[:2], (me * 4 + place) * (model // 32), model // 32, 1
    )
    first_out, second_out = terms[0], terms[1]
    multiplier = jnp.sqrt(clip_limit / jnp.maximum(head_max, clip_limit))
    key_ratio = jnp.min(multiplier.reshape(KEY_VALUE_HEADS, REPEAT), 1)
    return (
        result.reshape(1, rows, model),
        grad_input.astype(bf16).reshape(1, rows, model),
        first_out,
        query_out,
        key_out,
        value_out,
        output_out,
        second_out,
        gate_grad,
        up_grad,
        down_grad,
        head_max,
        clipped(query_weight, multiplier),
        clipped(key_matrix, key_ratio),
    )


def solution(mesh):
    shard, whole = P(None, "fsdp"), P()
    token, block = P("fsdp", "ctx", None), P("ctx", "fsdp")
    gain = P(("ctx", "fsdp"))
    chips = mesh.shape["ctx"] == 8 and mesh.shape["fsdp"] == 4
    return jax.shard_map(
        on_row_of_chips if chips else on_device,
        mesh=mesh,
        in_specs=(token, token, P("fsdp", None), whole, P("fsdp"))
        + (shard,) * 4
        + (P("fsdp"),)
        + (shard,) * 3
        + (whole,),
        out_specs=(token, token, gain)
        + (block,) * 4
        + (gain,)
        + (block,) * 3
        + (whole, shard, shard),
        check_vma=False,
    )
```
